32 devices in a mesh: vox: 8 (over z, x), smp: 4 (over y, core).
Axes of the slice: x: 2, y: 2, z: 4, core: 2. Of those that a mesh axis runs over, the one named last changes fastest.
Arguments:
- ensemble: float32 [1024, 32, 128], P('vox', 'smp'), may hold values from -6 to 6
- voxel_factor: float32 [1024, 128], P('vox'), may hold values from -6 to 6
- sample_factor: float32 [32, 128], P('smp'), may hold values from -6 to 6
- time_factor: float32 [128, 128], replicated, may hold values from -6 to 6
- weights: float32 [128], replicated, may hold values from 0.005 to 0.02
Outputs:
- voxel_result: float32 [1024, 128], P('vox')
- sample_result: float32 [32, 128], P('smp')
- time_result: float32 [128, 128], replicated
- scale_result: float32 [128], replicated
The draws below stay inside these ranges and needn't reach their ends.
All inputs are finite; a program needn't handle non-finite values. Where the reference program divides by a largest or mean magnitude, that divisor is 1e-20 or more.
Results may differ from the reference program's by a relative error of at most 0.0001.
Values sent between devices are 32-bit elements; how exact they have to be, the bound alone decides.
No kernel may reach another device: no remote copies, remote signals or barrier semaphores. Data moves between devices by JAX's collectives and lax.ppermute only.
A program may use at most 64 MiB of HBM per device.

```python
import math
import jax
import jax.numpy as jnp
from jax import lax

VOX_DEV = 128
TIMES = 128
RANK = 128
SWEEPS = 1
VOXELS = 1024
SAMPLES = 32
N_VOX = 8


def levels(own_key, shape, pieces, low, high):
    gain, own = 1.0, jax.random.fold_in(own_key, 6)
    for dim, parts in pieces:
        steps = jnp.exp(jax.random.uniform(jax.random.fold_in(own, dim), (parts,), jnp.float32, low / len(pieces), high / len(pieces)))
        gain = gain * jnp.repeat(steps, shape[dim] // parts).reshape([-1 if axis == dim else 1 for axis in range(len(shape))])
    return gain


def bell_draw(rng, extent, scale, limit, shards=(), held_as=jnp.bfloat16):
    factor_of = levels(rng, extent, shards, -0.22, 0.18) if shards else 1.0
    drawn = jax.random.normal(rng, extent, jnp.float32) * scale * factor_of
    return jnp.minimum(jnp.maximum(drawn, -limit), limit).astype(held_as)


def setup_inputs(seed: int = 0) -> dict:
    key_list = jax.random.split(jax.random.key(seed), 6)
    ensemble = bell_draw(key_list[0], (VOXELS, SAMPLES, TIMES), 1.0, 6.0, ((0, 8), (1, 4)), jnp.float32)
    voxel_factor = bell_draw(key_list[1], (VOXELS, RANK), 1.0, 6.0, ((0, 8),), jnp.float32)
    sample_factor = bell_draw(key_list[2], (SAMPLES, RANK), 1.0, 6.0, ((0, 4),), jnp.float32)
    time_factor = bell_draw(key_list[3], (TIMES, RANK), 1.0, 6.0, (), jnp.float32)
    weights = jnp.clip(jnp.exp(jax.random.uniform(key_list[4], (RANK,), jnp.float32, math.log(0.005), math.log(0.02))), 0.005, 0.02)
    return dict(ensemble=ensemble, voxel_factor=voxel_factor, sample_factor=sample_factor, time_factor=time_factor, weights=weights)


HIGH = lax.Precision.HIGHEST

def descend(factor, terms, hadamard, weights):
    coupled = weights[:, None] * weights[None, :] * hadamard
    step_size = 1.0 / jnp.max(lax.optimization_barrier(jnp.sum(jnp.abs(coupled), axis=1)))
    product = jnp.dot(factor, coupled, precision=HIGH, preferred_element_type=jnp.float32)
    return factor - step_size * (product - terms * weights[None, :])

def rescale(moved, gram, row_count):
    scales = jnp.sqrt(jnp.diagonal(gram) / row_count + 1e-06)
    return (moved / scales[None, :], gram / (scales[:, None] * scales[None, :]), scales)

def reference(ensemble, voxel_factor, sample_factor, time_factor, weights):
    blocks = ensemble.reshape(N_VOX, VOX_DEV, SAMPLES, TIMES)
    gram_b = jnp.dot(sample_factor.T, sample_factor, precision=HIGH, preferred_element_type=jnp.float32)
    gram_c = jnp.dot(time_factor.T, time_factor, precision=HIGH, preferred_element_type=jnp.float32)
    for sweep_index in range(SWEEPS):
        current_b = sample_factor
        current_c = time_factor

        def voxel_block(block):
            contracted = jnp.einsum('ijk,kr->ijr', block, current_c, precision=HIGH)
            return jnp.einsum('ijr,jr->ir', contracted, current_b, precision=HIGH)
        terms_a = lax.map(voxel_block, blocks).reshape(VOXELS, RANK)
        moved = descend(voxel_factor, terms_a, gram_b * gram_c, weights)
        gram = jnp.dot(moved.T, moved, precision=HIGH, preferred_element_type=jnp.float32)
        voxel_factor, gram_a, scales = rescale(moved, gram, VOXELS)
        weights = weights * scales
        voxel_blocks = voxel_factor.reshape(N_VOX, VOX_DEV, RANK)

        def sample_block(pair):
            block, rows_a = pair
            contracted = jnp.einsum('ijk,kr->ijr', block, current_c, precision=HIGH)
            return jnp.einsum('ijr,ir->jr', contracted, rows_a, precision=HIGH)
        terms_b = lax.optimization_barrier(jnp.sum(lax.map(sample_block, (blocks, voxel_blocks)), axis=0))
        moved = descend(sample_factor, terms_b, gram_a * gram_c, weights)
        gram = jnp.dot(moved.T, moved, precision=HIGH, preferred_element_type=jnp.float32)
        sample_factor, gram_b, scales = rescale(moved, gram, SAMPLES)
        weights = weights * scales
        newer_b = sample_factor

        def time_block(pair):
            block, rows_a = pair
            paired = rows_a[:, None, :] * newer_b[None, :, :]
            return jnp.einsum('ijk,ijr->kr', block, paired, precision=HIGH)
        terms_c = lax.optimization_barrier(jnp.sum(lax.map(time_block, (blocks, voxel_blocks)), axis=0))
        moved = descend(time_factor, terms_c, gram_a * gram_b, weights)
        gram = jnp.dot(moved.T, moved, precision=HIGH, preferred_element_type=jnp.float32)
        time_factor, gram_c, scales = rescale(moved, gram, TIMES)
        weights = weights * scales
    return (voxel_factor, sample_factor, time_factor, weights)
```

```python
import jax
import jax.numpy as jnp
from jax import lax
from jax.sharding import PartitionSpec as P

HIGH = lax.Precision.HIGHEST


def exchange_sum(values, axes, bits_per_round):
    count = lax.axis_size(axes)
    if count & (count - 1):
        return lax.psum(values, axes)
    low = 1
    while low < count:
        width = min(bits_per_round, (count // low).bit_length() - 1)
        parts = [values]
        for pattern in range(1, 1 << width):
            pairs = [(i, i ^ (pattern * low)) for i in range(count)]
            parts.append(lax.ppermute(values, axes, pairs))
        while len(parts) > 1:
            parts = [a + b for a, b in zip(parts[::2], parts[1::2])]
        values = parts[0]
        low <<= width
    return values


def descend(factor, terms, hadamard, weights):
    coupled = weights[:, None] * weights[None, :] * hadamard
    step_size = 1.0 / jnp.max(jnp.sum(jnp.abs(coupled), axis=1))
    product = jnp.dot(factor, coupled, precision=HIGH, preferred_element_type=jnp.float32)
    return factor - step_size * (product - terms * weights[None, :])


def scales_of(moved_gram, row_count):
    eye = jnp.eye(moved_gram.shape[0], dtype=jnp.float32)
    return jnp.sqrt(jnp.sum(moved_gram * eye, axis=0) / row_count + 1e-06)


def rescale(moved, gram, row_count):
    scales = scales_of(gram, row_count)
    return (moved / scales[None, :], gram / (scales[:, None] * scales[None, :]), scales)


def local_gram(moved):
    return jnp.dot(moved.T, moved, precision=HIGH, preferred_element_type=jnp.float32)


def per_device(ensemble, voxel_factor, sample_factor, time_factor, weights):
    vox_rows, smp_rows, time_count = ensemble.shape
    rank_count = voxel_factor.shape[1]
    voxel_total = vox_rows * lax.axis_size("vox")
    sample_total = smp_rows * lax.axis_size("smp")
    vox_count = lax.axis_size("vox")
    flat = ensemble.reshape(vox_rows * smp_rows, time_count)
    gram_c = local_gram(time_factor)
    contracted = jnp.dot(flat, time_factor, precision=HIGH, preferred_element_type=jnp.float32)
    contracted = contracted.reshape(vox_rows, smp_rows, rank_count)
    partial_value = jnp.einsum("ijr,jr->ir", contracted, sample_factor, precision=HIGH)
    both = exchange_sum(jnp.concatenate([partial_value, local_gram(sample_factor)], axis=0), "smp", 2)
    terms_a, gram_b = both[:vox_rows], both[vox_rows:]
    moved = descend(voxel_factor, terms_a, gram_b * gram_c, weights)
    raw_b = jnp.einsum("ijr,ir->jr", contracted, moved, precision=HIGH)
    both = exchange_sum(jnp.concatenate([local_gram(moved), raw_b], axis=0), "vox", 1)
    gram, summed_b = both[:rank_count], both[rank_count:]
    voxel_factor, gram_a, scales = rescale(moved, gram, voxel_total)
    terms_b = summed_b / scales[None, :]
    weights = weights * scales
    moved = descend(sample_factor, terms_b, gram_a * gram_c, weights)
    paired = (voxel_factor[:, None, :] * moved[None, :, :]).reshape(vox_rows * smp_rows, rank_count)
    raw_c = jnp.einsum("nk,nr->kr", flat, paired, precision=HIGH)
    both = exchange_sum(jnp.concatenate([raw_c, local_gram(moved)], axis=0), ("vox", "smp"), 1)
    summed_c, gram_sum = both[:time_count], both[time_count:]
    sample_factor, gram_b, scales = rescale(moved, gram_sum / vox_count, sample_total)
    terms_c = summed_c / scales[None, :]
    weights = weights * scales
    moved = descend(time_factor, terms_c, gram_a * gram_b, weights)
    time_factor, gram_c, scales = rescale(moved, local_gram(moved), time_count)
    weights = weights * scales
    return (voxel_factor, sample_factor, time_factor, weights)


def solution(mesh):
    return jax.shard_map(
        per_device,
        mesh=mesh,
        in_specs=(P("vox", "smp", None), P("vox", None), P("smp", None), P(), P()),
        out_specs=(P("vox", None), P("smp", None), P(), P()),
        check_vma=False,
    )
```

```python
import jax
import jax.numpy as jnp
from jax import lax
from jax.sharding import PartitionSpec as P

HIGH = lax.Precision.HIGHEST


def exchange_sum(values, axes, bits_per_round):
    count = lax.axis_size(axes)
    if count & (count - 1):
        return lax.psum(values, axes)
    low = 1
    while low < count:
        width = min(bits_per_round, (count // low).bit_length() - 1)
        parts = [values]
        for pattern in range(1, 1 << width):
            pairs = [(i, i ^ (pattern * low)) for i in range(count)]
            parts.append(lax.ppermute(values, axes, pairs))
        while len(parts) > 1:
            parts = [a + b for a, b in zip(parts[::2], parts[1::2])]
        values = parts[0]
        low <<= width
    return values


def scatter_sum(values, axes):
    count = lax.axis_size(axes)
    rows, columns = values.shape
    if rows % count:
        return exchange_sum(values, axes, 1)
    pieces = values.reshape(count, rows // count, columns)
    held = jnp.sum(lax.all_to_all(pieces, axes, 0, 0), axis=0)
    return lax.all_to_all(jnp.broadcast_to(held, pieces.shape), axes, 0, 0).reshape(rows, columns)


def descend(factor, terms, hadamard, weights):
    coupled = weights[:, None] * weights[None, :] * hadamard
    step_size = 1.0 / jnp.max(jnp.sum(jnp.abs(coupled), axis=1))
    product = jnp.dot(factor, coupled, precision=HIGH, preferred_element_type=jnp.float32)
    return factor - step_size * (product - terms * weights[None, :])


def scales_of(moved_gram, row_count):
    eye = jnp.eye(moved_gram.shape[0], dtype=jnp.float32)
    return jnp.sqrt(jnp.sum(moved_gram * eye, axis=0) / row_count + 1e-06)


def rescale(moved, gram, row_count):
    scales = scales_of(gram, row_count)
    return (moved / scales[None, :], gram / (scales[:, None] * scales[None, :]), scales)


def local_gram(moved):
    return jnp.dot(moved.T, moved, precision=HIGH, preferred_element_type=jnp.float32)


def per_device(ensemble, voxel_factor, sample_factor, time_factor, weights):
    vox_rows, smp_rows, time_count = ensemble.shape
    rank_count = voxel_factor.shape[1]
    voxel_total = vox_rows * lax.axis_size("vox")
    sample_total = smp_rows * lax.axis_size("smp")
    vox_count = lax.axis_size("vox")
    flat = ensemble.reshape(vox_rows * smp_rows, time_count)
    gram_c = local_gram(time_factor)
    contracted = jnp.dot(flat, time_factor, precision=HIGH, preferred_element_type=jnp.float32)
    contracted = contracted.reshape(vox_rows, smp_rows, rank_count)
    partial_value = jnp.einsum("ijr,jr->ir", contracted, sample_factor, precision=HIGH)
    both = exchange_sum(jnp.concatenate([partial_value, local_gram(sample_factor)], axis=0), "smp", 1)
    terms_a, gram_b = both[:vox_rows], both[vox_rows:]
    moved = descend(voxel_factor, terms_a, gram_b * gram_c, weights)
    raw_b = jnp.einsum("ijr,ir->jr", contracted, moved, precision=HIGH)
    both = scatter_sum(jnp.concatenate([local_gram(moved), raw_b], axis=0), "vox")
    gram, summed_b = both[:rank_count], both[rank_count:]
    voxel_factor, gram_a, scales = rescale(moved, gram, voxel_total)
    terms_b = summed_b / scales[None, :]
    weights = weights * scales
    moved = descend(sample_factor, terms_b, gram_a * gram_c, weights)
    paired = (voxel_factor[:, None, :] * moved[None, :, :]).reshape(vox_rows * smp_rows, rank_count)
    raw_c = jnp.einsum("nk,nr->kr", flat, paired, precision=HIGH)
    both = scatter_sum(jnp.concatenate([raw_c, local_gram(moved)], axis=0), ("vox", "smp"))
    summed_c, gram_sum = both[:time_count], both[time_count:]
    sample_factor, gram_b, scales = rescale(moved, gram_sum / vox_count, sample_total)
    terms_c = summed_c / scales[None, :]
    weights = weights * scales
    moved = descend(time_factor, terms_c, gram_a * gram_b, weights)
    time_factor, gram_c, scales = rescale(moved, local_gram(moved), time_count)
    weights = weights * scales
    return (voxel_factor, sample_factor, time_factor, weights)


def solution(mesh):
    return jax.shard_map(
        per_device,
        mesh=mesh,
        in_specs=(P("vox", "smp", None), P("vox", None), P("smp", None), P(), P()),
        out_specs=(P("vox", None), P("smp", None), P(), P()),
        check_vma=False,
    )
```

```python
import jax
import jax.numpy as jnp
from jax import lax
from jax.experimental import pallas as pl
from jax.experimental.pallas import tpu as pltpu
from jax.sharding import PartitionSpec as P

HIGH = lax.Precision.HIGHEST
F32 = jnp.float32
VMEM_LIMIT = 12 * 1024 * 1024


def dot(a, b):
    return jnp.dot(a, b, precision=HIGH, preferred_element_type=F32)


def dot_rows(a, b):
    return lax.dot_general(a, b, (((0,), (0,)), ((), ())), precision=HIGH, preferred_element_type=F32)


def step_of(coupled):
    sums = jnp.sum(jnp.abs(coupled), axis=0, keepdims=True)
    return 1.0 / jnp.max(sums, axis=1, keepdims=True)


def diagonal_row(gram):
    rows = lax.broadcasted_iota(jnp.int32, gram.shape, 0)
    columns = lax.broadcasted_iota(jnp.int32, gram.shape, 1)
    return jnp.sum(jnp.where(rows == columns, gram, 0.0), axis=0, keepdims=True)


def call(kernel, outs, operands, flops, scratch=(), in_hbm=0):
    spaces = [pltpu.HBM if i < in_hbm else pltpu.VMEM for i in range(len(operands))]
    placed = [pltpu.with_memory_space_constraint(x, space) for x, space in zip(operands, spaces)]
    specs = [pl.BlockSpec(memory_space=space) for space in spaces]
    return pl.pallas_call(
        kernel,
        out_shape=outs,
        in_specs=specs,
        out_specs=[pl.BlockSpec(memory_space=pltpu.VMEM)] * len(outs),
        scratch_shapes=list(scratch),
        compiler_params=pltpu.CompilerParams(vmem_limit_bytes=VMEM_LIMIT),
        cost_estimate=pl.CostEstimate(flops=flops, bytes_accessed=1 << 16, transcendentals=0),
    )(*placed)


def near(shape):
    return pltpu.VMEM(shape, F32)


def far(shape):
    return jax.ShapeDtypeStruct(shape, F32)


def in_order(position, own, received, scratch):
    size = scratch.shape[0]
    half = size // 2
    block = size // lax.axis_size("smp")
    for p in range(size // block):
        source = own if p * block < half else received
        start = p * block % half
        scratch[pl.ds(pl.multiple_of((position ^ p) * block, block), block), :] = source[start : start + block, :]
    return scratch[...]


def partner(values, axes, bit):
    count = lax.axis_size(axes)
    return lax.ppermute(values, axes, [(i, i ^ bit) for i in range(count)])


def bits_of(count):
    if count & (count - 1):
        raise ValueError("axis size")
    return [1 << b for b in range(count.bit_length() - 1)]


def per_device(ensemble, voxel_factor, sample_factor, time_factor, weights):
    vox_rows, smp_rows, times = ensemble.shape
    rank = voxel_factor.shape[1]
    flat_rows = vox_rows * smp_rows
    vox_count, smp_count = lax.axis_size("vox"), lax.axis_size("smp")
    vox_total, smp_total = vox_rows * vox_count, smp_rows * smp_count
    vox_bits, smp_bits = bits_of(vox_count), bits_of(smp_count)
    gram_half, time_half = rank // 2, times // 2
    chunks = 4 if vox_rows % 32 == 0 else 1
    chunk_vox = vox_rows // chunks
    chunk_rows = chunk_vox * smp_rows
    position = lambda: lax.axis_index("smp")
    wide = (rank, rank)

    def open_kernel(x_hbm, c_hbm, b_hbm, x, send, con, c, sems):
        copies = [pltpu.make_async_copy(c_hbm, c, sems.at[0])]
        copies += [pltpu.make_async_copy(b_hbm, send.at[pl.ds(vox_rows, smp_rows), :], sems.at[1])]
        for n in range(chunks):
            part = pl.ds(n * chunk_rows, chunk_rows)
            copies.append(pltpu.make_async_copy(x_hbm.at[part, :], x.at[part, :], sems.at[2 + n]))
        for copy in copies:
            copy.start()
        copies[0].wait()
        copies[1].wait()
        factor = c[...]
        b = send[pl.ds(vox_rows, smp_rows), :]
        for n in range(chunks):
            copies[2 + n].wait()
            total = None
            rows = pl.ds(n * chunk_vox, chunk_vox)
            for j in range(smp_rows):
                block = x[pl.ds(n * chunk_rows + j, chunk_vox, stride=smp_rows), :]
                made = dot(block, factor)
                con[j, rows, :] = made
                made = made * b[j : j + 1, :]
                total = made if total is None else total + made
            send[rows, :] = total

    flat = ensemble.reshape(flat_rows, times)
    x, sent, con = call(
        open_kernel,
        (near((flat_rows, times)), near((vox_rows + smp_rows, rank)), near((smp_rows, vox_rows, rank))),
        (flat, time_factor, sample_factor),
        2 * flat_rows * times * rank * 6,
        scratch=(near((times, rank)), pltpu.SemaphoreType.DMA((2 + chunks,))),
        in_hbm=3,
    )

    def weigh_kernel(c, w, outer, outer_c):
        row = w[...]
        squared = dot_rows(row, row)
        outer[...] = squared
        outer_c[...] = squared * dot_rows(c[...], c[...])

    w_row = weights.reshape(1, rank)
    outer, outer_c = call(weigh_kernel, (near(wide), near(wide)), (time_factor, w_row), 2 * rank * rank * times * 6)

    for bit in smp_bits[:-1]:
        got = partner(sent, "smp", bit)
        sent = jnp.concatenate([sent[:vox_rows] + got[:vox_rows], sent[vox_rows:], got[vox_rows:]], axis=0)
    got = partner(sent, "smp", smp_bits[-1])

    def voxel_kernel(own, other, a, w, outer_c, con, moved_out, keep, all_b, gram_all):
        b = in_order(position(), own.at[pl.ds(vox_rows, smp_total // 2), :], other.at[pl.ds(vox_rows, smp_total // 2), :], all_b)
        coupled = outer_c[...] * dot_rows(b, b)
        terms = own[:vox_rows, :] + other[:vox_rows, :]
        moved = a[...] - step_of(coupled) * (dot(a[...], coupled) - terms * w[...])
        moved_out[...] = moved
        gram_all[...] = dot_rows(moved, moved)
        mine = (position() & 1) * gram_half
        keep[:gram_half, :] = gram_all[pl.ds(pl.multiple_of(mine, gram_half), gram_half), :]
        for j in range(smp_rows):
            keep[gram_half + j : gram_half + j + 1, :] = jnp.sum(con[j] * moved, axis=0, keepdims=True)

    moved_a, sums = call(
        voxel_kernel,
        (near((vox_rows, rank)), near((gram_half + smp_rows, rank))),
        (sent, got, voxel_factor, w_row, outer_c, con),
        2 * rank * rank * vox_rows * 12,
        scratch=(near((smp_total, rank)), near(wide)),
    )

    def time_kernel(x, moved, each):
        for j in range(smp_rows):
            each[j] = dot_rows(x[pl.ds(j, vox_rows, stride=smp_rows), :], moved[...])

    (each,) = call(
        time_kernel, (near((smp_rows, times, rank)),), (x, moved_a), 2 * flat_rows * times * rank * 6
    )

    for bit in vox_bits:
        sums = sums + partner(sums, "vox", bit)
    other_half = partner(sums[:gram_half], "smp", 1)

    def sample_kernel(sums, half, b, w, outer_c, each, moved_out, gram_out, keep, give):
        mine = (position() & 1) * gram_half
        gram_out[pl.ds(pl.multiple_of(mine, gram_half), gram_half), :] = sums[:gram_half, :]
        gram_out[pl.ds(pl.multiple_of(gram_half - mine, gram_half), gram_half), :] = half[...]
        coupled = outer_c[...] * gram_out[...]
        moved = b[...] - step_of(coupled) * (dot(b[...], coupled) - sums[gram_half:, :] * w[...])
        moved_out[...] = moved
        first = (position() & 1) * time_half
        for start, out in ((time_half - first, give), (first, keep)):
            total = None
            for j in range(smp_rows):
                made = each[j, pl.ds(pl.multiple_of(start, time_half), time_half), :] * moved[j : j + 1, :]
                total = made if total is None else total + made
            out[:time_half, :] = total
        give[time_half:, :] = moved

    moved_b, gram_a, kept, given = call(
        sample_kernel,
        (near((smp_rows, rank)), near(wide), near((time_half, rank)), near((time_half + smp_rows, rank))),
        (sums, other_half, sample_factor, w_row, outer_c, each),
        2 * rank * rank * smp_rows * 6,
    )

    def scale_kernel(gram, moved, outer, result, scales_out, weighed):
        scales = jnp.sqrt(diagonal_row(gram[...]) / vox_total + 1e-06)
        scales_out[...] = scales
        result[...] = moved[...] / scales
        weighed[...] = outer[...] * gram[...]

    voxel_result, scales_a, weighed = call(
        scale_kernel,
        (far((vox_rows, rank)), near((1, rank)), near(wide)),
        (gram_a, moved_a, outer),
        vox_rows * rank * 8,
    )

    got = partner(given, "smp", 1)
    kept = kept + got[:time_half]
    rows_b = jnp.concatenate([moved_b, got[time_half:]], axis=0)
    for bit in smp_bits[1:]:
        got = partner(jnp.concatenate([kept, rows_b], axis=0), "smp", bit)
        kept = kept + got[:time_half]
        rows_b = jnp.concatenate([rows_b, got[time_half:]], axis=0)
    for bit in vox_bits:
        kept = kept + partner(kept, "vox", bit)
    other_half = partner(kept, "smp", 1)

    def last_kernel(kept, half, rows, moved_b, c, w, weighed, scales_a, b_out, c_out, w_out, all_b, terms):
        half_rows = smp_total // 2
        b = in_order(position(), rows.at[pl.ds(0, half_rows), :], rows.at[pl.ds(half_rows, half_rows), :], all_b)
        coupled = weighed[...] * dot_rows(b, b)
        scales_b = jnp.sqrt(jnp.sum(b * b, axis=0, keepdims=True) / smp_total + 1e-06)
        b_out[...] = moved_b[...] / scales_b
        mine = (position() & 1) * time_half
        terms[pl.ds(pl.multiple_of(mine, time_half), time_half), :] = kept[...]
        terms[pl.ds(pl.multiple_of(time_half - mine, time_half), time_half), :] = half[...]
        moved = c[...] - step_of(coupled) * (dot(c[...], coupled) - terms[...] * w[...])
        scales_c = jnp.sqrt(jnp.sum(moved * moved, axis=0, keepdims=True) / times + 1e-06)
        c_out[...] = moved / scales_c
        w_out[...] = w[...] * scales_a[...] * scales_b * scales_c

    sample_result, time_result, scale_result = call(
        last_kernel,
        (far((smp_rows, rank)), far((times, rank)), far((1, rank))),
        (kept, other_half, rows_b, moved_b, time_factor, w_row, weighed, scales_a),
        2 * rank * rank * times * 6,
        scratch=(near((smp_total, rank)), near((times, rank))),
    )
    return voxel_result, sample_result, time_result, scale_result.reshape(rank)


def solution(mesh):
    return jax.shard_map(
        per_device,
        mesh=mesh,
        in_specs=(P("vox", "smp", None), P("vox", None), P("smp", None), P(), P()),
        out_specs=(P("vox", None), P("smp", None), P(), P()),
        check_vma=False,
    )
```

```python
import jax
import jax.numpy as jnp
from jax import lax
from jax.experimental import pallas as pl
from jax.experimental.pallas import tpu as pltpu
from jax.sharding import PartitionSpec as P

HIGH = lax.Precision.HIGHEST
F32 = jnp.float32
VMEM_LIMIT = 12 * 1024 * 1024
ALL = ("vox", "smp")


def dot(a, b):
    return jnp.dot(a, b, precision=HIGH, preferred_element_type=F32)


def dot_rows(a, b):
    return lax.dot_general(a, b, (((0,), (0,)), ((), ())), precision=HIGH, preferred_element_type=F32)


def step_of(coupled):
    sums = jnp.sum(jnp.abs(coupled), axis=0, keepdims=True)
    return 1.0 / jnp.max(sums, axis=1, keepdims=True)


def diagonal_row(gram):
    rows = lax.broadcasted_iota(jnp.int32, gram.shape, 0)
    columns = lax.broadcasted_iota(jnp.int32, gram.shape, 1)
    return jnp.sum(jnp.where(rows == columns, gram, 0.0), axis=0, keepdims=True)


def call(kernel, outs, operands, flops, scratch=(), in_hbm=0):
    spaces = [pltpu.HBM if i < in_hbm else pltpu.VMEM for i in range(len(operands))]
    placed = [pltpu.with_memory_space_constraint(x, space) for x, space in zip(operands, spaces)]
    specs = [pl.BlockSpec(memory_space=space) for space in spaces]
    return pl.pallas_call(
        kernel,
        out_shape=outs,
        in_specs=specs,
        out_specs=[pl.BlockSpec(memory_space=pltpu.VMEM)] * len(outs),
        scratch_shapes=list(scratch),
        compiler_params=pltpu.CompilerParams(vmem_limit_bytes=VMEM_LIMIT),
        cost_estimate=pl.CostEstimate(flops=flops, bytes_accessed=1 << 16, transcendentals=0),
    )(*placed)


def near(*shape):
    return pltpu.VMEM(shape, F32)


def far(*shape):
    return jax.ShapeDtypeStruct(shape, F32)


def bits_of(count):
    if count & (count - 1):
        raise ValueError("axis size")
    return [1 << b for b in range(count.bit_length() - 1)]


def groups_of(bits, size=2):
    return [bits[i : i + size] for i in range(0, len(bits), size)]


def masks_of(group):
    masks = [0]
    for bit in group:
        masks = masks + [mask | bit for mask in masks]
    return masks


def send(values, holder, mask=0):
    count = lax.axis_size(ALL)
    pairs = [(i, i ^ 1 ^ mask) for i in range(count) if i & 1 == holder]
    return lax.ppermute(values, ALL, pairs)


def fan(values, holder, masks):
    sent = [send(values, holder, mask) for mask in reversed(masks)]
    return sent[::-1]


def tree(parts):
    while len(parts) > 1:
        parts = [a + b for a, b in zip(parts[::2], parts[1::2])]
    return parts[0]


def smp_index():
    return lax.axis_index("smp")


def on_core(core, own, got):
    return jnp.where(smp_index() & 1 == core, own, got)


def in_order(rows, scratch, chips):
    block = scratch.shape[0] // chips
    chip = smp_index() // 2
    for p in range(chips):
        scratch[pl.ds(pl.multiple_of((chip ^ p) * block, block), block), :] = rows[p * block : (p + 1) * block, :]
    return scratch[...]


def per_device(ensemble, voxel_factor, sample_factor, time_factor, weights):
    vox_rows, smp_rows, times = ensemble.shape
    rank = voxel_factor.shape[1]
    flat_rows = vox_rows * smp_rows
    vox_count, smp_count = lax.axis_size("vox"), lax.axis_size("smp")
    vox_total, smp_total = vox_rows * vox_count, smp_rows * smp_count
    chips, chip_rows = smp_count // 2, 2 * smp_rows
    chip_bits = bits_of(smp_count)[1:]
    vox_bits = [bit * smp_count for bit in bits_of(vox_count)]
    chunks = 4 if vox_rows % 32 == 0 else 1
    chunk_vox = vox_rows // chunks
    chunk_rows = chunk_vox * smp_rows
    w_row = weights.reshape(1, rank)

    def open_kernel(x_hbm, c_hbm, b_hbm, x, out, con, c, sems):
        copies = [pltpu.make_async_copy(c_hbm, c, sems.at[0])]
        copies += [pltpu.make_async_copy(b_hbm, out.at[pl.ds(vox_rows, smp_rows), :], sems.at[1])]
        for n in range(chunks):
            part = pl.ds(n * chunk_rows, chunk_rows)
            copies.append(pltpu.make_async_copy(x_hbm.at[part, :], x.at[part, :], sems.at[2 + n]))
        for copy in copies:
            copy.start()
        copies[0].wait()
        copies[1].wait()
        factor = c[...]
        b = out[pl.ds(vox_rows, smp_rows), :]
        for n in range(chunks):
            copies[2 + n].wait()
            total = None
            rows = pl.ds(n * chunk_vox, chunk_vox)
            for j in range(smp_rows):
                block = x[pl.ds(n * chunk_rows + j, chunk_vox, stride=smp_rows), :]
                made = dot(block, factor)
                con[j, rows, :] = made
                made = made * b[j : j + 1, :]
                total = made if total is None else total + made
            out[rows, :] = total

    x, opened, con = call(
        open_kernel,
        (near(flat_rows, times), near(vox_rows + smp_rows, rank), near(smp_rows, vox_rows, rank)),
        (ensemble.reshape(flat_rows, times), time_factor, sample_factor),
        2 * flat_rows * times * rank * 6,
        scratch=(near(times, rank), pltpu.SemaphoreType.DMA((2 + chunks,))),
        in_hbm=3,
    )

    def weigh_kernel(c, w, outer, outer_c):
        squared = dot_rows(w[...], w[...])
        outer[...] = squared
        outer_c[...] = squared * dot_rows(c[...], c[...])

    outer, outer_c = call(
        weigh_kernel, (near(rank, rank), near(rank, rank)), (time_factor, w_row), 2 * rank * rank * times * 6
    )

    got = send(opened, 0)
    terms = opened[:vox_rows] + got[:vox_rows]
    rows_b = jnp.concatenate([got[vox_rows:], opened[vox_rows:]], axis=0)
    holder = 1
    for group in groups_of(chip_bits):
        parts = fan(jnp.concatenate([terms, rows_b], axis=0), holder, masks_of(group))
        terms = tree([part[:vox_rows] for part in parts])
        rows_b = jnp.concatenate([part[vox_rows:] for part in parts], axis=0)
        holder ^= 1
    voxel_core = holder
    mate_con = send(con, 1 - voxel_core)

    def voxel_kernel(terms, rows, a, w, outer_c, con, mate_con, moved_out, chip_b, out, all_b):
        b = in_order(rows, all_b, chips)
        chip_b[...] = all_b[pl.ds(pl.multiple_of(smp_index() // 2 * chip_rows, chip_rows), chip_rows), :]
        coupled = outer_c[...] * dot_rows(b, b)
        moved = a[...] - step_of(coupled) * (dot(a[...], coupled) - terms[...] * w[...])
        moved_out[...] = moved
        out[:rank, :] = dot_rows(moved, moved)
        for core in range(2):
            for j in range(smp_rows):
                block = con[j] if core == voxel_core else mate_con[j]
                row = rank + core * smp_rows + j
                out[row : row + 1, :] = jnp.sum(block * moved, axis=0, keepdims=True)

    moved_a, chip_b, sums = call(
        voxel_kernel,
        (near(vox_rows, rank), near(chip_rows, rank), near(rank + chip_rows, rank)),
        (terms, rows_b, voxel_factor, w_row, outer_c, con, mate_con),
        2 * rank * rank * vox_rows * 12,
        scratch=(near(smp_total, rank),),
    )
    mate_moved_a = send(moved_a, voxel_core)

    for group in groups_of(vox_bits):
        sums = tree(fan(sums, holder, masks_of(group)))
        holder ^= 1
    sample_core = holder
    if sample_core != voxel_core:
        chip_b = send(chip_b, voxel_core)
    mate_x = send(x, 1 - sample_core)

    def time_kernel(x, mate_x, moved, mate_moved, each):
        moved = on_core(voxel_core, moved[...], mate_moved[...])
        for core in range(2):
            for j in range(smp_rows):
                source = x if core == sample_core else mate_x
                each[core * smp_rows + j] = dot_rows(source[pl.ds(j, vox_rows, stride=smp_rows), :], moved)

    (each,) = call(
        time_kernel,
        (near(chip_rows, times, rank),),
        (x, mate_x, moved_a, mate_moved_a),
        4 * flat_rows * times * rank * 6,
    )

    def sample_kernel(sums, b, w, outer_c, each, out):
        coupled = outer_c[...] * sums[:rank, :]
        moved = b[...] - step_of(coupled) * (dot(b[...], coupled) - sums[rank:, :] * w[...])
        out[times:, :] = moved
        total = None
        for j in range(chip_rows):
            made = each[j] * moved[j : j + 1, :]
            total = made if total is None else total + made
        out[:times, :] = total

    (payload,) = call(
        sample_kernel,
        (near(times + chip_rows, rank),),
        (sums, chip_b, w_row, outer_c, each),
        2 * rank * rank * chip_rows * 6,
    )
    mate_sums = send(sums, sample_core)

    def scale_kernel(sums, mate_sums, moved, mate_moved, outer, result, scales_out, weighed):
        gram = on_core(sample_core, sums[:rank, :], mate_sums[:rank, :])
        scales = jnp.sqrt(diagonal_row(gram) / vox_total + 1e-06)
        scales_out[...] = scales
        result[...] = on_core(voxel_core, moved[...], mate_moved[...]) / scales
        weighed[...] = outer[...] * gram

    voxel_result, scales_a, weighed = call(
        scale_kernel,
        (far(vox_rows, rank), near(1, rank), near(rank, rank)),
        (sums, mate_sums, moved_a, mate_moved_a, outer),
        vox_rows * rank * 8,
    )

    terms, rows_b, rows_core = payload[:times], payload[times:], holder
    smp_mask = sum(chip_bits)
    for group in groups_of(chip_bits + vox_bits):
        masks = masks_of(group)
        with_rows = any(mask & smp_mask for mask in masks)
        parts = fan(jnp.concatenate([terms, rows_b], axis=0) if with_rows else terms, holder, masks)
        terms = tree([part[:times] for part in parts])
        holder ^= 1
        if with_rows:
            parts = [part for part, mask in zip(parts, masks) if not mask & ~smp_mask]
            rows_b = jnp.concatenate([part[times:] for part in parts], axis=0)
            rows_core = holder
    last_core = holder
    mate_rows_b = send(rows_b, rows_core)
    mate_terms = send(terms, last_core)

    def last_kernel(terms, mate_terms, rows, mate_rows, c, w, weighed, scales_a, b_out, c_out, w_out, all_b):
        b = in_order(on_core(rows_core, rows[...], mate_rows[...]), all_b, chips)
        coupled = weighed[...] * dot_rows(b, b)
        scales_b = jnp.sqrt(jnp.sum(b * b, axis=0, keepdims=True) / smp_total + 1e-06)
        b_out[...] = all_b[pl.ds(pl.multiple_of(smp_index() * smp_rows, smp_rows), smp_rows), :] / scales_b
        summed = on_core(last_core, terms[...], mate_terms[...])
        moved = c[...] - step_of(coupled) * (dot(c[...], coupled) - summed * w[...])
        scales_c = jnp.sqrt(jnp.sum(moved * moved, axis=0, keepdims=True) / times + 1e-06)
        c_out[...] = moved / scales_c
        w_out[...] = w[...] * scales_a[...] * scales_b * scales_c

    sample_result, time_result, scale_result = call(
        last_kernel,
        (far(smp_rows, rank), far(times, rank), far(1, rank)),
        (terms, mate_terms, rows_b, mate_rows_b, time_factor, w_row, weighed, scales_a),
        2 * rank * rank * times * 6,
        scratch=(near(smp_total, rank),),
    )
    return voxel_result, sample_result, time_result, scale_result.reshape(rank)


def solution(mesh):
    return jax.shard_map(
        per_device,
        mesh=mesh,
        in_specs=(P("vox", "smp", None), P("vox", None), P("smp", None), P(), P()),
        out_specs=(P("vox", None), P("smp", None), P(), P()),
        check_vma=False,
    )
```

```python
import jax
import jax.numpy as jnp
from jax import lax
from jax.experimental import pallas as pl
from jax.experimental.pallas import tpu as pltpu
from jax.sharding import PartitionSpec as P

HIGH = lax.Precision.HIGHEST
F32 = jnp.float32
VMEM_LIMIT = 12 * 1024 * 1024
ALL = ("vox", "smp")


def dot(a, b):
    return jnp.dot(a, b, precision=HIGH, preferred_element_type=F32)


def dot_rows(a, b):
    return lax.dot_general(a, b, (((0,), (0,)), ((), ())), precision=HIGH, preferred_element_type=F32)


def step_of(coupled):
    sums = jnp.sum(jnp.abs(coupled), axis=0, keepdims=True)
    return 1.0 / jnp.max(sums, axis=1, keepdims=True)


def diagonal_row(gram):
    rows = lax.broadcasted_iota(jnp.int32, gram.shape, 0)
    columns = lax.broadcasted_iota(jnp.int32, gram.shape, 1)
    return jnp.sum(jnp.where(rows == columns, gram, 0.0), axis=0, keepdims=True)


def call(kernel, outs, operands, flops, scratch=(), in_hbm=0):
    spaces = [pltpu.HBM if i < in_hbm else pltpu.VMEM for i in range(len(operands))]
    placed = [pltpu.with_memory_space_constraint(x, space) for x, space in zip(operands, spaces)]
    specs = [pl.BlockSpec(memory_space=space) for space in spaces]
    return pl.pallas_call(
        kernel,
        out_shape=outs,
        in_specs=specs,
        out_specs=[pl.BlockSpec(memory_space=pltpu.VMEM)] * len(outs),
        scratch_shapes=list(scratch),
        compiler_params=pltpu.CompilerParams(vmem_limit_bytes=VMEM_LIMIT),
        cost_estimate=pl.CostEstimate(flops=flops, bytes_accessed=1 << 16, transcendentals=0),
    )(*placed)


def near(*shape):
    return pltpu.VMEM(shape, F32)


def far(*shape):
    return jax.ShapeDtypeStruct(shape, F32)


def bits_of(count):
    if count & (count - 1):
        raise ValueError("axis size")
    return [1 << b for b in range(count.bit_length() - 1)]


def groups_of(bits, size=1):
    return [bits[i : i + size] for i in range(0, len(bits), size)]


def masks_of(group):
    masks = [0]
    for bit in group:
        masks = masks + [mask | bit for mask in masks]
    return masks


def send(values, holder, mask=0):
    count = lax.axis_size(ALL)
    pairs = [(i, i ^ 1 ^ mask if i & 1 == holder else i ^ 1) for i in range(count)]
    return lax.ppermute(values, ALL, pairs)


def fan(values, holder, masks):
    return [send(values, holder, mask) for mask in masks]


def tree(parts):
    parts = parts[::-1]
    while len(parts) > 1:
        parts = [a + b for a, b in zip(parts[::2], parts[1::2])]
    return parts[0]


def smp_index():
    return lax.axis_index("smp")


def on_core(core, own, got):
    return jnp.where(smp_index() & 1 == core, own, got)


def in_order(rows, scratch, chips):
    block = scratch.shape[0] // chips
    chip = smp_index() // 2
    for p in range(chips):
        scratch[pl.ds(pl.multiple_of((chip ^ (chips - 1 - p)) * block, block), block), :] = rows[p * block : (p + 1) * block, :]
    return scratch[...]


def per_device(ensemble, voxel_factor, sample_factor, time_factor, weights):
    vox_rows, smp_rows, times = ensemble.shape
    rank = voxel_factor.shape[1]
    flat_rows = vox_rows * smp_rows
    vox_count, smp_count = lax.axis_size("vox"), lax.axis_size("smp")
    vox_total, smp_total = vox_rows * vox_count, smp_rows * smp_count
    chips, chip_rows = smp_count // 2, 2 * smp_rows
    chip_bits = bits_of(smp_count)[1:]
    vox_bits = [bit * smp_count for bit in bits_of(vox_count)]
    chunks = 4 if vox_rows % 32 == 0 else 1
    chunk_vox = vox_rows // chunks
    chunk_rows = chunk_vox * smp_rows
    w_row = weights.reshape(1, rank)

    def open_kernel(x_hbm, c_hbm, b_hbm, x, out, con, c, sems):
        copies = [pltpu.make_async_copy(c_hbm, c, sems.at[0])]
        copies += [pltpu.make_async_copy(b_hbm, out.at[pl.ds(vox_rows, smp_rows), :], sems.at[1])]
        for n in range(chunks):
            part = pl.ds(n * chunk_rows, chunk_rows)
            copies.append(pltpu.make_async_copy(x_hbm.at[part, :], x.at[part, :], sems.at[2 + n]))
        for copy in copies:
            copy.start()
        copies[0].wait()
        copies[1].wait()
        factor = c[...]
        b = out[pl.ds(vox_rows, smp_rows), :]
        for n in range(chunks):
            copies[2 + n].wait()
            total = None
            rows = pl.ds(n * chunk_vox, chunk_vox)
            for j in range(smp_rows):
                block = x[pl.ds(n * chunk_rows + j, chunk_vox, stride=smp_rows), :]
                made = dot(block, factor)
                con[j, rows, :] = made
                made = made * b[j : j + 1, :]
                total = made if total is None else total + made
            out[rows, :] = total

    x, opened, con = call(
        open_kernel,
        (near(flat_rows, times), near(vox_rows + smp_rows, rank), near(smp_rows, vox_rows, rank)),
        (ensemble.reshape(flat_rows, times), time_factor, sample_factor),
        2 * flat_rows * times * rank * 6,
        scratch=(near(times, rank), pltpu.SemaphoreType.DMA((2 + chunks,))),
        in_hbm=3,
    )

    def weigh_kernel(c, w, outer, outer_c):
        squared = dot_rows(w[...], w[...])
        outer[...] = squared
        outer_c[...] = squared * dot_rows(c[...], c[...])

    outer, outer_c = call(
        weigh_kernel, (near(rank, rank), near(rank, rank)), (time_factor, w_row), 2 * rank * rank * times * 6
    )

    got = send(opened, 0)
    terms = opened[:vox_rows] + got[:vox_rows]
    rows_b = jnp.concatenate([got[vox_rows:], opened[vox_rows:]], axis=0)
    holder = 1
    for group in groups_of(chip_bits):
        parts = fan(jnp.concatenate([terms, rows_b], axis=0), holder, masks_of(group))
        terms = tree([part[:vox_rows] for part in parts])
        rows_b = jnp.concatenate([part[vox_rows:] for part in parts[::-1]], axis=0)
        holder ^= 1
    voxel_core = holder
    mate_con = send(con, 1 - voxel_core)

    def voxel_kernel(terms, rows, a, w, outer_c, con, mate_con, moved_out, chip_b, out, all_b):
        b = in_order(rows, all_b, chips)
        chip_b[...] = all_b[pl.ds(pl.multiple_of(smp_index() // 2 * chip_rows, chip_rows), chip_rows), :]
        coupled = outer_c[...] * dot_rows(b, b)
        moved = a[...] - step_of(coupled) * (dot(a[...], coupled) - terms[...] * w[...])
        moved_out[...] = moved
        out[:rank, :] = dot_rows(moved, moved)
        for core in range(2):
            for j in range(smp_rows):
                block = con[j] if core == voxel_core else mate_con[j]
                row = rank + core * smp_rows + j
                out[row : row + 1, :] = jnp.sum(block * moved, axis=0, keepdims=True)

    moved_a, chip_b, sums = call(
        voxel_kernel,
        (near(vox_rows, rank), near(chip_rows, rank), near(rank + chip_rows, rank)),
        (terms, rows_b, voxel_factor, w_row, outer_c, con, mate_con),
        2 * rank * rank * vox_rows * 12,
        scratch=(near(smp_total, rank),),
    )
    mate_moved_a = send(moved_a, voxel_core)

    for group in groups_of(vox_bits):
        sums = tree(fan(sums, holder, masks_of(group)))
        holder ^= 1
    sample_core = holder
    if sample_core != voxel_core:
        chip_b = send(chip_b, voxel_core)
    mate_x = send(x, 1 - sample_core)

    def time_kernel(x, mate_x, moved, mate_moved, each):
        moved = on_core(voxel_core, moved[...], mate_moved[...])
        for core in range(2):
            for j in range(smp_rows):
                source = x if core == sample_core else mate_x
                each[core * smp_rows + j] = dot_rows(source[pl.ds(j, vox_rows, stride=smp_rows), :], moved)

    (each,) = call(
        time_kernel,
        (near(chip_rows, times, rank),),
        (x, mate_x, moved_a, mate_moved_a),
        4 * flat_rows * times * rank * 6,
    )

    def sample_kernel(sums, b, w, outer_c, each, out):
        coupled = outer_c[...] * sums[:rank, :]
        moved = b[...] - step_of(coupled) * (dot(b[...], coupled) - sums[rank:, :] * w[...])
        out[times:, :] = moved
        total = None
        for j in range(chip_rows):
            made = each[j] * moved[j : j + 1, :]
            total = made if total is None else total + made
        out[:times, :] = total

    (payload,) = call(
        sample_kernel,
        (near(times + chip_rows, rank),),
        (sums, chip_b, w_row, outer_c, each),
        2 * rank * rank * chip_rows * 6,
    )
    mate_sums = send(sums, sample_core)

    def scale_kernel(sums, mate_sums, moved, mate_moved, outer, result, scales_out, weighed):
        gram = on_core(sample_core, sums[:rank, :], mate_sums[:rank, :])
        scales = jnp.sqrt(diagonal_row(gram) / vox_total + 1e-06)
        scales_out[...] = scales
        result[...] = on_core(voxel_core, moved[...], mate_moved[...]) / scales
        weighed[...] = outer[...] * gram

    voxel_result, scales_a, weighed = call(
        scale_kernel,
        (far(vox_rows, rank), near(1, rank), near(rank, rank)),
        (sums, mate_sums, moved_a, mate_moved_a, outer),
        vox_rows * rank * 8,
    )

    terms, rows_b, rows_core = payload[:times], payload[times:], holder
    smp_mask = sum(chip_bits)
    for group in groups_of(chip_bits + vox_bits):
        masks = masks_of(group)
        with_rows = any(mask & smp_mask for mask in masks)
        parts = fan(jnp.concatenate([terms, rows_b], axis=0) if with_rows else terms, holder, masks)
        terms = tree([part[:times] for part in parts])
        holder ^= 1
        if with_rows:
            parts = [part for part, mask in zip(parts, masks) if not mask & ~smp_mask]
            rows_b = jnp.concatenate([part[times:] for part in parts[::-1]], axis=0)
            rows_core = holder
    last_core = holder
    mate_rows_b = send(rows_b, rows_core)
    mate_terms = send(terms, last_core)

    def last_kernel(terms, mate_terms, rows, mate_rows, c, w, weighed, scales_a, b_out, c_out, w_out, all_b):
        b = in_order(on_core(rows_core, rows[...], mate_rows[...]), all_b, chips)
        coupled = weighed[...] * dot_rows(b, b)
        scales_b = jnp.sqrt(jnp.sum(b * b, axis=0, keepdims=True) / smp_total + 1e-06)
        b_out[...] = all_b[pl.ds(pl.multiple_of(smp_index() * smp_rows, smp_rows), smp_rows), :] / scales_b
        summed = on_core(last_core, terms[...], mate_terms[...])
        moved = c[...] - step_of(coupled) * (dot(c[...], coupled) - summed * w[...])
        scales_c = jnp.sqrt(jnp.sum(moved * moved, axis=0, keepdims=True) / times + 1e-06)
        c_out[...] = moved / scales_c
        w_out[...] = w[...] * scales_a[...] * scales_b * scales_c

    sample_result, time_result, scale_result = call(
        last_kernel,
        (far(smp_rows, rank), far(times, rank), far(1, rank)),
        (terms, mate_terms, rows_b, mate_rows_b, time_factor, w_row, weighed, scales_a),
        2 * rank * rank * times * 6,
        scratch=(near(smp_total, rank),),
    )
    return voxel_result, sample_result, time_result, scale_result.reshape(rank)


def solution(mesh):
    return jax.shard_map(
        per_device,
        mesh=mesh,
        in_specs=(P("vox", "smp", None), P("vox", None), P("smp", None), P(), P()),
        out_specs=(P("vox", None), P("smp", None), P(), P()),
        check_vma=False,
    )
```

```python
import jax
import jax.numpy as jnp
from jax import lax
from jax.experimental import pallas as pl
from jax.experimental.pallas import tpu as pltpu
from jax.sharding import PartitionSpec as P

HIGH = lax.Precision.HIGHEST
F32 = jnp.float32
VMEM_LIMIT = 12 * 1024 * 1024
ALL = ("vox", "smp")


def dot(a, b):
    return jnp.dot(a, b, precision=HIGH, preferred_element_type=F32)


def dot_rows(a, b):
    return lax.dot_general(a, b, (((0,), (0,)), ((), ())), precision=HIGH, preferred_element_type=F32)


def step_of(coupled):
    sums = jnp.sum(jnp.abs(coupled), axis=0, keepdims=True)
    return 1.0 / jnp.max(sums, axis=1, keepdims=True)


def diagonal_row(gram):
    rows = lax.broadcasted_iota(jnp.int32, gram.shape, 0)
    columns = lax.broadcasted_iota(jnp.int32, gram.shape, 1)
    return jnp.sum(jnp.where(rows == columns, gram, 0.0), axis=0, keepdims=True)


def call(kernel, outs, operands, flops, scratch=(), in_hbm=0):
    spaces = [pltpu.HBM if i < in_hbm else pltpu.VMEM for i in range(len(operands))]
    placed = [pltpu.with_memory_space_constraint(x, space) for x, space in zip(operands, spaces)]
    specs = [pl.BlockSpec(memory_space=space) for space in spaces]
    return pl.pallas_call(
        kernel,
        out_shape=outs,
        in_specs=specs,
        out_specs=[pl.BlockSpec(memory_space=pltpu.VMEM)] * len(outs),
        scratch_shapes=list(scratch),
        compiler_params=pltpu.CompilerParams(vmem_limit_bytes=VMEM_LIMIT),
        cost_estimate=pl.CostEstimate(flops=flops, bytes_accessed=1 << 16, transcendentals=0),
    )(*placed)


def near(*shape):
    return pltpu.VMEM(shape, F32)


def far(*shape):
    return jax.ShapeDtypeStruct(shape, F32)


def bits_of(count):
    if count & (count - 1):
        raise ValueError("axis size")
    return [1 << b for b in range(count.bit_length() - 1)]


def groups_of(bits, size=2):
    return [bits[i : i + size] for i in range(0, len(bits), size)]


def masks_of(group):
    masks = [0]
    for bit in group:
        masks = masks + [mask | bit for mask in masks]
    return masks


def swap(values):
    return lax.ppermute(values, ALL, [(i, i ^ 1) for i in range(lax.axis_size(ALL))])


def cross(values, mask):
    pairs = [(i, i ^ 1 ^ mask if i & 1 else i ^ 1) for i in range(lax.axis_size(ALL))]
    return lax.ppermute(values, ALL, pairs)


def tree(parts):
    while len(parts) > 1:
        parts = [a + b for a, b in zip(parts[::2], parts[1::2])]
    return parts[0]


def smp_index():
    return lax.axis_index("smp")


def from_core_0(own, got):
    return jnp.where(smp_index() & 1 == 0, own, got)


def in_order(rows, scratch, chips):
    block = scratch.shape[0] // chips
    chip = smp_index() // 2
    for p in range(chips):
        scratch[pl.ds(pl.multiple_of((chip ^ p) * block, block), block), :] = rows[p * block : (p + 1) * block, :]
    return scratch[...]


def per_device(ensemble, voxel_factor, sample_factor, time_factor, weights):
    vox_rows, smp_rows, times = ensemble.shape
    rank = voxel_factor.shape[1]
    flat_rows = vox_rows * smp_rows
    vox_count, smp_count = lax.axis_size("vox"), lax.axis_size("smp")
    vox_total, smp_total = vox_rows * vox_count, smp_rows * smp_count
    chips, chip_rows = smp_count // 2, 2 * smp_rows
    chip_bits = bits_of(smp_count)[1:]
    vox_bits = [bit * smp_count for bit in bits_of(vox_count)]
    chunks = 4 if vox_rows % 32 == 0 else 1
    chunk_vox = vox_rows // chunks
    chunk_rows = chunk_vox * smp_rows

    def open_kernel(x_hbm, c_hbm, b_hbm, a_hbm, w_hbm, x, c, a, w, out, con, sems):
        copies = [pltpu.make_async_copy(c_hbm, c, sems.at[0])]
        copies += [pltpu.make_async_copy(b_hbm, out.at[pl.ds(vox_rows, smp_rows), :], sems.at[1])]
        for n in range(chunks):
            part = pl.ds(n * chunk_rows, chunk_rows)
            copies.append(pltpu.make_async_copy(x_hbm.at[part, :], x.at[part, :], sems.at[2 + n]))
        copies.append(pltpu.make_async_copy(a_hbm, a, sems.at[2 + chunks]))
        copies.append(pltpu.make_async_copy(w_hbm, w, sems.at[3 + chunks]))
        for copy in copies:
            copy.start()
        copies[0].wait()
        copies[1].wait()
        factor = c[...]
        b = out[pl.ds(vox_rows, smp_rows), :]
        for n in range(chunks):
            copies[2 + n].wait()
            total = None
            rows = pl.ds(n * chunk_vox, chunk_vox)
            for j in range(smp_rows):
                block = x[pl.ds(n * chunk_rows + j, chunk_vox, stride=smp_rows), :]
                made = dot(block, factor)
                con[j, rows, :] = made
                made = made * b[j : j + 1, :]
                total = made if total is None else total + made
            out[rows, :] = total
        copies[2 + chunks].wait()
        copies[3 + chunks].wait()

    x, c_near, a_near, w_row, opened, con = call(
        open_kernel,
        (
            near(flat_rows, times),
            near(times, rank),
            near(vox_rows, rank),
            near(1, rank),
            near(vox_rows + smp_rows, rank),
            near(smp_rows, vox_rows, rank),
        ),
        (ensemble.reshape(flat_rows, times), time_factor, sample_factor, voxel_factor, weights.reshape(1, rank)),
        2 * flat_rows * times * rank * 6,
        scratch=(pltpu.SemaphoreType.DMA((4 + chunks,)),),
        in_hbm=5,
    )

    def weigh_kernel(c, w, outer, outer_c):
        squared = dot_rows(w[...], w[...])
        outer[...] = squared
        outer_c[...] = squared * dot_rows(c[...], c[...])

    outer, outer_c = call(
        weigh_kernel, (near(rank, rank), near(rank, rank)), (c_near, w_row), 2 * rank * rank * times * 6
    )

    got = swap(opened)
    terms = opened[:vox_rows] + got[:vox_rows]
    rows_b = jnp.concatenate([got[vox_rows:], opened[vox_rows:]], axis=0)
    handed = jnp.concatenate([terms, rows_b], axis=0)
    rows_b = jnp.concatenate([opened[vox_rows:], got[vox_rows:]], axis=0)
    for group in groups_of(chip_bits):
        if handed is None:
            handed = swap(jnp.concatenate([terms, rows_b], axis=0))
        parts = [cross(handed, mask) for mask in masks_of(group)[1:]]
        terms = tree([terms] + [part[:vox_rows] for part in parts])
        rows_b = jnp.concatenate([rows_b] + [part[vox_rows:] for part in parts], axis=0)
        handed = None
    mate_con = swap(con)

    def voxel_kernel(terms, rows, a, w, outer_c, con, mate_con, moved_out, chip_b, out, all_b):
        b = in_order(rows, all_b, chips)
        chip_b[...] = all_b[pl.ds(pl.multiple_of(smp_index() // 2 * chip_rows, chip_rows), chip_rows), :]
        coupled = outer_c[...] * dot_rows(b, b)
        moved = a[...] - step_of(coupled) * (dot(a[...], coupled) - terms[...] * w[...])
        moved_out[...] = moved
        out[:rank, :] = dot_rows(moved, moved)
        for core in range(2):
            for j in range(smp_rows):
                row = rank + core * smp_rows + j
                out[row : row + 1, :] = jnp.sum((con, mate_con)[core][j] * moved, axis=0, keepdims=True)

    moved_a, chip_b, sums = call(
        voxel_kernel,
        (near(vox_rows, rank), near(chip_rows, rank), near(rank + chip_rows, rank)),
        (terms, rows_b, a_near, w_row, outer_c, con, mate_con),
        2 * rank * rank * vox_rows * 12,
        scratch=(near(smp_total, rank),),
    )

    for group in groups_of(vox_bits):
        handed = swap(sums)
        sums = tree([sums] + [cross(handed, mask) for mask in masks_of(group)[1:]])
    mate_x = swap(x)

    def time_kernel(x, mate_x, moved, each):
        for core in range(2):
            for j in range(smp_rows):
                block = (x, mate_x)[core][pl.ds(j, vox_rows, stride=smp_rows), :]
                each[core * smp_rows + j] = dot_rows(block, moved[...])

    (each,) = call(
        time_kernel, (near(chip_rows, times, rank),), (x, mate_x, moved_a), 4 * flat_rows * times * rank * 6
    )

    def sample_kernel(sums, b, w, outer_c, each, out):
        coupled = outer_c[...] * sums[:rank, :]
        moved = b[...] - step_of(coupled) * (dot(b[...], coupled) - sums[rank:, :] * w[...])
        out[times:, :] = moved
        total = None
        for j in range(chip_rows):
            made = each[j] * moved[j : j + 1, :]
            total = made if total is None else total + made
        out[:times, :] = total

    (payload,) = call(
        sample_kernel,
        (near(times + chip_rows, rank),),
        (sums, chip_b, w_row, outer_c, each),
        2 * rank * rank * chip_rows * 6,
    )
    mate_sums = swap(sums)
    mate_moved_a = swap(moved_a)

    def scale_kernel(sums, mate_sums, moved, mate_moved, outer, result, scales_out, weighed):
        gram = from_core_0(sums[:rank, :], mate_sums[:rank, :])
        scales = jnp.sqrt(diagonal_row(gram) / vox_total + 1e-06)
        scales_out[...] = scales
        result[...] = from_core_0(moved[...], mate_moved[...]) / scales
        weighed[...] = outer[...] * gram

    voxel_result, scales_a, weighed = call(
        scale_kernel,
        (far(vox_rows, rank), near(1, rank), near(rank, rank)),
        (sums, mate_sums, moved_a, mate_moved_a, outer),
        vox_rows * rank * 8,
    )

    terms, rows_b = payload[:times], payload[times:]
    smp_mask = sum(chip_bits)
    for group in groups_of(chip_bits + vox_bits):
        masks = masks_of(group)[1:]
        with_rows = any(mask & smp_mask for mask in masks)
        handed = swap(jnp.concatenate([terms, rows_b], axis=0) if with_rows else terms)
        parts = [cross(handed, mask) for mask in masks]
        terms = tree([terms] + [part[:times] for part in parts])
        if with_rows:
            parts = [part for part, mask in zip(parts, masks) if not mask & ~smp_mask]
            rows_b = jnp.concatenate([rows_b] + [part[times:] for part in parts], axis=0)
    mate_rows_b = swap(rows_b)
    mate_terms = swap(terms)

    def last_kernel(terms, mate_terms, rows, mate_rows, c, w, weighed, scales_a, b_out, c_out, w_out, all_b):
        b = in_order(from_core_0(rows[...], mate_rows[...]), all_b, chips)
        coupled = weighed[...] * dot_rows(b, b)
        scales_b = jnp.sqrt(jnp.sum(b * b, axis=0, keepdims=True) / smp_total + 1e-06)
        b_out[...] = all_b[pl.ds(pl.multiple_of(smp_index() * smp_rows, smp_rows), smp_rows), :] / scales_b
        summed = from_core_0(terms[...], mate_terms[...])
        moved = c[...] - step_of(coupled) * (dot(c[...], coupled) - summed * w[...])
        scales_c = jnp.sqrt(jnp.sum(moved * moved, axis=0, keepdims=True) / times + 1e-06)
        c_out[...] = moved / scales_c
        w_out[...] = w[...] * scales_a[...] * scales_b * scales_c

    sample_result, time_result, scale_result = call(
        last_kernel,
        (far(smp_rows, rank), far(times, rank), far(1, rank)),
        (terms, mate_terms, rows_b, mate_rows_b, c_near, w_row, weighed, scales_a),
        2 * rank * rank * times * 6,
        scratch=(near(smp_total, rank),),
    )
    return voxel_result, sample_result, time_result, scale_result.reshape(rank)


def solution(mesh):
    return jax.shard_map(
        per_device,
        mesh=mesh,
        in_specs=(P("vox", "smp", None), P("vox", None), P("smp", None), P(), P()),
        out_specs=(P("vox", None), P("smp", None), P(), P()),
        check_vma=False,
    )
```

```python
import jax
import jax.numpy as jnp
from jax import lax
from jax.experimental import pallas as pl
from jax.experimental.pallas import tpu as pltpu
from jax.sharding import PartitionSpec as P

HIGH = lax.Precision.HIGHEST
F32 = jnp.float32
VMEM_LIMIT = 12 * 1024 * 1024
ALL = ("vox", "smp")


def dot(a, b):
    return jnp.dot(a, b, precision=HIGH, preferred_element_type=F32)


def dot_rows(a, b):
    return lax.dot_general(a, b, (((0,), (0,)), ((), ())), precision=HIGH, preferred_element_type=F32)


def step_of(coupled):
    sums = jnp.sum(jnp.abs(coupled), axis=0, keepdims=True)
    return 1.0 / jnp.max(sums, axis=1, keepdims=True)


def diagonal_row(gram):
    rows = lax.broadcasted_iota(jnp.int32, gram.shape, 0)
    columns = lax.broadcasted_iota(jnp.int32, gram.shape, 1)
    return jnp.sum(jnp.where(rows == columns, gram, 0.0), axis=0, keepdims=True)


def call(kernel, outs, operands, flops, scratch=(), in_hbm=0):
    spaces = [pltpu.HBM if i < in_hbm else pltpu.VMEM for i in range(len(operands))]
    placed = [pltpu.with_memory_space_constraint(x, space) for x, space in zip(operands, spaces)]
    specs = [pl.BlockSpec(memory_space=space) for space in spaces]
    return pl.pallas_call(
        kernel,
        out_shape=outs,
        in_specs=specs,
        out_specs=[pl.BlockSpec(memory_space=pltpu.VMEM)] * len(outs),
        scratch_shapes=list(scratch),
        compiler_params=pltpu.CompilerParams(vmem_limit_bytes=VMEM_LIMIT),
        cost_estimate=pl.CostEstimate(flops=flops, bytes_accessed=1 << 16, transcendentals=0),
    )(*placed)


def near(*shape):
    return pltpu.VMEM(shape, F32)


def far(*shape):
    return jax.ShapeDtypeStruct(shape, F32)


def bits_of(count):
    if count & (count - 1):
        raise ValueError("axis size")
    return [1 << b for b in range(count.bit_length() - 1)]


def groups_of(bits, size=2):
    return [bits[i : i + size] for i in range(0, len(bits), size)]


def masks_of(group):
    masks = [0]
    for bit in group:
        masks = masks + [mask | bit for mask in masks]
    return masks


def swap(values):
    return lax.ppermute(values, ALL, [(i, i ^ 1) for i in range(lax.axis_size(ALL))])


def exchange(values, mask):
    pairs = [(i, i ^ mask if i & 1 else i) for i in range(lax.axis_size(ALL))]
    return lax.ppermute(values, ALL, pairs)


def exchange_sum(values, group):
    return tree([values] + [exchange(values, mask) for mask in masks_of(group)[1:]])


def tree(parts):
    while len(parts) > 1:
        parts = [a + b for a, b in zip(parts[::2], parts[1::2])]
    return parts[0]


def smp_index():
    return lax.axis_index("smp")


def from_core_1(own, got):
    return jnp.where(smp_index() & 1 == 1, own, got)


def pack(gram):
    half = gram.shape[0] // 2
    rows = lax.broadcasted_iota(jnp.int32, (half, 2 * half), 0)
    columns = lax.broadcasted_iota(jnp.int32, (half, 2 * half), 1)
    top, bottom = gram[:half], gram[half:]
    packed = jnp.where(rows <= columns, top, pltpu.roll(bottom, half, 1))
    return packed, jnp.sum(jnp.where(columns == rows + half, bottom, 0.0), axis=0, keepdims=True)


def unpack(packed, diagonal):
    half = packed.shape[0]
    rows = lax.broadcasted_iota(jnp.int32, packed.shape, 0)
    columns = lax.broadcasted_iota(jnp.int32, packed.shape, 1)
    turned = jnp.concatenate([packed, packed], axis=0).T
    top = jnp.where(rows <= columns, packed, turned[:half])
    corner = jnp.where(columns < rows + half, pltpu.roll(packed, half, 1), turned[:half])
    corner = jnp.where(columns == rows + half, diagonal, corner)
    return jnp.concatenate([top, jnp.where(columns < half, turned[half:], corner)], axis=0)


def in_order(rows, scratch, chips):
    block = scratch.shape[0] // chips
    chip = smp_index() // 2
    for p in range(chips):
        scratch[pl.ds(pl.multiple_of((chip ^ p) * block, block), block), :] = rows[p * block : (p + 1) * block, :]
    return scratch[...]


def per_device(ensemble, voxel_factor, sample_factor, time_factor, weights):
    vox_rows, smp_rows, times = ensemble.shape
    rank = voxel_factor.shape[1]
    flat_rows = vox_rows * smp_rows
    vox_count, smp_count = lax.axis_size("vox"), lax.axis_size("smp")
    vox_total, smp_total = vox_rows * vox_count, smp_rows * smp_count
    chips, chip_rows = smp_count // 2, 2 * smp_rows
    chip_bits = bits_of(smp_count)[1:]
    vox_bits = [bit * smp_count for bit in bits_of(vox_count)]
    chunks = 4 if vox_rows % 32 == 0 else 1
    chunk_vox = vox_rows // chunks
    chunk_rows = chunk_vox * smp_rows

    def open_kernel(x_hbm, c_hbm, b_hbm, a_hbm, w_hbm, x, c, a, w, out, con, sems):
        copies = [pltpu.make_async_copy(c_hbm, c, sems.at[0])]
        copies += [pltpu.make_async_copy(b_hbm, out.at[pl.ds(vox_rows, smp_rows), :], sems.at[1])]
        for n in range(chunks):
            part = pl.ds(n * chunk_rows, chunk_rows)
            copies.append(pltpu.make_async_copy(x_hbm.at[part, :], x.at[part, :], sems.at[2 + n]))
        copies.append(pltpu.make_async_copy(a_hbm, a, sems.at[2 + chunks]))
        copies.append(pltpu.make_async_copy(w_hbm, w, sems.at[3 + chunks]))
        for copy in copies:
            copy.start()
        copies[0].wait()
        copies[1].wait()
        factor = c[...]
        b = out[pl.ds(vox_rows, smp_rows), :]
        for n in range(chunks):
            copies[2 + n].wait()
            total = None
            rows = pl.ds(n * chunk_vox, chunk_vox)
            for j in range(smp_rows):
                block = x[pl.ds(n * chunk_rows + j, chunk_vox, stride=smp_rows), :]
                made = dot(block, factor)
                con[j, rows, :] = made
                made = made * b[j : j + 1, :]
                total = made if total is None else total + made
            out[rows, :] = total
        copies[2 + chunks].wait()
        copies[3 + chunks].wait()

    x, c_near, a_near, w_row, opened, con = call(
        open_kernel,
        (
            near(flat_rows, times),
            near(times, rank),
            near(vox_rows, rank),
            near(1, rank),
            near(vox_rows + smp_rows, rank),
            near(smp_rows, vox_rows, rank),
        ),
        (ensemble.reshape(flat_rows, times), time_factor, sample_factor, voxel_factor, weights.reshape(1, rank)),
        2 * flat_rows * times * rank * 6,
        scratch=(pltpu.SemaphoreType.DMA((4 + chunks,)),),
        in_hbm=5,
    )

    def weigh_kernel(c, w, outer, outer_c):
        squared = dot_rows(w[...], w[...])
        outer[...] = squared
        outer_c[...] = squared * dot_rows(c[...], c[...])

    outer, outer_c = call(
        weigh_kernel, (near(rank, rank), near(rank, rank)), (c_near, w_row), 2 * rank * rank * times * 6
    )

    got = swap(opened)
    terms = opened[:vox_rows] + got[:vox_rows]
    rows_b = jnp.concatenate([got[vox_rows:], opened[vox_rows:]], axis=0)
    for group in groups_of(chip_bits):
        packet = jnp.concatenate([terms, rows_b], axis=0)
        parts = [exchange(packet, mask) for mask in masks_of(group)[1:]]
        terms = tree([terms] + [part[:vox_rows] for part in parts])
        rows_b = jnp.concatenate([rows_b] + [part[vox_rows:] for part in parts], axis=0)
    mate_con = swap(con)

    half, sums_rows = rank // 2, rank // 2 + chip_rows

    def voxel_kernel(terms, rows, a, w, outer_c, con, mate_con, moved_out, chip_b, out, all_b):
        b = in_order(rows, all_b, chips)
        chip_b[...] = all_b[pl.ds(pl.multiple_of(smp_index() // 2 * chip_rows, chip_rows), chip_rows), :]
        coupled = outer_c[...] * dot_rows(b, b)
        moved = a[...] - step_of(coupled) * (dot(a[...], coupled) - terms[...] * w[...])
        moved_out[...] = moved
        packed, diagonal = pack(dot_rows(moved, moved))
        out[:half, :] = packed
        for core in range(2):
            for j in range(smp_rows):
                row = half + core * smp_rows + j
                out[row : row + 1, :] = jnp.sum((mate_con, con)[core][j] * moved, axis=0, keepdims=True)
        out[sums_rows:, :] = jnp.broadcast_to(diagonal, (8, rank))

    moved_a, chip_b, sums = call(
        voxel_kernel,
        (near(vox_rows, rank), near(chip_rows, rank), near(sums_rows + 8, rank)),
        (terms, rows_b, a_near, w_row, outer_c, con, mate_con),
        2 * rank * rank * vox_rows * 12,
        scratch=(near(smp_total, rank),),
    )

    for group in groups_of(vox_bits):
        sums = exchange_sum(sums, group)
    mate_x = swap(x)

    def time_kernel(x, mate_x, moved, each):
        for core in range(2):
            for j in range(smp_rows):
                block = (mate_x, x)[core][pl.ds(j, vox_rows, stride=smp_rows), :]
                each[core * smp_rows + j] = dot_rows(block, moved[...])

    (each,) = call(
        time_kernel, (near(chip_rows, times, rank),), (x, mate_x, moved_a), 4 * flat_rows * times * rank * 6
    )

    def sample_kernel(sums, b, w, outer_c, each, gram_out, out):
        gram_out[...] = unpack(sums[:half, :], sums[sums_rows : sums_rows + 1, :])
        coupled = outer_c[...] * gram_out[...]
        moved = b[...] - step_of(coupled) * (dot(b[...], coupled) - sums[half:sums_rows, :] * w[...])
        out[times:, :] = moved
        total = None
        for j in range(chip_rows):
            made = each[j] * moved[j : j + 1, :]
            total = made if total is None else total + made
        out[:times, :] = total

    gram_a, payload = call(
        sample_kernel,
        (near(rank, rank), near(times + chip_rows, rank)),
        (sums, chip_b, w_row, outer_c, each),
        2 * rank * rank * chip_rows * 6,
    )
    mate_gram_a = swap(gram_a)
    mate_moved_a = swap(moved_a)

    def scale_kernel(gram, mate_gram, moved, mate_moved, outer, result, scales_out, weighed):
        gram = from_core_1(gram[...], mate_gram[...])
        scales = jnp.sqrt(diagonal_row(gram) / vox_total + 1e-06)
        scales_out[...] = scales
        result[...] = from_core_1(moved[...], mate_moved[...]) / scales
        weighed[...] = outer[...] * gram

    voxel_result, scales_a, weighed = call(
        scale_kernel,
        (far(vox_rows, rank), near(1, rank), near(rank, rank)),
        (gram_a, mate_gram_a, moved_a, mate_moved_a, outer),
        vox_rows * rank * 8,
    )

    terms, rows_b = payload[:times], payload[times:]
    smp_mask = sum(chip_bits)
    for group in groups_of(chip_bits + vox_bits):
        masks = masks_of(group)[1:]
        if any(mask & smp_mask for mask in masks):
            packet = jnp.concatenate([terms, rows_b], axis=0)
            parts = [exchange(packet, mask) for mask in masks]
            terms = tree([terms] + [part[:times] for part in parts])
            parts = [part for part, mask in zip(parts, masks) if not mask & ~smp_mask]
            rows_b = jnp.concatenate([rows_b] + [part[times:] for part in parts], axis=0)
        else:
            terms = exchange_sum(terms, group)
    mate_rows_b = swap(rows_b)
    mate_terms = swap(terms)

    def last_kernel(terms, mate_terms, rows, mate_rows, c, w, weighed, scales_a, b_out, c_out, w_out, all_b):
        b = in_order(from_core_1(rows[...], mate_rows[...]), all_b, chips)
        coupled = weighed[...] * dot_rows(b, b)
        scales_b = jnp.sqrt(jnp.sum(b * b, axis=0, keepdims=True) / smp_total + 1e-06)
        b_out[...] = all_b[pl.ds(pl.multiple_of(smp_index() * smp_rows, smp_rows), smp_rows), :] / scales_b
        summed = from_core_1(terms[...], mate_terms[...])
        moved = c[...] - step_of(coupled) * (dot(c[...], coupled) - summed * w[...])
        scales_c = jnp.sqrt(jnp.sum(moved * moved, axis=0, keepdims=True) / times + 1e-06)
        c_out[...] = moved / scales_c
        w_out[...] = w[...] * scales_a[...] * scales_b * scales_c

    sample_result, time_result, scale_result = call(
        last_kernel,
        (far(smp_rows, rank), far(times, rank), far(1, rank)),
        (terms, mate_terms, rows_b, mate_rows_b, c_near, w_row, weighed, scales_a),
        2 * rank * rank * times * 6,
        scratch=(near(smp_total, rank),),
    )
    return voxel_result, sample_result, time_result, scale_result.reshape(rank)


def solution(mesh):
    return jax.shard_map(
        per_device,
        mesh=mesh,
        in_specs=(P("vox", "smp", None), P("vox", None), P("smp", None), P(), P()),
        out_specs=(P("vox", None), P("smp", None), P(), P()),
        check_vma=False,
    )
```

```python
import jax
import jax.numpy as jnp
from jax import lax
from jax.experimental import pallas as pl
from jax.experimental.pallas import tpu as pltpu
from jax.sharding import PartitionSpec as P

HIGH = lax.Precision.HIGHEST
F32 = jnp.float32
VMEM_LIMIT = 12 * 1024 * 1024
ALL = ("vox", "smp")


def dot(a, b):
    return jnp.dot(a, b, precision=HIGH, preferred_element_type=F32)


def dot_rows(a, b):
    return lax.dot_general(a, b, (((0,), (0,)), ((), ())), precision=HIGH, preferred_element_type=F32)


def step_of(coupled):
    sums = jnp.sum(jnp.abs(coupled), axis=0, keepdims=True)
    return 1.0 / jnp.max(sums, axis=1, keepdims=True)


def diagonal_row(gram):
    rows = lax.broadcasted_iota(jnp.int32, gram.shape, 0)
    columns = lax.broadcasted_iota(jnp.int32, gram.shape, 1)
    return jnp.sum(jnp.where(rows == columns, gram, 0.0), axis=0, keepdims=True)


def call(kernel, outs, operands, flops, scratch=(), in_hbm=0):
    spaces = [pltpu.HBM if i < in_hbm else pltpu.VMEM for i in range(len(operands))]
    placed = [pltpu.with_memory_space_constraint(x, space) for x, space in zip(operands, spaces)]
    specs = [pl.BlockSpec(memory_space=space) for space in spaces]
    return pl.pallas_call(
        kernel,
        out_shape=outs,
        in_specs=specs,
        out_specs=[pl.BlockSpec(memory_space=pltpu.VMEM)] * len(outs),
        scratch_shapes=list(scratch),
        compiler_params=pltpu.CompilerParams(vmem_limit_bytes=VMEM_LIMIT),
        cost_estimate=pl.CostEstimate(flops=flops, bytes_accessed=1 << 16, transcendentals=0),
    )(*placed)


def near(*shape):
    return pltpu.VMEM(shape, F32)


def far(*shape):
    return jax.ShapeDtypeStruct(shape, F32)


def bits_of(count):
    if count & (count - 1):
        raise ValueError("axis size")
    return [1 << b for b in range(count.bit_length() - 1)]


def groups_of(bits, size=2):
    return [bits[i : i + size] for i in range(0, len(bits), size)]


def masks_of(group):
    masks = [0]
    for bit in group:
        masks = [mask | bit for mask in masks] + masks
    return masks


def swap(values):
    return lax.ppermute(values, ALL, [(i, i ^ 1) for i in range(lax.axis_size(ALL))])


def send(values, holder, mask):
    count = lax.axis_size(ALL)
    pairs = [(i, i ^ 1 ^ mask if i & 1 == holder else i ^ 1) for i in range(count)]
    return lax.ppermute(values, ALL, pairs)


def fan(values, holder, masks):
    sent = [send(values, holder, mask) if mask else swap(values) for mask in reversed(masks)]
    return sent[::-1]


def tree(parts):
    parts = parts[::-1]
    while len(parts) > 1:
        parts = [a + b for a, b in zip(parts[::2], parts[1::2])]
    return parts[0]


def smp_index():
    return lax.axis_index("smp")


def on_core(core, own, got):
    return jnp.where(smp_index() & 1 == core, own, got)


def pack(gram):
    half = gram.shape[0] // 2
    rows = lax.broadcasted_iota(jnp.int32, (half, 2 * half), 0)
    columns = lax.broadcasted_iota(jnp.int32, (half, 2 * half), 1)
    top, bottom = gram[:half], gram[half:]
    packed = jnp.where(rows <= columns, top, pltpu.roll(bottom, half, 1))
    return packed, jnp.sum(jnp.where(columns == rows + half, bottom, 0.0), axis=0, keepdims=True)


def unpack(packed, diagonal):
    half = packed.shape[0]
    rows = lax.broadcasted_iota(jnp.int32, packed.shape, 0)
    columns = lax.broadcasted_iota(jnp.int32, packed.shape, 1)
    turned = jnp.concatenate([packed, packed], axis=0).T
    top = jnp.where(rows <= columns, packed, turned[:half])
    corner = jnp.where(columns < rows + half, pltpu.roll(packed, half, 1), turned[:half])
    corner = jnp.where(columns == rows + half, diagonal, corner)
    return jnp.concatenate([top, jnp.where(columns < half, turned[half:], corner)], axis=0)


def in_order(rows, scratch, chips):
    block = scratch.shape[0] // chips
    chip = smp_index() // 2
    for p in range(chips):
        scratch[pl.ds(pl.multiple_of((chip ^ (chips - 1 - p)) * block, block), block), :] = rows[p * block : (p + 1) * block, :]
    return scratch[...]


def per_device(ensemble, voxel_factor, sample_factor, time_factor, weights):
    vox_rows, smp_rows, times = ensemble.shape
    rank = voxel_factor.shape[1]
    flat_rows = vox_rows * smp_rows
    vox_count, smp_count = lax.axis_size("vox"), lax.axis_size("smp")
    vox_total, smp_total = vox_rows * vox_count, smp_rows * smp_count
    chips, chip_rows = smp_count // 2, 2 * smp_rows
    chip_bits = bits_of(smp_count)[1:]
    vox_bits = [bit * smp_count for bit in bits_of(vox_count)]
    chunks = 4 if vox_rows % 32 == 0 else 1
    chunk_vox = vox_rows // chunks
    chunk_rows = chunk_vox * smp_rows

    def open_kernel(x_hbm, c_hbm, b_hbm, a_hbm, w_hbm, x, c, a, w, out, con, sems):
        copies = [pltpu.make_async_copy(c_hbm, c, sems.at[0])]
        copies += [pltpu.make_async_copy(b_hbm, out.at[pl.ds(vox_rows, smp_rows), :], sems.at[1])]
        for n in range(chunks):
            part = pl.ds(n * chunk_rows, chunk_rows)
            copies.append(pltpu.make_async_copy(x_hbm.at[part, :], x.at[part, :], sems.at[2 + n]))
        copies.append(pltpu.make_async_copy(a_hbm, a, sems.at[2 + chunks]))
        copies.append(pltpu.make_async_copy(w_hbm, w, sems.at[3 + chunks]))
        for copy in copies:
            copy.start()
        copies[0].wait()
        copies[1].wait()
        factor = c[...]
        b = out[pl.ds(vox_rows, smp_rows), :]
        for n in range(chunks):
            copies[2 + n].wait()
            total = None
            rows = pl.ds(n * chunk_vox, chunk_vox)
            for j in range(smp_rows):
                block = x[pl.ds(n * chunk_rows + j, chunk_vox, stride=smp_rows), :]
                made = dot(block, factor)
                con[j, rows, :] = made
                made = made * b[j : j + 1, :]
                total = made if total is None else total + made
            out[rows, :] = total
        copies[2 + chunks].wait()
        copies[3 + chunks].wait()

    x, c_near, a_near, w_row, opened, con = call(
        open_kernel,
        (
            near(flat_rows, times),
            near(times, rank),
            near(vox_rows, rank),
            near(1, rank),
            near(vox_rows + smp_rows, rank),
            near(smp_rows, vox_rows, rank),
        ),
        (ensemble.reshape(flat_rows, times), time_factor, sample_factor, voxel_factor, weights.reshape(1, rank)),
        2 * flat_rows * times * rank * 6,
        scratch=(pltpu.SemaphoreType.DMA((4 + chunks,)),),
        in_hbm=5,
    )

    def weigh_kernel(c, w, outer, outer_c):
        squared = dot_rows(w[...], w[...])
        outer[...] = squared
        outer_c[...] = squared * dot_rows(c[...], c[...])

    outer, outer_c = call(
        weigh_kernel, (near(rank, rank), near(rank, rank)), (c_near, w_row), 2 * rank * rank * times * 6
    )

    got = swap(opened)
    terms = opened[:vox_rows] + got[:vox_rows]
    rows_b = jnp.concatenate([got[vox_rows:], opened[vox_rows:]], axis=0)
    holder = 1
    for group in groups_of(chip_bits):
        parts = fan(jnp.concatenate([terms, rows_b], axis=0), holder, masks_of(group))
        terms = tree([part[:vox_rows] for part in parts])
        rows_b = jnp.concatenate([part[vox_rows:] for part in parts], axis=0)
        holder ^= 1
    voxel_core = holder
    mate_con = swap(con)

    half, sums_rows = rank // 2, rank // 2 + chip_rows

    def voxel_kernel(terms, rows, a, w, outer_c, con, mate_con, moved_out, chip_b, out, all_b):
        b = in_order(rows, all_b, chips)
        chip_b[...] = all_b[pl.ds(pl.multiple_of(smp_index() // 2 * chip_rows, chip_rows), chip_rows), :]
        coupled = outer_c[...] * dot_rows(b, b)
        moved = a[...] - step_of(coupled) * (dot(a[...], coupled) - terms[...] * w[...])
        moved_out[...] = moved
        packed, diagonal = pack(dot_rows(moved, moved))
        out[:half, :] = packed
        for core in range(2):
            for j in range(smp_rows):
                row = half + core * smp_rows + j
                out[row : row + 1, :] = jnp.sum((con if core == voxel_core else mate_con)[j] * moved, axis=0, keepdims=True)
        out[sums_rows:, :] = jnp.broadcast_to(diagonal, (8, rank))

    moved_a, chip_b, sums = call(
        voxel_kernel,
        (near(vox_rows, rank), near(chip_rows, rank), near(sums_rows + 8, rank)),
        (terms, rows_b, a_near, w_row, outer_c, con, mate_con),
        2 * rank * rank * vox_rows * 12,
        scratch=(near(smp_total, rank),),
    )

    mate_moved_a = swap(moved_a)

    for group in groups_of(vox_bits):
        sums = tree(fan(sums, holder, masks_of(group)))
        holder ^= 1
    sample_core = holder
    if sample_core != voxel_core:
        chip_b = swap(chip_b)
    mate_x = swap(x)

    def time_kernel(x, mate_x, moved, mate_moved, each):
        moved = on_core(voxel_core, moved[...], mate_moved[...])
        for core in range(2):
            for j in range(smp_rows):
                block = (x if core == sample_core else mate_x)[pl.ds(j, vox_rows, stride=smp_rows), :]
                each[core * smp_rows + j] = dot_rows(block, moved)

    (each,) = call(
        time_kernel,
        (near(chip_rows, times, rank),),
        (x, mate_x, moved_a, mate_moved_a),
        4 * flat_rows * times * rank * 6,
    )

    def sample_kernel(sums, b, w, outer_c, each, gram_out, out):
        gram_out[...] = unpack(sums[:half, :], sums[sums_rows : sums_rows + 1, :])
        coupled = outer_c[...] * gram_out[...]
        moved = b[...] - step_of(coupled) * (dot(b[...], coupled) - sums[half:sums_rows, :] * w[...])
        out[times:, :] = moved
        total = None
        for j in range(chip_rows):
            made = each[j] * moved[j : j + 1, :]
            total = made if total is None else total + made
        out[:times, :] = total

    gram_a, payload = call(
        sample_kernel,
        (near(rank, rank), near(times + chip_rows, rank)),
        (sums, chip_b, w_row, outer_c, each),
        2 * rank * rank * chip_rows * 6,
    )
    mate_gram_a = swap(gram_a)

    def scale_kernel(gram, mate_gram, moved, mate_moved, outer, result, scales_out, weighed):
        gram = on_core(sample_core, gram[...], mate_gram[...])
        scales = jnp.sqrt(diagonal_row(gram) / vox_total + 1e-06)
        scales_out[...] = scales
        result[...] = on_core(voxel_core, moved[...], mate_moved[...]) / scales
        weighed[...] = outer[...] * gram

    voxel_result, scales_a, weighed = call(
        scale_kernel,
        (far(vox_rows, rank), near(1, rank), near(rank, rank)),
        (gram_a, mate_gram_a, moved_a, mate_moved_a, outer),
        vox_rows * rank * 8,
    )

    terms, rows_b, rows_core = payload[:times], payload[times:], holder
    smp_mask = sum(chip_bits)
    for group in groups_of(chip_bits + vox_bits):
        masks = masks_of(group)
        with_rows = any(mask & smp_mask for mask in masks)
        parts = fan(jnp.concatenate([terms, rows_b], axis=0) if with_rows else terms, holder, masks)
        terms = tree([part[:times] for part in parts])
        holder ^= 1
        if with_rows:
            parts = [part for part, mask in zip(parts, masks) if not mask & ~smp_mask]
            rows_b = jnp.concatenate([part[times:] for part in parts], axis=0)
            rows_core = holder
    last_core = holder
    mate_rows_b = swap(rows_b)
    terms, mate_rows_b, voxel_result, scales_a, weighed = lax.optimization_barrier(
        (terms, mate_rows_b, voxel_result, scales_a, weighed)
    )
    mate_terms = swap(terms)

    def last_kernel(terms, mate_terms, rows, mate_rows, c, w, weighed, scales_a, b_out, c_out, w_out, all_b):
        b = in_order(on_core(rows_core, rows[...], mate_rows[...]), all_b, chips)
        coupled = weighed[...] * dot_rows(b, b)
        scales_b = jnp.sqrt(jnp.sum(b * b, axis=0, keepdims=True) / smp_total + 1e-06)
        b_out[...] = all_b[pl.ds(pl.multiple_of(smp_index() * smp_rows, smp_rows), smp_rows), :] / scales_b
        summed = on_core(last_core, terms[...], mate_terms[...])
        moved = c[...] - step_of(coupled) * (dot(c[...], coupled) - summed * w[...])
        scales_c = jnp.sqrt(jnp.sum(moved * moved, axis=0, keepdims=True) / times + 1e-06)
        c_out[...] = moved / scales_c
        w_out[...] = w[...] * scales_a[...] * scales_b * scales_c

    sample_result, time_result, scale_result = call(
        last_kernel,
        (far(smp_rows, rank), far(times, rank), far(1, rank)),
        (terms, mate_terms, rows_b, mate_rows_b, c_near, w_row, weighed, scales_a),
        2 * rank * rank * times * 6,
        scratch=(near(smp_total, rank),),
    )
    return voxel_result, sample_result, time_result, scale_result.reshape(rank)


def solution(mesh):
    return jax.shard_map(
        per_device,
        mesh=mesh,
        in_specs=(P("vox", "smp", None), P("vox", None), P("smp", None), P(), P()),
        out_specs=(P("vox", None), P("smp", None), P(), P()),
        check_vma=False,
    )
```

```python
import jax
import jax.numpy as jnp
from jax import lax
from jax.experimental import pallas as pl
from jax.experimental.pallas import tpu as pltpu
from jax.sharding import PartitionSpec as P

F32 = jnp.float32
BF16 = jnp.bfloat16
VMEM_LIMIT = 12 * 1024 * 1024
ALL = ("vox", "smp")


def halves(a, axis):
    high = a.astype(BF16)
    return jnp.concatenate([high, (a - high.astype(F32)).astype(BF16)], axis=axis)


def both(b):
    parts = halves(b, 1)
    return jnp.concatenate([parts, parts], axis=0)


def fold(product):
    width = product.shape[1] // 2
    return product[:, :width] + product[:, width:]


def dot(a, b):
    return fold(jnp.dot(halves(a, 1), both(b), preferred_element_type=F32))


def dot_rows(a, b):
    return fold(lax.dot_general(halves(a, 0), both(b), (((0,), (0,)), ((), ())), preferred_element_type=F32))


def step_of(coupled):
    sums = jnp.sum(jnp.abs(coupled), axis=0, keepdims=True)
    return 1.0 / jnp.max(sums, axis=1, keepdims=True)


def diagonal_row(gram):
    rows = lax.broadcasted_iota(jnp.int32, gram.shape, 0)
    columns = lax.broadcasted_iota(jnp.int32, gram.shape, 1)
    return jnp.sum(jnp.where(rows == columns, gram, 0.0), axis=0, keepdims=True)


def call(kernel, outs, operands, flops, scratch=(), in_hbm=0):
    spaces = [pltpu.HBM if i < in_hbm else pltpu.VMEM for i in range(len(operands))]
    placed = [pltpu.with_memory_space_constraint(x, space) for x, space in zip(operands, spaces)]
    specs = [pl.BlockSpec(memory_space=space) for space in spaces]
    return pl.pallas_call(
        kernel,
        out_shape=outs,
        in_specs=specs,
        out_specs=[pl.BlockSpec(memory_space=pltpu.VMEM)] * len(outs),
        scratch_shapes=list(scratch),
        compiler_params=pltpu.CompilerParams(vmem_limit_bytes=VMEM_LIMIT),
        cost_estimate=pl.CostEstimate(flops=flops, bytes_accessed=1 << 16, transcendentals=0),
    )(*placed)


def near(*shape):
    return pltpu.VMEM(shape, F32)


def far(*shape):
    return jax.ShapeDtypeStruct(shape, F32)


def bits_of(count):
    if count & (count - 1):
        raise ValueError("axis size")
    return [1 << b for b in range(count.bit_length() - 1)]


def groups_of(bits, size=2):
    return [bits[i : i + size] for i in range(0, len(bits), size)]


def masks_of(group):
    masks = [0]
    for bit in group:
        masks = [mask | bit for mask in masks] + masks
    return masks


def swap(values):
    return lax.ppermute(values, ALL, [(i, i ^ 1) for i in range(lax.axis_size(ALL))])


def send(values, holder, mask):
    count = lax.axis_size(ALL)
    pairs = [(i, i ^ 1 ^ mask if i & 1 == holder else i ^ 1) for i in range(count)]
    return lax.ppermute(values, ALL, pairs)


def fan(values, holder, masks):
    sent = [send(values, holder, mask) if mask else swap(values) for mask in reversed(masks)]
    return sent[::-1]


def tree(parts):
    parts = parts[::-1]
    while len(parts) > 1:
        parts = [a + b for a, b in zip(parts[::2], parts[1::2])]
    return parts[0]


def smp_index():
    return lax.axis_index("smp")


def on_core(core, own, got):
    return jnp.where(smp_index() & 1 == core, own, got)


def pack(gram):
    half = gram.shape[0] // 2
    rows = lax.broadcasted_iota(jnp.int32, (half, 2 * half), 0)
    columns = lax.broadcasted_iota(jnp.int32, (half, 2 * half), 1)
    top, bottom = gram[:half], gram[half:]
    packed = jnp.where(rows <= columns, top, pltpu.roll(bottom, half, 1))
    return packed, jnp.sum(jnp.where(columns == rows + half, bottom, 0.0), axis=0, keepdims=True)


def unpack(packed, diagonal):
    half = packed.shape[0]
    rows = lax.broadcasted_iota(jnp.int32, packed.shape, 0)
    columns = lax.broadcasted_iota(jnp.int32, packed.shape, 1)
    turned = jnp.concatenate([packed, packed], axis=0).T
    top = jnp.where(rows <= columns, packed, turned[:half])
    corner = jnp.where(columns < rows + half, pltpu.roll(packed, half, 1), turned[:half])
    corner = jnp.where(columns == rows + half, diagonal, corner)
    return jnp.concatenate([top, jnp.where(columns < half, turned[half:], corner)], axis=0)


def in_order(rows, scratch, chips):
    block = scratch.shape[0] // chips
    chip = smp_index() // 2
    for p in range(chips):
        scratch[pl.ds(pl.multiple_of((chip ^ (chips - 1 - p)) * block, block), block), :] = rows[p * block : (p + 1) * block, :]
    return scratch[...]


def per_device(ensemble, voxel_factor, sample_factor, time_factor, weights):
    vox_rows, smp_rows, times = ensemble.shape
    rank = voxel_factor.shape[1]
    flat_rows = vox_rows * smp_rows
    vox_count, smp_count = lax.axis_size("vox"), lax.axis_size("smp")
    vox_total, smp_total = vox_rows * vox_count, smp_rows * smp_count
    chips, chip_rows = smp_count // 2, 2 * smp_rows
    chip_bits = bits_of(smp_count)[1:]
    vox_bits = [bit * smp_count for bit in bits_of(vox_count)]
    chunks = 4 if vox_rows % 32 == 0 else 1
    chunk_vox = vox_rows // chunks
    chunk_rows = chunk_vox * smp_rows

    def open_kernel(x_hbm, c_hbm, b_hbm, a_hbm, w_hbm, x, c, a, w, out, con, sems):
        copies = [pltpu.make_async_copy(c_hbm, c, sems.at[0])]
        copies += [pltpu.make_async_copy(b_hbm, out.at[pl.ds(vox_rows, smp_rows), :], sems.at[1])]
        for n in range(chunks):
            part = pl.ds(n * chunk_rows, chunk_rows)
            copies.append(pltpu.make_async_copy(x_hbm.at[part, :], x.at[part, :], sems.at[2 + n]))
        copies.append(pltpu.make_async_copy(a_hbm, a, sems.at[2 + chunks]))
        copies.append(pltpu.make_async_copy(w_hbm, w, sems.at[3 + chunks]))
        for copy in copies:
            copy.start()
        copies[0].wait()
        copies[1].wait()
        factor = both(c[...])
        b = out[pl.ds(vox_rows, smp_rows), :]
        for n in range(chunks):
            copies[2 + n].wait()
            rows = pl.ds(n * chunk_vox, chunk_vox)
            blocks = [x[pl.ds(n * chunk_rows + j, chunk_vox, stride=smp_rows), :] for j in range(smp_rows)]
            blocks = jnp.concatenate([halves(block, 1) for block in blocks], axis=0)
            made = fold(jnp.dot(blocks, factor, preferred_element_type=F32)).reshape(smp_rows, chunk_vox, rank)
            con[:, rows, :] = made
            total = made[0] * b[:1, :]
            for j in range(1, smp_rows):
                total = total + made[j] * b[j : j + 1, :]
            out[rows, :] = total
        copies[2 + chunks].wait()
        copies[3 + chunks].wait()

    x, c_near, a_near, w_row, opened, con = call(
        open_kernel,
        (
            near(flat_rows, times),
            near(times, rank),
            near(vox_rows, rank),
            near(1, rank),
            near(vox_rows + smp_rows, rank),
            near(smp_rows, vox_rows, rank),
        ),
        (ensemble.reshape(flat_rows, times), time_factor, sample_factor, voxel_factor, weights.reshape(1, rank)),
        2 * flat_rows * times * rank * 6,
        scratch=(pltpu.SemaphoreType.DMA((4 + chunks,)),),
        in_hbm=5,
    )

    def weigh_kernel(c, w, outer, outer_c):
        squared = dot_rows(w[...], w[...])
        outer[...] = squared
        outer_c[...] = squared * dot_rows(c[...], c[...])

    outer, outer_c = call(
        weigh_kernel, (near(rank, rank), near(rank, rank)), (c_near, w_row), 2 * rank * rank * times * 6
    )

    got = swap(opened)
    terms = opened[:vox_rows] + got[:vox_rows]
    rows_b = jnp.concatenate([got[vox_rows:], opened[vox_rows:]], axis=0)
    holder = 1
    for group in groups_of(chip_bits):
        parts = fan(jnp.concatenate([terms, rows_b], axis=0), holder, masks_of(group))
        terms = tree([part[:vox_rows] for part in parts])
        rows_b = jnp.concatenate([part[vox_rows:] for part in parts], axis=0)
        holder ^= 1
    voxel_core = holder
    mate_con = swap(con)

    half, sums_rows = rank // 2, rank // 2 + chip_rows

    def voxel_kernel(terms, rows, a, w, outer_c, con, mate_con, moved_out, chip_b, out, all_b):
        b = in_order(rows, all_b, chips)
        chip_b[...] = all_b[pl.ds(pl.multiple_of(smp_index() // 2 * chip_rows, chip_rows), chip_rows), :]
        coupled = outer_c[...] * dot_rows(b, b)
        moved = a[...] - step_of(coupled) * (dot(a[...], coupled) - terms[...] * w[...])
        moved_out[...] = moved
        packed, diagonal = pack(dot_rows(moved, moved))
        out[:half, :] = packed
        for core in range(2):
            for j in range(smp_rows):
                row = half + core * smp_rows + j
                out[row : row + 1, :] = jnp.sum((con if core == voxel_core else mate_con)[j] * moved, axis=0, keepdims=True)
        out[sums_rows:, :] = jnp.broadcast_to(diagonal, (8, rank))

    moved_a, chip_b, sums = call(
        voxel_kernel,
        (near(vox_rows, rank), near(chip_rows, rank), near(sums_rows + 8, rank)),
        (terms, rows_b, a_near, w_row, outer_c, con, mate_con),
        2 * rank * rank * vox_rows * 12,
        scratch=(near(smp_total, rank),),
    )

    mate_moved_a = swap(moved_a)

    for group in groups_of(vox_bits):
        sums = tree(fan(sums, holder, masks_of(group)))
        holder ^= 1
    sample_core = holder
    if sample_core != voxel_core:
        chip_b = swap(chip_b)
    mate_x = swap(x)

    def time_kernel(x, mate_x, moved, mate_moved, each):
        moved = on_core(voxel_core, moved[...], mate_moved[...])
        for core in range(2):
            for j in range(smp_rows):
                block = (x if core == sample_core else mate_x)[pl.ds(j, vox_rows, stride=smp_rows), :]
                each[core * smp_rows + j] = dot_rows(block, moved)

    (each,) = call(
        time_kernel,
        (near(chip_rows, times, rank),),
        (x, mate_x, moved_a, mate_moved_a),
        4 * flat_rows * times * rank * 6,
    )

    def sample_kernel(sums, b, w, outer_c, each, gram_out, out):
        gram_out[...] = unpack(sums[:half, :], sums[sums_rows : sums_rows + 1, :])
        coupled = outer_c[...] * gram_out[...]
        moved = b[...] - step_of(coupled) * (dot(b[...], coupled) - sums[half:sums_rows, :] * w[...])
        out[times:, :] = moved
        total = None
        for j in range(chip_rows):
            made = each[j] * moved[j : j + 1, :]
            total = made if total is None else total + made
        out[:times, :] = total

    gram_a, payload = call(
        sample_kernel,
        (near(rank, rank), near(times + chip_rows, rank)),
        (sums, chip_b, w_row, outer_c, each),
        2 * rank * rank * chip_rows * 6,
    )
    mate_gram_a = swap(gram_a)

    def scale_kernel(gram, mate_gram, moved, mate_moved, outer, result, scales_out, weighed):
        gram = on_core(sample_core, gram[...], mate_gram[...])
        scales = jnp.sqrt(diagonal_row(gram) / vox_total + 1e-06)
        scales_out[...] = scales
        result[...] = on_core(voxel_core, moved[...], mate_moved[...]) / scales
        weighed[...] = outer[...] * gram

    voxel_result, scales_a, weighed = call(
        scale_kernel,
        (far(vox_rows, rank), near(1, rank), near(rank, rank)),
        (gram_a, mate_gram_a, moved_a, mate_moved_a, outer),
        vox_rows * rank * 8,
    )

    terms, rows_b, rows_core = payload[:times], payload[times:], holder
    smp_mask = sum(chip_bits)
    for group in groups_of(chip_bits + vox_bits):
        masks = masks_of(group)
        with_rows = any(mask & smp_mask for mask in masks)
        parts = fan(jnp.concatenate([terms, rows_b], axis=0) if with_rows else terms, holder, masks)
        terms = tree([part[:times] for part in parts])
        holder ^= 1
        if with_rows:
            parts = [part for part, mask in zip(parts, masks) if not mask & ~smp_mask]
            rows_b = jnp.concatenate([part[times:] for part in parts], axis=0)
            rows_core = holder
    last_core = holder
    mate_rows_b = swap(rows_b)

    def ready_kernel(rows, mate_rows, c, w, weighed, scales_a, b_out, base, gain, scale, all_b):
        b = in_order(on_core(rows_core, rows[...], mate_rows[...]), all_b, chips)
        coupled = weighed[...] * dot_rows(b, b)
        step = step_of(coupled)
        base[...] = c[...] - step * dot(c[...], coupled)
        gain[...] = step * w[...]
        scales_b = jnp.sqrt(jnp.sum(b * b, axis=0, keepdims=True) / smp_total + 1e-06)
        scale[...] = w[...] * scales_a[...] * scales_b
        b_out[...] = all_b[pl.ds(pl.multiple_of(smp_index() * smp_rows, smp_rows), smp_rows), :] / scales_b

    sample_result, base, gain, scale = call(
        ready_kernel,
        (far(smp_rows, rank), near(times, rank), near(1, rank), near(1, rank)),
        (rows_b, mate_rows_b, c_near, w_row, weighed, scales_a),
        2 * rank * rank * times * 4,
        scratch=(near(smp_total, rank),),
    )
    terms, base, gain, scale, voxel_result, sample_result = lax.optimization_barrier(
        (terms, base, gain, scale, voxel_result, sample_result)
    )
    mate_terms = swap(terms)

    def last_kernel(terms, mate_terms, base, gain, scale, c_out, w_out):
        moved = base[...] + on_core(last_core, terms[...], mate_terms[...]) * gain[...]
        scales_c = jnp.sqrt(jnp.sum(moved * moved, axis=0, keepdims=True) / times + 1e-06)
        c_out[...] = moved / scales_c
        w_out[...] = scale[...] * scales_c

    time_result, scale_result = call(
        last_kernel,
        (far(times, rank), far(1, rank)),
        (terms, mate_terms, base, gain, scale),
        rank * times * 8,
    )
    return voxel_result, sample_result, time_result, scale_result.reshape(rank)


def solution(mesh):
    return jax.shard_map(
        per_device,
        mesh=mesh,
        in_specs=(P("vox", "smp", None), P("vox", None), P("smp", None), P(), P()),
        out_specs=(P("vox", None), P("smp", None), P(), P()),
        check_vma=False,
    )
```

```python
import jax
import jax.numpy as jnp
from jax import lax
from jax.experimental import pallas as pl
from jax.experimental.pallas import tpu as pltpu
from jax.sharding import PartitionSpec as P

F32 = jnp.float32
BF16 = jnp.bfloat16
VMEM_LIMIT = 12 * 1024 * 1024
ALL = ("vox", "smp")


def halves(a, axis):
    high = a.astype(BF16)
    return jnp.concatenate([high, (a - high.astype(F32)).astype(BF16)], axis=axis)


def both(b):
    parts = halves(b, 1)
    return jnp.concatenate([parts, parts], axis=0)


def fold(product):
    width = product.shape[1] // 2
    return product[:, :width] + product[:, width:]


def dot(a, b):
    return fold(jnp.dot(halves(a, 1), both(b), preferred_element_type=F32))


def dot_rows(a, b):
    return fold(lax.dot_general(halves(a, 0), both(b), (((0,), (0,)), ((), ())), preferred_element_type=F32))


def step_of(coupled):
    sums = jnp.sum(jnp.abs(coupled), axis=0, keepdims=True)
    return 1.0 / jnp.max(sums, axis=1, keepdims=True)


def diagonal_row(gram):
    rows = lax.broadcasted_iota(jnp.int32, gram.shape, 0)
    columns = lax.broadcasted_iota(jnp.int32, gram.shape, 1)
    return jnp.sum(jnp.where(rows == columns, gram, 0.0), axis=0, keepdims=True)


def call(kernel, outs, operands, flops, scratch=(), in_hbm=0):
    spaces = [pltpu.HBM if i < in_hbm else pltpu.VMEM for i in range(len(operands))]
    placed = [pltpu.with_memory_space_constraint(x, space) for x, space in zip(operands, spaces)]
    specs = [pl.BlockSpec(memory_space=space) for space in spaces]
    return pl.pallas_call(
        kernel,
        out_shape=outs,
        in_specs=specs,
        out_specs=[pl.BlockSpec(memory_space=pltpu.VMEM)] * len(outs),
        scratch_shapes=list(scratch),
        compiler_params=pltpu.CompilerParams(vmem_limit_bytes=VMEM_LIMIT),
        cost_estimate=pl.CostEstimate(flops=flops, bytes_accessed=1 << 16, transcendentals=0),
    )(*placed)


def near(*shape):
    return pltpu.VMEM(shape, F32)


def far(*shape):
    return jax.ShapeDtypeStruct(shape, F32)


def bits_of(count):
    if count & (count - 1):
        raise ValueError("axis size")
    return [1 << b for b in range(count.bit_length() - 1)]


def groups_of(bits, size=2):
    return [bits[i : i + size] for i in range(0, len(bits), size)]


def masks_of(group):
    masks = [0]
    for bit in group:
        masks = [mask | bit for mask in masks] + masks
    return masks


def swap(values):
    return lax.ppermute(values, ALL, [(i, i ^ 1) for i in range(lax.axis_size(ALL))])


def send(values, holder, mask):
    count = lax.axis_size(ALL)
    pairs = [(i, i ^ 1 ^ mask if i & 1 == holder else i ^ 1) for i in range(count)]
    return lax.ppermute(values, ALL, pairs)


def fan(values, holder, masks):
    sent = [send(values, holder, mask) if mask else swap(values) for mask in reversed(masks)]
    return sent[::-1]


def tree(parts):
    parts = parts[::-1]
    while len(parts) > 1:
        parts = [a + b for a, b in zip(parts[::2], parts[1::2])]
    return parts[0]


def smp_index():
    return lax.axis_index("smp")


def on_core(core, own, got):
    return jnp.where(smp_index() & 1 == core, own, got)


def pack(gram):
    half = gram.shape[0] // 2
    rows = lax.broadcasted_iota(jnp.int32, (half, 2 * half), 0)
    columns = lax.broadcasted_iota(jnp.int32, (half, 2 * half), 1)
    top, bottom = gram[:half], gram[half:]
    packed = jnp.where(rows <= columns, top, pltpu.roll(bottom, half, 1))
    return packed, jnp.sum(jnp.where(columns == rows + half, bottom, 0.0), axis=0, keepdims=True)


def unpack(packed, diagonal):
    half = packed.shape[0]
    rows = lax.broadcasted_iota(jnp.int32, packed.shape, 0)
    columns = lax.broadcasted_iota(jnp.int32, packed.shape, 1)
    turned = jnp.concatenate([packed, packed], axis=0).T
    top = jnp.where(rows <= columns, packed, turned[:half])
    corner = jnp.where(columns < rows + half, pltpu.roll(packed, half, 1), turned[:half])
    corner = jnp.where(columns == rows + half, diagonal, corner)
    return jnp.concatenate([top, jnp.where(columns < half, turned[half:], corner)], axis=0)


def in_order(rows, scratch, chips):
    block = scratch.shape[0] // chips
    chip = smp_index() // 2
    for p in range(chips):
        scratch[pl.ds(pl.multiple_of((chip ^ (chips - 1 - p)) * block, block), block), :] = rows[p * block : (p + 1) * block, :]
    return scratch[...]


def per_device(ensemble, voxel_factor, sample_factor, time_factor, weights):
    vox_rows, smp_rows, times = ensemble.shape
    rank = voxel_factor.shape[1]
    flat_rows = vox_rows * smp_rows
    vox_count, smp_count = lax.axis_size("vox"), lax.axis_size("smp")
    vox_total, smp_total = vox_rows * vox_count, smp_rows * smp_count
    chips, chip_rows = smp_count // 2, 2 * smp_rows
    chip_bits = bits_of(smp_count)[1:]
    vox_bits = [bit * smp_count for bit in bits_of(vox_count)]
    chunks = 4 if vox_rows % 32 == 0 else 1
    chunk_vox = vox_rows // chunks
    chunk_rows = chunk_vox * smp_rows

    def open_kernel(x_hbm, c_hbm, b_hbm, a_hbm, w_hbm, x, c, a, w, out, con, sems):
        copies = [pltpu.make_async_copy(c_hbm, c, sems.at[0])]
        copies += [pltpu.make_async_copy(b_hbm, out.at[pl.ds(vox_rows, smp_rows), :], sems.at[1])]
        for n in range(chunks):
            part = pl.ds(n * chunk_rows, chunk_rows)
            copies.append(pltpu.make_async_copy(x_hbm.at[part, :], x.at[part, :], sems.at[2 + n]))
        copies.append(pltpu.make_async_copy(a_hbm, a, sems.at[2 + chunks]))
        copies.append(pltpu.make_async_copy(w_hbm, w, sems.at[3 + chunks]))
        for copy in copies:
            copy.start()
        copies[0].wait()
        copies[1].wait()
        factor = both(c[...])
        b = out[pl.ds(vox_rows, smp_rows), :]
        for n in range(chunks):
            copies[2 + n].wait()
            rows = pl.ds(n * chunk_vox, chunk_vox)
            blocks = [x[pl.ds(n * chunk_rows + j, chunk_vox, stride=smp_rows), :] for j in range(smp_rows)]
            blocks = jnp.concatenate([halves(block, 1) for block in blocks], axis=0)
            made = fold(jnp.dot(blocks, factor, preferred_element_type=F32)).reshape(smp_rows, chunk_vox, rank)
            con[:, rows, :] = made
            total = made[0] * b[:1, :]
            for j in range(1, smp_rows):
                total = total + made[j] * b[j : j + 1, :]
            out[rows, :] = total
        copies[2 + chunks].wait()
        copies[3 + chunks].wait()

    x, c_near, a_near, w_row, opened, con = call(
        open_kernel,
        (
            near(flat_rows, times),
            near(times, rank),
            near(vox_rows, rank),
            near(1, rank),
            near(vox_rows + smp_rows, rank),
            near(smp_rows, vox_rows, rank),
        ),
        (ensemble.reshape(flat_rows, times), time_factor, sample_factor, voxel_factor, weights.reshape(1, rank)),
        2 * flat_rows * times * rank * 6,
        scratch=(pltpu.SemaphoreType.DMA((4 + chunks,)),),
        in_hbm=5,
    )

    def weigh_kernel(c, w, outer, outer_c):
        squared = dot_rows(w[...], w[...])
        outer[...] = squared
        outer_c[...] = squared * dot_rows(c[...], c[...])

    outer, outer_c = call(
        weigh_kernel, (near(rank, rank), near(rank, rank)), (c_near, w_row), 2 * rank * rank * times * 6
    )

    got = swap(opened)
    terms = opened[:vox_rows] + got[:vox_rows]
    rows_b = jnp.concatenate([opened[vox_rows:], got[vox_rows:]], axis=0)
    holder = 0
    for group in groups_of(chip_bits):
        parts = fan(jnp.concatenate([terms, rows_b], axis=0), holder, masks_of(group))
        terms = tree([part[:vox_rows] for part in parts])
        rows_b = jnp.concatenate([part[vox_rows:] for part in parts], axis=0)
        holder ^= 1
    voxel_core = holder
    mate_con = swap(con)

    half, sums_rows = rank // 2, rank // 2 + chip_rows

    def voxel_kernel(terms, rows, a, w, outer_c, con, mate_con, moved_out, chip_b, out, all_b):
        b = in_order(rows, all_b, chips)
        chip_b[...] = all_b[pl.ds(pl.multiple_of(smp_index() // 2 * chip_rows, chip_rows), chip_rows), :]
        coupled = outer_c[...] * dot_rows(b, b)
        moved = a[...] - step_of(coupled) * (dot(a[...], coupled) - terms[...] * w[...])
        moved_out[...] = moved
        packed, diagonal = pack(dot_rows(moved, moved))
        out[:half, :] = packed
        for core in range(2):
            for j in range(smp_rows):
                row = half + core * smp_rows + j
                out[row : row + 1, :] = jnp.sum((con if core == voxel_core else mate_con)[j] * moved, axis=0, keepdims=True)
        out[sums_rows:, :] = jnp.broadcast_to(diagonal, (8, rank))

    moved_a, chip_b, sums = call(
        voxel_kernel,
        (near(vox_rows, rank), near(chip_rows, rank), near(sums_rows + 8, rank)),
        (terms, rows_b, a_near, w_row, outer_c, con, mate_con),
        2 * rank * rank * vox_rows * 12,
        scratch=(near(smp_total, rank),),
    )

    mate_moved_a = swap(moved_a)

    for group in groups_of(vox_bits):
        sums = tree(fan(sums, holder, masks_of(group)))
        holder ^= 1
    sample_core = holder
    if sample_core != voxel_core:
        chip_b = swap(chip_b)
    mate_x = swap(x)

    def time_kernel(x, mate_x, moved, mate_moved, each):
        moved = on_core(voxel_core, moved[...], mate_moved[...])
        for core in range(2):
            for j in range(smp_rows):
                block = (x if core == sample_core else mate_x)[pl.ds(j, vox_rows, stride=smp_rows), :]
                each[core * smp_rows + j] = dot_rows(block, moved)

    (each,) = call(
        time_kernel,
        (near(chip_rows, times, rank),),
        (x, mate_x, moved_a, mate_moved_a),
        4 * flat_rows * times * rank * 6,
    )

    def sample_kernel(sums, b, w, outer_c, each, gram_out, out):
        gram_out[...] = unpack(sums[:half, :], sums[sums_rows : sums_rows + 1, :])
        coupled = outer_c[...] * gram_out[...]
        moved = b[...] - step_of(coupled) * (dot(b[...], coupled) - sums[half:sums_rows, :] * w[...])
        out[times:, :] = moved
        total = None
        for j in range(chip_rows):
            made = each[j] * moved[j : j + 1, :]
            total = made if total is None else total + made
        out[:times, :] = total

    gram_a, payload = call(
        sample_kernel,
        (near(rank, rank), near(times + chip_rows, rank)),
        (sums, chip_b, w_row, outer_c, each),
        2 * rank * rank * chip_rows * 6,
    )
    mate_gram_a = swap(gram_a)

    def scale_kernel(gram, mate_gram, moved, mate_moved, outer, result, scales_out, weighed):
        gram = on_core(sample_core, gram[...], mate_gram[...])
        scales = jnp.sqrt(diagonal_row(gram) / vox_total + 1e-06)
        scales_out[...] = scales
        result[...] = on_core(voxel_core, moved[...], mate_moved[...]) / scales
        weighed[...] = outer[...] * gram

    voxel_result, scales_a, weighed = call(
        scale_kernel,
        (far(vox_rows, rank), near(1, rank), near(rank, rank)),
        (gram_a, mate_gram_a, moved_a, mate_moved_a, outer),
        vox_rows * rank * 8,
    )

    terms, rows_b, rows_core = payload[:times], payload[times:], holder
    smp_mask = sum(chip_bits)
    for group in groups_of(chip_bits + vox_bits):
        masks = masks_of(group)
        with_rows = any(mask & smp_mask for mask in masks)
        parts = fan(jnp.concatenate([terms, rows_b], axis=0) if with_rows else terms, holder, masks)
        terms = tree([part[:times] for part in parts])
        holder ^= 1
        if with_rows:
            parts = [part for part, mask in zip(parts, masks) if not mask & ~smp_mask]
            rows_b = jnp.concatenate([part[times:] for part in parts], axis=0)
            rows_core = holder
            terms, rows_b, voxel_result, scales_a, weighed = lax.optimization_barrier(
                (terms, rows_b, voxel_result, scales_a, weighed)
            )
    last_core = holder
    mate_rows_b = swap(rows_b)

    def ready_kernel(rows, mate_rows, c, w, weighed, scales_a, b_out, base, gain, scale, all_b):
        b = in_order(on_core(rows_core, rows[...], mate_rows[...]), all_b, chips)
        coupled = weighed[...] * dot_rows(b, b)
        step = step_of(coupled)
        base[...] = c[...] - step * dot(c[...], coupled)
        gain[...] = step * w[...]
        scales_b = jnp.sqrt(jnp.sum(b * b, axis=0, keepdims=True) / smp_total + 1e-06)
        scale[...] = w[...] * scales_a[...] * scales_b
        b_out[...] = all_b[pl.ds(pl.multiple_of(smp_index() * smp_rows, smp_rows), smp_rows), :] / scales_b

    sample_result, base, gain, scale = call(
        ready_kernel,
        (far(smp_rows, rank), near(times, rank), near(1, rank), near(1, rank)),
        (rows_b, mate_rows_b, c_near, w_row, weighed, scales_a),
        2 * rank * rank * times * 4,
        scratch=(near(smp_total, rank),),
    )
    terms, base, gain, scale, sample_result = lax.optimization_barrier((terms, base, gain, scale, sample_result))
    mate_terms = swap(terms)

    def last_kernel(terms, mate_terms, base, gain, scale, c_out, w_out):
        moved = base[...] + on_core(last_core, terms[...], mate_terms[...]) * gain[...]
        scales_c = jnp.sqrt(jnp.sum(moved * moved, axis=0, keepdims=True) / times + 1e-06)
        c_out[...] = moved / scales_c
        w_out[...] = scale[...] * scales_c

    time_result, scale_result = call(
        last_kernel,
        (far(times, rank), far(1, rank)),
        (terms, mate_terms, base, gain, scale),
        rank * times * 8,
    )
    return voxel_result, sample_result, time_result, scale_result.reshape(rank)


def solution(mesh):
    return jax.shard_map(
        per_device,
        mesh=mesh,
        in_specs=(P("vox", "smp", None), P("vox", None), P("smp", None), P(), P()),
        out_specs=(P("vox", None), P("smp", None), P(), P()),
        check_vma=False,
    )
```

```python
import jax
import jax.numpy as jnp
from jax import lax
from jax.experimental import pallas as pl
from jax.experimental.pallas import tpu as pltpu
from jax.sharding import PartitionSpec as P

F32 = jnp.float32
BF16 = jnp.bfloat16
VMEM_LIMIT = 12 * 1024 * 1024
ALL = ("vox", "smp")


def halves(a, axis):
    high = a.astype(BF16)
    return jnp.concatenate([high, (a - high.astype(F32)).astype(BF16)], axis=axis)


def both(b):
    parts = halves(b, 1)
    return jnp.concatenate([parts, parts], axis=0)


def fold(product):
    width = product.shape[1] // 2
    return product[:, :width] + product[:, width:]


def dot(a, b):
    return fold(jnp.dot(halves(a, 1), both(b), preferred_element_type=F32))


def dot_rows(a, b):
    return fold(lax.dot_general(halves(a, 0), both(b), (((0,), (0,)), ((), ())), preferred_element_type=F32))


def step_of(coupled):
    sums = jnp.sum(jnp.abs(coupled), axis=0, keepdims=True)
    return 1.0 / jnp.max(sums, axis=1, keepdims=True)


def diagonal_row(gram):
    rows = lax.broadcasted_iota(jnp.int32, gram.shape, 0)
    columns = lax.broadcasted_iota(jnp.int32, gram.shape, 1)
    return jnp.sum(jnp.where(rows == columns, gram, 0.0), axis=0, keepdims=True)


def call(kernel, outs, operands, flops, scratch=(), in_hbm=0):
    spaces = [pltpu.HBM if i < in_hbm else pltpu.VMEM for i in range(len(operands))]
    placed = [pltpu.with_memory_space_constraint(x, space) for x, space in zip(operands, spaces)]
    specs = [pl.BlockSpec(memory_space=space) for space in spaces]
    return pl.pallas_call(
        kernel,
        out_shape=outs,
        in_specs=specs,
        out_specs=[pl.BlockSpec(memory_space=pltpu.VMEM)] * len(outs),
        scratch_shapes=list(scratch),
        compiler_params=pltpu.CompilerParams(vmem_limit_bytes=VMEM_LIMIT),
        cost_estimate=pl.CostEstimate(flops=flops, bytes_accessed=1 << 16, transcendentals=0),
    )(*placed)


def near(*shape):
    return pltpu.VMEM(shape, F32)


def far(*shape):
    return jax.ShapeDtypeStruct(shape, F32)


def bits_of(count):
    if count & (count - 1):
        raise ValueError("axis size")
    return [1 << b for b in range(count.bit_length() - 1)]


def groups_of(bits, size=2):
    return [bits[i : i + size] for i in range(0, len(bits), size)]


def masks_of(group):
    masks = [0]
    for bit in group:
        masks = [mask | bit for mask in masks] + masks
    return masks


def swap(values):
    return lax.ppermute(values, ALL, [(i, i ^ 1) for i in range(lax.axis_size(ALL))])


def exchange(values, mask, other_core=True):
    return lax.ppermute(values, ALL, [(i, i ^ mask ^ other_core) for i in range(lax.axis_size(ALL))])


def tree(parts):
    while len(parts) > 1:
        parts = [a + b for a, b in zip(parts[::2], parts[1::2])]
    return parts[0]


def smp_index():
    return lax.axis_index("smp")


def pack(gram):
    half = gram.shape[0] // 2
    rows = lax.broadcasted_iota(jnp.int32, (half, 2 * half), 0)
    columns = lax.broadcasted_iota(jnp.int32, (half, 2 * half), 1)
    top, bottom = gram[:half], gram[half:]
    packed = jnp.where(rows <= columns, top, pltpu.roll(bottom, half, 1))
    return packed, jnp.sum(jnp.where(columns == rows + half, bottom, 0.0), axis=0, keepdims=True)


def unpack(packed, diagonal):
    half = packed.shape[0]
    rows = lax.broadcasted_iota(jnp.int32, packed.shape, 0)
    columns = lax.broadcasted_iota(jnp.int32, packed.shape, 1)
    turned = jnp.concatenate([packed, packed], axis=0).T
    top = jnp.where(rows <= columns, packed, turned[:half])
    corner = jnp.where(columns < rows + half, pltpu.roll(packed, half, 1), turned[:half])
    corner = jnp.where(columns == rows + half, diagonal, corner)
    return jnp.concatenate([top, jnp.where(columns < half, turned[half:], corner)], axis=0)


def core_rows(core, rows, block=0):
    return pl.ds(pl.multiple_of((2 * block + core) * rows, rows), rows)


def per_device(ensemble, voxel_factor, sample_factor, time_factor, weights):
    vox_rows, smp_rows, times = ensemble.shape
    rank = voxel_factor.shape[1]
    flat_rows = vox_rows * smp_rows
    vox_count, smp_count = lax.axis_size("vox"), lax.axis_size("smp")
    vox_total, smp_total = vox_rows * vox_count, smp_rows * smp_count
    chips, chip_rows = smp_count // 2, 2 * smp_rows
    chip_bits = bits_of(smp_count)[1:]
    vox_bits = [bit * smp_count for bit in bits_of(vox_count)]
    chunks = 4 if vox_rows % 32 == 0 else 1
    chunk_vox = vox_rows // chunks
    chunk_rows = chunk_vox * smp_rows

    def open_kernel(x_hbm, c_hbm, b_hbm, a_hbm, w_hbm, x, c, a, w, out, con, sems):
        copies = [pltpu.make_async_copy(c_hbm, c, sems.at[0])]
        copies += [pltpu.make_async_copy(b_hbm, out.at[pl.ds(vox_rows, smp_rows), :], sems.at[1])]
        for n in range(chunks):
            part = pl.ds(n * chunk_rows, chunk_rows)
            copies.append(pltpu.make_async_copy(x_hbm.at[part, :], x.at[part, :], sems.at[2 + n]))
        copies.append(pltpu.make_async_copy(a_hbm, a, sems.at[2 + chunks]))
        copies.append(pltpu.make_async_copy(w_hbm, w, sems.at[3 + chunks]))
        for copy in copies:
            copy.start()
        copies[0].wait()
        copies[1].wait()
        factor = both(c[...])
        b = out[pl.ds(vox_rows, smp_rows), :]
        for n in range(chunks):
            copies[2 + n].wait()
            rows = pl.ds(n * chunk_vox, chunk_vox)
            blocks = [x[pl.ds(n * chunk_rows + j, chunk_vox, stride=smp_rows), :] for j in range(smp_rows)]
            blocks = jnp.concatenate([halves(block, 1) for block in blocks], axis=0)
            made = fold(jnp.dot(blocks, factor, preferred_element_type=F32)).reshape(smp_rows, chunk_vox, rank)
            con[:, rows, :] = made
            total = made[0] * b[:1, :]
            for j in range(1, smp_rows):
                total = total + made[j] * b[j : j + 1, :]
            out[rows, :] = total
        copies[2 + chunks].wait()
        copies[3 + chunks].wait()

    x, c_near, a_near, w_row, opened, con = call(
        open_kernel,
        (
            near(flat_rows, times),
            near(times, rank),
            near(vox_rows, rank),
            near(1, rank),
            near(vox_rows + smp_rows, rank),
            near(smp_rows, vox_rows, rank),
        ),
        (ensemble.reshape(flat_rows, times), time_factor, sample_factor, voxel_factor, weights.reshape(1, rank)),
        2 * flat_rows * times * rank * 6,
        scratch=(pltpu.SemaphoreType.DMA((4 + chunks,)),),
        in_hbm=5,
    )

    def weigh_kernel(c, w, outer, outer_c):
        squared = dot_rows(w[...], w[...])
        outer[...] = squared
        outer_c[...] = squared * dot_rows(c[...], c[...])

    outer, outer_c = call(
        weigh_kernel, (near(rank, rank), near(rank, rank)), (c_near, w_row), 2 * rank * rank * times * 6
    )

    got = swap(opened)
    terms = opened[:vox_rows] + got[:vox_rows]
    own_b = jnp.concatenate([opened[vox_rows:], got[vox_rows:]], axis=0)
    for group in groups_of(chip_bits):
        packet = jnp.concatenate([terms, own_b], axis=0)
        parts = [exchange(packet, mask) for mask in masks_of(group)[:-1]] + [packet]
        terms = tree([part[:vox_rows] for part in parts])
        own_b = jnp.concatenate([part[vox_rows:] for part in parts], axis=0)

    half, rail = rank // 2, rank // 4

    def voxel_kernel(terms, rows, a, w, outer_c, con, moved_out, chip_b, out, all_b, packed_all):
        core, chip = smp_index() & 1, smp_index() // 2
        for p in range(chips):
            flip = chips - 1 - p
            hops = sum(1 for group in groups_of(bits_of(chips)) if flip & sum(group))
            for q in range(2):
                place = core_rows(core ^ (hops & 1) ^ q, smp_rows, block=chip ^ flip)
                start = (2 * p + q) * smp_rows
                all_b[place, :] = rows[start : start + smp_rows, :]
        b = all_b[...]
        chip_b[...] = all_b[pl.ds(pl.multiple_of(chip * chip_rows, chip_rows), chip_rows), :]
        coupled = outer_c[...] * dot_rows(b, b)
        moved = a[...] - step_of(coupled) * (dot(a[...], coupled) - terms[...] * w[...])
        moved_out[...] = moved
        packed, diagonal = pack(dot_rows(moved, moved))
        packed_all[...] = packed
        out[:rail, :] = packed_all[core_rows(core, rail), :]
        for j in range(smp_rows):
            out[rail + j : rail + j + 1, :] = jnp.sum(con[j] * moved, axis=0, keepdims=True)
        out[rail + smp_rows :, :] = jnp.broadcast_to(diagonal, (8, rank))

    moved_a, chip_b, sums = call(
        voxel_kernel,
        (near(vox_rows, rank), near(chip_rows, rank), near(rail + smp_rows + 8, rank)),
        (terms, own_b, a_near, w_row, outer_c, con),
        2 * rank * rank * vox_rows * 12,
        scratch=(near(smp_total, rank), near(half, rank)),
    )
    mate_x = swap(x)

    turns = 0
    groups = groups_of(vox_bits)
    for group in groups[:-1]:
        sums = tree([exchange(sums, mask) for mask in masks_of(group)])
        turns ^= 1
    masks = masks_of(groups[-1])
    same = tree([exchange(sums, mask, False) for mask in masks[:-1]] + [sums])
    other = tree([exchange(sums, mask) for mask in masks])

    def time_kernel(x, mate_x, moved, each):
        for i, source in enumerate((x, mate_x)):
            for j in range(smp_rows):
                block = source[pl.ds(j, vox_rows, stride=smp_rows), :]
                each[i * smp_rows + j] = dot_rows(block, moved[...])

    (each,) = call(
        time_kernel, (near(chip_rows, times, rank),), (x, mate_x, moved_a), 4 * flat_rows * times * rank * 4
    )

    time_half = times // 2

    def sample_kernel(same, other, b, w, outer_c, each, gram_out, out, packed, raw, moved_all):
        core = smp_index() & 1
        for part, owner in ((same, core ^ turns), (other, core ^ turns ^ 1)):
            packed[core_rows(owner, rail), :] = part[:rail, :]
            raw[core_rows(owner, smp_rows), :] = part[rail : rail + smp_rows, :]
        gram_out[...] = unpack(packed[...], same[rail + smp_rows : rail + smp_rows + 1, :])
        coupled = outer_c[...] * gram_out[...]
        moved_all[...] = b[...] - step_of(coupled) * (dot(b[...], coupled) - raw[...] * w[...])
        total = None
        for i in range(2):
            moved = moved_all[core_rows(core ^ i, smp_rows), :]
            if i == 0:
                out[time_half:, :] = moved
            for j in range(smp_rows):
                made = each[i * smp_rows + j, core_rows(core, time_half), :] * moved[j : j + 1, :]
                total = made if total is None else total + made
        out[:time_half, :] = total

    gram_a, payload = call(
        sample_kernel,
        (near(rank, rank), near(time_half + smp_rows, rank)),
        (same, other, chip_b, w_row, outer_c, each),
        2 * rank * rank * chip_rows * 4,
        scratch=(near(half, rank), near(chip_rows, rank), near(chip_rows, rank)),
    )

    def scale_kernel(gram, moved, outer, result, scales_out, weighed):
        scales = jnp.sqrt(diagonal_row(gram[...]) / vox_total + 1e-06)
        scales_out[...] = scales
        result[...] = moved[...] / scales
        weighed[...] = outer[...] * gram[...]

    voxel_result, scales_a, weighed = call(
        scale_kernel,
        (far(vox_rows, rank), near(1, rank), near(rank, rank)),
        (gram_a, moved_a, outer),
        vox_rows * rank * 8,
    )

    terms, rows_b = payload[:time_half], payload[time_half:]
    turns = rows_turns = 0
    smp_mask = sum(chip_bits)
    for group in groups_of(chip_bits + vox_bits):
        masks = masks_of(group)
        with_rows = any(mask & smp_mask for mask in masks)
        packet = jnp.concatenate([terms, rows_b], axis=0) if with_rows else terms
        parts = [exchange(packet, mask) for mask in masks]
        terms = tree([part[:time_half] for part in parts])
        turns ^= 1
        if with_rows:
            parts = [part for part, mask in zip(parts, masks) if not mask & ~smp_mask]
            rows_b = jnp.concatenate([part[time_half:] for part in parts], axis=0)
            rows_turns ^= 1
    mate_rows_b = swap(rows_b)

    def ready_kernel(rows, mate_rows, c, w, weighed, scales_a, b_out, base, gain, scale, all_b):
        core, chip = smp_index() & 1, smp_index() // 2
        for part, owner in ((rows, core ^ rows_turns), (mate_rows, core ^ rows_turns ^ 1)):
            for p in range(chips):
                place = core_rows(owner, smp_rows, block=chip ^ (chips - 1 - p))
                all_b[place, :] = part[p * smp_rows : (p + 1) * smp_rows, :]
        b = all_b[...]
        coupled = weighed[...] * dot_rows(b, b)
        step = step_of(coupled)
        base[...] = c[...] - step * dot(c[...], coupled)
        gain[...] = step * w[...]
        scales_b = jnp.sqrt(jnp.sum(b * b, axis=0, keepdims=True) / smp_total + 1e-06)
        scale[...] = w[...] * scales_a[...] * scales_b
        b_out[...] = all_b[core_rows(core, smp_rows, block=chip), :] / scales_b

    sample_result, base, gain, scale = call(
        ready_kernel,
        (far(smp_rows, rank), near(times, rank), near(1, rank), near(1, rank)),
        (rows_b, mate_rows_b, c_near, w_row, weighed, scales_a),
        2 * rank * rank * times * 4,
        scratch=(near(smp_total, rank),),
    )
    terms, base, gain, scale, voxel_result, sample_result = lax.optimization_barrier(
        (terms, base, gain, scale, voxel_result, sample_result)
    )
    mate_terms = swap(terms)

    def last_kernel(terms, mate_terms, base, gain, scale, c_out, w_out, summed):
        owner = smp_index() & 1 ^ turns
        summed[core_rows(owner, time_half), :] = terms[...]
        summed[core_rows(owner ^ 1, time_half), :] = mate_terms[...]
        moved = base[...] + summed[...] * gain[...]
        scales_c = jnp.sqrt(jnp.sum(moved * moved, axis=0, keepdims=True) / times + 1e-06)
        c_out[...] = moved / scales_c
        w_out[...] = scale[...] * scales_c

    time_result, scale_result = call(
        last_kernel,
        (far(times, rank), far(1, rank)),
        (terms, mate_terms, base, gain, scale),
        rank * times * 8,
        scratch=(near(times, rank),),
    )
    return voxel_result, sample_result, time_result, scale_result.reshape(rank)


def solution(mesh):
    return jax.shard_map(
        per_device,
        mesh=mesh,
        in_specs=(P("vox", "smp", None), P("vox", None), P("smp", None), P(), P()),
        out_specs=(P("vox", None), P("smp", None), P(), P()),
        check_vma=False,
    )
```

```python
import jax
import jax.numpy as jnp
from jax import lax
from jax.experimental import pallas as pl
from jax.experimental.pallas import tpu as pltpu
from jax.sharding import PartitionSpec as P

F32 = jnp.float32
BF16 = jnp.bfloat16
VMEM_LIMIT = 12 * 1024 * 1024
ALL = ("vox", "smp")


def halves(a, axis):
    high = a.astype(BF16)
    return jnp.concatenate([high, (a - high.astype(F32)).astype(BF16)], axis=axis)


def both(b):
    parts = halves(b, 1)
    return jnp.concatenate([parts, parts], axis=0)


def fold(product):
    width = product.shape[1] // 2
    return product[:, :width] + product[:, width:]


def dot(a, b):
    return fold(jnp.dot(halves(a, 1), both(b), preferred_element_type=F32))


def dot_rows(a, b):
    return fold(lax.dot_general(halves(a, 0), both(b), (((0,), (0,)), ((), ())), preferred_element_type=F32))


def step_of(coupled):
    sums = jnp.sum(jnp.abs(coupled), axis=0, keepdims=True)
    return 1.0 / jnp.max(sums, axis=1, keepdims=True)


def diagonal_row(gram):
    rows = lax.broadcasted_iota(jnp.int32, gram.shape, 0)
    columns = lax.broadcasted_iota(jnp.int32, gram.shape, 1)
    return jnp.sum(jnp.where(rows == columns, gram, 0.0), axis=0, keepdims=True)


def call(kernel, outs, operands, flops, scratch=(), in_hbm=0):
    spaces = [pltpu.HBM if i < in_hbm else pltpu.VMEM for i in range(len(operands))]
    placed = [pltpu.with_memory_space_constraint(x, space) for x, space in zip(operands, spaces)]
    specs = [pl.BlockSpec(memory_space=space) for space in spaces]
    return pl.pallas_call(
        kernel,
        out_shape=outs,
        in_specs=specs,
        out_specs=[pl.BlockSpec(memory_space=pltpu.VMEM)] * len(outs),
        scratch_shapes=list(scratch),
        compiler_params=pltpu.CompilerParams(vmem_limit_bytes=VMEM_LIMIT),
        cost_estimate=pl.CostEstimate(flops=flops, bytes_accessed=1 << 16, transcendentals=0),
    )(*placed)


def near(*shape):
    return pltpu.VMEM(shape, F32)


def far(*shape):
    return jax.ShapeDtypeStruct(shape, F32)


def bits_of(count):
    if count & (count - 1):
        raise ValueError("axis size")
    return [1 << b for b in range(count.bit_length() - 1)]


def groups_of(bits, size=2):
    return [bits[i : i + size] for i in range(0, len(bits), size)]


def masks_of(group):
    masks = [0]
    for bit in group:
        masks = [mask | bit for mask in masks] + masks
    return masks


def swap(values):
    return lax.ppermute(values, ALL, [(i, i ^ 1) for i in range(lax.axis_size(ALL))])


def send(values, holder, mask):
    count = lax.axis_size(ALL)
    pairs = [(i, i ^ 1 ^ mask if i & 1 == holder else i ^ 1) for i in range(count)]
    return lax.ppermute(values, ALL, pairs)


def fan(values, holder, masks):
    sent = [send(values, holder, mask) if mask else swap(values) for mask in reversed(masks)]
    return sent[::-1]


def tree(parts):
    parts = parts[::-1]
    while len(parts) > 1:
        parts = [a + b for a, b in zip(parts[::2], parts[1::2])]
    return parts[0]


def smp_index():
    return lax.axis_index("smp")


def on_core(core, own, got):
    return jnp.where(smp_index() & 1 == core, own, got)


def pack(gram):
    half = gram.shape[0] // 2
    rows = lax.broadcasted_iota(jnp.int32, (half, 2 * half), 0)
    columns = lax.broadcasted_iota(jnp.int32, (half, 2 * half), 1)
    top, bottom = gram[:half], gram[half:]
    packed = jnp.where(rows <= columns, top, pltpu.roll(bottom, half, 1))
    return packed, jnp.sum(jnp.where(columns == rows + half, bottom, 0.0), axis=0, keepdims=True)


def unpack(packed, diagonal):
    half = packed.shape[0]
    rows = lax.broadcasted_iota(jnp.int32, packed.shape, 0)
    columns = lax.broadcasted_iota(jnp.int32, packed.shape, 1)
    turned = jnp.concatenate([packed, packed], axis=0).T
    top = jnp.where(rows <= columns, packed, turned[:half])
    corner = jnp.where(columns < rows + half, pltpu.roll(packed, half, 1), turned[:half])
    corner = jnp.where(columns == rows + half, diagonal, corner)
    return jnp.concatenate([top, jnp.where(columns < half, turned[half:], corner)], axis=0)


def in_order(rows, scratch, chips):
    block = scratch.shape[0] // chips
    chip = smp_index() // 2
    for p in range(chips):
        scratch[pl.ds(pl.multiple_of((chip ^ (chips - 1 - p)) * block, block), block), :] = rows[p * block : (p + 1) * block, :]
    return scratch[...]


def per_device(ensemble, voxel_factor, sample_factor, time_factor, weights):
    vox_rows, smp_rows, times = ensemble.shape
    rank = voxel_factor.shape[1]
    flat_rows = vox_rows * smp_rows
    vox_count, smp_count = lax.axis_size("vox"), lax.axis_size("smp")
    vox_total, smp_total = vox_rows * vox_count, smp_rows * smp_count
    chips, chip_rows = smp_count // 2, 2 * smp_rows
    chip_bits = bits_of(smp_count)[1:]
    vox_bits = [bit * smp_count for bit in bits_of(vox_count)]
    chunks = 4 if vox_rows % 32 == 0 else 1
    chunk_vox = vox_rows // chunks
    chunk_rows = chunk_vox * smp_rows

    def open_kernel(x_hbm, c_hbm, b_hbm, a_hbm, w_hbm, x, c, a, w, out, con, sems):
        copies = [pltpu.make_async_copy(c_hbm, c, sems.at[0])]
        copies += [pltpu.make_async_copy(b_hbm, out.at[pl.ds(vox_rows, smp_rows), :], sems.at[1])]
        for n in range(chunks):
            part = pl.ds(n * chunk_rows, chunk_rows)
            copies.append(pltpu.make_async_copy(x_hbm.at[part, :], x.at[part, :], sems.at[2 + n]))
        copies.append(pltpu.make_async_copy(a_hbm, a, sems.at[2 + chunks]))
        copies.append(pltpu.make_async_copy(w_hbm, w, sems.at[3 + chunks]))
        for copy in copies:
            copy.start()
        copies[0].wait()
        copies[1].wait()
        factor = both(c[...])
        b = out[pl.ds(vox_rows, smp_rows), :]
        for n in range(chunks):
            copies[2 + n].wait()
            rows = pl.ds(n * chunk_vox, chunk_vox)
            blocks = [x[pl.ds(n * chunk_rows + j, chunk_vox, stride=smp_rows), :] for j in range(smp_rows)]
            blocks = jnp.concatenate([halves(block, 1) for block in blocks], axis=0)
            made = fold(jnp.dot(blocks, factor, preferred_element_type=F32)).reshape(smp_rows, chunk_vox, rank)
            con[:, rows, :] = made
            total = made[0] * b[:1, :]
            for j in range(1, smp_rows):
                total = total + made[j] * b[j : j + 1, :]
            out[rows, :] = total
        copies[2 + chunks].wait()
        copies[3 + chunks].wait()

    x, c_near, a_near, w_row, opened, con = call(
        open_kernel,
        (
            near(flat_rows, times),
            near(times, rank),
            near(vox_rows, rank),
            near(1, rank),
            near(vox_rows + smp_rows, rank),
            near(smp_rows, vox_rows, rank),
        ),
        (ensemble.reshape(flat_rows, times), time_factor, sample_factor, voxel_factor, weights.reshape(1, rank)),
        2 * flat_rows * times * rank * 6,
        scratch=(pltpu.SemaphoreType.DMA((4 + chunks,)),),
        in_hbm=5,
    )

    def weigh_kernel(c, w, outer, outer_c):
        squared = dot_rows(w[...], w[...])
        outer[...] = squared
        outer_c[...] = squared * dot_rows(c[...], c[...])

    outer, outer_c = call(
        weigh_kernel, (near(rank, rank), near(rank, rank)), (c_near, w_row), 2 * rank * rank * times * 6
    )

    got = swap(opened)
    terms = opened[:vox_rows] + got[:vox_rows]
    mate_con, mate_x = swap(con), swap(x)
    packet = jnp.concatenate([terms, got[vox_rows:], opened[vox_rows:]], axis=0)
    own = jnp.concatenate([terms, opened[vox_rows:], got[vox_rows:]], axis=0)
    rows_b = own[vox_rows:]
    holder = 1
    for group in groups_of(chip_bits):
        parts = [send(packet, holder, mask) for mask in masks_of(group)[:-1]] + [own]
        terms = tree([part[:vox_rows] for part in parts])
        rows_b = jnp.concatenate([part[vox_rows:] for part in parts], axis=0)
        packet = jnp.concatenate([terms, rows_b], axis=0)
        own = swap(packet)
        holder ^= 1
    voxel_core = holder

    half, sums_rows = rank // 2, rank // 2 + chip_rows

    def voxel_kernel(terms, rows, a, w, outer_c, con, mate_con, mate_x, moved_out, chip_b, out, all_b):
        b = in_order(rows, all_b, chips)
        chip_b[...] = all_b[pl.ds(pl.multiple_of(smp_index() // 2 * chip_rows, chip_rows), chip_rows), :]
        coupled = outer_c[...] * dot_rows(b, b)
        moved = a[...] - step_of(coupled) * (dot(a[...], coupled) - terms[...] * w[...])
        moved_out[...] = moved
        packed, diagonal = pack(dot_rows(moved, moved))
        out[:half, :] = packed
        for core in range(2):
            for j in range(smp_rows):
                row = half + core * smp_rows + j
                out[row : row + 1, :] = jnp.sum((con if core == voxel_core else mate_con)[j] * moved, axis=0, keepdims=True)
        out[sums_rows:, :] = jnp.broadcast_to(diagonal, (8, rank))

    moved_a, chip_b, sums = call(
        voxel_kernel,
        (near(vox_rows, rank), near(chip_rows, rank), near(sums_rows + 8, rank)),
        (terms, rows_b, a_near, w_row, outer_c, con, mate_con, mate_x),
        2 * rank * rank * vox_rows * 12,
        scratch=(near(smp_total, rank),),
    )

    mate_moved_a = swap(moved_a)

    for group in groups_of(vox_bits):
        sums = tree(fan(sums, holder, masks_of(group)))
        holder ^= 1
    sample_core = holder
    if sample_core != voxel_core:
        chip_b = swap(chip_b)

    def time_kernel(x, mate_x, moved, mate_moved, each):
        moved = on_core(voxel_core, moved[...], mate_moved[...])
        for core in range(2):
            for j in range(smp_rows):
                block = (x if core == sample_core else mate_x)[pl.ds(j, vox_rows, stride=smp_rows), :]
                each[core * smp_rows + j] = dot_rows(block, moved)

    (each,) = call(
        time_kernel,
        (near(chip_rows, times, rank),),
        (x, mate_x, moved_a, mate_moved_a),
        4 * flat_rows * times * rank * 6,
    )

    def sample_kernel(sums, b, w, outer_c, each, gram_out, out):
        gram = unpack(sums[:half, :], sums[sums_rows : sums_rows + 1, :])
        gram_out[...] = gram
        coupled = outer_c[...] * gram
        moved = b[...] - step_of(coupled) * (dot(b[...], coupled) - sums[half:sums_rows, :] * w[...])
        out[times:, :] = moved
        total = None
        for j in range(chip_rows):
            made = each[j] * moved[j : j + 1, :]
            total = made if total is None else total + made
        out[:times, :] = total

    gram_a, payload = call(
        sample_kernel,
        (near(rank, rank), near(times + chip_rows, rank)),
        (sums, chip_b, w_row, outer_c, each),
        2 * rank * rank * chip_rows * 6,
    )
    mate_gram_a = swap(gram_a)

    def scale_kernel(gram, mate_gram, moved, mate_moved, outer, result, scales_out, weighed):
        gram = on_core(sample_core, gram[...], mate_gram[...])
        scales = jnp.sqrt(diagonal_row(gram) / vox_total + 1e-06)
        scales_out[...] = scales
        result[...] = on_core(voxel_core, moved[...], mate_moved[...]) / scales
        weighed[...] = outer[...] * gram

    voxel_result, scales_a, weighed = call(
        scale_kernel,
        (far(vox_rows, rank), near(1, rank), near(rank, rank)),
        (gram_a, mate_gram_a, moved_a, mate_moved_a, outer),
        vox_rows * rank * 8,
    )

    terms, rows_b, rows_core = payload[:times], payload[times:], holder
    smp_mask = sum(chip_bits)
    for group in groups_of(chip_bits + vox_bits):
        masks = masks_of(group)
        if any(mask & smp_mask for mask in masks):
            packet = payload if rows_b.shape[0] == chip_rows else jnp.concatenate([terms, rows_b], axis=0)
            parts = fan(packet, holder, masks)
            gathered = [i for i, mask in enumerate(masks) if not mask & ~smp_mask]
            rows = rows_b.shape[0]

            def gather_kernel(*refs, gathered=gathered, rows=rows):
                parts, (terms, rows_out) = refs[-3::-1], refs[-2:]
                terms[...] = tree([part[:times, :] for part in parts])
                for p, i in enumerate(gathered):
                    rows_out[p * rows : (p + 1) * rows, :] = parts[i][times:, :]

            terms, rows_b = call(
                gather_kernel,
                (near(times, rank), near(len(gathered) * rows, rank)),
                parts[::-1],
                len(masks) * times * rank,
            )
            rows_core = holder ^ 1
        else:
            terms = tree(fan(terms, holder, masks))
        holder ^= 1
    last_core = holder
    mate_rows_b = swap(rows_b)

    def ready_kernel(rows, mate_rows, c, w, weighed, scales_a, b_out, base, gain, scale, all_b):
        b = in_order(on_core(rows_core, rows[...], mate_rows[...]), all_b, chips)
        coupled = weighed[...] * dot_rows(b, b)
        step = step_of(coupled)
        base[...] = c[...] - step * dot(c[...], coupled)
        gain[...] = step * w[...]
        scales_b = jnp.sqrt(jnp.sum(b * b, axis=0, keepdims=True) / smp_total + 1e-06)
        scale[...] = w[...] * scales_a[...] * scales_b
        b_out[...] = all_b[pl.ds(pl.multiple_of(smp_index() * smp_rows, smp_rows), smp_rows), :] / scales_b

    sample_result, base, gain, scale = call(
        ready_kernel,
        (far(smp_rows, rank), near(times, rank), near(1, rank), near(1, rank)),
        (rows_b, mate_rows_b, c_near, w_row, weighed, scales_a),
        2 * rank * rank * times * 4,
        scratch=(near(smp_total, rank),),
    )
    terms, base, gain, scale, voxel_result, sample_result = lax.optimization_barrier(
        (terms, base, gain, scale, voxel_result, sample_result)
    )
    mate_terms = swap(terms)

    def last_kernel(terms, mate_terms, base, gain, scale, c_out, w_out):
        moved = base[...] + on_core(last_core, terms[...], mate_terms[...]) * gain[...]
        scales_c = jnp.sqrt(jnp.sum(moved * moved, axis=0, keepdims=True) / times + 1e-06)
        c_out[...] = moved / scales_c
        w_out[...] = scale[...] * scales_c

    time_result, scale_result = call(
        last_kernel,
        (far(times, rank), far(1, rank)),
        (terms, mate_terms, base, gain, scale),
        rank * times * 8,
    )
    return voxel_result, sample_result, time_result, scale_result.reshape(rank)


def solution(mesh):
    return jax.shard_map(
        per_device,
        mesh=mesh,
        in_specs=(P("vox", "smp", None), P("vox", None), P("smp", None), P(), P()),
        out_specs=(P("vox", None), P("smp", None), P(), P()),
        check_vma=False,
    )
```

```python
import jax
import jax.numpy as jnp
from jax import lax
from jax.experimental import pallas as pl
from jax.experimental.pallas import tpu as pltpu
from jax.sharding import PartitionSpec as P

F32 = jnp.float32
BF16 = jnp.bfloat16
VMEM_LIMIT = 12 * 1024 * 1024
ALL = ("vox", "smp")


def halves(a, axis):
    high = a.astype(BF16)
    return jnp.concatenate([high, (a - high.astype(F32)).astype(BF16)], axis=axis)


def both(b):
    parts = halves(b, 1)
    return jnp.concatenate([parts, parts], axis=0)


def fold(product):
    width = product.shape[1] // 2
    return product[:, :width] + product[:, width:]


def dot(a, b):
    return fold(jnp.dot(halves(a, 1), both(b), preferred_element_type=F32))


def dot_rows(a, b):
    return fold(lax.dot_general(halves(a, 0), both(b), (((0,), (0,)), ((), ())), preferred_element_type=F32))


def step_of(coupled):
    sums = jnp.sum(jnp.abs(coupled), axis=0, keepdims=True)
    return 1.0 / jnp.max(sums, axis=1, keepdims=True)


def diagonal_row(gram):
    rows = lax.broadcasted_iota(jnp.int32, gram.shape, 0)
    columns = lax.broadcasted_iota(jnp.int32, gram.shape, 1)
    return jnp.sum(jnp.where(rows == columns, gram, 0.0), axis=0, keepdims=True)


def call(kernel, outs, operands, flops, scratch=(), in_hbm=0):
    spaces = [pltpu.HBM if i < in_hbm else pltpu.VMEM for i in range(len(operands))]
    placed = [pltpu.with_memory_space_constraint(x, space) for x, space in zip(operands, spaces)]
    specs = [pl.BlockSpec(memory_space=space) for space in spaces]
    return pl.pallas_call(
        kernel,
        out_shape=outs,
        in_specs=specs,
        out_specs=[pl.BlockSpec(memory_space=pltpu.VMEM)] * len(outs),
        scratch_shapes=list(scratch),
        compiler_params=pltpu.CompilerParams(vmem_limit_bytes=VMEM_LIMIT),
        cost_estimate=pl.CostEstimate(flops=flops, bytes_accessed=1 << 16, transcendentals=0),
    )(*placed)


def near(*shape):
    return pltpu.VMEM(shape, F32)


def far(*shape):
    return jax.ShapeDtypeStruct(shape, F32)


def bits_of(count):
    if count & (count - 1):
        raise ValueError("axis size")
    return [1 << b for b in range(count.bit_length() - 1)]


def groups_of(bits, size=2):
    return [bits[i : i + size] for i in range(0, len(bits), size)]


def masks_of(group):
    masks = [0]
    for bit in group:
        masks = [mask | bit for mask in masks] + masks
    return masks


def swap(values):
    return lax.ppermute(values, ALL, [(i, i ^ 1) for i in range(lax.axis_size(ALL))])


def send(values, holder, mask):
    count = lax.axis_size(ALL)
    pairs = [(i, i ^ 1 ^ mask if i & 1 == holder else i ^ 1) for i in range(count)]
    return lax.ppermute(values, ALL, pairs)


def fan(values, holder, masks):
    sent = [send(values, holder, mask) if mask else swap(values) for mask in reversed(masks)]
    return sent[::-1]


def tree(parts):
    parts = parts[::-1]
    while len(parts) > 1:
        parts = [a + b for a, b in zip(parts[::2], parts[1::2])]
    return parts[0]


def smp_index():
    return lax.axis_index("smp")


def on_core(core, own, got):
    return jnp.where(smp_index() & 1 == core, own, got)


def pack(gram):
    half = gram.shape[0] // 2
    rows = lax.broadcasted_iota(jnp.int32, (half, 2 * half), 0)
    columns = lax.broadcasted_iota(jnp.int32, (half, 2 * half), 1)
    top, bottom = gram[:half], gram[half:]
    packed = jnp.where(rows <= columns, top, pltpu.roll(bottom, half, 1))
    return packed, jnp.sum(jnp.where(columns == rows + half, bottom, 0.0), axis=0, keepdims=True)


def unpack(packed, diagonal):
    half = packed.shape[0]
    rows = lax.broadcasted_iota(jnp.int32, packed.shape, 0)
    columns = lax.broadcasted_iota(jnp.int32, packed.shape, 1)
    turned = jnp.concatenate([packed, packed], axis=0).T
    top = jnp.where(rows <= columns, packed, turned[:half])
    corner = jnp.where(columns < rows + half, pltpu.roll(packed, half, 1), turned[:half])
    corner = jnp.where(columns == rows + half, diagonal, corner)
    return jnp.concatenate([top, jnp.where(columns < half, turned[half:], corner)], axis=0)


def in_order(rows, scratch, chips):
    block = scratch.shape[0] // chips
    chip = smp_index() // 2
    for p in range(chips):
        scratch[pl.ds(pl.multiple_of((chip ^ (chips - 1 - p)) * block, block), block), :] = rows[p * block : (p + 1) * block, :]
    return scratch[...]


def per_device(ensemble, voxel_factor, sample_factor, time_factor, weights):
    vox_rows, smp_rows, times = ensemble.shape
    rank = voxel_factor.shape[1]
    flat_rows = vox_rows * smp_rows
    vox_count, smp_count = lax.axis_size("vox"), lax.axis_size("smp")
    vox_total, smp_total = vox_rows * vox_count, smp_rows * smp_count
    chips, chip_rows = smp_count // 2, 2 * smp_rows
    chip_bits = bits_of(smp_count)[1:]
    vox_bits = [bit * smp_count for bit in bits_of(vox_count)]
    chunks = 1
    chunk_vox = vox_rows // chunks
    chunk_rows = chunk_vox * smp_rows

    def open_kernel(x_hbm, c_hbm, b_hbm, a_hbm, w_hbm, x, c, a, w, out, con, sems):
        copies = [pltpu.make_async_copy(c_hbm, c, sems.at[0])]
        copies += [pltpu.make_async_copy(b_hbm, out.at[pl.ds(vox_rows, smp_rows), :], sems.at[1])]
        for n in range(chunks):
            part = pl.ds(n * chunk_rows, chunk_rows)
            copies.append(pltpu.make_async_copy(x_hbm.at[part, :], x.at[part, :], sems.at[2 + n]))
        copies.append(pltpu.make_async_copy(a_hbm, a, sems.at[2 + chunks]))
        copies.append(pltpu.make_async_copy(w_hbm, w, sems.at[3 + chunks]))
        for copy in copies:
            copy.start()
        copies[0].wait()
        copies[1].wait()
        factor = both(c[...])
        b = out[pl.ds(vox_rows, smp_rows), :]
        for n in range(chunks):
            copies[2 + n].wait()
            rows = pl.ds(n * chunk_vox, chunk_vox)
            blocks = [x[pl.ds(n * chunk_rows + j, chunk_vox, stride=smp_rows), :] for j in range(smp_rows)]
            blocks = jnp.concatenate([halves(block, 1) for block in blocks], axis=0)
            made = fold(jnp.dot(blocks, factor, preferred_element_type=F32)).reshape(smp_rows, chunk_vox, rank)
            con[:, rows, :] = made
            total = made[0] * b[:1, :]
            for j in range(1, smp_rows):
                total = total + made[j] * b[j : j + 1, :]
            out[rows, :] = total
        copies[2 + chunks].wait()
        copies[3 + chunks].wait()

    x, c_near, a_near, w_row, opened, con = call(
        open_kernel,
        (
            near(flat_rows, times),
            near(times, rank),
            near(vox_rows, rank),
            near(1, rank),
            near(vox_rows + smp_rows, rank),
            near(smp_rows, vox_rows, rank),
        ),
        (ensemble.reshape(flat_rows, times), time_factor, sample_factor, voxel_factor, weights.reshape(1, rank)),
        2 * flat_rows * times * rank * 6,
        scratch=(pltpu.SemaphoreType.DMA((4 + chunks,)),),
        in_hbm=5,
    )

    def weigh_kernel(c, w, outer, outer_c):
        squared = dot_rows(w[...], w[...])
        outer[...] = squared
        outer_c[...] = squared * dot_rows(c[...], c[...])

    outer, outer_c = call(
        weigh_kernel, (near(rank, rank), near(rank, rank)), (c_near, w_row), 2 * rank * rank * times * 6
    )

    got = swap(opened)
    terms = opened[:vox_rows] + got[:vox_rows]
    mate_con, mate_x = swap(con), swap(x)
    packet = jnp.concatenate([terms, got[vox_rows:], opened[vox_rows:]], axis=0)
    own = jnp.concatenate([terms, opened[vox_rows:], got[vox_rows:]], axis=0)
    rows_b = own[vox_rows:]
    holder = 1
    for group in groups_of(chip_bits):
        parts = [send(packet, holder, mask) for mask in masks_of(group)[:-1]] + [own]
        terms = tree([part[:vox_rows] for part in parts])
        rows_b = jnp.concatenate([part[vox_rows:] for part in parts], axis=0)
        packet = jnp.concatenate([terms, rows_b], axis=0)
        own = swap(packet)
        holder ^= 1
    voxel_core = holder

    half, sums_rows = rank // 2, rank // 2 + chip_rows

    def voxel_kernel(terms, rows, a, w, outer_c, con, mate_con, mate_x, moved_out, chip_b, out, all_b):
        b = in_order(rows, all_b, chips)
        chip_b[...] = all_b[pl.ds(pl.multiple_of(smp_index() // 2 * chip_rows, chip_rows), chip_rows), :]
        coupled = outer_c[...] * dot_rows(b, b)
        moved = a[...] - step_of(coupled) * (dot(a[...], coupled) - terms[...] * w[...])
        moved_out[...] = moved
        packed, diagonal = pack(dot_rows(moved, moved))
        out[:half, :] = packed
        for core in range(2):
            for j in range(smp_rows):
                row = half + core * smp_rows + j
                out[row : row + 1, :] = jnp.sum((con if core == voxel_core else mate_con)[j] * moved, axis=0, keepdims=True)
        out[sums_rows:, :] = jnp.broadcast_to(diagonal, (8, rank))

    moved_a, chip_b, sums = call(
        voxel_kernel,
        (near(vox_rows, rank), near(chip_rows, rank), near(sums_rows + 8, rank)),
        (terms, rows_b, a_near, w_row, outer_c, con, mate_con, mate_x),
        2 * rank * rank * vox_rows * 12,
        scratch=(near(smp_total, rank),),
    )

    mate_moved_a = swap(moved_a)

    for group in groups_of(vox_bits):
        sums = tree(fan(sums, holder, masks_of(group)))
        holder ^= 1
    sample_core = holder
    if sample_core != voxel_core:
        chip_b = swap(chip_b)

    def time_kernel(x, mate_x, moved, mate_moved, each):
        moved = on_core(voxel_core, moved[...], mate_moved[...])
        for core in range(2):
            for j in range(smp_rows):
                block = (x if core == sample_core else mate_x)[pl.ds(j, vox_rows, stride=smp_rows), :]
                each[core * smp_rows + j] = dot_rows(block, moved)

    (each,) = call(
        time_kernel,
        (near(chip_rows, times, rank),),
        (x, mate_x, moved_a, mate_moved_a),
        4 * flat_rows * times * rank * 6,
    )

    def sample_kernel(sums, b, w, outer_c, each, gram_out, out):
        gram = unpack(sums[:half, :], sums[sums_rows : sums_rows + 1, :])
        gram_out[...] = gram
        coupled = outer_c[...] * gram
        moved = b[...] - step_of(coupled) * (dot(b[...], coupled) - sums[half:sums_rows, :] * w[...])
        out[times:, :] = moved
        total = None
        for j in range(chip_rows):
            made = each[j] * moved[j : j + 1, :]
            total = made if total is None else total + made
        out[:times, :] = total

    gram_a, payload = call(
        sample_kernel,
        (near(rank, rank), near(times + chip_rows, rank)),
        (sums, chip_b, w_row, outer_c, each),
        2 * rank * rank * chip_rows * 6,
    )
    mate_gram_a = swap(gram_a)

    def scale_kernel(gram, mate_gram, moved, mate_moved, outer, result, scales_out, weighed):
        gram = on_core(sample_core, gram[...], mate_gram[...])
        scales = jnp.sqrt(diagonal_row(gram) / vox_total + 1e-06)
        scales_out[...] = scales
        result[...] = on_core(voxel_core, moved[...], mate_moved[...]) / scales
        weighed[...] = outer[...] * gram

    voxel_result, scales_a, weighed = call(
        scale_kernel,
        (far(vox_rows, rank), near(1, rank), near(rank, rank)),
        (gram_a, mate_gram_a, moved_a, mate_moved_a, outer),
        vox_rows * rank * 8,
    )

    terms, rows_b, rows_core = payload[:times], payload[times:], holder
    smp_mask = sum(chip_bits)
    for group in groups_of(chip_bits + vox_bits):
        masks = masks_of(group)
        if any(mask & smp_mask for mask in masks):
            packet = payload if rows_b.shape[0] == chip_rows else jnp.concatenate([terms, rows_b], axis=0)
            parts = fan(packet, holder, masks)
            gathered = [i for i, mask in enumerate(masks) if not mask & ~smp_mask]
            rows = rows_b.shape[0]

            def gather_kernel(*refs, gathered=gathered, rows=rows):
                parts, (terms, rows_out) = refs[-3::-1], refs[-2:]
                terms[...] = tree([part[:times, :] for part in parts])
                for p, i in enumerate(gathered):
                    rows_out[p * rows : (p + 1) * rows, :] = parts[i][times:, :]

            terms, rows_b = call(
                gather_kernel,
                (near(times, rank), near(len(gathered) * rows, rank)),
                parts[::-1],
                len(masks) * times * rank,
            )
            rows_core = holder ^ 1
        else:
            terms = tree(fan(terms, holder, masks))
        holder ^= 1
    last_core = holder
    mate_rows_b = swap(rows_b)

    def ready_kernel(rows, mate_rows, c, w, weighed, scales_a, b_out, base, gain, scale, all_b):
        b = in_order(on_core(rows_core, rows[...], mate_rows[...]), all_b, chips)
        coupled = weighed[...] * dot_rows(b, b)
        step = step_of(coupled)
        base[...] = c[...] - step * dot(c[...], coupled)
        gain[...] = step * w[...]
        scales_b = jnp.sqrt(jnp.sum(b * b, axis=0, keepdims=True) / smp_total + 1e-06)
        scale[...] = w[...] * scales_a[...] * scales_b
        b_out[...] = all_b[pl.ds(pl.multiple_of(smp_index() * smp_rows, smp_rows), smp_rows), :] / scales_b

    sample_result, base, gain, scale = call(
        ready_kernel,
        (far(smp_rows, rank), near(times, rank), near(1, rank), near(1, rank)),
        (rows_b, mate_rows_b, c_near, w_row, weighed, scales_a),
        2 * rank * rank * times * 4,
        scratch=(near(smp_total, rank),),
    )
    terms, base, gain, scale, voxel_result, sample_result = lax.optimization_barrier(
        (terms, base, gain, scale, voxel_result, sample_result)
    )
    mate_terms = swap(terms)

    def last_kernel(terms, mate_terms, base, gain, scale, c_out, w_out):
        moved = base[...] + on_core(last_core, terms[...], mate_terms[...]) * gain[...]
        scales_c = jnp.sqrt(jnp.sum(moved * moved, axis=0, keepdims=True) / times + 1e-06)
        c_out[...] = moved / scales_c
        w_out[...] = scale[...] * scales_c

    time_result, scale_result = call(
        last_kernel,
        (far(times, rank), far(1, rank)),
        (terms, mate_terms, base, gain, scale),
        rank * times * 8,
    )
    return voxel_result, sample_result, time_result, scale_result.reshape(rank)


def solution(mesh):
    return jax.shard_map(
        per_device,
        mesh=mesh,
        in_specs=(P("vox", "smp", None), P("vox", None), P("smp", None), P(), P()),
        out_specs=(P("vox", None), P("smp", None), P(), P()),
        check_vma=False,
    )
```

```python
import jax
import jax.numpy as jnp
from jax import lax
from jax.experimental import pallas as pl
from jax.experimental.pallas import tpu as pltpu
from jax.sharding import PartitionSpec as P

F32 = jnp.float32
BF16 = jnp.bfloat16
VMEM_LIMIT = 12 * 1024 * 1024
ALL = ("vox", "smp")


def halves(a, axis):
    high = a.astype(BF16)
    return jnp.concatenate([high, (a - high.astype(F32)).astype(BF16)], axis=axis)


def both(b):
    parts = halves(b, 1)
    return jnp.concatenate([parts, parts], axis=0)


def fold(product):
    width = product.shape[1] // 2
    return product[:, :width] + product[:, width:]


def dot(a, b):
    return fold(jnp.dot(halves(a, 1), both(b), preferred_element_type=F32))


def dot_rows(a, b):
    return fold(lax.dot_general(halves(a, 0), both(b), (((0,), (0,)), ((), ())), preferred_element_type=F32))


def step_of(coupled):
    sums = jnp.sum(jnp.abs(coupled), axis=0, keepdims=True)
    return 1.0 / jnp.max(sums, axis=1, keepdims=True)


def diagonal_row(gram):
    rows = lax.broadcasted_iota(jnp.int32, gram.shape, 0)
    columns = lax.broadcasted_iota(jnp.int32, gram.shape, 1)
    return jnp.sum(jnp.where(rows == columns, gram, 0.0), axis=0, keepdims=True)


def call(kernel, outs, operands, flops, scratch=(), in_hbm=0):
    spaces = [pltpu.HBM if i < in_hbm else pltpu.VMEM for i in range(len(operands))]
    placed = [pltpu.with_memory_space_constraint(x, space) for x, space in zip(operands, spaces)]
    specs = [pl.BlockSpec(memory_space=space) for space in spaces]
    return pl.pallas_call(
        kernel,
        out_shape=outs,
        in_specs=specs,
        out_specs=[pl.BlockSpec(memory_space=pltpu.VMEM)] * len(outs),
        scratch_shapes=list(scratch),
        compiler_params=pltpu.CompilerParams(vmem_limit_bytes=VMEM_LIMIT),
        cost_estimate=pl.CostEstimate(flops=flops, bytes_accessed=1 << 16, transcendentals=0),
    )(*placed)


def near(*shape):
    return pltpu.VMEM(shape, F32)


def far(*shape):
    return jax.ShapeDtypeStruct(shape, F32)


def bits_of(count):
    if count & (count - 1):
        raise ValueError("axis size")
    return [1 << b for b in range(count.bit_length() - 1)]


def groups_of(bits, size=2):
    return [bits[i : i + size] for i in range(0, len(bits), size)]


def masks_of(group):
    masks = [0]
    for bit in group:
        masks = [mask | bit for mask in masks] + masks
    return masks


def swap(values):
    return lax.ppermute(values, ALL, [(i, i ^ 1) for i in range(lax.axis_size(ALL))])


def send(values, holder, mask):
    count = lax.axis_size(ALL)
    pairs = [(i, i ^ 1 ^ mask if i & 1 == holder else i ^ 1) for i in range(count)]
    return lax.ppermute(values, ALL, pairs)


def fan(values, holder, masks):
    sent = [send(values, holder, mask) if mask else swap(values) for mask in reversed(masks)]
    return sent[::-1]


def tree(parts):
    parts = parts[::-1]
    while len(parts) > 1:
        parts = [a + b for a, b in zip(parts[::2], parts[1::2])]
    return parts[0]


def smp_index():
    return lax.axis_index("smp")


def on_core(core, own, got):
    return jnp.where(smp_index() & 1 == core, own, got)


def pack(gram):
    half = gram.shape[0] // 2
    rows = lax.broadcasted_iota(jnp.int32, (half, 2 * half), 0)
    columns = lax.broadcasted_iota(jnp.int32, (half, 2 * half), 1)
    top, bottom = gram[:half], gram[half:]
    packed = jnp.where(rows <= columns, top, pltpu.roll(bottom, half, 1))
    return packed, jnp.sum(jnp.where(columns == rows + half, bottom, 0.0), axis=0, keepdims=True)


def unpack(packed, diagonal):
    half = packed.shape[0]
    rows = lax.broadcasted_iota(jnp.int32, packed.shape, 0)
    columns = lax.broadcasted_iota(jnp.int32, packed.shape, 1)
    turned = jnp.concatenate([packed, packed], axis=0).T
    top = jnp.where(rows <= columns, packed, turned[:half])
    corner = jnp.where(columns < rows + half, pltpu.roll(packed, half, 1), turned[:half])
    corner = jnp.where(columns == rows + half, diagonal, corner)
    return jnp.concatenate([top, jnp.where(columns < half, turned[half:], corner)], axis=0)


def in_order(rows, scratch, chips):
    block = scratch.shape[0] // chips
    chip = smp_index() // 2
    for p in range(chips):
        scratch[pl.ds(pl.multiple_of((chip ^ (chips - 1 - p)) * block, block), block), :] = rows[p * block : (p + 1) * block, :]
    return scratch[...]


def per_device(ensemble, voxel_factor, sample_factor, time_factor, weights):
    vox_rows, smp_rows, times = ensemble.shape
    rank = voxel_factor.shape[1]
    flat_rows = vox_rows * smp_rows
    vox_count, smp_count = lax.axis_size("vox"), lax.axis_size("smp")
    vox_total, smp_total = vox_rows * vox_count, smp_rows * smp_count
    chips, chip_rows = smp_count // 2, 2 * smp_rows
    chip_bits = bits_of(smp_count)[1:]
    vox_bits = [bit * smp_count for bit in bits_of(vox_count)]
    chunks = 1
    chunk_vox = vox_rows // chunks
    chunk_rows = chunk_vox * smp_rows

    def open_kernel(x_hbm, c_hbm, b_hbm, a_hbm, w_hbm, x, c, a, w, out, con, sems):
        copies = [pltpu.make_async_copy(c_hbm, c, sems.at[0])]
        copies += [pltpu.make_async_copy(b_hbm, out.at[pl.ds(vox_rows, smp_rows), :], sems.at[1])]
        for n in range(chunks):
            part = pl.ds(n * chunk_rows, chunk_rows)
            copies.append(pltpu.make_async_copy(x_hbm.at[part, :], x.at[part, :], sems.at[2 + n]))
        copies.append(pltpu.make_async_copy(a_hbm, a, sems.at[2 + chunks]))
        copies.append(pltpu.make_async_copy(w_hbm, w, sems.at[3 + chunks]))
        for copy in copies:
            copy.start()
        copies[0].wait()
        copies[1].wait()
        factor = both(c[...])
        b = out[pl.ds(vox_rows, smp_rows), :]
        for n in range(chunks):
            copies[2 + n].wait()
            rows = pl.ds(n * chunk_vox, chunk_vox)
            blocks = [x[pl.ds(n * chunk_rows + j, chunk_vox, stride=smp_rows), :] for j in range(smp_rows)]
            blocks = jnp.concatenate([halves(block, 1) for block in blocks], axis=0)
            made = fold(jnp.dot(blocks, factor, preferred_element_type=F32)).reshape(smp_rows, chunk_vox, rank)
            con[:, rows, :] = made
            total = made[0] * b[:1, :]
            for j in range(1, smp_rows):
                total = total + made[j] * b[j : j + 1, :]
            out[rows, :] = total
        copies[2 + chunks].wait()
        copies[3 + chunks].wait()

    x, c_near, a_near, w_row, opened, con = call(
        open_kernel,
        (
            near(flat_rows, times),
            near(times, rank),
            near(vox_rows, rank),
            near(1, rank),
            near(vox_rows + smp_rows, rank),
            near(smp_rows, vox_rows, rank),
        ),
        (ensemble.reshape(flat_rows, times), time_factor, sample_factor, voxel_factor, weights.reshape(1, rank)),
        2 * flat_rows * times * rank * 6,
        scratch=(pltpu.SemaphoreType.DMA((4 + chunks,)),),
        in_hbm=5,
    )

    def weigh_kernel(c, w, outer, outer_c):
        squared = dot_rows(w[...], w[...])
        outer[...] = squared
        outer_c[...] = squared * dot_rows(c[...], c[...])

    outer, outer_c = call(
        weigh_kernel, (near(rank, rank), near(rank, rank)), (c_near, w_row), 2 * rank * rank * times * 6
    )

    got = swap(opened)
    terms = opened[:vox_rows] + got[:vox_rows]
    mate_con, mate_x = swap(con), swap(x)
    packet = jnp.concatenate([terms, got[vox_rows:], opened[vox_rows:]], axis=0)
    own = jnp.concatenate([terms, opened[vox_rows:], got[vox_rows:]], axis=0)
    rows_b = own[vox_rows:]
    holder = 1
    for group in groups_of(chip_bits):
        parts = [send(packet, holder, mask) for mask in masks_of(group)[:-1]] + [own]
        terms = tree([part[:vox_rows] for part in parts])
        rows_b = jnp.concatenate([part[vox_rows:] for part in parts], axis=0)
        packet = jnp.concatenate([terms, rows_b], axis=0)
        own = swap(packet)
        holder ^= 1
    voxel_core = holder

    half, sums_rows = rank // 2, rank // 2 + chip_rows

    def voxel_kernel(terms, rows, a, w, outer_c, con, mate_con, mate_x, moved_out, chip_b, out, all_b):
        b = in_order(rows, all_b, chips)
        chip_b[...] = all_b[pl.ds(pl.multiple_of(smp_index() // 2 * chip_rows, chip_rows), chip_rows), :]
        coupled = outer_c[...] * dot_rows(b, b)
        moved = a[...] - step_of(coupled) * (dot(a[...], coupled) - terms[...] * w[...])
        moved_out[...] = moved
        packed, diagonal = pack(dot_rows(moved, moved))
        out[:half, :] = packed
        for core in range(2):
            for j in range(smp_rows):
                row = half + core * smp_rows + j
                out[row : row + 1, :] = jnp.sum((con if core == voxel_core else mate_con)[j] * moved, axis=0, keepdims=True)
        out[sums_rows:, :] = jnp.broadcast_to(diagonal, (8, rank))

    moved_a, chip_b, sums = call(
        voxel_kernel,
        (near(vox_rows, rank), near(chip_rows, rank), near(sums_rows + 8, rank)),
        (terms, rows_b, a_near, w_row, outer_c, con, mate_con, mate_x),
        2 * rank * rank * vox_rows * 12,
        scratch=(near(smp_total, rank),),
    )

    mate_moved_a = swap(moved_a)

    for group in groups_of(vox_bits):
        sums = tree(fan(sums, holder, masks_of(group)))
        holder ^= 1
    sample_core = holder
    if sample_core != voxel_core:
        chip_b = swap(chip_b)

    def time_kernel(x, mate_x, moved, mate_moved, each):
        moved = on_core(voxel_core, moved[...], mate_moved[...])
        for core in range(2):
            for j in range(smp_rows):
                block = (x if core == sample_core else mate_x)[pl.ds(j, vox_rows, stride=smp_rows), :]
                each[core * smp_rows + j] = dot_rows(block, moved)

    (each,) = call(
        time_kernel,
        (near(chip_rows, times, rank),),
        (x, mate_x, moved_a, mate_moved_a),
        4 * flat_rows * times * rank * 6,
    )

    def sample_kernel(sums, b, w, outer_c, each, gram_out, out):
        gram = unpack(sums[:half, :], sums[sums_rows : sums_rows + 1, :])
        gram_out[...] = gram
        coupled = outer_c[...] * gram
        moved = b[...] - step_of(coupled) * (dot(b[...], coupled) - sums[half:sums_rows, :] * w[...])
        out[times:, :] = moved
        total = None
        for j in range(chip_rows):
            made = each[j] * moved[j : j + 1, :]
            total = made if total is None else total + made
        out[:times, :] = total

    gram_a, payload = call(
        sample_kernel,
        (near(rank, rank), near(times + chip_rows, rank)),
        (sums, chip_b, w_row, outer_c, each),
        2 * rank * rank * chip_rows * 6,
    )
    mate_gram_a = swap(gram_a)

    def scale_kernel(gram, mate_gram, moved, mate_moved, outer, result, scales_out, weighed):
        gram = on_core(sample_core, gram[...], mate_gram[...])
        scales = jnp.sqrt(diagonal_row(gram) / vox_total + 1e-06)
        scales_out[...] = scales
        result[...] = on_core(voxel_core, moved[...], mate_moved[...]) / scales
        weighed[...] = outer[...] * gram

    voxel_result, scales_a, weighed = call(
        scale_kernel,
        (far(vox_rows, rank), near(1, rank), near(rank, rank)),
        (gram_a, mate_gram_a, moved_a, mate_moved_a, outer),
        vox_rows * rank * 8,
    )

    terms, rows_b, rows_core = payload[:times], payload[times:], holder
    smp_mask = sum(chip_bits)
    for group in groups_of(chip_bits + vox_bits):
        masks = masks_of(group if smp_mask & sum(group) else group[::-1])
        if any(mask & smp_mask for mask in masks):
            packet = payload if rows_b.shape[0] == chip_rows else jnp.concatenate([terms, rows_b], axis=0)
            parts = fan(packet, holder, masks)
            gathered = [i for i, mask in enumerate(masks) if not mask & ~smp_mask]
            rows = rows_b.shape[0]

            def gather_kernel(*refs, gathered=gathered, rows=rows):
                parts, (terms, rows_out) = refs[-3::-1], refs[-2:]
                terms[...] = tree([part[:times, :] for part in parts])
                for p, i in enumerate(gathered):
                    rows_out[p * rows : (p + 1) * rows, :] = parts[i][times:, :]

            terms, rows_b = call(
                gather_kernel,
                (near(times, rank), near(len(gathered) * rows, rank)),
                parts[::-1],
                len(masks) * times * rank,
            )
            rows_core = holder ^ 1
        else:
            terms = tree(fan(terms, holder, masks))
        holder ^= 1
    last_core = holder
    mate_rows_b = swap(rows_b)

    def ready_kernel(rows, mate_rows, c, w, weighed, scales_a, b_out, base, gain, scale, all_b):
        b = in_order(on_core(rows_core, rows[...], mate_rows[...]), all_b, chips)
        coupled = weighed[...] * dot_rows(b, b)
        step = step_of(coupled)
        base[...] = c[...] - step * dot(c[...], coupled)
        gain[...] = step * w[...]
        scales_b = jnp.sqrt(jnp.sum(b * b, axis=0, keepdims=True) / smp_total + 1e-06)
        scale[...] = w[...] * scales_a[...] * scales_b
        b_out[...] = all_b[pl.ds(pl.multiple_of(smp_index() * smp_rows, smp_rows), smp_rows), :] / scales_b

    sample_result, base, gain, scale = call(
        ready_kernel,
        (far(smp_rows, rank), near(times, rank), near(1, rank), near(1, rank)),
        (rows_b, mate_rows_b, c_near, w_row, weighed, scales_a),
        2 * rank * rank * times * 4,
        scratch=(near(smp_total, rank),),
    )
    terms, base, gain, scale, voxel_result, sample_result = lax.optimization_barrier(
        (terms, base, gain, scale, voxel_result, sample_result)
    )
    mate_terms = swap(terms)

    def last_kernel(terms, mate_terms, base, gain, scale, c_out, w_out):
        moved = base[...] + on_core(last_core, terms[...], mate_terms[...]) * gain[...]
        scales_c = jnp.sqrt(jnp.sum(moved * moved, axis=0, keepdims=True) / times + 1e-06)
        c_out[...] = moved / scales_c
        w_out[...] = scale[...] * scales_c

    time_result, scale_result = call(
        last_kernel,
        (far(times, rank), far(1, rank)),
        (terms, mate_terms, base, gain, scale),
        rank * times * 8,
    )
    return voxel_result, sample_result, time_result, scale_result.reshape(rank)


def solution(mesh):
    return jax.shard_map(
        per_device,
        mesh=mesh,
        in_specs=(P("vox", "smp", None), P("vox", None), P("smp", None), P(), P()),
        out_specs=(P("vox", None), P("smp", None), P(), P()),
        check_vma=False,
    )
```

```python
import jax
import jax.numpy as jnp
from jax import lax
from jax.experimental import pallas as pl
from jax.experimental.pallas import tpu as pltpu
from jax.sharding import PartitionSpec as P

F32 = jnp.float32
BF16 = jnp.bfloat16
VMEM_LIMIT = 12 * 1024 * 1024
ALL = ("vox", "smp")


def halves(a, axis):
    high = a.astype(BF16)
    return jnp.concatenate([high, (a - high.astype(F32)).astype(BF16)], axis=axis)


def both(b):
    parts = halves(b, 1)
    return jnp.concatenate([parts, parts], axis=0)


def fold(product):
    width = product.shape[1] // 2
    return product[:, :width] + product[:, width:]


def dot(a, b):
    return fold(jnp.dot(halves(a, 1), both(b), preferred_element_type=F32))


def dot_rows(a, b):
    return fold(lax.dot_general(halves(a, 0), both(b), (((0,), (0,)), ((), ())), preferred_element_type=F32))


def step_of(coupled):
    sums = jnp.sum(jnp.abs(coupled), axis=0, keepdims=True)
    return 1.0 / jnp.max(sums, axis=1, keepdims=True)


def diagonal_row(gram):
    rows = lax.broadcasted_iota(jnp.int32, gram.shape, 0)
    columns = lax.broadcasted_iota(jnp.int32, gram.shape, 1)
    return jnp.sum(jnp.where(rows == columns, gram, 0.0), axis=0, keepdims=True)


def call(kernel, outs, operands, flops, scratch=(), in_hbm=0):
    spaces = [pltpu.HBM if i < in_hbm else pltpu.VMEM for i in range(len(operands))]
    placed = [pltpu.with_memory_space_constraint(x, space) for x, space in zip(operands, spaces)]
    specs = [pl.BlockSpec(memory_space=space) for space in spaces]
    return pl.pallas_call(
        kernel,
        out_shape=outs,
        in_specs=specs,
        out_specs=[pl.BlockSpec(memory_space=pltpu.VMEM)] * len(outs),
        scratch_shapes=list(scratch),
        compiler_params=pltpu.CompilerParams(vmem_limit_bytes=VMEM_LIMIT),
        cost_estimate=pl.CostEstimate(flops=flops, bytes_accessed=1 << 16, transcendentals=0),
    )(*placed)


def near(*shape):
    return pltpu.VMEM(shape, F32)


def far(*shape):
    return jax.ShapeDtypeStruct(shape, F32)


def bits_of(count):
    if count & (count - 1):
        raise ValueError("axis size")
    return [1 << b for b in range(count.bit_length() - 1)]


def groups_of(bits, size=2):
    return [bits[i : i + size] for i in range(0, len(bits), size)]


def masks_of(group):
    masks = [0]
    for bit in group:
        masks = [mask | bit for mask in masks] + masks
    return masks


def swap(values):
    return lax.ppermute(values, ALL, [(i, i ^ 1) for i in range(lax.axis_size(ALL))])


def send(values, holder, mask):
    count = lax.axis_size(ALL)
    pairs = [(i, i ^ 1 ^ mask if i & 1 == holder else i ^ 1) for i in range(count)]
    return lax.ppermute(values, ALL, pairs)


def fan(values, holder, masks):
    sent = [send(values, holder, mask) if mask else swap(values) for mask in reversed(masks)]
    return sent[::-1]


def tree(parts):
    parts = parts[::-1]
    while len(parts) > 1:
        parts = [a + b for a, b in zip(parts[::2], parts[1::2])]
    return parts[0]


def smp_index():
    return lax.axis_index("smp")


def on_core(core, own, got):
    return jnp.where(smp_index() & 1 == core, own, got)


def pack(gram):
    half = gram.shape[0] // 2
    rows = lax.broadcasted_iota(jnp.int32, (half, 2 * half), 0)
    columns = lax.broadcasted_iota(jnp.int32, (half, 2 * half), 1)
    top, bottom = gram[:half], gram[half:]
    packed = jnp.where(rows <= columns, top, pltpu.roll(bottom, half, 1))
    return packed, jnp.sum(jnp.where(columns == rows + half, bottom, 0.0), axis=0, keepdims=True)


def unpack(packed, diagonal):
    half = packed.shape[0]
    rows = lax.broadcasted_iota(jnp.int32, packed.shape, 0)
    columns = lax.broadcasted_iota(jnp.int32, packed.shape, 1)
    turned = jnp.concatenate([packed, packed], axis=0).T
    top = jnp.where(rows <= columns, packed, turned[:half])
    corner = jnp.where(columns < rows + half, pltpu.roll(packed, half, 1), turned[:half])
    corner = jnp.where(columns == rows + half, diagonal, corner)
    return jnp.concatenate([top, jnp.where(columns < half, turned[half:], corner)], axis=0)


def in_order(rows, scratch, chips):
    block = scratch.shape[0] // chips
    chip = smp_index() // 2
    for p in range(chips):
        scratch[pl.ds(pl.multiple_of((chip ^ (chips - 1 - p)) * block, block), block), :] = rows[p * block : (p + 1) * block, :]
    return scratch[...]


def per_device(ensemble, voxel_factor, sample_factor, time_factor, weights):
    vox_rows, smp_rows, times = ensemble.shape
    rank = voxel_factor.shape[1]
    flat_rows = vox_rows * smp_rows
    vox_count, smp_count = lax.axis_size("vox"), lax.axis_size("smp")
    vox_total, smp_total = vox_rows * vox_count, smp_rows * smp_count
    chips, chip_rows = smp_count // 2, 2 * smp_rows
    chip_bits = bits_of(smp_count)[1:]
    vox_bits = [bit * smp_count for bit in bits_of(vox_count)]
    chunks = 1
    chunk_vox = vox_rows // chunks
    chunk_rows = chunk_vox * smp_rows

    def open_kernel(x_hbm, c_hbm, b_hbm, a_hbm, w_hbm, x, c, a, w, out, con, sems):
        copies = [pltpu.make_async_copy(c_hbm, c, sems.at[0])]
        copies += [pltpu.make_async_copy(b_hbm, out.at[pl.ds(vox_rows, smp_rows), :], sems.at[1])]
        for n in range(chunks):
            part = pl.ds(n * chunk_rows, chunk_rows)
            copies.append(pltpu.make_async_copy(x_hbm.at[part, :], x.at[part, :], sems.at[2 + n]))
        copies.append(pltpu.make_async_copy(a_hbm, a, sems.at[2 + chunks]))
        copies.append(pltpu.make_async_copy(w_hbm, w, sems.at[3 + chunks]))
        for copy in copies:
            copy.start()
        copies[0].wait()
        copies[1].wait()
        factor = both(c[...])
        b = out[pl.ds(vox_rows, smp_rows), :]
        for n in range(chunks):
            copies[2 + n].wait()
            rows = pl.ds(n * chunk_vox, chunk_vox)
            blocks = [x[pl.ds(n * chunk_rows + j, chunk_vox, stride=smp_rows), :] for j in range(smp_rows)]
            blocks = jnp.concatenate([halves(block, 1) for block in blocks], axis=0)
            made = fold(jnp.dot(blocks, factor, preferred_element_type=F32)).reshape(smp_rows, chunk_vox, rank)
            con[:, rows, :] = made
            total = made[0] * b[:1, :]
            for j in range(1, smp_rows):
                total = total + made[j] * b[j : j + 1, :]
            out[rows, :] = total
        copies[2 + chunks].wait()
        copies[3 + chunks].wait()

    x, c_near, a_near, w_row, opened, con = call(
        open_kernel,
        (
            near(flat_rows, times),
            near(times, rank),
            near(vox_rows, rank),
            near(1, rank),
            near(vox_rows + smp_rows, rank),
            near(smp_rows, vox_rows, rank),
        ),
        (ensemble.reshape(flat_rows, times), time_factor, sample_factor, voxel_factor, weights.reshape(1, rank)),
        2 * flat_rows * times * rank * 6,
        scratch=(pltpu.SemaphoreType.DMA((4 + chunks,)),),
        in_hbm=5,
    )

    def weigh_kernel(c, w, outer, outer_c):
        squared = dot_rows(w[...], w[...])
        outer[...] = squared
        outer_c[...] = squared * dot_rows(c[...], c[...])

    outer, outer_c = call(
        weigh_kernel, (near(rank, rank), near(rank, rank)), (c_near, w_row), 2 * rank * rank * times * 6
    )

    got = swap(opened)
    terms = opened[:vox_rows] + got[:vox_rows]
    mate_con, mate_x = swap(con), swap(x)
    packet = jnp.concatenate([terms, got[vox_rows:], opened[vox_rows:]], axis=0)
    own = jnp.concatenate([terms, opened[vox_rows:], got[vox_rows:]], axis=0)
    rows_b = own[vox_rows:]
    holder = 1
    for group in groups_of(chip_bits):
        parts = [send(packet, holder, mask) for mask in masks_of(group)[:-1]] + [own]
        terms = tree([part[:vox_rows] for part in parts])
        rows_b = jnp.concatenate([part[vox_rows:] for part in parts], axis=0)
        packet = jnp.concatenate([terms, rows_b], axis=0)
        own = swap(packet)
        holder ^= 1
    voxel_core = holder

    half, sums_rows = rank // 2, rank // 2 + chip_rows

    def voxel_kernel(terms, rows, a, w, outer_c, con, mate_con, mate_x, moved_out, chip_b, out, all_b):
        b = in_order(rows, all_b, chips)
        chip_b[...] = all_b[pl.ds(pl.multiple_of(smp_index() // 2 * chip_rows, chip_rows), chip_rows), :]
        coupled = outer_c[...] * dot_rows(b, b)
        moved = a[...] - step_of(coupled) * (dot(a[...], coupled) - terms[...] * w[...])
        moved_out[...] = moved
        packed, diagonal = pack(dot_rows(moved, moved))
        out[:half, :] = packed
        for core in range(2):
            for j in range(smp_rows):
                row = half + core * smp_rows + j
                out[row : row + 1, :] = jnp.sum((con if core == voxel_core else mate_con)[j] * moved, axis=0, keepdims=True)
        out[sums_rows:, :] = jnp.broadcast_to(diagonal, (8, rank))

    moved_a, chip_b, sums = call(
        voxel_kernel,
        (near(vox_rows, rank), near(chip_rows, rank), near(sums_rows + 8, rank)),
        (terms, rows_b, a_near, w_row, outer_c, con, mate_con, mate_x),
        2 * rank * rank * vox_rows * 12,
        scratch=(near(smp_total, rank),),
    )

    mate_moved_a = swap(moved_a)

    for group in groups_of(vox_bits[:1] + vox_bits[:0:-1]):
        sums = tree(fan(sums, holder, masks_of(group)))
        holder ^= 1
    sample_core = holder
    if sample_core != voxel_core:
        chip_b = swap(chip_b)

    def time_kernel(x, mate_x, moved, mate_moved, each):
        moved = on_core(voxel_core, moved[...], mate_moved[...])
        for core in range(2):
            for j in range(smp_rows):
                block = (x if core == sample_core else mate_x)[pl.ds(j, vox_rows, stride=smp_rows), :]
                each[core * smp_rows + j] = dot_rows(block, moved)

    (each,) = call(
        time_kernel,
        (near(chip_rows, times, rank),),
        (x, mate_x, moved_a, mate_moved_a),
        4 * flat_rows * times * rank * 6,
    )

    def sample_kernel(sums, b, w, outer_c, each, gram_out, out):
        gram = unpack(sums[:half, :], sums[sums_rows : sums_rows + 1, :])
        gram_out[...] = gram
        coupled = outer_c[...] * gram
        moved = b[...] - step_of(coupled) * (dot(b[...], coupled) - sums[half:sums_rows, :] * w[...])
        out[times:, :] = moved
        total = None
        for j in range(chip_rows):
            made = each[j] * moved[j : j + 1, :]
            total = made if total is None else total + made
        out[:times, :] = total

    gram_a, payload = call(
        sample_kernel,
        (near(rank, rank), near(times + chip_rows, rank)),
        (sums, chip_b, w_row, outer_c, each),
        2 * rank * rank * chip_rows * 6,
    )
    mate_gram_a = swap(gram_a)

    def scale_kernel(gram, mate_gram, moved, mate_moved, outer, result, scales_out, weighed):
        gram = on_core(sample_core, gram[...], mate_gram[...])
        scales = jnp.sqrt(diagonal_row(gram) / vox_total + 1e-06)
        scales_out[...] = scales
        result[...] = on_core(voxel_core, moved[...], mate_moved[...]) / scales
        weighed[...] = outer[...] * gram

    voxel_result, scales_a, weighed = call(
        scale_kernel,
        (far(vox_rows, rank), near(1, rank), near(rank, rank)),
        (gram_a, mate_gram_a, moved_a, mate_moved_a, outer),
        vox_rows * rank * 8,
    )

    terms, rows_b, rows_core = payload[:times], payload[times:], holder
    smp_mask = sum(chip_bits)
    for group in groups_of(chip_bits + vox_bits):
        masks = masks_of(group)
        if any(mask & smp_mask for mask in masks):
            packet = payload if rows_b.shape[0] == chip_rows else jnp.concatenate([terms, rows_b], axis=0)
            parts = fan(packet, holder, masks)
            gathered = [i for i, mask in enumerate(masks) if not mask & ~smp_mask]
            rows = rows_b.shape[0]

            def gather_kernel(*refs, gathered=gathered, rows=rows):
                parts, (terms, rows_out) = refs[-3::-1], refs[-2:]
                terms[...] = tree([part[:times, :] for part in parts])
                for p, i in enumerate(gathered):
                    rows_out[p * rows : (p + 1) * rows, :] = parts[i][times:, :]

            terms, rows_b = call(
                gather_kernel,
                (near(times, rank), near(len(gathered) * rows, rank)),
                parts[::-1],
                len(masks) * times * rank,
            )
            rows_core = holder ^ 1
        else:
            terms = tree(fan(terms, holder, masks))
        holder ^= 1
    last_core = holder
    mate_rows_b = swap(rows_b)

    def ready_kernel(rows, mate_rows, c, w, weighed, scales_a, b_out, base, gain, scale, all_b):
        b = in_order(on_core(rows_core, rows[...], mate_rows[...]), all_b, chips)
        coupled = weighed[...] * dot_rows(b, b)
        step = step_of(coupled)
        base[...] = c[...] - step * dot(c[...], coupled)
        gain[...] = step * w[...]
        scales_b = jnp.sqrt(jnp.sum(b * b, axis=0, keepdims=True) / smp_total + 1e-06)
        scale[...] = w[...] * scales_a[...] * scales_b
        b_out[...] = all_b[pl.ds(pl.multiple_of(smp_index() * smp_rows, smp_rows), smp_rows), :] / scales_b

    sample_result, base, gain, scale = call(
        ready_kernel,
        (far(smp_rows, rank), near(times, rank), near(1, rank), near(1, rank)),
        (rows_b, mate_rows_b, c_near, w_row, weighed, scales_a),
        2 * rank * rank * times * 4,
        scratch=(near(smp_total, rank),),
    )
    terms, base, gain, scale, voxel_result, sample_result = lax.optimization_barrier(
        (terms, base, gain, scale, voxel_result, sample_result)
    )
    mate_terms = swap(terms)

    def last_kernel(terms, mate_terms, base, gain, scale, c_out, w_out):
        moved = base[...] + on_core(last_core, terms[...], mate_terms[...]) * gain[...]
        scales_c = jnp.sqrt(jnp.sum(moved * moved, axis=0, keepdims=True) / times + 1e-06)
        c_out[...] = moved / scales_c
        w_out[...] = scale[...] * scales_c

    time_result, scale_result = call(
        last_kernel,
        (far(times, rank), far(1, rank)),
        (terms, mate_terms, base, gain, scale),
        rank * times * 8,
    )
    return voxel_result, sample_result, time_result, scale_result.reshape(rank)


def solution(mesh):
    return jax.shard_map(
        per_device,
        mesh=mesh,
        in_specs=(P("vox", "smp", None), P("vox", None), P("smp", None), P(), P()),
        out_specs=(P("vox", None), P("smp", None), P(), P()),
        check_vma=False,
    )
```

```python
import jax
import jax.numpy as jnp
from jax import lax
from jax.experimental import pallas as pl
from jax.experimental.pallas import tpu as pltpu
from jax.sharding import PartitionSpec as P

F32 = jnp.float32
BF16 = jnp.bfloat16
VMEM_LIMIT = 12 * 1024 * 1024
ALL = ("vox", "smp")


def halves(a, axis):
    high = a.astype(BF16)
    return jnp.concatenate([high, (a - high.astype(F32)).astype(BF16)], axis=axis)


def both(b):
    parts = halves(b, 1)
    return jnp.concatenate([parts, parts], axis=0)


def fold(product):
    width = product.shape[1] // 2
    return product[:, :width] + product[:, width:]


def dot(a, b):
    return fold(jnp.dot(halves(a, 1), both(b), preferred_element_type=F32))


def dot_rows(a, b):
    return fold(lax.dot_general(halves(a, 0), both(b), (((0,), (0,)), ((), ())), preferred_element_type=F32))


def step_of(coupled):
    sums = jnp.sum(jnp.abs(coupled), axis=0, keepdims=True)
    return 1.0 / jnp.max(sums, axis=1, keepdims=True)


def diagonal_row(gram):
    rows = lax.broadcasted_iota(jnp.int32, gram.shape, 0)
    columns = lax.broadcasted_iota(jnp.int32, gram.shape, 1)
    return jnp.sum(jnp.where(rows == columns, gram, 0.0), axis=0, keepdims=True)


def only_on(core, kernel):
    def run(*refs):
        pl.when(smp_index() & 1 == core)(lambda: kernel(*refs))

    return run


def call(kernel, outs, operands, flops, scratch=(), in_hbm=0):
    spaces = [pltpu.HBM if i < in_hbm else pltpu.VMEM for i in range(len(operands))]
    placed = [pltpu.with_memory_space_constraint(x, space) for x, space in zip(operands, spaces)]
    specs = [pl.BlockSpec(memory_space=space) for space in spaces]
    return pl.pallas_call(
        kernel,
        out_shape=outs,
        in_specs=specs,
        out_specs=[pl.BlockSpec(memory_space=pltpu.VMEM)] * len(outs),
        scratch_shapes=list(scratch),
        compiler_params=pltpu.CompilerParams(vmem_limit_bytes=VMEM_LIMIT),
        cost_estimate=pl.CostEstimate(flops=flops, bytes_accessed=1 << 16, transcendentals=0),
    )(*placed)


def near(*shape):
    return pltpu.VMEM(shape, F32)


def far(*shape):
    return jax.ShapeDtypeStruct(shape, F32)


def bits_of(count):
    if count & (count - 1):
        raise ValueError("axis size")
    return [1 << b for b in range(count.bit_length() - 1)]


def groups_of(bits, size=2):
    return [bits[i : i + size] for i in range(0, len(bits), size)]


def masks_of(group):
    masks = [0]
    for bit in group:
        masks = [mask | bit for mask in masks] + masks
    return masks


def swap(values):
    return lax.ppermute(values, ALL, [(i, i ^ 1) for i in range(lax.axis_size(ALL))])


def send(values, holder, mask):
    count = lax.axis_size(ALL)
    pairs = [(i, i ^ 1 ^ mask if i & 1 == holder else i ^ 1) for i in range(count)]
    return lax.ppermute(values, ALL, pairs)


def fan(values, holder, masks):
    sent = [send(values, holder, mask) if mask else swap(values) for mask in reversed(masks)]
    return sent[::-1]


def tree(parts):
    parts = parts[::-1]
    while len(parts) > 1:
        parts = [a + b for a, b in zip(parts[::2], parts[1::2])]
    return parts[0]


def smp_index():
    return lax.axis_index("smp")


def on_core(core, own, got):
    return jnp.where(smp_index() & 1 == core, own, got)


def pack(gram):
    half = gram.shape[0] // 2
    rows = lax.broadcasted_iota(jnp.int32, (half, 2 * half), 0)
    columns = lax.broadcasted_iota(jnp.int32, (half, 2 * half), 1)
    top, bottom = gram[:half], gram[half:]
    packed = jnp.where(rows <= columns, top, pltpu.roll(bottom, half, 1))
    return packed, jnp.sum(jnp.where(columns == rows + half, bottom, 0.0), axis=0, keepdims=True)


def unpack(packed, diagonal):
    half = packed.shape[0]
    rows = lax.broadcasted_iota(jnp.int32, packed.shape, 0)
    columns = lax.broadcasted_iota(jnp.int32, packed.shape, 1)
    turned = jnp.concatenate([packed, packed], axis=0).T
    top = jnp.where(rows <= columns, packed, turned[:half])
    corner = jnp.where(columns < rows + half, pltpu.roll(packed, half, 1), turned[:half])
    corner = jnp.where(columns == rows + half, diagonal, corner)
    return jnp.concatenate([top, jnp.where(columns < half, turned[half:], corner)], axis=0)


def in_order(rows, scratch, chips):
    block = scratch.shape[0] // chips
    chip = smp_index() // 2
    for p in range(chips):
        scratch[pl.ds(pl.multiple_of((chip ^ (chips - 1 - p)) * block, block), block), :] = rows[p * block : (p + 1) * block, :]
    return scratch[...]


def per_device(ensemble, voxel_factor, sample_factor, time_factor, weights):
    vox_rows, smp_rows, times = ensemble.shape
    rank = voxel_factor.shape[1]
    flat_rows = vox_rows * smp_rows
    vox_count, smp_count = lax.axis_size("vox"), lax.axis_size("smp")
    vox_total, smp_total = vox_rows * vox_count, smp_rows * smp_count
    chips, chip_rows = smp_count // 2, 2 * smp_rows
    chip_bits = bits_of(smp_count)[1:]
    vox_bits = [bit * smp_count for bit in bits_of(vox_count)]
    pieces = 4 if flat_rows % 32 == 0 else 1
    piece_rows = flat_rows // pieces

    def open_kernel(x_hbm, c_hbm, b_hbm, a_hbm, w_hbm, x, c, a, w, out, con, sems):
        copies = [pltpu.make_async_copy(c_hbm, c, sems.at[0])]
        copies += [pltpu.make_async_copy(b_hbm, out.at[pl.ds(vox_rows, smp_rows), :], sems.at[1])]
        for n in range(pieces):
            piece = pl.ds(n * piece_rows, piece_rows)
            copies.append(pltpu.make_async_copy(x_hbm.at[piece, :], x.at[piece, :], sems.at[2 + n]))
        copies.append(pltpu.make_async_copy(a_hbm, a, sems.at[2 + pieces]))
        copies.append(pltpu.make_async_copy(w_hbm, w, sems.at[3 + pieces]))
        for copy in copies:
            copy.start()
        copies[0].wait()
        copies[1].wait()
        factor = both(c[...])
        b = out[pl.ds(vox_rows, smp_rows), :]
        for n in range(pieces):
            copies[2 + n].wait()
        blocks = [x[pl.ds(j, vox_rows, stride=smp_rows), :] for j in range(smp_rows)]
        blocks = jnp.concatenate([halves(block, 1) for block in blocks], axis=0)
        made = fold(jnp.dot(blocks, factor, preferred_element_type=F32)).reshape(smp_rows, vox_rows, rank)
        con[...] = made
        total = made[0] * b[:1, :]
        for j in range(1, smp_rows):
            total = total + made[j] * b[j : j + 1, :]
        out[:vox_rows, :] = total
        copies[2 + pieces].wait()
        copies[3 + pieces].wait()

    x, c_near, a_near, w_row, opened, con = call(
        open_kernel,
        (
            near(flat_rows, times),
            near(times, rank),
            near(vox_rows, rank),
            near(1, rank),
            near(vox_rows + smp_rows, rank),
            near(smp_rows, vox_rows, rank),
        ),
        (ensemble.reshape(flat_rows, times), time_factor, sample_factor, voxel_factor, weights.reshape(1, rank)),
        2 * flat_rows * times * rank * 6,
        scratch=(pltpu.SemaphoreType.DMA((4 + pieces,)),),
        in_hbm=5,
    )

    def weigh_kernel(c, w, outer, outer_c):
        squared = dot_rows(w[...], w[...])
        outer[...] = squared
        outer_c[...] = squared * dot_rows(c[...], c[...])

    outer, outer_c = call(
        weigh_kernel, (near(rank, rank), near(rank, rank)), (c_near, w_row), 2 * rank * rank * times * 6
    )

    got = swap(opened)
    terms = opened[:vox_rows] + got[:vox_rows]
    mate_con, mate_x = swap(con), swap(x)
    packet = jnp.concatenate([terms, got[vox_rows:], opened[vox_rows:]], axis=0)
    own = jnp.concatenate([terms, opened[vox_rows:], got[vox_rows:]], axis=0)
    rows_b = own[vox_rows:]
    holder = 1
    for group in groups_of(chip_bits):
        parts = [send(packet, holder, mask) for mask in masks_of(group)[:-1]] + [own]
        terms = tree([part[:vox_rows] for part in parts])
        rows_b = jnp.concatenate([part[vox_rows:] for part in parts], axis=0)
        packet = jnp.concatenate([terms, rows_b], axis=0)
        own = swap(packet)
        holder ^= 1
    voxel_core = holder

    half, sums_rows = rank // 2, rank // 2 + chip_rows

    def voxel_kernel(terms, rows, a, w, outer_c, con, mate_con, mate_x, moved_out, chip_b, out, all_b):
        b = in_order(rows, all_b, chips)
        chip_b[...] = all_b[pl.ds(pl.multiple_of(smp_index() // 2 * chip_rows, chip_rows), chip_rows), :]
        coupled = outer_c[...] * dot_rows(b, b)
        moved = a[...] - step_of(coupled) * (dot(a[...], coupled) - terms[...] * w[...])
        moved_out[...] = moved
        packed, diagonal = pack(dot_rows(moved, moved))
        out[:half, :] = packed
        for core in range(2):
            for j in range(smp_rows):
                row = half + core * smp_rows + j
                out[row : row + 1, :] = jnp.sum((con if core == voxel_core else mate_con)[j] * moved, axis=0, keepdims=True)
        out[sums_rows:, :] = jnp.broadcast_to(diagonal, (8, rank))

    moved_a, chip_b, sums = call(
        only_on(voxel_core, voxel_kernel),
        (near(vox_rows, rank), near(chip_rows, rank), near(sums_rows + 8, rank)),
        (terms, rows_b, a_near, w_row, outer_c, con, mate_con, mate_x),
        2 * rank * rank * vox_rows * 12,
        scratch=(near(smp_total, rank),),
    )

    mate_moved_a = swap(moved_a)

    for group in groups_of(vox_bits[:1] + vox_bits[:0:-1]):
        sums = tree(fan(sums, holder, masks_of(group)))
        holder ^= 1
    sample_core = holder
    if sample_core != voxel_core:
        chip_b = swap(chip_b)

    def time_kernel(x, mate_x, moved, mate_moved, each):
        moved = on_core(voxel_core, moved[...], mate_moved[...])
        for core in range(2):
            for j in range(smp_rows):
                block = (x if core == sample_core else mate_x)[pl.ds(j, vox_rows, stride=smp_rows), :]
                each[core * smp_rows + j] = dot_rows(block, moved)

    (each,) = call(
        only_on(sample_core, time_kernel),
        (near(chip_rows, times, rank),),
        (x, mate_x, moved_a, mate_moved_a),
        4 * flat_rows * times * rank * 6,
    )

    def sample_kernel(sums, b, w, outer_c, each, gram_out, out):
        gram = unpack(sums[:half, :], sums[sums_rows : sums_rows + 1, :])
        gram_out[...] = gram
        coupled = outer_c[...] * gram
        moved = b[...] - step_of(coupled) * (dot(b[...], coupled) - sums[half:sums_rows, :] * w[...])
        out[times:, :] = moved
        total = None
        for j in range(chip_rows):
            made = each[j] * moved[j : j + 1, :]
            total = made if total is None else total + made
        out[:times, :] = total

    gram_a, payload = call(
        only_on(sample_core, sample_kernel),
        (near(rank, rank), near(times + chip_rows, rank)),
        (sums, chip_b, w_row, outer_c, each),
        2 * rank * rank * chip_rows * 6,
    )
    mate_gram_a = swap(gram_a)

    def scale_kernel(gram, mate_gram, moved, mate_moved, outer, result, scales_out, weighed):
        gram = on_core(sample_core, gram[...], mate_gram[...])
        scales = jnp.sqrt(diagonal_row(gram) / vox_total + 1e-06)
        scales_out[...] = scales
        result[...] = on_core(voxel_core, moved[...], mate_moved[...]) / scales
        weighed[...] = outer[...] * gram

    voxel_result, scales_a, weighed = call(
        scale_kernel,
        (far(vox_rows, rank), near(1, rank), near(rank, rank)),
        (gram_a, mate_gram_a, moved_a, mate_moved_a, outer),
        vox_rows * rank * 8,
    )

    terms, rows_b, rows_core = payload[:times], payload[times:], holder
    smp_mask = sum(chip_bits)
    for group in groups_of(chip_bits + vox_bits):
        masks = masks_of(group)
        if any(mask & smp_mask for mask in masks):
            packet = payload if rows_b.shape[0] == chip_rows else jnp.concatenate([terms, rows_b], axis=0)
            parts = fan(packet, holder, masks)
            gathered = [i for i, mask in enumerate(masks) if not mask & ~smp_mask]
            rows = rows_b.shape[0]

            def gather_kernel(*refs, gathered=gathered, rows=rows):
                parts, (terms, rows_out) = refs[-3::-1], refs[-2:]
                terms[...] = tree([part[:times, :] for part in parts])
                for p, i in enumerate(gathered):
                    rows_out[p * rows : (p + 1) * rows, :] = parts[i][times:, :]

            terms, rows_b = call(
                gather_kernel,
                (near(times, rank), near(len(gathered) * rows, rank)),
                parts[::-1],
                len(masks) * times * rank,
            )
            rows_core = holder ^ 1
        else:
            terms = tree(fan(terms, holder, masks))
        holder ^= 1
    last_core = holder
    mate_rows_b = swap(rows_b)

    def ready_kernel(rows, mate_rows, c, w, weighed, scales_a, b_out, base, gain, scale, all_b):
        b = in_order(on_core(rows_core, rows[...], mate_rows[...]), all_b, chips)
        coupled = weighed[...] * dot_rows(b, b)
        step = step_of(coupled)
        base[...] = c[...] - step * dot(c[...], coupled)
        gain[...] = step * w[...]
        scales_b = jnp.sqrt(jnp.sum(b * b, axis=0, keepdims=True) / smp_total + 1e-06)
        scale[...] = w[...] * scales_a[...] * scales_b
        b_out[...] = all_b[pl.ds(pl.multiple_of(smp_index() * smp_rows, smp_rows), smp_rows), :] / scales_b

    sample_result, base, gain, scale = call(
        ready_kernel,
        (far(smp_rows, rank), near(times, rank), near(1, rank), near(1, rank)),
        (rows_b, mate_rows_b, c_near, w_row, weighed, scales_a),
        2 * rank * rank * times * 4,
        scratch=(near(smp_total, rank),),
    )
    terms, base, gain, scale, voxel_result, sample_result = lax.optimization_barrier(
        (terms, base, gain, scale, voxel_result, sample_result)
    )
    mate_terms = swap(terms)

    def last_kernel(terms, mate_terms, base, gain, scale, c_out, w_out):
        moved = base[...] + on_core(last_core, terms[...], mate_terms[...]) * gain[...]
        scales_c = jnp.sqrt(jnp.sum(moved * moved, axis=0, keepdims=True) / times + 1e-06)
        c_out[...] = moved / scales_c
        w_out[...] = scale[...] * scales_c

    time_result, scale_result = call(
        last_kernel,
        (far(times, rank), far(1, rank)),
        (terms, mate_terms, base, gain, scale),
        rank * times * 8,
    )
    return voxel_result, sample_result, time_result, scale_result.reshape(rank)


def solution(mesh):
    return jax.shard_map(
        per_device,
        mesh=mesh,
        in_specs=(P("vox", "smp", None), P("vox", None), P("smp", None), P(), P()),
        out_specs=(P("vox", None), P("smp", None), P(), P()),
        check_vma=False,
    )
```

```python
import jax
import jax.numpy as jnp
from jax import lax
from jax.experimental import pallas as pl
from jax.experimental.pallas import tpu as pltpu
from jax.sharding import PartitionSpec as P

F32 = jnp.float32
BF16 = jnp.bfloat16
VMEM_LIMIT = 12 * 1024 * 1024
ALL = ("vox", "smp")


def halves(a, axis):
    high = a.astype(BF16)
    return jnp.concatenate([high, (a - high.astype(F32)).astype(BF16)], axis=axis)


def both(b):
    parts = halves(b, 1)
    return jnp.concatenate([parts, parts], axis=0)


def fold(product):
    width = product.shape[1] // 2
    return product[:, :width] + product[:, width:]


def dot(a, b):
    return fold(jnp.dot(halves(a, 1), both(b), preferred_element_type=F32))


def dot_rows(a, b):
    return fold(lax.dot_general(halves(a, 0), both(b), (((0,), (0,)), ((), ())), preferred_element_type=F32))


def step_of(coupled):
    sums = jnp.sum(jnp.abs(coupled), axis=0, keepdims=True)
    return 1.0 / jnp.max(sums, axis=1, keepdims=True)


def diagonal_row(gram):
    rows = lax.broadcasted_iota(jnp.int32, gram.shape, 0)
    columns = lax.broadcasted_iota(jnp.int32, gram.shape, 1)
    return jnp.sum(jnp.where(rows == columns, gram, 0.0), axis=0, keepdims=True)


def only_on(core, kernel):
    def run(*refs):
        pl.when(smp_index() & 1 == core)(lambda: kernel(*refs))

    return run


def call(kernel, outs, operands, flops, scratch=(), in_hbm=0):
    spaces = [pltpu.HBM if i < in_hbm else pltpu.VMEM for i in range(len(operands))]
    placed = [pltpu.with_memory_space_constraint(x, space) for x, space in zip(operands, spaces)]
    specs = [pl.BlockSpec(memory_space=space) for space in spaces]
    return pl.pallas_call(
        kernel,
        out_shape=outs,
        in_specs=specs,
        out_specs=[pl.BlockSpec(memory_space=pltpu.VMEM)] * len(outs),
        scratch_shapes=list(scratch),
        compiler_params=pltpu.CompilerParams(vmem_limit_bytes=VMEM_LIMIT),
        cost_estimate=pl.CostEstimate(flops=flops, bytes_accessed=1 << 16, transcendentals=0),
    )(*placed)


def near(*shape):
    return pltpu.VMEM(shape, F32)


def far(*shape):
    return jax.ShapeDtypeStruct(shape, F32)


def bits_of(count):
    if count & (count - 1):
        raise ValueError("axis size")
    return [1 << b for b in range(count.bit_length() - 1)]


def groups_of(bits, size=2):
    return [bits[i : i + size] for i in range(0, len(bits), size)]


def masks_of(group):
    masks = [0]
    for bit in group:
        masks = [mask | bit for mask in masks] + masks
    return masks


def swap(values):
    return lax.ppermute(values, ALL, [(i, i ^ 1) for i in range(lax.axis_size(ALL))])


def send(values, holder, mask):
    count = lax.axis_size(ALL)
    pairs = [(i, i ^ 1 ^ mask if i & 1 == holder else i ^ 1) for i in range(count)]
    return lax.ppermute(values, ALL, pairs)


def fan(values, holder, masks):
    sent = [send(values, holder, mask) if mask else swap(values) for mask in reversed(masks)]
    return sent[::-1]


def tree(parts):
    parts = parts[::-1]
    while len(parts) > 1:
        parts = [a + b for a, b in zip(parts[::2], parts[1::2])]
    return parts[0]


def smp_index():
    return lax.axis_index("smp")


def on_core(core, own, got):
    return jnp.where(smp_index() & 1 == core, own, got)


def pack(gram):
    half = gram.shape[0] // 2
    rows = lax.broadcasted_iota(jnp.int32, (half, 2 * half), 0)
    columns = lax.broadcasted_iota(jnp.int32, (half, 2 * half), 1)
    top, bottom = gram[:half], gram[half:]
    packed = jnp.where(rows <= columns, top, pltpu.roll(bottom, half, 1))
    return packed, jnp.sum(jnp.where(columns == rows + half, bottom, 0.0), axis=0, keepdims=True)


def unpack(packed, diagonal):
    half = packed.shape[0]
    rows = lax.broadcasted_iota(jnp.int32, packed.shape, 0)
    columns = lax.broadcasted_iota(jnp.int32, packed.shape, 1)
    turned = jnp.concatenate([packed, packed], axis=0).T
    top = jnp.where(rows <= columns, packed, turned[:half])
    corner = jnp.where(columns < rows + half, pltpu.roll(packed, half, 1), turned[:half])
    corner = jnp.where(columns == rows + half, diagonal, corner)
    return jnp.concatenate([top, jnp.where(columns < half, turned[half:], corner)], axis=0)


def in_order(rows, scratch, chips):
    block = scratch.shape[0] // chips
    chip = smp_index() // 2
    for p in range(chips):
        scratch[pl.ds(pl.multiple_of((chip ^ (chips - 1 - p)) * block, block), block), :] = rows[p * block : (p + 1) * block, :]
    return scratch[...]


def per_device(ensemble, voxel_factor, sample_factor, time_factor, weights):
    vox_rows, smp_rows, times = ensemble.shape
    rank = voxel_factor.shape[1]
    flat_rows = vox_rows * smp_rows
    vox_count, smp_count = lax.axis_size("vox"), lax.axis_size("smp")
    vox_total, smp_total = vox_rows * vox_count, smp_rows * smp_count
    chips, chip_rows = smp_count // 2, 2 * smp_rows
    chip_bits = bits_of(smp_count)[1:]
    vox_bits = [bit * smp_count for bit in bits_of(vox_count)]
    pieces = 4 if flat_rows % 32 == 0 else 1
    piece_rows = flat_rows // pieces

    def open_kernel(x_hbm, c_hbm, b_hbm, a_hbm, w_hbm, x, c, a, w, out, con, sems):
        copies = [pltpu.make_async_copy(c_hbm, c, sems.at[0])]
        copies += [pltpu.make_async_copy(b_hbm, out.at[pl.ds(vox_rows, smp_rows), :], sems.at[1])]
        for n in range(pieces):
            piece = pl.ds(n * piece_rows, piece_rows)
            copies.append(pltpu.make_async_copy(x_hbm.at[piece, :], x.at[piece, :], sems.at[2 + n]))
        copies.append(pltpu.make_async_copy(a_hbm, a, sems.at[2 + pieces]))
        copies.append(pltpu.make_async_copy(w_hbm, w, sems.at[3 + pieces]))
        for copy in copies:
            copy.start()
        copies[0].wait()
        copies[1].wait()
        factor = both(c[...])
        b = out[pl.ds(vox_rows, smp_rows), :]
        for n in range(pieces):
            copies[2 + n].wait()
        blocks = [x[pl.ds(j, vox_rows, stride=smp_rows), :] for j in range(smp_rows)]
        blocks = jnp.concatenate([halves(block, 1) for block in blocks], axis=0)
        made = fold(jnp.dot(blocks, factor, preferred_element_type=F32)).reshape(smp_rows, vox_rows, rank)
        con[...] = made
        total = made[0] * b[:1, :]
        for j in range(1, smp_rows):
            total = total + made[j] * b[j : j + 1, :]
        out[:vox_rows, :] = total
        copies[2 + pieces].wait()
        copies[3 + pieces].wait()

    x, c_near, a_near, w_row, opened, con = call(
        open_kernel,
        (
            near(flat_rows, times),
            near(times, rank),
            near(vox_rows, rank),
            near(1, rank),
            near(vox_rows + smp_rows, rank),
            near(smp_rows, vox_rows, rank),
        ),
        (ensemble.reshape(flat_rows, times), time_factor, sample_factor, voxel_factor, weights.reshape(1, rank)),
        2 * flat_rows * times * rank * 6,
        scratch=(pltpu.SemaphoreType.DMA((4 + pieces,)),),
        in_hbm=5,
    )

    def weigh_kernel(c, w, outer, outer_c):
        squared = dot_rows(w[...], w[...])
        outer[...] = squared
        outer_c[...] = squared * dot_rows(c[...], c[...])

    outer, outer_c = call(
        weigh_kernel, (near(rank, rank), near(rank, rank)), (c_near, w_row), 2 * rank * rank * times * 6
    )

    got = swap(opened)
    terms = opened[:vox_rows] + got[:vox_rows]
    mate_con, mate_x = swap(con), swap(x)
    packet = jnp.concatenate([terms, got[vox_rows:], opened[vox_rows:]], axis=0)
    own = jnp.concatenate([terms, opened[vox_rows:], got[vox_rows:]], axis=0)
    rows_b = own[vox_rows:]
    holder = 1
    for group in groups_of(chip_bits):
        parts = [send(packet, holder, mask) for mask in masks_of(group)[:-1]] + [own]
        terms = tree([part[:vox_rows] for part in parts])
        rows_b = jnp.concatenate([part[vox_rows:] for part in parts], axis=0)
        packet = jnp.concatenate([terms, rows_b], axis=0)
        own = swap(packet)
        holder ^= 1
    voxel_core = holder

    half, sums_rows = rank // 2, rank // 2 + chip_rows

    def voxel_kernel(terms, rows, a, w, outer_c, con, mate_con, mate_x, moved_out, chip_b, out, all_b):
        b = in_order(rows, all_b, chips)
        chip_b[...] = all_b[pl.ds(pl.multiple_of(smp_index() // 2 * chip_rows, chip_rows), chip_rows), :]
        coupled = outer_c[...] * dot_rows(b, b)
        moved = a[...] - step_of(coupled) * (dot(a[...], coupled) - terms[...] * w[...])
        moved_out[...] = moved
        packed, diagonal = pack(dot_rows(moved, moved))
        out[:half, :] = packed
        for core in range(2):
            for j in range(smp_rows):
                row = half + core * smp_rows + j
                out[row : row + 1, :] = jnp.sum((con if core == voxel_core else mate_con)[j] * moved, axis=0, keepdims=True)
        out[sums_rows:, :] = jnp.broadcast_to(diagonal, (8, rank))

    moved_a, chip_b, sums = call(
        only_on(voxel_core, voxel_kernel),
        (near(vox_rows, rank), near(chip_rows, rank), near(sums_rows + 8, rank)),
        (terms, rows_b, a_near, w_row, outer_c, con, mate_con, mate_x),
        2 * rank * rank * vox_rows * 12,
        scratch=(near(smp_total, rank),),
    )

    mate_moved_a = swap(moved_a)

    for group in groups_of(vox_bits[:1] + vox_bits[:0:-1]):
        sums = tree(fan(sums, holder, masks_of(group)))
        holder ^= 1
    sample_core = holder
    if sample_core != voxel_core:
        chip_b = swap(chip_b)

    def time_kernel(x, mate_x, moved, mate_moved, each):
        moved = on_core(voxel_core, moved[...], mate_moved[...])
        for core in range(2):
            for j in range(smp_rows):
                block = (x if core == sample_core else mate_x)[pl.ds(j, vox_rows, stride=smp_rows), :]
                each[core * smp_rows + j] = dot_rows(block, moved)

    (each,) = call(
        only_on(sample_core, time_kernel),
        (near(chip_rows, times, rank),),
        (x, mate_x, moved_a, mate_moved_a),
        4 * flat_rows * times * rank * 6,
    )

    def sample_kernel(sums, b, w, outer_c, each, gram_out, out):
        gram = unpack(sums[:half, :], sums[sums_rows : sums_rows + 1, :])
        gram_out[...] = gram
        coupled = outer_c[...] * gram
        moved = b[...] - step_of(coupled) * (dot(b[...], coupled) - sums[half:sums_rows, :] * w[...])
        out[times:, :] = moved
        total = None
        for j in range(chip_rows):
            made = each[j] * moved[j : j + 1, :]
            total = made if total is None else total + made
        out[:times, :] = total

    gram_a, payload = call(
        only_on(sample_core, sample_kernel),
        (near(rank, rank), near(times + chip_rows, rank)),
        (sums, chip_b, w_row, outer_c, each),
        2 * rank * rank * chip_rows * 6,
    )
    mate_gram_a = swap(gram_a)

    def scale_kernel(gram, mate_gram, moved, mate_moved, outer, result, scales_out, weighed):
        gram = on_core(sample_core, gram[...], mate_gram[...])
        scales = jnp.sqrt(diagonal_row(gram) / vox_total + 1e-06)
        scales_out[...] = scales
        result[...] = on_core(voxel_core, moved[...], mate_moved[...]) / scales
        weighed[...] = outer[...] * gram

    voxel_result, scales_a, weighed = call(
        scale_kernel,
        (far(vox_rows, rank), near(1, rank), near(rank, rank)),
        (gram_a, mate_gram_a, moved_a, mate_moved_a, outer),
        vox_rows * rank * 8,
    )

    terms, rows_b, rows_core = payload[:times], payload[times:], holder
    smp_mask = sum(chip_bits)
    for group in groups_of(chip_bits + vox_bits[1:2] + vox_bits[:1] + vox_bits[2:]):
        masks = masks_of(group)
        if any(mask & smp_mask for mask in masks):
            packet = payload if rows_b.shape[0] == chip_rows else jnp.concatenate([terms, rows_b], axis=0)
            parts = fan(packet, holder, masks)
            gathered = [i for i, mask in enumerate(masks) if not mask & ~smp_mask]
            rows = rows_b.shape[0]

            def gather_kernel(*refs, gathered=gathered, rows=rows):
                parts, (terms, rows_out) = refs[-3::-1], refs[-2:]
                terms[...] = tree([part[:times, :] for part in parts])
                for p, i in enumerate(gathered):
                    rows_out[p * rows : (p + 1) * rows, :] = parts[i][times:, :]

            terms, rows_b = call(
                gather_kernel,
                (near(times, rank), near(len(gathered) * rows, rank)),
                parts[::-1],
                len(masks) * times * rank,
            )
            rows_core = holder ^ 1
        else:
            terms = tree(fan(terms, holder, masks))
        holder ^= 1
    last_core = holder
    mate_rows_b = swap(rows_b)

    def ready_kernel(rows, mate_rows, c, w, weighed, scales_a, b_out, base, gain, scale, all_b):
        b = in_order(on_core(rows_core, rows[...], mate_rows[...]), all_b, chips)
        coupled = weighed[...] * dot_rows(b, b)
        step = step_of(coupled)
        base[...] = c[...] - step * dot(c[...], coupled)
        gain[...] = step * w[...]
        scales_b = jnp.sqrt(jnp.sum(b * b, axis=0, keepdims=True) / smp_total + 1e-06)
        scale[...] = w[...] * scales_a[...] * scales_b
        b_out[...] = all_b[pl.ds(pl.multiple_of(smp_index() * smp_rows, smp_rows), smp_rows), :] / scales_b

    sample_result, base, gain, scale = call(
        ready_kernel,
        (far(smp_rows, rank), near(times, rank), near(1, rank), near(1, rank)),
        (rows_b, mate_rows_b, c_near, w_row, weighed, scales_a),
        2 * rank * rank * times * 4,
        scratch=(near(smp_total, rank),),
    )
    terms, base, gain, scale, voxel_result, sample_result = lax.optimization_barrier(
        (terms, base, gain, scale, voxel_result, sample_result)
    )
    mate_terms = swap(terms)

    def last_kernel(terms, mate_terms, base, gain, scale, c_out, w_out):
        moved = base[...] + on_core(last_core, terms[...], mate_terms[...]) * gain[...]
        scales_c = jnp.sqrt(jnp.sum(moved * moved, axis=0, keepdims=True) / times + 1e-06)
        c_out[...] = moved / scales_c
        w_out[...] = scale[...] * scales_c

    time_result, scale_result = call(
        last_kernel,
        (far(times, rank), far(1, rank)),
        (terms, mate_terms, base, gain, scale),
        rank * times * 8,
    )
    return voxel_result, sample_result, time_result, scale_result.reshape(rank)


def solution(mesh):
    return jax.shard_map(
        per_device,
        mesh=mesh,
        in_specs=(P("vox", "smp", None), P("vox", None), P("smp", None), P(), P()),
        out_specs=(P("vox", None), P("smp", None), P(), P()),
        check_vma=False,
    )
```

```python
import jax
import jax.numpy as jnp
from jax import lax
from jax.experimental import pallas as pl
from jax.experimental.pallas import tpu as pltpu
from jax.sharding import PartitionSpec as P

F32 = jnp.float32
BF16 = jnp.bfloat16
VMEM_LIMIT = 12 * 1024 * 1024
ALL = ("vox", "smp")


def halves(a, axis):
    high = a.astype(BF16)
    return jnp.concatenate([high, (a - high.astype(F32)).astype(BF16)], axis=axis)


def both(b):
    parts = halves(b, 1)
    return jnp.concatenate([parts, parts], axis=0)


def fold(product):
    width = product.shape[1] // 2
    return product[:, :width] + product[:, width:]


def dot(a, b):
    return fold(jnp.dot(halves(a, 1), both(b), preferred_element_type=F32))


def dot_rows(a, b):
    return fold(lax.dot_general(halves(a, 0), both(b), (((0,), (0,)), ((), ())), preferred_element_type=F32))


def step_of(coupled):
    sums = jnp.sum(jnp.abs(coupled), axis=0, keepdims=True)
    return 1.0 / jnp.max(sums, axis=1, keepdims=True)


def diagonal_row(gram):
    rows = lax.broadcasted_iota(jnp.int32, gram.shape, 0)
    columns = lax.broadcasted_iota(jnp.int32, gram.shape, 1)
    return jnp.sum(jnp.where(rows == columns, gram, 0.0), axis=0, keepdims=True)


def role_index():
    return (smp_index() ^ lax.axis_index("vox")) & 1


def only_on(role, kernel):
    def run(*refs):
        pl.when(role_index() == role)(lambda: kernel(*refs))

    return run


def call(kernel, outs, operands, flops, scratch=(), in_hbm=0):
    spaces = [pltpu.HBM if i < in_hbm else pltpu.VMEM for i in range(len(operands))]
    placed = [pltpu.with_memory_space_constraint(x, space) for x, space in zip(operands, spaces)]
    specs = [pl.BlockSpec(memory_space=space) for space in spaces]
    return pl.pallas_call(
        kernel,
        out_shape=outs,
        in_specs=specs,
        out_specs=[pl.BlockSpec(memory_space=pltpu.VMEM)] * len(outs),
        scratch_shapes=list(scratch),
        compiler_params=pltpu.CompilerParams(vmem_limit_bytes=VMEM_LIMIT),
        cost_estimate=pl.CostEstimate(flops=flops, bytes_accessed=1 << 16, transcendentals=0),
    )(*placed)


def near(*shape):
    return pltpu.VMEM(shape, F32)


def far(*shape):
    return jax.ShapeDtypeStruct(shape, F32)


def bits_of(count):
    if count & (count - 1):
        raise ValueError("axis size")
    return [1 << b for b in range(count.bit_length() - 1)]


def groups_of(bits, size=2):
    return [bits[i : i + size] for i in range(0, len(bits), size)]


def masks_of(group):
    masks = [0]
    for bit in group:
        masks = [mask | bit for mask in masks] + masks
    return masks


def swap(values):
    return lax.ppermute(values, ALL, [(i, i ^ 1) for i in range(lax.axis_size(ALL))])


def send(values, holder, mask):
    smp_count, count = lax.axis_size("smp"), lax.axis_size(ALL)
    role = lambda i: (i ^ i // smp_count) & 1
    pairs = []
    for i in range(count):
        target = i ^ mask if role(i) == holder else i
        pairs.append((i, target ^ 1 if role(target) == role(i) else target))
    return lax.ppermute(values, ALL, pairs)


def fan(values, holder, masks):
    sent = [send(values, holder, mask) if mask else swap(values) for mask in reversed(masks)]
    return sent[::-1]


def tree(parts):
    parts = parts[::-1]
    while len(parts) > 1:
        parts = [a + b for a, b in zip(parts[::2], parts[1::2])]
    return parts[0]


def smp_index():
    return lax.axis_index("smp")


def on_role(role, own, got):
    return jnp.where(role_index() == role, own, got)


def pack(gram):
    half = gram.shape[0] // 2
    rows = lax.broadcasted_iota(jnp.int32, (half, 2 * half), 0)
    columns = lax.broadcasted_iota(jnp.int32, (half, 2 * half), 1)
    top, bottom = gram[:half], gram[half:]
    packed = jnp.where(rows <= columns, top, pltpu.roll(bottom, half, 1))
    return packed, jnp.sum(jnp.where(columns == rows + half, bottom, 0.0), axis=0, keepdims=True)


def unpack(packed, diagonal):
    half = packed.shape[0]
    rows = lax.broadcasted_iota(jnp.int32, packed.shape, 0)
    columns = lax.broadcasted_iota(jnp.int32, packed.shape, 1)
    turned = jnp.concatenate([packed, packed], axis=0).T
    top = jnp.where(rows <= columns, packed, turned[:half])
    corner = jnp.where(columns < rows + half, pltpu.roll(packed, half, 1), turned[:half])
    corner = jnp.where(columns == rows + half, diagonal, corner)
    return jnp.concatenate([top, jnp.where(columns < half, turned[half:], corner)], axis=0)


def in_order(rows, scratch, chips, flip=0):
    size = scratch.shape[0] // chips // 2
    chip = smp_index() // 2
    for p in range(chips):
        for q in range(2):
            start = (2 * p + q) * size
            place = (chip ^ (chips - 1 - p)) * 2 + (q ^ flip)
            scratch[pl.ds(pl.multiple_of(place * size, size), size), :] = rows[start : start + size, :]
    return scratch[...]


def per_device(ensemble, voxel_factor, sample_factor, time_factor, weights):
    vox_rows, smp_rows, times = ensemble.shape
    rank = voxel_factor.shape[1]
    flat_rows = vox_rows * smp_rows
    vox_count, smp_count = lax.axis_size("vox"), lax.axis_size("smp")
    vox_total, smp_total = vox_rows * vox_count, smp_rows * smp_count
    chips, chip_rows = smp_count // 2, 2 * smp_rows
    chip_bits = bits_of(smp_count)[1:]
    vox_bits = [bit * smp_count for bit in bits_of(vox_count)]
    pieces = 4 if flat_rows % 32 == 0 else 1
    piece_rows = flat_rows // pieces

    def open_kernel(x_hbm, c_hbm, b_hbm, a_hbm, w_hbm, x, c, a, w, out, con, sems):
        copies = [pltpu.make_async_copy(c_hbm, c, sems.at[0])]
        copies += [pltpu.make_async_copy(b_hbm, out.at[pl.ds(vox_rows, smp_rows), :], sems.at[1])]
        for n in range(pieces):
            piece = pl.ds(n * piece_rows, piece_rows)
            copies.append(pltpu.make_async_copy(x_hbm.at[piece, :], x.at[piece, :], sems.at[2 + n]))
        copies.append(pltpu.make_async_copy(a_hbm, a, sems.at[2 + pieces]))
        copies.append(pltpu.make_async_copy(w_hbm, w, sems.at[3 + pieces]))
        for copy in copies:
            copy.start()
        copies[0].wait()
        copies[1].wait()
        factor = both(c[...])
        b = out[pl.ds(vox_rows, smp_rows), :]
        for n in range(pieces):
            copies[2 + n].wait()
        blocks = [x[pl.ds(j, vox_rows, stride=smp_rows), :] for j in range(smp_rows)]
        blocks = jnp.concatenate([halves(block, 1) for block in blocks], axis=0)
        made = fold(jnp.dot(blocks, factor, preferred_element_type=F32)).reshape(smp_rows, vox_rows, rank)
        con[...] = made
        total = made[0] * b[:1, :]
        for j in range(1, smp_rows):
            total = total + made[j] * b[j : j + 1, :]
        out[:vox_rows, :] = total
        copies[2 + pieces].wait()
        copies[3 + pieces].wait()

    x, c_near, a_near, w_row, opened, con = call(
        open_kernel,
        (
            near(flat_rows, times),
            near(times, rank),
            near(vox_rows, rank),
            near(1, rank),
            near(vox_rows + smp_rows, rank),
            near(smp_rows, vox_rows, rank),
        ),
        (ensemble.reshape(flat_rows, times), time_factor, sample_factor, voxel_factor, weights.reshape(1, rank)),
        2 * flat_rows * times * rank * 6,
        scratch=(pltpu.SemaphoreType.DMA((4 + pieces,)),),
        in_hbm=5,
    )

    def weigh_kernel(c, w, outer, outer_c):
        squared = dot_rows(w[...], w[...])
        outer[...] = squared
        outer_c[...] = squared * dot_rows(c[...], c[...])

    outer, outer_c = call(
        weigh_kernel, (near(rank, rank), near(rank, rank)), (c_near, w_row), 2 * rank * rank * times * 6
    )

    got = swap(opened)
    terms = opened[:vox_rows] + got[:vox_rows]
    mate_con, mate_x = swap(con), swap(x)
    packet = jnp.concatenate([terms, got[vox_rows:], opened[vox_rows:]], axis=0)
    own = jnp.concatenate([terms, opened[vox_rows:], got[vox_rows:]], axis=0)
    rows_b = own[vox_rows:]
    holder = 1
    for group in groups_of(chip_bits):
        parts = [send(packet, holder, mask) for mask in masks_of(group)[:-1]] + [own]
        terms = tree([part[:vox_rows] for part in parts])
        rows_b = jnp.concatenate([part[vox_rows:] for part in parts], axis=0)
        packet = jnp.concatenate([terms, rows_b], axis=0)
        own = swap(packet)
        holder ^= 1
    voxel_role = holder

    half, sums_rows = rank // 2, rank // 2 + chip_rows

    def voxel_kernel(terms, rows, a, w, outer_c, con, mate_con, mate_x, moved_out, chip_b, out, all_b):
        b = in_order(rows, all_b, chips, lax.axis_index("vox") & 1)
        chip_b[...] = all_b[pl.ds(pl.multiple_of(smp_index() // 2 * chip_rows, chip_rows), chip_rows), :]
        coupled = outer_c[...] * dot_rows(b, b)
        moved = a[...] - step_of(coupled) * (dot(a[...], coupled) - terms[...] * w[...])
        moved_out[...] = moved
        packed, diagonal = pack(dot_rows(moved, moved))
        out[:half, :] = packed
        core = smp_index() & 1
        for place, source in ((core, con), (1 - core, mate_con)):
            made = [jnp.sum(source[j] * moved, axis=0, keepdims=True) for j in range(smp_rows)]
            start = pl.multiple_of(half + place * smp_rows, smp_rows)
            out[pl.ds(start, smp_rows), :] = jnp.concatenate(made, axis=0)
        out[sums_rows:, :] = jnp.broadcast_to(diagonal, (8, rank))

    moved_a, chip_b, sums = call(
        only_on(voxel_role, voxel_kernel),
        (near(vox_rows, rank), near(chip_rows, rank), near(sums_rows + 8, rank)),
        (terms, rows_b, a_near, w_row, outer_c, con, mate_con, mate_x),
        2 * rank * rank * vox_rows * 12,
        scratch=(near(smp_total, rank),),
    )

    mate_moved_a = swap(moved_a)

    for group in groups_of(vox_bits[:1] + vox_bits[:0:-1]):
        sums = tree(fan(sums, holder, masks_of(group)))
        holder ^= 1
    sample_role = holder
    if sample_role != voxel_role:
        chip_b = swap(chip_b)

    def time_kernel(x, mate_x, moved, mate_moved, each):
        moved = on_role(voxel_role, moved[...], mate_moved[...])
        core = smp_index() & 1
        for place, source in ((core, x), (1 - core, mate_x)):
            for j in range(smp_rows):
                block = source[pl.ds(j, vox_rows, stride=smp_rows), :]
                each[place * smp_rows + j] = dot_rows(block, moved)

    (each,) = call(
        only_on(sample_role, time_kernel),
        (near(chip_rows, times, rank),),
        (x, mate_x, moved_a, mate_moved_a),
        4 * flat_rows * times * rank * 6,
    )

    def sample_kernel(sums, b, w, outer_c, each, gram_out, out):
        gram = unpack(sums[:half, :], sums[sums_rows : sums_rows + 1, :])
        gram_out[...] = gram
        coupled = outer_c[...] * gram
        moved = b[...] - step_of(coupled) * (dot(b[...], coupled) - sums[half:sums_rows, :] * w[...])
        out[times:, :] = moved
        total = None
        for j in range(chip_rows):
            made = each[j] * moved[j : j + 1, :]
            total = made if total is None else total + made
        out[:times, :] = total

    gram_a, payload = call(
        only_on(sample_role, sample_kernel),
        (near(rank, rank), near(times + chip_rows, rank)),
        (sums, chip_b, w_row, outer_c, each),
        2 * rank * rank * chip_rows * 6,
    )
    mate_gram_a = swap(gram_a)

    def scale_kernel(gram, mate_gram, moved, mate_moved, outer, result, scales_out, weighed):
        gram = on_role(sample_role, gram[...], mate_gram[...])
        scales = jnp.sqrt(diagonal_row(gram) / vox_total + 1e-06)
        scales_out[...] = scales
        result[...] = on_role(voxel_role, moved[...], mate_moved[...]) / scales
        weighed[...] = outer[...] * gram

    voxel_result, scales_a, weighed = call(
        scale_kernel,
        (far(vox_rows, rank), near(1, rank), near(rank, rank)),
        (gram_a, mate_gram_a, moved_a, mate_moved_a, outer),
        vox_rows * rank * 8,
    )

    terms, rows_b, rows_role = payload[:times], payload[times:], holder
    smp_mask = sum(chip_bits)
    for group in groups_of(chip_bits + vox_bits[1:2] + vox_bits[:1] + vox_bits[2:]):
        masks = masks_of(group)
        if any(mask & smp_mask for mask in masks):
            packet = payload if rows_b.shape[0] == chip_rows else jnp.concatenate([terms, rows_b], axis=0)
            parts = fan(packet, holder, masks)
            gathered = [i for i, mask in enumerate(masks) if not mask & ~smp_mask]
            rows = rows_b.shape[0]

            def gather_kernel(*refs, gathered=gathered, rows=rows):
                parts, (terms, rows_out) = refs[-3::-1], refs[-2:]
                terms[...] = tree([part[:times, :] for part in parts])
                for p, i in enumerate(gathered):
                    rows_out[p * rows : (p + 1) * rows, :] = parts[i][times:, :]

            terms, rows_b = call(
                gather_kernel,
                (near(times, rank), near(len(gathered) * rows, rank)),
                parts[::-1],
                len(masks) * times * rank,
            )
            rows_role = holder ^ 1
        else:
            terms = tree(fan(terms, holder, masks))
        holder ^= 1
    last_role = holder
    mate_rows_b = swap(rows_b)

    def ready_kernel(rows, mate_rows, c, w, weighed, scales_a, b_out, base, gain, scale, all_b):
        b = in_order(on_role(rows_role, rows[...], mate_rows[...]), all_b, chips)
        coupled = weighed[...] * dot_rows(b, b)
        step = step_of(coupled)
        base[...] = c[...] - step * dot(c[...], coupled)
        gain[...] = step * w[...]
        scales_b = jnp.sqrt(jnp.sum(b * b, axis=0, keepdims=True) / smp_total + 1e-06)
        scale[...] = w[...] * scales_a[...] * scales_b
        b_out[...] = all_b[pl.ds(pl.multiple_of(smp_index() * smp_rows, smp_rows), smp_rows), :] / scales_b

    sample_result, base, gain, scale = call(
        ready_kernel,
        (far(smp_rows, rank), near(times, rank), near(1, rank), near(1, rank)),
        (rows_b, mate_rows_b, c_near, w_row, weighed, scales_a),
        2 * rank * rank * times * 4,
        scratch=(near(smp_total, rank),),
    )
    terms, base, gain, scale, voxel_result, sample_result = lax.optimization_barrier(
        (terms, base, gain, scale, voxel_result, sample_result)
    )
    mate_terms = swap(terms)

    def last_kernel(terms, mate_terms, base, gain, scale, c_out, w_out):
        moved = base[...] + on_role(last_role, terms[...], mate_terms[...]) * gain[...]
        scales_c = jnp.sqrt(jnp.sum(moved * moved, axis=0, keepdims=True) / times + 1e-06)
        c_out[...] = moved / scales_c
        w_out[...] = scale[...] * scales_c

    time_result, scale_result = call(
        last_kernel,
        (far(times, rank), far(1, rank)),
        (terms, mate_terms, base, gain, scale),
        rank * times * 8,
    )
    return voxel_result, sample_result, time_result, scale_result.reshape(rank)


def solution(mesh):
    return jax.shard_map(
        per_device,
        mesh=mesh,
        in_specs=(P("vox", "smp", None), P("vox", None), P("smp", None), P(), P()),
        out_specs=(P("vox", None), P("smp", None), P(), P()),
        check_vma=False,
    )
```

```python
import jax
import jax.numpy as jnp
from jax import lax
from jax.experimental import pallas as pl
from jax.experimental.pallas import tpu as pltpu
from jax.sharding import PartitionSpec as P

F32 = jnp.float32
BF16 = jnp.bfloat16
VMEM_LIMIT = 12 * 1024 * 1024
ALL = ("vox", "smp")


def halves(a, axis):
    high = a.astype(BF16)
    return jnp.concatenate([high, (a - high.astype(F32)).astype(BF16)], axis=axis)


def both(b):
    parts = halves(b, 1)
    return jnp.concatenate([parts, parts], axis=0)


def fold(product):
    width = product.shape[1] // 2
    return product[:, :width] + product[:, width:]


def dot(a, b):
    return fold(jnp.dot(halves(a, 1), both(b), preferred_element_type=F32))


def dot_rows(a, b):
    return fold(lax.dot_general(halves(a, 0), both(b), (((0,), (0,)), ((), ())), preferred_element_type=F32))


def step_of(coupled):
    sums = jnp.sum(jnp.abs(coupled), axis=0, keepdims=True)
    return 1.0 / jnp.max(sums, axis=1, keepdims=True)


def diagonal_row(gram):
    rows = lax.broadcasted_iota(jnp.int32, gram.shape, 0)
    columns = lax.broadcasted_iota(jnp.int32, gram.shape, 1)
    return jnp.sum(jnp.where(rows == columns, gram, 0.0), axis=0, keepdims=True)


def role_index():
    return (smp_index() ^ lax.axis_index("vox") // 2) & 1


def only_on(role, kernel):
    def run(*refs):
        pl.when(role_index() == role)(lambda: kernel(*refs))

    return run


def call(kernel, outs, operands, flops, scratch=(), in_hbm=0):
    spaces = [pltpu.HBM if i < in_hbm else pltpu.VMEM for i in range(len(operands))]
    placed = [pltpu.with_memory_space_constraint(x, space) for x, space in zip(operands, spaces)]
    specs = [pl.BlockSpec(memory_space=space) for space in spaces]
    return pl.pallas_call(
        kernel,
        out_shape=outs,
        in_specs=specs,
        out_specs=[pl.BlockSpec(memory_space=pltpu.VMEM)] * len(outs),
        scratch_shapes=list(scratch),
        compiler_params=pltpu.CompilerParams(vmem_limit_bytes=VMEM_LIMIT),
        cost_estimate=pl.CostEstimate(flops=flops, bytes_accessed=1 << 16, transcendentals=0),
    )(*placed)


def near(*shape):
    return pltpu.VMEM(shape, F32)


def far(*shape):
    return jax.ShapeDtypeStruct(shape, F32)


def bits_of(count):
    if count & (count - 1):
        raise ValueError("axis size")
    return [1 << b for b in range(count.bit_length() - 1)]


def groups_of(bits, size=2):
    return [bits[i : i + size] for i in range(0, len(bits), size)]


def masks_of(group):
    masks = [0]
    for bit in group:
        masks = [mask | bit for mask in masks] + masks
    return masks


def swap(values):
    return lax.ppermute(values, ALL, [(i, i ^ 1) for i in range(lax.axis_size(ALL))])


def send(values, holder, mask):
    smp_count, count = lax.axis_size("smp"), lax.axis_size(ALL)
    role = lambda i: (i ^ i // (2 * smp_count)) & 1
    pairs = []
    for i in range(count):
        target = i ^ mask if role(i) == holder else i
        pairs.append((i, target ^ 1 if role(target) == role(i) else target))
    return lax.ppermute(values, ALL, pairs)


def fan(values, holder, masks):
    sent = [send(values, holder, mask) if mask else swap(values) for mask in reversed(masks)]
    return sent[::-1]


def tree(parts):
    parts = parts[::-1]
    while len(parts) > 1:
        parts = [a + b for a, b in zip(parts[::2], parts[1::2])]
    return parts[0]


def smp_index():
    return lax.axis_index("smp")


def on_role(role, own, got):
    return jnp.where(role_index() == role, own, got)


def pack(gram):
    half = gram.shape[0] // 2
    rows = lax.broadcasted_iota(jnp.int32, (half, 2 * half), 0)
    columns = lax.broadcasted_iota(jnp.int32, (half, 2 * half), 1)
    top, bottom = gram[:half], gram[half:]
    packed = jnp.where(rows <= columns, top, pltpu.roll(bottom, half, 1))
    return packed, jnp.sum(jnp.where(columns == rows + half, bottom, 0.0), axis=0, keepdims=True)


def unpack(packed, diagonal):
    half = packed.shape[0]
    rows = lax.broadcasted_iota(jnp.int32, packed.shape, 0)
    columns = lax.broadcasted_iota(jnp.int32, packed.shape, 1)
    turned = jnp.concatenate([packed, packed], axis=0).T
    top = jnp.where(rows <= columns, packed, turned[:half])
    corner = jnp.where(columns < rows + half, pltpu.roll(packed, half, 1), turned[:half])
    corner = jnp.where(columns == rows + half, diagonal, corner)
    return jnp.concatenate([top, jnp.where(columns < half, turned[half:], corner)], axis=0)


def in_order(rows, scratch, chips, flip=0):
    size = scratch.shape[0] // chips // 2
    chip = smp_index() // 2
    for p in range(chips):
        for q in range(2):
            start = (2 * p + q) * size
            place = (chip ^ (chips - 1 - p)) * 2 + (q ^ flip)
            scratch[pl.ds(pl.multiple_of(place * size, size), size), :] = rows[start : start + size, :]
    return scratch[...]


def per_device(ensemble, voxel_factor, sample_factor, time_factor, weights):
    vox_rows, smp_rows, times = ensemble.shape
    rank = voxel_factor.shape[1]
    flat_rows = vox_rows * smp_rows
    vox_count, smp_count = lax.axis_size("vox"), lax.axis_size("smp")
    vox_total, smp_total = vox_rows * vox_count, smp_rows * smp_count
    chips, chip_rows = smp_count // 2, 2 * smp_rows
    chip_bits = bits_of(smp_count)[1:]
    vox_bits = [bit * smp_count for bit in bits_of(vox_count)]
    pieces = 4 if flat_rows % 32 == 0 else 1
    piece_rows = flat_rows // pieces

    def open_kernel(x_hbm, c_hbm, b_hbm, a_hbm, w_hbm, x, c, a, w, out, con, sems):
        copies = [pltpu.make_async_copy(c_hbm, c, sems.at[0])]
        copies += [pltpu.make_async_copy(b_hbm, out.at[pl.ds(vox_rows, smp_rows), :], sems.at[1])]
        for n in range(pieces):
            piece = pl.ds(n * piece_rows, piece_rows)
            copies.append(pltpu.make_async_copy(x_hbm.at[piece, :], x.at[piece, :], sems.at[2 + n]))
        copies.append(pltpu.make_async_copy(a_hbm, a, sems.at[2 + pieces]))
        copies.append(pltpu.make_async_copy(w_hbm, w, sems.at[3 + pieces]))
        for copy in copies:
            copy.start()
        copies[0].wait()
        copies[1].wait()
        factor = both(c[...])
        b = out[pl.ds(vox_rows, smp_rows), :]
        for n in range(pieces):
            copies[2 + n].wait()
        blocks = [x[pl.ds(j, vox_rows, stride=smp_rows), :] for j in range(smp_rows)]
        blocks = jnp.concatenate([halves(block, 1) for block in blocks], axis=0)
        made = fold(jnp.dot(blocks, factor, preferred_element_type=F32)).reshape(smp_rows, vox_rows, rank)
        con[...] = made
        total = made[0] * b[:1, :]
        for j in range(1, smp_rows):
            total = total + made[j] * b[j : j + 1, :]
        out[:vox_rows, :] = total
        copies[2 + pieces].wait()
        copies[3 + pieces].wait()

    x, c_near, a_near, w_row, opened, con = call(
        open_kernel,
        (
            near(flat_rows, times),
            near(times, rank),
            near(vox_rows, rank),
            near(1, rank),
            near(vox_rows + smp_rows, rank),
            near(smp_rows, vox_rows, rank),
        ),
        (ensemble.reshape(flat_rows, times), time_factor, sample_factor, voxel_factor, weights.reshape(1, rank)),
        2 * flat_rows * times * rank * 6,
        scratch=(pltpu.SemaphoreType.DMA((4 + pieces,)),),
        in_hbm=5,
    )

    def weigh_kernel(c, w, outer, outer_c):
        squared = dot_rows(w[...], w[...])
        outer[...] = squared
        outer_c[...] = squared * dot_rows(c[...], c[...])

    outer, outer_c = call(
        weigh_kernel, (near(rank, rank), near(rank, rank)), (c_near, w_row), 2 * rank * rank * times * 6
    )

    got = swap(opened)
    terms = opened[:vox_rows] + got[:vox_rows]
    mate_con, mate_x = swap(con), swap(x)
    packet = jnp.concatenate([terms, got[vox_rows:], opened[vox_rows:]], axis=0)
    own = jnp.concatenate([terms, opened[vox_rows:], got[vox_rows:]], axis=0)
    rows_b = own[vox_rows:]
    holder = 1
    for group in groups_of(chip_bits):
        parts = [send(packet, holder, mask) for mask in masks_of(group)[:-1]] + [own]
        terms = tree([part[:vox_rows] for part in parts])
        rows_b = jnp.concatenate([part[vox_rows:] for part in parts], axis=0)
        packet = jnp.concatenate([terms, rows_b], axis=0)
        own = swap(packet)
        holder ^= 1
    voxel_role = holder

    half, sums_rows = rank // 2, rank // 2 + chip_rows

    def voxel_kernel(terms, rows, a, w, outer_c, con, mate_con, mate_x, moved_out, chip_b, out, all_b):
        b = in_order(rows, all_b, chips, lax.axis_index("vox") // 2 & 1)
        chip_b[...] = all_b[pl.ds(pl.multiple_of(smp_index() // 2 * chip_rows, chip_rows), chip_rows), :]
        coupled = outer_c[...] * dot_rows(b, b)
        moved = a[...] - step_of(coupled) * (dot(a[...], coupled) - terms[...] * w[...])
        moved_out[...] = moved
        packed, diagonal = pack(dot_rows(moved, moved))
        out[:half, :] = packed
        core = smp_index() & 1
        for place, source in ((core, con), (1 - core, mate_con)):
            made = [jnp.sum(source[j] * moved, axis=0, keepdims=True) for j in range(smp_rows)]
            start = pl.multiple_of(half + place * smp_rows, smp_rows)
            out[pl.ds(start, smp_rows), :] = jnp.concatenate(made, axis=0)
        out[sums_rows:, :] = jnp.broadcast_to(diagonal, (8, rank))

    moved_a, chip_b, sums = call(
        only_on(voxel_role, voxel_kernel),
        (near(vox_rows, rank), near(chip_rows, rank), near(sums_rows + 8, rank)),
        (terms, rows_b, a_near, w_row, outer_c, con, mate_con, mate_x),
        2 * rank * rank * vox_rows * 12,
        scratch=(near(smp_total, rank),),
    )

    mate_moved_a = swap(moved_a)

    for group in groups_of(vox_bits[:1] + vox_bits[:0:-1]):
        sums = tree(fan(sums, holder, masks_of(group)))
        holder ^= 1
    sample_role = holder
    if sample_role != voxel_role:
        chip_b = swap(chip_b)

    def time_kernel(x, mate_x, moved, mate_moved, each):
        moved = on_role(voxel_role, moved[...], mate_moved[...])
        core = smp_index() & 1
        for place, source in ((core, x), (1 - core, mate_x)):
            for j in range(smp_rows):
                block = source[pl.ds(j, vox_rows, stride=smp_rows), :]
                each[place * smp_rows + j] = dot_rows(block, moved)

    (each,) = call(
        only_on(sample_role, time_kernel),
        (near(chip_rows, times, rank),),
        (x, mate_x, moved_a, mate_moved_a),
        4 * flat_rows * times * rank * 6,
    )

    def sample_kernel(sums, b, w, outer_c, each, gram_out, out):
        gram = unpack(sums[:half, :], sums[sums_rows : sums_rows + 1, :])
        gram_out[...] = gram
        coupled = outer_c[...] * gram
        moved = b[...] - step_of(coupled) * (dot(b[...], coupled) - sums[half:sums_rows, :] * w[...])
        out[times:, :] = moved
        total = None
        for j in range(chip_rows):
            made = each[j] * moved[j : j + 1, :]
            total = made if total is None else total + made
        out[:times, :] = total

    gram_a, payload = call(
        only_on(sample_role, sample_kernel),
        (near(rank, rank), near(times + chip_rows, rank)),
        (sums, chip_b, w_row, outer_c, each),
        2 * rank * rank * chip_rows * 6,
    )
    mate_gram_a = swap(gram_a)

    def scale_kernel(gram, mate_gram, moved, mate_moved, outer, result, scales_out, weighed):
        gram = on_role(sample_role, gram[...], mate_gram[...])
        scales = jnp.sqrt(diagonal_row(gram) / vox_total + 1e-06)
        scales_out[...] = scales
        result[...] = on_role(voxel_role, moved[...], mate_moved[...]) / scales
        weighed[...] = outer[...] * gram

    voxel_result, scales_a, weighed = call(
        scale_kernel,
        (far(vox_rows, rank), near(1, rank), near(rank, rank)),
        (gram_a, mate_gram_a, moved_a, mate_moved_a, outer),
        vox_rows * rank * 8,
    )

    terms, rows_b, rows_role = payload[:times], payload[times:], holder
    smp_mask = sum(chip_bits)
    for group in groups_of(chip_bits + vox_bits[1:2] + vox_bits[:1] + vox_bits[2:]):
        masks = masks_of(group)
        if any(mask & smp_mask for mask in masks):
            packet = payload if rows_b.shape[0] == chip_rows else jnp.concatenate([terms, rows_b], axis=0)
            parts = fan(packet, holder, masks)
            gathered = [i for i, mask in enumerate(masks) if not mask & ~smp_mask]
            rows = rows_b.shape[0]

            def gather_kernel(*refs, gathered=gathered, rows=rows):
                parts, (terms, rows_out) = refs[-3::-1], refs[-2:]
                terms[...] = tree([part[:times, :] for part in parts])
                for p, i in enumerate(gathered):
                    rows_out[p * rows : (p + 1) * rows, :] = parts[i][times:, :]

            terms, rows_b = call(
                gather_kernel,
                (near(times, rank), near(len(gathered) * rows, rank)),
                parts[::-1],
                len(masks) * times * rank,
            )
            rows_role = holder ^ 1
        else:
            terms = tree(fan(terms, holder, masks))
        holder ^= 1
    last_role = holder
    mate_rows_b = swap(rows_b)

    def ready_kernel(rows, mate_rows, c, w, weighed, scales_a, b_out, base, gain, scale, all_b):
        b = in_order(on_role(rows_role, rows[...], mate_rows[...]), all_b, chips)
        coupled = weighed[...] * dot_rows(b, b)
        step = step_of(coupled)
        base[...] = c[...] - step * dot(c[...], coupled)
        gain[...] = step * w[...]
        scales_b = jnp.sqrt(jnp.sum(b * b, axis=0, keepdims=True) / smp_total + 1e-06)
        scale[...] = w[...] * scales_a[...] * scales_b
        b_out[...] = all_b[pl.ds(pl.multiple_of(smp_index() * smp_rows, smp_rows), smp_rows), :] / scales_b

    sample_result, base, gain, scale = call(
        ready_kernel,
        (far(smp_rows, rank), near(times, rank), near(1, rank), near(1, rank)),
        (rows_b, mate_rows_b, c_near, w_row, weighed, scales_a),
        2 * rank * rank * times * 4,
        scratch=(near(smp_total, rank),),
    )
    terms, base, gain, scale, voxel_result, sample_result = lax.optimization_barrier(
        (terms, base, gain, scale, voxel_result, sample_result)
    )
    mate_terms = swap(terms)

    def last_kernel(terms, mate_terms, base, gain, scale, c_out, w_out):
        moved = base[...] + on_role(last_role, terms[...], mate_terms[...]) * gain[...]
        scales_c = jnp.sqrt(jnp.sum(moved * moved, axis=0, keepdims=True) / times + 1e-06)
        c_out[...] = moved / scales_c
        w_out[...] = scale[...] * scales_c

    time_result, scale_result = call(
        last_kernel,
        (far(times, rank), far(1, rank)),
        (terms, mate_terms, base, gain, scale),
        rank * times * 8,
    )
    return voxel_result, sample_result, time_result, scale_result.reshape(rank)


def solution(mesh):
    return jax.shard_map(
        per_device,
        mesh=mesh,
        in_specs=(P("vox", "smp", None), P("vox", None), P("smp", None), P(), P()),
        out_specs=(P("vox", None), P("smp", None), P(), P()),
        check_vma=False,
    )
```

```python
import jax
import jax.numpy as jnp
from jax import lax
from jax.experimental import pallas as pl
from jax.experimental.pallas import tpu as pltpu
from jax.sharding import PartitionSpec as P

F32 = jnp.float32
BF16 = jnp.bfloat16
VMEM_LIMIT = 12 * 1024 * 1024
ALL = ("vox", "smp")


def halves(a, axis):
    high = a.astype(BF16)
    return jnp.concatenate([high, (a - high.astype(F32)).astype(BF16)], axis=axis)


def both(b):
    parts = halves(b, 1)
    return jnp.concatenate([parts, parts], axis=0)


def fold(product):
    width = product.shape[1] // 2
    return product[:, :width] + product[:, width:]


def dot(a, b):
    return fold(jnp.dot(halves(a, 1), both(b), preferred_element_type=F32))


def dot_rows(a, b):
    return fold(lax.dot_general(halves(a, 0), both(b), (((0,), (0,)), ((), ())), preferred_element_type=F32))


def step_of(coupled):
    sums = jnp.sum(jnp.abs(coupled), axis=0, keepdims=True)
    return 1.0 / jnp.max(sums, axis=1, keepdims=True)


def diagonal_row(gram):
    rows = lax.broadcasted_iota(jnp.int32, gram.shape, 0)
    columns = lax.broadcasted_iota(jnp.int32, gram.shape, 1)
    return jnp.sum(jnp.where(rows == columns, gram, 0.0), axis=0, keepdims=True)


def role_index():
    return (smp_index() ^ lax.axis_index("vox") // 2) & 1


def only_on(role, kernel):
    def run(*refs):
        pl.when(role_index() == role)(lambda: kernel(*refs))

    return run


def call(kernel, outs, operands, flops, scratch=(), in_hbm=0):
    spaces = [pltpu.HBM if i < in_hbm else pltpu.VMEM for i in range(len(operands))]
    placed = [pltpu.with_memory_space_constraint(x, space) for x, space in zip(operands, spaces)]
    specs = [pl.BlockSpec(memory_space=space) for space in spaces]
    return pl.pallas_call(
        kernel,
        out_shape=outs,
        in_specs=specs,
        out_specs=[pl.BlockSpec(memory_space=pltpu.VMEM)] * len(outs),
        scratch_shapes=list(scratch),
        compiler_params=pltpu.CompilerParams(vmem_limit_bytes=VMEM_LIMIT),
        cost_estimate=pl.CostEstimate(flops=flops, bytes_accessed=1 << 16, transcendentals=0),
    )(*placed)


def near(*shape):
    return pltpu.VMEM(shape, F32)


def far(*shape):
    return jax.ShapeDtypeStruct(shape, F32)


def bits_of(count):
    if count & (count - 1):
        raise ValueError("axis size")
    return [1 << b for b in range(count.bit_length() - 1)]


def groups_of(bits, size=2):
    return [bits[i : i + size] for i in range(0, len(bits), size)]


def masks_of(group):
    masks = [0]
    for bit in group:
        masks = [mask | bit for mask in masks] + masks
    return masks


def swap(values):
    return lax.ppermute(values, ALL, [(i, i ^ 1) for i in range(lax.axis_size(ALL))])


def send(values, holder, mask):
    smp_count, count = lax.axis_size("smp"), lax.axis_size(ALL)
    role = lambda i: (i ^ i // (2 * smp_count)) & 1
    pairs = []
    for i in range(count):
        target = i ^ mask if role(i) == holder else i
        pairs.append((i, target ^ 1 if role(target) == role(i) else target))
    return lax.ppermute(values, ALL, pairs)


def fan(values, holder, masks):
    sent = [send(values, holder, mask) if mask else swap(values) for mask in reversed(masks)]
    return sent[::-1]


def tree(parts):
    parts = parts[::-1]
    while len(parts) > 1:
        parts = [a + b for a, b in zip(parts[::2], parts[1::2])]
    return parts[0]


def smp_index():
    return lax.axis_index("smp")


def on_role(role, own, got):
    return jnp.where(role_index() == role, own, got)


def pack(gram):
    half = gram.shape[0] // 2
    rows = lax.broadcasted_iota(jnp.int32, (half, 2 * half), 0)
    columns = lax.broadcasted_iota(jnp.int32, (half, 2 * half), 1)
    top, bottom = gram[:half], gram[half:]
    packed = jnp.where(rows <= columns, top, pltpu.roll(bottom, half, 1))
    return packed, jnp.sum(jnp.where(columns == rows + half, bottom, 0.0), axis=0, keepdims=True)


def unpack(packed, diagonal):
    half = packed.shape[0]
    rows = lax.broadcasted_iota(jnp.int32, packed.shape, 0)
    columns = lax.broadcasted_iota(jnp.int32, packed.shape, 1)
    turned = jnp.concatenate([packed, packed], axis=0).T
    top = jnp.where(rows <= columns, packed, turned[:half])
    corner = jnp.where(columns < rows + half, pltpu.roll(packed, half, 1), turned[:half])
    corner = jnp.where(columns == rows + half, diagonal, corner)
    return jnp.concatenate([top, jnp.where(columns < half, turned[half:], corner)], axis=0)


def in_order(rows, scratch, chips, flip=0):
    size = scratch.shape[0] // chips // 2
    chip = smp_index() // 2
    for p in range(chips):
        for q in range(2):
            start = (2 * p + q) * size
            place = (chip ^ (chips - 1 - p)) * 2 + (q ^ flip)
            scratch[pl.ds(pl.multiple_of(place * size, size), size), :] = rows[start : start + size, :]
    return scratch[...]


def per_device(ensemble, voxel_factor, sample_factor, time_factor, weights):
    vox_rows, smp_rows, times = ensemble.shape
    rank = voxel_factor.shape[1]
    flat_rows = vox_rows * smp_rows
    vox_count, smp_count = lax.axis_size("vox"), lax.axis_size("smp")
    vox_total, smp_total = vox_rows * vox_count, smp_rows * smp_count
    chips, chip_rows = smp_count // 2, 2 * smp_rows
    chip_bits = bits_of(smp_count)[1:]
    vox_bits = [bit * smp_count for bit in bits_of(vox_count)]
    pieces = 4 if flat_rows % 32 == 0 else 1
    piece_rows = flat_rows // pieces

    def open_kernel(x_hbm, c_hbm, b_hbm, a_hbm, w_hbm, x, c, a, w, out, con, sems):
        copies = [pltpu.make_async_copy(c_hbm, c, sems.at[0])]
        copies += [pltpu.make_async_copy(b_hbm, out.at[pl.ds(vox_rows, smp_rows), :], sems.at[1])]
        for n in range(pieces):
            piece = pl.ds(n * piece_rows, piece_rows)
            copies.append(pltpu.make_async_copy(x_hbm.at[piece, :], x.at[piece, :], sems.at[2 + n]))
        copies.append(pltpu.make_async_copy(a_hbm, a, sems.at[2 + pieces]))
        copies.append(pltpu.make_async_copy(w_hbm, w, sems.at[3 + pieces]))
        for copy in copies:
            copy.start()
        copies[0].wait()
        copies[1].wait()
        factor = both(c[...])
        b = out[pl.ds(vox_rows, smp_rows), :]
        for n in range(pieces):
            copies[2 + n].wait()
        blocks = [x[pl.ds(j, vox_rows, stride=smp_rows), :] for j in range(smp_rows)]
        blocks = jnp.concatenate([halves(block, 1) for block in blocks], axis=0)
        made = fold(jnp.dot(blocks, factor, preferred_element_type=F32)).reshape(smp_rows, vox_rows, rank)
        con[...] = made
        total = made[0] * b[:1, :]
        for j in range(1, smp_rows):
            total = total + made[j] * b[j : j + 1, :]
        out[:vox_rows, :] = total
        copies[2 + pieces].wait()
        copies[3 + pieces].wait()

    x, c_near, a_near, w_row, opened, con = call(
        open_kernel,
        (
            near(flat_rows, times),
            near(times, rank),
            near(vox_rows, rank),
            near(1, rank),
            near(vox_rows + smp_rows, rank),
            near(smp_rows, vox_rows, rank),
        ),
        (ensemble.reshape(flat_rows, times), time_factor, sample_factor, voxel_factor, weights.reshape(1, rank)),
        2 * flat_rows * times * rank * 6,
        scratch=(pltpu.SemaphoreType.DMA((4 + pieces,)),),
        in_hbm=5,
    )

    def weigh_kernel(c, w, outer, outer_c):
        squared = dot_rows(w[...], w[...])
        outer[...] = squared
        outer_c[...] = squared * dot_rows(c[...], c[...])

    outer, outer_c = call(
        weigh_kernel, (near(rank, rank), near(rank, rank)), (c_near, w_row), 2 * rank * rank * times * 6
    )

    got = swap(opened)
    terms = opened[:vox_rows] + got[:vox_rows]
    mate_con, mate_x = swap(con), swap(x)
    packet = jnp.concatenate([terms, got[vox_rows:], opened[vox_rows:]], axis=0)
    own = jnp.concatenate([terms, opened[vox_rows:], got[vox_rows:]], axis=0)
    rows_b = own[vox_rows:]
    holder = 1
    for group in groups_of(chip_bits):
        parts = [send(packet, holder, mask) for mask in masks_of(group)[:-1]] + [own]
        terms = tree([part[:vox_rows] for part in parts])
        rows_b = jnp.concatenate([part[vox_rows:] for part in parts], axis=0)
        packet = jnp.concatenate([terms, rows_b], axis=0)
        own = swap(packet)
        holder ^= 1
    voxel_role = holder

    half, sums_rows = rank // 2, rank // 2 + chip_rows

    def voxel_kernel(terms, rows, a, w, outer_c, con, mate_con, mate_x, moved_out, chip_b, out, all_b):
        b = in_order(rows, all_b, chips, lax.axis_index("vox") // 2 & 1)
        chip_b[...] = all_b[pl.ds(pl.multiple_of(smp_index() // 2 * chip_rows, chip_rows), chip_rows), :]
        coupled = outer_c[...] * dot_rows(b, b)
        moved = a[...] - step_of(coupled) * (dot(a[...], coupled) - terms[...] * w[...])
        moved_out[...] = moved
        packed, diagonal = pack(dot_rows(moved, moved))
        out[:half, :] = packed
        core = smp_index() & 1
        for place, source in ((core, con), (1 - core, mate_con)):
            made = [jnp.sum(source[j] * moved, axis=0, keepdims=True) for j in range(smp_rows)]
            start = pl.multiple_of(half + place * smp_rows, smp_rows)
            out[pl.ds(start, smp_rows), :] = jnp.concatenate(made, axis=0)
        out[sums_rows:, :] = jnp.broadcast_to(diagonal, (8, rank))

    moved_a, chip_b, sums = call(
        only_on(voxel_role, voxel_kernel),
        (near(vox_rows, rank), near(chip_rows, rank), near(sums_rows + 8, rank)),
        (terms, rows_b, a_near, w_row, outer_c, con, mate_con, mate_x),
        2 * rank * rank * vox_rows * 12,
        scratch=(near(smp_total, rank),),
    )

    mate_moved_a = swap(moved_a)

    for group in groups_of(vox_bits[:1] + vox_bits[:0:-1]):
        sums = tree(fan(sums, holder, masks_of(group)))
        holder ^= 1
    sample_role = holder
    if sample_role != voxel_role:
        chip_b = swap(chip_b)

    def time_kernel(x, mate_x, moved, mate_moved, each):
        moved = on_role(voxel_role, moved[...], mate_moved[...])
        core = smp_index() & 1
        for place, source in ((core, x), (1 - core, mate_x)):
            for j in range(smp_rows):
                block = source[pl.ds(j, vox_rows, stride=smp_rows), :]
                each[place * smp_rows + j] = dot_rows(block, moved)

    (each,) = call(
        only_on(sample_role, time_kernel),
        (near(chip_rows, times, rank),),
        (x, mate_x, moved_a, mate_moved_a),
        4 * flat_rows * times * rank * 6,
    )

    def sample_kernel(sums, b, w, outer_c, each, gram_out, out):
        gram = unpack(sums[:half, :], sums[sums_rows : sums_rows + 1, :])
        gram_out[...] = gram
        coupled = outer_c[...] * gram
        moved = b[...] - step_of(coupled) * (dot(b[...], coupled) - sums[half:sums_rows, :] * w[...])
        out[times:, :] = moved
        total = None
        for j in range(chip_rows):
            made = each[j] * moved[j : j + 1, :]
            total = made if total is None else total + made
        out[:times, :] = total

    gram_a, payload = call(
        only_on(sample_role, sample_kernel),
        (near(rank, rank), near(times + chip_rows, rank)),
        (sums, chip_b, w_row, outer_c, each),
        2 * rank * rank * chip_rows * 6,
    )
    mate_gram_a = swap(gram_a)

    def scale_kernel(gram, mate_gram, moved, mate_moved, outer, result, scales_out, weighed):
        gram = on_role(sample_role, gram[...], mate_gram[...])
        scales = jnp.sqrt(diagonal_row(gram) / vox_total + 1e-06)
        scales_out[...] = scales
        result[...] = on_role(voxel_role, moved[...], mate_moved[...]) / scales
        weighed[...] = outer[...] * gram

    voxel_result, scales_a, weighed = call(
        scale_kernel,
        (far(vox_rows, rank), near(1, rank), near(rank, rank)),
        (gram_a, mate_gram_a, moved_a, mate_moved_a, outer),
        vox_rows * rank * 8,
    )

    terms, rows_b, rows_role = payload[:times], payload[times:], holder
    smp_mask = sum(chip_bits)
    for group in groups_of(chip_bits + vox_bits[-1:] + vox_bits[:-1]):
        masks = masks_of(group)
        if any(mask & smp_mask for mask in masks):
            packet = payload if rows_b.shape[0] == chip_rows else jnp.concatenate([terms, rows_b], axis=0)
            parts = fan(packet, holder, masks)
            gathered = [i for i, mask in enumerate(masks) if not mask & ~smp_mask]
            rows = rows_b.shape[0]

            def gather_kernel(*refs, gathered=gathered, rows=rows):
                parts, (terms, rows_out) = refs[-3::-1], refs[-2:]
                terms[...] = tree([part[:times, :] for part in parts])
                for p, i in enumerate(gathered):
                    rows_out[p * rows : (p + 1) * rows, :] = parts[i][times:, :]

            terms, rows_b = call(
                gather_kernel,
                (near(times, rank), near(len(gathered) * rows, rank)),
                parts[::-1],
                len(masks) * times * rank,
            )
            rows_role = holder ^ 1
        else:
            terms = tree(fan(terms, holder, masks))
        holder ^= 1
    last_role = holder
    mate_rows_b = swap(rows_b)

    def ready_kernel(rows, mate_rows, c, w, weighed, scales_a, b_out, base, gain, scale, all_b):
        b = in_order(on_role(rows_role, rows[...], mate_rows[...]), all_b, chips)
        coupled = weighed[...] * dot_rows(b, b)
        step = step_of(coupled)
        base[...] = c[...] - step * dot(c[...], coupled)
        gain[...] = step * w[...]
        scales_b = jnp.sqrt(jnp.sum(b * b, axis=0, keepdims=True) / smp_total + 1e-06)
        scale[...] = w[...] * scales_a[...] * scales_b
        b_out[...] = all_b[pl.ds(pl.multiple_of(smp_index() * smp_rows, smp_rows), smp_rows), :] / scales_b

    sample_result, base, gain, scale = call(
        ready_kernel,
        (far(smp_rows, rank), near(times, rank), near(1, rank), near(1, rank)),
        (rows_b, mate_rows_b, c_near, w_row, weighed, scales_a),
        2 * rank * rank * times * 4,
        scratch=(near(smp_total, rank),),
    )
    terms, base, gain, scale, voxel_result, sample_result = lax.optimization_barrier(
        (terms, base, gain, scale, voxel_result, sample_result)
    )
    mate_terms = swap(terms)

    def last_kernel(terms, mate_terms, base, gain, scale, c_out, w_out):
        moved = base[...] + on_role(last_role, terms[...], mate_terms[...]) * gain[...]
        scales_c = jnp.sqrt(jnp.sum(moved * moved, axis=0, keepdims=True) / times + 1e-06)
        c_out[...] = moved / scales_c
        w_out[...] = scale[...] * scales_c

    time_result, scale_result = call(
        last_kernel,
        (far(times, rank), far(1, rank)),
        (terms, mate_terms, base, gain, scale),
        rank * times * 8,
    )
    return voxel_result, sample_result, time_result, scale_result.reshape(rank)


def solution(mesh):
    return jax.shard_map(
        per_device,
        mesh=mesh,
        in_specs=(P("vox", "smp", None), P("vox", None), P("smp", None), P(), P()),
        out_specs=(P("vox", None), P("smp", None), P(), P()),
        check_vma=False,
    )
```

```python
import jax
import jax.numpy as jnp
from jax import lax
from jax.experimental import pallas as pl
from jax.experimental.pallas import tpu as pltpu
from jax.sharding import PartitionSpec as P

F32 = jnp.float32
BF16 = jnp.bfloat16
VMEM_LIMIT = 12 * 1024 * 1024
ALL = ("vox", "smp")


def halves(a, axis):
    high = a.astype(BF16)
    return jnp.concatenate([high, (a - high.astype(F32)).astype(BF16)], axis=axis)


def both(b):
    parts = halves(b, 1)
    return jnp.concatenate([parts, parts], axis=0)


def fold(product):
    width = product.shape[1] // 2
    return product[:, :width] + product[:, width:]


def dot(a, b):
    return fold(jnp.dot(halves(a, 1), both(b), preferred_element_type=F32))


def dot_rows(a, b):
    return fold(lax.dot_general(halves(a, 0), both(b), (((0,), (0,)), ((), ())), preferred_element_type=F32))


def step_of(coupled):
    sums = jnp.sum(jnp.abs(coupled), axis=0, keepdims=True)
    return 1.0 / jnp.max(sums, axis=1, keepdims=True)


def diagonal_row(gram):
    rows = lax.broadcasted_iota(jnp.int32, gram.shape, 0)
    columns = lax.broadcasted_iota(jnp.int32, gram.shape, 1)
    return jnp.sum(jnp.where(rows == columns, gram, 0.0), axis=0, keepdims=True)


def role_index():
    return (smp_index() ^ lax.axis_index("vox") // 2) & 1


def only_on(role, kernel):
    def run(*refs):
        pl.when(role_index() == role)(lambda: kernel(*refs))

    return run


def call(kernel, outs, operands, flops, scratch=(), in_hbm=0):
    spaces = [pltpu.HBM if i < in_hbm else pltpu.VMEM for i in range(len(operands))]
    placed = [pltpu.with_memory_space_constraint(x, space) for x, space in zip(operands, spaces)]
    specs = [pl.BlockSpec(memory_space=space) for space in spaces]
    return pl.pallas_call(
        kernel,
        out_shape=outs,
        in_specs=specs,
        out_specs=[pl.BlockSpec(memory_space=pltpu.VMEM)] * len(outs),
        scratch_shapes=list(scratch),
        compiler_params=pltpu.CompilerParams(vmem_limit_bytes=VMEM_LIMIT),
        cost_estimate=pl.CostEstimate(flops=flops, bytes_accessed=1 << 16, transcendentals=0),
    )(*placed)


def near(*shape):
    return pltpu.VMEM(shape, F32)


def far(*shape):
    return jax.ShapeDtypeStruct(shape, F32)


def bits_of(count):
    if count & (count - 1):
        raise ValueError("axis size")
    return [1 << b for b in range(count.bit_length() - 1)]


def groups_of(bits, size=2):
    return [bits[i : i + size] for i in range(0, len(bits), size)]


def masks_of(group):
    masks = [0]
    for bit in group:
        masks = [mask | bit for mask in masks] + masks
    return masks


def swap(values):
    return lax.ppermute(values, ALL, [(i, i ^ 1) for i in range(lax.axis_size(ALL))])


def send(values, holder, mask):
    smp_count, count = lax.axis_size("smp"), lax.axis_size(ALL)
    role = lambda i: (i ^ i // (2 * smp_count)) & 1
    pairs = []
    for i in range(count):
        target = i ^ mask if role(i) == holder else i
        pairs.append((i, target ^ 1 if role(target) == role(i) else target))
    return lax.ppermute(values, ALL, pairs)


def fan(values, holder, masks):
    sent = [send(values, holder, mask) if mask else swap(values) for mask in reversed(masks)]
    return sent[::-1]


def tree(parts):
    parts = parts[::-1]
    while len(parts) > 1:
        parts = [a + b for a, b in zip(parts[::2], parts[1::2])]
    return parts[0]


def smp_index():
    return lax.axis_index("smp")


def on_role(role, own, got):
    return jnp.where(role_index() == role, own, got)


def pack(gram):
    half = gram.shape[0] // 2
    rows = lax.broadcasted_iota(jnp.int32, (half, 2 * half), 0)
    columns = lax.broadcasted_iota(jnp.int32, (half, 2 * half), 1)
    top, bottom = gram[:half], gram[half:]
    packed = jnp.where(rows <= columns, top, pltpu.roll(bottom, half, 1))
    return packed, jnp.sum(jnp.where(columns == rows + half, bottom, 0.0), axis=0, keepdims=True)


def unpack(packed, diagonal):
    half = packed.shape[0]
    rows = lax.broadcasted_iota(jnp.int32, packed.shape, 0)
    columns = lax.broadcasted_iota(jnp.int32, packed.shape, 1)
    turned = jnp.concatenate([packed, packed], axis=0).T
    top = jnp.where(rows <= columns, packed, turned[:half])
    corner = jnp.where(columns < rows + half, pltpu.roll(packed, half, 1), turned[:half])
    corner = jnp.where(columns == rows + half, diagonal, corner)
    return jnp.concatenate([top, jnp.where(columns < half, turned[half:], corner)], axis=0)


def in_order(rows, scratch, chips, flip=0):
    size = scratch.shape[0] // chips // 2
    chip = smp_index() // 2
    for p in range(chips):
        for q in range(2):
            start = (2 * p + q) * size
            place = (chip ^ (chips - 1 - p)) * 2 + (q ^ flip)
            scratch[pl.ds(pl.multiple_of(place * size, size), size), :] = rows[start : start + size, :]
    return scratch[...]


def per_device(ensemble, voxel_factor, sample_factor, time_factor, weights):
    vox_rows, smp_rows, times = ensemble.shape
    rank = voxel_factor.shape[1]
    flat_rows = vox_rows * smp_rows
    vox_count, smp_count = lax.axis_size("vox"), lax.axis_size("smp")
    vox_total, smp_total = vox_rows * vox_count, smp_rows * smp_count
    chips, chip_rows = smp_count // 2, 2 * smp_rows
    chip_bits = bits_of(smp_count)[1:]
    vox_bits = [bit * smp_count for bit in bits_of(vox_count)]
    pieces = 4 if flat_rows % 32 == 0 else 1
    piece_rows = flat_rows // pieces

    def open_kernel(x_hbm, c_hbm, b_hbm, a_hbm, w_hbm, x, c, a, w, out, con, sems):
        copies = [pltpu.make_async_copy(c_hbm, c, sems.at[0])]
        copies += [pltpu.make_async_copy(b_hbm, out.at[pl.ds(vox_rows, smp_rows), :], sems.at[1])]
        for n in range(pieces):
            piece = pl.ds(n * piece_rows, piece_rows)
            copies.append(pltpu.make_async_copy(x_hbm.at[piece, :], x.at[piece, :], sems.at[2 + n]))
        copies.append(pltpu.make_async_copy(a_hbm, a, sems.at[2 + pieces]))
        copies.append(pltpu.make_async_copy(w_hbm, w, sems.at[3 + pieces]))
        for copy in copies:
            copy.start()
        copies[0].wait()
        copies[1].wait()
        factor = both(c[...])
        b = out[pl.ds(vox_rows, smp_rows), :]
        for n in range(pieces):
            copies[2 + n].wait()
        blocks = [x[pl.ds(j, vox_rows, stride=smp_rows), :] for j in range(smp_rows)]
        blocks = jnp.concatenate([halves(block, 1) for block in blocks], axis=0)
        made = fold(jnp.dot(blocks, factor, preferred_element_type=F32)).reshape(smp_rows, vox_rows, rank)
        con[...] = made
        total = made[0] * b[:1, :]
        for j in range(1, smp_rows):
            total = total + made[j] * b[j : j + 1, :]
        out[:vox_rows, :] = total
        copies[2 + pieces].wait()
        copies[3 + pieces].wait()

    x, c_near, a_near, w_row, opened, con = call(
        open_kernel,
        (
            near(flat_rows, times),
            near(times, rank),
            near(vox_rows, rank),
            near(1, rank),
            near(vox_rows + smp_rows, rank),
            near(smp_rows, vox_rows, rank),
        ),
        (ensemble.reshape(flat_rows, times), time_factor, sample_factor, voxel_factor, weights.reshape(1, rank)),
        2 * flat_rows * times * rank * 6,
        scratch=(pltpu.SemaphoreType.DMA((4 + pieces,)),),
        in_hbm=5,
    )

    def weigh_kernel(c, w, outer, outer_c):
        squared = dot_rows(w[...], w[...])
        outer[...] = squared
        outer_c[...] = squared * dot_rows(c[...], c[...])

    outer, outer_c = call(
        weigh_kernel, (near(rank, rank), near(rank, rank)), (c_near, w_row), 2 * rank * rank * times * 6
    )

    got = swap(opened)
    terms = opened[:vox_rows] + got[:vox_rows]
    mate_con, mate_x = swap(con), swap(x)
    packet = jnp.concatenate([terms, got[vox_rows:], opened[vox_rows:]], axis=0)
    own = jnp.concatenate([terms, opened[vox_rows:], got[vox_rows:]], axis=0)
    rows_b = own[vox_rows:]
    holder = 1
    for group in groups_of(chip_bits):
        parts = [send(packet, holder, mask) for mask in masks_of(group)[:-1]] + [own]
        terms = tree([part[:vox_rows] for part in parts])
        rows_b = jnp.concatenate([part[vox_rows:] for part in parts], axis=0)
        packet = jnp.concatenate([terms, rows_b], axis=0)
        own = swap(packet)
        holder ^= 1
    voxel_role = holder

    half, sums_rows = rank // 2, rank // 2 + chip_rows

    def voxel_kernel(terms, rows, a, w, outer_c, con, mate_con, mate_x, moved_out, chip_b, out, all_b):
        b = in_order(rows, all_b, chips, lax.axis_index("vox") // 2 & 1)
        chip_b[...] = all_b[pl.ds(pl.multiple_of(smp_index() // 2 * chip_rows, chip_rows), chip_rows), :]
        coupled = outer_c[...] * dot_rows(b, b)
        moved = a[...] - step_of(coupled) * (dot(a[...], coupled) - terms[...] * w[...])
        moved_out[...] = moved
        packed, diagonal = pack(dot_rows(moved, moved))
        out[:half, :] = packed
        core = smp_index() & 1
        for place, source in ((core, con), (1 - core, mate_con)):
            made = [jnp.sum(source[j] * moved, axis=0, keepdims=True) for j in range(smp_rows)]
            start = pl.multiple_of(half + place * smp_rows, smp_rows)
            out[pl.ds(start, smp_rows), :] = jnp.concatenate(made, axis=0)
        out[sums_rows:, :] = jnp.broadcast_to(diagonal, (8, rank))

    moved_a, chip_b, sums = call(
        only_on(voxel_role, voxel_kernel),
        (near(vox_rows, rank), near(chip_rows, rank), near(sums_rows + 8, rank)),
        (terms, rows_b, a_near, w_row, outer_c, con, mate_con, mate_x),
        2 * rank * rank * vox_rows * 12,
        scratch=(near(smp_total, rank),),
    )

    mate_moved_a = swap(moved_a)

    for group in groups_of(vox_bits[:1] + vox_bits[:0:-1]):
        sums = tree(fan(sums, holder, masks_of(group)))
        holder ^= 1
    sample_role = holder
    if sample_role != voxel_role:
        chip_b = swap(chip_b)

    def time_kernel(x, mate_x, moved, mate_moved, each):
        moved = on_role(voxel_role, moved[...], mate_moved[...])
        core = smp_index() & 1
        for place, source in ((core, x), (1 - core, mate_x)):
            for j in range(smp_rows):
                block = source[pl.ds(j, vox_rows, stride=smp_rows), :]
                each[place * smp_rows + j] = dot_rows(block, moved)

    (each,) = call(
        only_on(sample_role, time_kernel),
        (near(chip_rows, times, rank),),
        (x, mate_x, moved_a, mate_moved_a),
        4 * flat_rows * times * rank * 6,
    )

    def sample_kernel(sums, b, w, outer_c, each, gram_out, out):
        gram = unpack(sums[:half, :], sums[sums_rows : sums_rows + 1, :])
        gram_out[...] = gram
        coupled = outer_c[...] * gram
        moved = b[...] - step_of(coupled) * (dot(b[...], coupled) - sums[half:sums_rows, :] * w[...])
        out[times:, :] = moved
        total = None
        for j in range(chip_rows):
            made = each[j] * moved[j : j + 1, :]
            total = made if total is None else total + made
        out[:times, :] = total

    gram_a, payload = call(
        only_on(sample_role, sample_kernel),
        (near(rank, rank), near(times + chip_rows, rank)),
        (sums, chip_b, w_row, outer_c, each),
        2 * rank * rank * chip_rows * 6,
    )
    mate_gram_a = swap(gram_a)

    def scale_kernel(gram, mate_gram, moved, mate_moved, outer, result, scales_out, weighed):
        gram = on_role(sample_role, gram[...], mate_gram[...])
        scales = jnp.sqrt(diagonal_row(gram) / vox_total + 1e-06)
        scales_out[...] = scales
        result[...] = on_role(voxel_role, moved[...], mate_moved[...]) / scales
        weighed[...] = outer[...] * gram

    voxel_result, scales_a, weighed = call(
        scale_kernel,
        (far(vox_rows, rank), near(1, rank), near(rank, rank)),
        (gram_a, mate_gram_a, moved_a, mate_moved_a, outer),
        vox_rows * rank * 8,
    )

    terms, rows_b, rows_role = payload[:times], payload[times:], holder
    smp_mask = sum(chip_bits)
    for group in groups_of(chip_bits + vox_bits):
        masks = masks_of(group)
        if any(mask & smp_mask for mask in masks):
            packet = payload if rows_b.shape[0] == chip_rows else jnp.concatenate([terms, rows_b], axis=0)
            parts = fan(packet, holder, masks)
            gathered = [i for i, mask in enumerate(masks) if not mask & ~smp_mask]
            rows = rows_b.shape[0]

            def gather_kernel(*refs, gathered=gathered, rows=rows):
                parts, (terms, rows_out) = refs[-3::-1], refs[-2:]
                terms[...] = tree([part[:times, :] for part in parts])
                for p, i in enumerate(gathered):
                    rows_out[p * rows : (p + 1) * rows, :] = parts[i][times:, :]

            terms, rows_b = call(
                gather_kernel,
                (near(times, rank), near(len(gathered) * rows, rank)),
                parts[::-1],
                len(masks) * times * rank,
            )
            rows_role = holder ^ 1
        else:
            terms = tree(fan(terms, holder, masks))
        holder ^= 1
    last_role = holder
    mate_rows_b = swap(rows_b)

    def ready_kernel(rows, mate_rows, c, w, weighed, scales_a, b_out, base, gain, scale, all_b):
        b = in_order(on_role(rows_role, rows[...], mate_rows[...]), all_b, chips)
        coupled = weighed[...] * dot_rows(b, b)
        step = step_of(coupled)
        base[...] = c[...] - step * dot(c[...], coupled)
        gain[...] = step * w[...]
        scales_b = jnp.sqrt(jnp.sum(b * b, axis=0, keepdims=True) / smp_total + 1e-06)
        scale[...] = w[...] * scales_a[...] * scales_b
        b_out[...] = all_b[pl.ds(pl.multiple_of(smp_index() * smp_rows, smp_rows), smp_rows), :] / scales_b

    sample_result, base, gain, scale = call(
        ready_kernel,
        (far(smp_rows, rank), near(times, rank), near(1, rank), near(1, rank)),
        (rows_b, mate_rows_b, c_near, w_row, weighed, scales_a),
        2 * rank * rank * times * 4,
        scratch=(near(smp_total, rank),),
    )
    terms, base, gain, scale, voxel_result, sample_result = lax.optimization_barrier(
        (terms, base, gain, scale, voxel_result, sample_result)
    )
    mate_terms = swap(terms)

    def last_kernel(terms, mate_terms, base, gain, scale, c_out, w_out):
        moved = base[...] + on_role(last_role, terms[...], mate_terms[...]) * gain[...]
        scales_c = jnp.sqrt(jnp.sum(moved * moved, axis=0, keepdims=True) / times + 1e-06)
        c_out[...] = moved / scales_c
        w_out[...] = scale[...] * scales_c

    time_result, scale_result = call(
        last_kernel,
        (far(times, rank), far(1, rank)),
        (terms, mate_terms, base, gain, scale),
        rank * times * 8,
    )
    return voxel_result, sample_result, time_result, scale_result.reshape(rank)


def solution(mesh):
    return jax.shard_map(
        per_device,
        mesh=mesh,
        in_specs=(P("vox", "smp", None), P("vox", None), P("smp", None), P(), P()),
        out_specs=(P("vox", None), P("smp", None), P(), P()),
        check_vma=False,
    )
```

```python
import jax
import jax.numpy as jnp
from jax import lax
from jax.experimental import pallas as pl
from jax.experimental.pallas import tpu as pltpu
from jax.sharding import PartitionSpec as P

F32 = jnp.float32
BF16 = jnp.bfloat16
VMEM_LIMIT = 12 * 1024 * 1024
ALL = ("vox", "smp")


def halves(a, axis):
    high = a.astype(BF16)
    return jnp.concatenate([high, (a - high.astype(F32)).astype(BF16)], axis=axis)


def both(b):
    parts = halves(b, 1)
    return jnp.concatenate([parts, parts], axis=0)


def fold(product):
    width = product.shape[1] // 2
    return product[:, :width] + product[:, width:]


def dot(a, b):
    return fold(jnp.dot(halves(a, 1), both(b), preferred_element_type=F32))


def dot_rows(a, b):
    return fold(lax.dot_general(halves(a, 0), both(b), (((0,), (0,)), ((), ())), preferred_element_type=F32))


def step_of(coupled):
    sums = jnp.sum(jnp.abs(coupled), axis=0, keepdims=True)
    return 1.0 / jnp.max(sums, axis=1, keepdims=True)


def diagonal_row(gram):
    rows = lax.broadcasted_iota(jnp.int32, gram.shape, 0)
    columns = lax.broadcasted_iota(jnp.int32, gram.shape, 1)
    return jnp.sum(jnp.where(rows == columns, gram, 0.0), axis=0, keepdims=True)


def role_index():
    return (smp_index() ^ lax.axis_index("vox") // 2) & 1


def only_on(role, kernel):
    def run(*refs):
        pl.when(role_index() == role)(lambda: kernel(*refs))

    return run


def call(kernel, outs, operands, flops, scratch=(), in_hbm=0):
    spaces = [pltpu.HBM if i < in_hbm else pltpu.VMEM for i in range(len(operands))]
    placed = [pltpu.with_memory_space_constraint(x, space) for x, space in zip(operands, spaces)]
    specs = [pl.BlockSpec(memory_space=space) for space in spaces]
    return pl.pallas_call(
        kernel,
        out_shape=outs,
        in_specs=specs,
        out_specs=[pl.BlockSpec(memory_space=pltpu.VMEM)] * len(outs),
        scratch_shapes=list(scratch),
        compiler_params=pltpu.CompilerParams(vmem_limit_bytes=VMEM_LIMIT),
        cost_estimate=pl.CostEstimate(flops=flops, bytes_accessed=1 << 16, transcendentals=0),
    )(*placed)


def near(*shape):
    return pltpu.VMEM(shape, F32)


def far(*shape):
    return jax.ShapeDtypeStruct(shape, F32)


def bits_of(count):
    if count & (count - 1):
        raise ValueError("axis size")
    return [1 << b for b in range(count.bit_length() - 1)]


def groups_of(bits, size=2):
    return [bits[i : i + size] for i in range(0, len(bits), size)]


def masks_of(group):
    masks = [0]
    for bit in group:
        masks = [mask | bit for mask in masks] + masks
    return masks


def swap(values):
    return lax.ppermute(values, ALL, [(i, i ^ 1) for i in range(lax.axis_size(ALL))])


def send(values, holder, mask):
    smp_count, count = lax.axis_size("smp"), lax.axis_size(ALL)
    role = lambda i: (i ^ i // (2 * smp_count)) & 1
    pairs = []
    for i in range(count):
        target = i ^ mask if role(i) == holder else i
        pairs.append((i, target ^ 1 if role(target) == role(i) else target))
    return lax.ppermute(values, ALL, pairs)


def fan(values, holder, masks):
    sent = [send(values, holder, mask) if mask else swap(values) for mask in reversed(masks)]
    return sent[::-1]


def tree(parts):
    parts = parts[::-1]
    while len(parts) > 1:
        parts = [a + b for a, b in zip(parts[::2], parts[1::2])]
    return parts[0]


def smp_index():
    return lax.axis_index("smp")


def on_role(role, own, got):
    return jnp.where(role_index() == role, own, got)


def pack(gram):
    half = gram.shape[0] // 2
    rows = lax.broadcasted_iota(jnp.int32, (half, 2 * half), 0)
    columns = lax.broadcasted_iota(jnp.int32, (half, 2 * half), 1)
    top, bottom = gram[:half], gram[half:]
    packed = jnp.where(rows <= columns, top, pltpu.roll(bottom, half, 1))
    return packed, jnp.sum(jnp.where(columns == rows + half, bottom, 0.0), axis=0, keepdims=True)


def unpack(packed, diagonal):
    half = packed.shape[0]
    rows = lax.broadcasted_iota(jnp.int32, packed.shape, 0)
    columns = lax.broadcasted_iota(jnp.int32, packed.shape, 1)
    turned = jnp.concatenate([packed, packed], axis=0).T
    top = jnp.where(rows <= columns, packed, turned[:half])
    corner = jnp.where(columns < rows + half, pltpu.roll(packed, half, 1), turned[:half])
    corner = jnp.where(columns == rows + half, diagonal, corner)
    return jnp.concatenate([top, jnp.where(columns < half, turned[half:], corner)], axis=0)


def in_order(rows, scratch, chips, flip=0):
    size = scratch.shape[0] // chips // 2
    chip = smp_index() // 2
    for p in range(chips):
        for q in range(2):
            start = (2 * p + q) * size
            place = (chip ^ (chips - 1 - p)) * 2 + (q ^ flip)
            scratch[pl.ds(pl.multiple_of(place * size, size), size), :] = rows[start : start + size, :]
    return scratch[...]


def per_device(ensemble, voxel_factor, sample_factor, time_factor, weights):
    vox_rows, smp_rows, times = ensemble.shape
    rank = voxel_factor.shape[1]
    flat_rows = vox_rows * smp_rows
    vox_count, smp_count = lax.axis_size("vox"), lax.axis_size("smp")
    vox_total, smp_total = vox_rows * vox_count, smp_rows * smp_count
    chips, chip_rows = smp_count // 2, 2 * smp_rows
    chip_bits = bits_of(smp_count)[1:]
    vox_bits = [bit * smp_count for bit in bits_of(vox_count)]
    pieces = 1
    piece_rows = flat_rows // pieces

    def open_kernel(x_hbm, c_hbm, b_hbm, a_hbm, w_hbm, x, c, a, w, out, con, sems):
        copies = [pltpu.make_async_copy(c_hbm, c, sems.at[0])]
        copies += [pltpu.make_async_copy(b_hbm, out.at[pl.ds(vox_rows, smp_rows), :], sems.at[1])]
        for n in range(pieces):
            piece = pl.ds(n * piece_rows, piece_rows)
            copies.append(pltpu.make_async_copy(x_hbm.at[piece, :], x.at[piece, :], sems.at[2 + n]))
        copies.append(pltpu.make_async_copy(a_hbm, a, sems.at[2 + pieces]))
        copies.append(pltpu.make_async_copy(w_hbm, w, sems.at[3 + pieces]))
        for copy in copies:
            copy.start()
        copies[0].wait()
        copies[1].wait()
        factor = both(c[...])
        b = out[pl.ds(vox_rows, smp_rows), :]
        for n in range(pieces):
            copies[2 + n].wait()
        blocks = [x[pl.ds(j, vox_rows, stride=smp_rows), :] for j in range(smp_rows)]
        blocks = jnp.concatenate([halves(block, 1) for block in blocks], axis=0)
        made = fold(jnp.dot(blocks, factor, preferred_element_type=F32)).reshape(smp_rows, vox_rows, rank)
        con[...] = made
        total = made[0] * b[:1, :]
        for j in range(1, smp_rows):
            total = total + made[j] * b[j : j + 1, :]
        out[:vox_rows, :] = total
        copies[2 + pieces].wait()
        copies[3 + pieces].wait()

    x, c_near, a_near, w_row, opened, con = call(
        open_kernel,
        (
            near(flat_rows, times),
            near(times, rank),
            near(vox_rows, rank),
            near(1, rank),
            near(vox_rows + smp_rows, rank),
            near(smp_rows, vox_rows, rank),
        ),
        (ensemble.reshape(flat_rows, times), time_factor, sample_factor, voxel_factor, weights.reshape(1, rank)),
        2 * flat_rows * times * rank * 6,
        scratch=(pltpu.SemaphoreType.DMA((4 + pieces,)),),
        in_hbm=5,
    )

    def weigh_kernel(c, w, outer, outer_c):
        squared = dot_rows(w[...], w[...])
        outer[...] = squared
        outer_c[...] = squared * dot_rows(c[...], c[...])

    outer, outer_c = call(
        weigh_kernel, (near(rank, rank), near(rank, rank)), (c_near, w_row), 2 * rank * rank * times * 6
    )

    got = swap(opened)
    terms = opened[:vox_rows] + got[:vox_rows]
    mate_con, mate_x = swap(con), swap(x)
    packet = jnp.concatenate([terms, opened[vox_rows:], got[vox_rows:]], axis=0)
    own = jnp.concatenate([terms, got[vox_rows:], opened[vox_rows:]], axis=0)
    rows_b = own[vox_rows:]
    holder = 0
    for group in groups_of(chip_bits):
        parts = [send(packet, holder, mask) for mask in masks_of(group)[:-1]] + [own]
        terms = tree([part[:vox_rows] for part in parts])
        rows_b = jnp.concatenate([part[vox_rows:] for part in parts], axis=0)
        packet = jnp.concatenate([terms, rows_b], axis=0)
        own = swap(packet)
        holder ^= 1
    voxel_role = holder

    half, sums_rows = rank // 2, rank // 2 + chip_rows

    def voxel_kernel(terms, rows, a, w, outer_c, con, mate_con, mate_x, moved_out, chip_b, out, all_b):
        b = in_order(rows, all_b, chips, lax.axis_index("vox") // 2 & 1)
        chip_b[...] = all_b[pl.ds(pl.multiple_of(smp_index() // 2 * chip_rows, chip_rows), chip_rows), :]
        coupled = outer_c[...] * dot_rows(b, b)
        moved = a[...] - step_of(coupled) * (dot(a[...], coupled) - terms[...] * w[...])
        moved_out[...] = moved
        packed, diagonal = pack(dot_rows(moved, moved))
        out[:half, :] = packed
        core = smp_index() & 1
        for place, source in ((core, con), (1 - core, mate_con)):
            made = [jnp.sum(source[j] * moved, axis=0, keepdims=True) for j in range(smp_rows)]
            start = pl.multiple_of(half + place * smp_rows, smp_rows)
            out[pl.ds(start, smp_rows), :] = jnp.concatenate(made, axis=0)
        out[sums_rows:, :] = jnp.broadcast_to(diagonal, (8, rank))

    moved_a, chip_b, sums = call(
        only_on(voxel_role, voxel_kernel),
        (near(vox_rows, rank), near(chip_rows, rank), near(sums_rows + 8, rank)),
        (terms, rows_b, a_near, w_row, outer_c, con, mate_con, mate_x),
        2 * rank * rank * vox_rows * 12,
        scratch=(near(smp_total, rank),),
    )

    mate_moved_a = swap(moved_a)

    for group in groups_of(vox_bits[:1] + vox_bits[:0:-1]):
        sums = tree(fan(sums, holder, masks_of(group)))
        holder ^= 1
    sample_role = holder
    if sample_role != voxel_role:
        chip_b = swap(chip_b)

    def time_kernel(x, mate_x, moved, mate_moved, each):
        moved = on_role(voxel_role, moved[...], mate_moved[...])
        core = smp_index() & 1
        for place, source in ((core, x), (1 - core, mate_x)):
            for j in range(smp_rows):
                block = source[pl.ds(j, vox_rows, stride=smp_rows), :]
                each[place * smp_rows + j] = dot_rows(block, moved)

    (each,) = call(
        only_on(sample_role, time_kernel),
        (near(chip_rows, times, rank),),
        (x, mate_x, moved_a, mate_moved_a),
        4 * flat_rows * times * rank * 6,
    )

    def sample_kernel(sums, b, w, outer_c, each, gram_out, out):
        gram = unpack(sums[:half, :], sums[sums_rows : sums_rows + 1, :])
        gram_out[...] = gram
        coupled = outer_c[...] * gram
        moved = b[...] - step_of(coupled) * (dot(b[...], coupled) - sums[half:sums_rows, :] * w[...])
        out[times:, :] = moved
        total = None
        for j in range(chip_rows):
            made = each[j] * moved[j : j + 1, :]
            total = made if total is None else total + made
        out[:times, :] = total

    gram_a, payload = call(
        only_on(sample_role, sample_kernel),
        (near(rank, rank), near(times + chip_rows, rank)),
        (sums, chip_b, w_row, outer_c, each),
        2 * rank * rank * chip_rows * 6,
    )
    mate_gram_a = swap(gram_a)

    def scale_kernel(gram, mate_gram, moved, mate_moved, outer, result, scales_out, weighed):
        gram = on_role(sample_role, gram[...], mate_gram[...])
        scales = jnp.sqrt(diagonal_row(gram) / vox_total + 1e-06)
        scales_out[...] = scales
        result[...] = on_role(voxel_role, moved[...], mate_moved[...]) / scales
        weighed[...] = outer[...] * gram

    voxel_result, scales_a, weighed = call(
        scale_kernel,
        (far(vox_rows, rank), near(1, rank), near(rank, rank)),
        (gram_a, mate_gram_a, moved_a, mate_moved_a, outer),
        vox_rows * rank * 8,
    )

    terms, rows_b, rows_role = payload[:times], payload[times:], holder
    smp_mask = sum(chip_bits)
    for group in groups_of(chip_bits + vox_bits[1:2] + vox_bits[:1] + vox_bits[2:]):
        masks = masks_of(group)
        if any(mask & smp_mask for mask in masks):
            packet = payload if rows_b.shape[0] == chip_rows else jnp.concatenate([terms, rows_b], axis=0)
            parts = fan(packet, holder, masks)
            gathered = [i for i, mask in enumerate(masks) if not mask & ~smp_mask]
            rows = rows_b.shape[0]

            def gather_kernel(*refs, gathered=gathered, rows=rows):
                parts, (terms, rows_out) = refs[-3::-1], refs[-2:]
                terms[...] = tree([part[:times, :] for part in parts])
                for p, i in enumerate(gathered):
                    rows_out[p * rows : (p + 1) * rows, :] = parts[i][times:, :]

            terms, rows_b = call(
                gather_kernel,
                (near(times, rank), near(len(gathered) * rows, rank)),
                parts[::-1],
                len(masks) * times * rank,
            )
            rows_role = holder ^ 1
        else:
            terms = tree(fan(terms, holder, masks))
        holder ^= 1
    last_role = holder
    mate_rows_b = swap(rows_b)

    def ready_kernel(rows, mate_rows, c, w, weighed, scales_a, b_out, base, gain, scale, all_b):
        b = in_order(on_role(rows_role, rows[...], mate_rows[...]), all_b, chips)
        coupled = weighed[...] * dot_rows(b, b)
        step = step_of(coupled)
        base[...] = c[...] - step * dot(c[...], coupled)
        gain[...] = step * w[...]
        scales_b = jnp.sqrt(jnp.sum(b * b, axis=0, keepdims=True) / smp_total + 1e-06)
        scale[...] = w[...] * scales_a[...] * scales_b
        b_out[...] = all_b[pl.ds(pl.multiple_of(smp_index() * smp_rows, smp_rows), smp_rows), :] / scales_b

    sample_result, base, gain, scale = call(
        ready_kernel,
        (far(smp_rows, rank), near(times, rank), near(1, rank), near(1, rank)),
        (rows_b, mate_rows_b, c_near, w_row, weighed, scales_a),
        2 * rank * rank * times * 4,
        scratch=(near(smp_total, rank),),
    )
    terms, base, gain, scale, voxel_result, sample_result = lax.optimization_barrier(
        (terms, base, gain, scale, voxel_result, sample_result)
    )
    mate_terms = swap(terms)

    def last_kernel(terms, mate_terms, base, gain, scale, c_out, w_out):
        moved = base[...] + on_role(last_role, terms[...], mate_terms[...]) * gain[...]
        scales_c = jnp.sqrt(jnp.sum(moved * moved, axis=0, keepdims=True) / times + 1e-06)
        c_out[...] = moved / scales_c
        w_out[...] = scale[...] * scales_c

    time_result, scale_result = call(
        last_kernel,
        (far(times, rank), far(1, rank)),
        (terms, mate_terms, base, gain, scale),
        rank * times * 8,
    )
    return voxel_result, sample_result, time_result, scale_result.reshape(rank)


def solution(mesh):
    return jax.shard_map(
        per_device,
        mesh=mesh,
        in_specs=(P("vox", "smp", None), P("vox", None), P("smp", None), P(), P()),
        out_specs=(P("vox", None), P("smp", None), P(), P()),
        check_vma=False,
    )
```

```python
import jax
import jax.numpy as jnp
from jax import lax
from jax.experimental import pallas as pl
from jax.experimental.pallas import tpu as pltpu
from jax.sharding import PartitionSpec as P

F32 = jnp.float32
BF16 = jnp.bfloat16
VMEM_LIMIT = 12 * 1024 * 1024
ALL = ("vox", "smp")


def halves(a, axis):
    high = a.astype(BF16)
    return jnp.concatenate([high, (a - high.astype(F32)).astype(BF16)], axis=axis)


def both(b):
    parts = halves(b, 1)
    return jnp.concatenate([parts, parts], axis=0)


def fold(product):
    width = product.shape[1] // 2
    return product[:, :width] + product[:, width:]


def dot(a, b):
    return fold(jnp.dot(halves(a, 1), both(b), preferred_element_type=F32))


def dot_rows(a, b):
    return fold(lax.dot_general(halves(a, 0), both(b), (((0,), (0,)), ((), ())), preferred_element_type=F32))


def step_of(coupled):
    sums = jnp.sum(jnp.abs(coupled), axis=0, keepdims=True)
    return 1.0 / jnp.max(sums, axis=1, keepdims=True)


def diagonal_row(gram):
    rows = lax.broadcasted_iota(jnp.int32, gram.shape, 0)
    columns = lax.broadcasted_iota(jnp.int32, gram.shape, 1)
    return jnp.sum(jnp.where(rows == columns, gram, 0.0), axis=0, keepdims=True)


def role_index():
    return (smp_index() ^ lax.axis_index("vox") // 2) & 1


def only_on(role, kernel):
    def run(*refs):
        pl.when(role_index() == role)(lambda: kernel(*refs))

    return run


def call(kernel, outs, operands, flops, scratch=(), in_hbm=0):
    spaces = [pltpu.HBM if i < in_hbm else pltpu.VMEM for i in range(len(operands))]
    placed = [pltpu.with_memory_space_constraint(x, space) for x, space in zip(operands, spaces)]
    specs = [pl.BlockSpec(memory_space=space) for space in spaces]
    return pl.pallas_call(
        kernel,
        out_shape=outs,
        in_specs=specs,
        out_specs=[pl.BlockSpec(memory_space=pltpu.VMEM)] * len(outs),
        scratch_shapes=list(scratch),
        compiler_params=pltpu.CompilerParams(vmem_limit_bytes=VMEM_LIMIT),
        cost_estimate=pl.CostEstimate(flops=flops, bytes_accessed=1 << 16, transcendentals=0),
    )(*placed)


def near(*shape):
    return pltpu.VMEM(shape, F32)


def far(*shape):
    return jax.ShapeDtypeStruct(shape, F32)


def bits_of(count):
    if count & (count - 1):
        raise ValueError("axis size")
    return [1 << b for b in range(count.bit_length() - 1)]


def groups_of(bits, size=2):
    return [bits[i : i + size] for i in range(0, len(bits), size)]


def masks_of(group):
    masks = [0]
    for bit in group:
        masks = [mask | bit for mask in masks] + masks
    return masks


def swap(values):
    return lax.ppermute(values, ALL, [(i, i ^ 1) for i in range(lax.axis_size(ALL))])


def send(values, holder, mask):
    smp_count, count = lax.axis_size("smp"), lax.axis_size(ALL)
    role = lambda i: (i ^ i // (2 * smp_count)) & 1
    pairs = []
    for i in range(count):
        target = i ^ mask if role(i) == holder else i
        pairs.append((i, target ^ 1 if role(target) == role(i) else target))
    return lax.ppermute(values, ALL, pairs)


def fan(values, holder, masks):
    sent = [send(values, holder, mask) if mask else swap(values) for mask in reversed(masks)]
    return sent[::-1]


def tree(parts):
    parts = parts[::-1]
    while len(parts) > 1:
        parts = [a + b for a, b in zip(parts[::2], parts[1::2])]
    return parts[0]


def smp_index():
    return lax.axis_index("smp")


def on_role(role, own, got):
    return jnp.where(role_index() == role, own, got)


def pack(gram):
    half = gram.shape[0] // 2
    rows = lax.broadcasted_iota(jnp.int32, (half, 2 * half), 0)
    columns = lax.broadcasted_iota(jnp.int32, (half, 2 * half), 1)
    top, bottom = gram[:half], gram[half:]
    packed = jnp.where(rows <= columns, top, pltpu.roll(bottom, half, 1))
    return packed, jnp.sum(jnp.where(columns == rows + half, bottom, 0.0), axis=0, keepdims=True)


def unpack(packed, diagonal):
    half = packed.shape[0]
    rows = lax.broadcasted_iota(jnp.int32, packed.shape, 0)
    columns = lax.broadcasted_iota(jnp.int32, packed.shape, 1)
    turned = jnp.concatenate([packed, packed], axis=0).T
    top = jnp.where(rows <= columns, packed, turned[:half])
    corner = jnp.where(columns < rows + half, pltpu.roll(packed, half, 1), turned[:half])
    corner = jnp.where(columns == rows + half, diagonal, corner)
    return jnp.concatenate([top, jnp.where(columns < half, turned[half:], corner)], axis=0)


def in_order(rows, scratch, chips, flip=0):
    size = scratch.shape[0] // chips // 2
    chip = smp_index() // 2
    for p in range(chips):
        for q in range(2):
            start = (2 * p + q) * size
            place = (chip ^ (chips - 1 - p)) * 2 + (q ^ flip)
            scratch[pl.ds(pl.multiple_of(place * size, size), size), :] = rows[start : start + size, :]
    return scratch[...]


def per_device(ensemble, voxel_factor, sample_factor, time_factor, weights):
    vox_rows, smp_rows, times = ensemble.shape
    rank = voxel_factor.shape[1]
    flat_rows = vox_rows * smp_rows
    vox_count, smp_count = lax.axis_size("vox"), lax.axis_size("smp")
    vox_total, smp_total = vox_rows * vox_count, smp_rows * smp_count
    chips, chip_rows = smp_count // 2, 2 * smp_rows
    chip_bits = bits_of(smp_count)[1:]
    vox_bits = [bit * smp_count for bit in bits_of(vox_count)]
    pieces = 1
    piece_rows = flat_rows // pieces

    def open_kernel(x_hbm, c_hbm, b_hbm, a_hbm, w_hbm, x, c, a, w, out, con, sems):
        copies = [pltpu.make_async_copy(c_hbm, c, sems.at[0])]
        copies += [pltpu.make_async_copy(b_hbm, out.at[pl.ds(vox_rows, smp_rows), :], sems.at[1])]
        for n in range(pieces):
            piece = pl.ds(n * piece_rows, piece_rows)
            copies.append(pltpu.make_async_copy(x_hbm.at[piece, :], x.at[piece, :], sems.at[2 + n]))
        copies.append(pltpu.make_async_copy(a_hbm, a, sems.at[2 + pieces]))
        copies.append(pltpu.make_async_copy(w_hbm, w, sems.at[3 + pieces]))
        for copy in copies:
            copy.start()
        copies[0].wait()
        copies[1].wait()
        factor = both(c[...])
        b = out[pl.ds(vox_rows, smp_rows), :]
        for n in range(pieces):
            copies[2 + n].wait()
        blocks = [x[pl.ds(j, vox_rows, stride=smp_rows), :] for j in range(smp_rows)]
        blocks = jnp.concatenate([halves(block, 1) for block in blocks], axis=0)
        made = fold(jnp.dot(blocks, factor, preferred_element_type=F32)).reshape(smp_rows, vox_rows, rank)
        con[...] = made
        total = made[0] * b[:1, :]
        for j in range(1, smp_rows):
            total = total + made[j] * b[j : j + 1, :]
        out[:vox_rows, :] = total
        copies[2 + pieces].wait()
        copies[3 + pieces].wait()

    x, c_near, a_near, w_row, opened, con = call(
        open_kernel,
        (
            near(flat_rows, times),
            near(times, rank),
            near(vox_rows, rank),
            near(1, rank),
            near(vox_rows + smp_rows, rank),
            near(smp_rows, vox_rows, rank),
        ),
        (ensemble.reshape(flat_rows, times), time_factor, sample_factor, voxel_factor, weights.reshape(1, rank)),
        2 * flat_rows * times * rank * 6,
        scratch=(pltpu.SemaphoreType.DMA((4 + pieces,)),),
        in_hbm=5,
    )

    def weigh_kernel(c, w, outer, outer_c):
        squared = dot_rows(w[...], w[...])
        outer[...] = squared
        outer_c[...] = squared * dot_rows(c[...], c[...])

    outer, outer_c = call(
        weigh_kernel, (near(rank, rank), near(rank, rank)), (c_near, w_row), 2 * rank * rank * times * 6
    )

    got = swap(opened)
    terms = opened[:vox_rows] + got[:vox_rows]
    mate_con, mate_x = swap(con), swap(x)
    packet = jnp.concatenate([terms, got[vox_rows:], opened[vox_rows:]], axis=0)
    own = jnp.concatenate([terms, opened[vox_rows:], got[vox_rows:]], axis=0)
    rows_b = own[vox_rows:]
    holder = 1
    for group in groups_of(chip_bits):
        parts = [send(packet, holder, mask) for mask in masks_of(group)[:-1]] + [own]
        terms = tree([part[:vox_rows] for part in parts])
        rows_b = jnp.concatenate([part[vox_rows:] for part in parts], axis=0)
        packet = jnp.concatenate([terms, rows_b], axis=0)
        own = swap(packet)
        holder ^= 1
    voxel_role = holder

    half, sums_rows = rank // 2, rank // 2 + chip_rows

    def voxel_kernel(terms, rows, a, w, outer_c, con, mate_con, mate_x, moved_out, chip_b, out, all_b):
        b = in_order(rows, all_b, chips, lax.axis_index("vox") // 2 & 1)
        chip_b[...] = all_b[pl.ds(pl.multiple_of(smp_index() // 2 * chip_rows, chip_rows), chip_rows), :]
        coupled = outer_c[...] * dot_rows(b, b)
        moved = a[...] - step_of(coupled) * (dot(a[...], coupled) - terms[...] * w[...])
        moved_out[...] = moved
        packed, diagonal = pack(dot_rows(moved, moved))
        out[:half, :] = packed
        core = smp_index() & 1
        for place, source in ((core, con), (1 - core, mate_con)):
            made = [jnp.sum(source[j] * moved, axis=0, keepdims=True) for j in range(smp_rows)]
            start = pl.multiple_of(half + place * smp_rows, smp_rows)
            out[pl.ds(start, smp_rows), :] = jnp.concatenate(made, axis=0)
        out[sums_rows:, :] = jnp.broadcast_to(diagonal, (8, rank))

    moved_a, chip_b, sums = call(
        only_on(voxel_role, voxel_kernel),
        (near(vox_rows, rank), near(chip_rows, rank), near(sums_rows + 8, rank)),
        (terms, rows_b, a_near, w_row, outer_c, con, mate_con, mate_x),
        2 * rank * rank * vox_rows * 12,
        scratch=(near(smp_total, rank),),
    )

    mate_moved_a = swap(moved_a)

    for group in groups_of(vox_bits[1:] + vox_bits[:1]):
        sums = tree(fan(sums, holder, masks_of(group)))
        holder ^= 1
    sample_role = holder
    if sample_role != voxel_role:
        chip_b = swap(chip_b)

    def time_kernel(x, mate_x, moved, mate_moved, each):
        moved = on_role(voxel_role, moved[...], mate_moved[...])
        core = smp_index() & 1
        for place, source in ((core, x), (1 - core, mate_x)):
            for j in range(smp_rows):
                block = source[pl.ds(j, vox_rows, stride=smp_rows), :]
                each[place * smp_rows + j] = dot_rows(block, moved)

    (each,) = call(
        only_on(sample_role, time_kernel),
        (near(chip_rows, times, rank),),
        (x, mate_x, moved_a, mate_moved_a),
        4 * flat_rows * times * rank * 6,
    )

    def sample_kernel(sums, b, w, outer_c, each, gram_out, out):
        gram = unpack(sums[:half, :], sums[sums_rows : sums_rows + 1, :])
        gram_out[...] = gram
        coupled = outer_c[...] * gram
        moved = b[...] - step_of(coupled) * (dot(b[...], coupled) - sums[half:sums_rows, :] * w[...])
        out[times:, :] = moved
        total = None
        for j in range(chip_rows):
            made = each[j] * moved[j : j + 1, :]
            total = made if total is None else total + made
        out[:times, :] = total

    gram_a, payload = call(
        only_on(sample_role, sample_kernel),
        (near(rank, rank), near(times + chip_rows, rank)),
        (sums, chip_b, w_row, outer_c, each),
        2 * rank * rank * chip_rows * 6,
    )
    mate_gram_a = swap(gram_a)

    def scale_kernel(gram, mate_gram, moved, mate_moved, outer, result, scales_out, weighed):
        gram = on_role(sample_role, gram[...], mate_gram[...])
        scales = jnp.sqrt(diagonal_row(gram) / vox_total + 1e-06)
        scales_out[...] = scales
        result[...] = on_role(voxel_role, moved[...], mate_moved[...]) / scales
        weighed[...] = outer[...] * gram

    voxel_result, scales_a, weighed = call(
        scale_kernel,
        (far(vox_rows, rank), near(1, rank), near(rank, rank)),
        (gram_a, mate_gram_a, moved_a, mate_moved_a, outer),
        vox_rows * rank * 8,
    )

    terms, rows_b, rows_role = payload[:times], payload[times:], holder
    smp_mask = sum(chip_bits)
    for group in groups_of(chip_bits + vox_bits[1:2] + vox_bits[:1] + vox_bits[2:]):
        masks = masks_of(group)
        if any(mask & smp_mask for mask in masks):
            packet = payload if rows_b.shape[0] == chip_rows else jnp.concatenate([terms, rows_b], axis=0)
            parts = fan(packet, holder, masks)
            gathered = [i for i, mask in enumerate(masks) if not mask & ~smp_mask]
            rows = rows_b.shape[0]

            def gather_kernel(*refs, gathered=gathered, rows=rows):
                parts, (terms, rows_out) = refs[-3::-1], refs[-2:]
                terms[...] = tree([part[:times, :] for part in parts])
                for p, i in enumerate(gathered):
                    rows_out[p * rows : (p + 1) * rows, :] = parts[i][times:, :]

            terms, rows_b = call(
                gather_kernel,
                (near(times, rank), near(len(gathered) * rows, rank)),
                parts[::-1],
                len(masks) * times * rank,
            )
            rows_role = holder ^ 1
        else:
            terms = tree(fan(terms, holder, masks))
        holder ^= 1
    last_role = holder
    mate_rows_b = swap(rows_b)

    def ready_kernel(rows, mate_rows, c, w, weighed, scales_a, b_out, base, gain, scale, all_b):
        b = in_order(on_role(rows_role, rows[...], mate_rows[...]), all_b, chips)
        coupled = weighed[...] * dot_rows(b, b)
        step = step_of(coupled)
        base[...] = c[...] - step * dot(c[...], coupled)
        gain[...] = step * w[...]
        scales_b = jnp.sqrt(jnp.sum(b * b, axis=0, keepdims=True) / smp_total + 1e-06)
        scale[...] = w[...] * scales_a[...] * scales_b
        b_out[...] = all_b[pl.ds(pl.multiple_of(smp_index() * smp_rows, smp_rows), smp_rows), :] / scales_b

    sample_result, base, gain, scale = call(
        ready_kernel,
        (far(smp_rows, rank), near(times, rank), near(1, rank), near(1, rank)),
        (rows_b, mate_rows_b, c_near, w_row, weighed, scales_a),
        2 * rank * rank * times * 4,
        scratch=(near(smp_total, rank),),
    )
    terms, base, gain, scale, voxel_result, sample_result = lax.optimization_barrier(
        (terms, base, gain, scale, voxel_result, sample_result)
    )
    mate_terms = swap(terms)

    def last_kernel(terms, mate_terms, base, gain, scale, c_out, w_out):
        moved = base[...] + on_role(last_role, terms[...], mate_terms[...]) * gain[...]
        scales_c = jnp.sqrt(jnp.sum(moved * moved, axis=0, keepdims=True) / times + 1e-06)
        c_out[...] = moved / scales_c
        w_out[...] = scale[...] * scales_c

    time_result, scale_result = call(
        last_kernel,
        (far(times, rank), far(1, rank)),
        (terms, mate_terms, base, gain, scale),
        rank * times * 8,
    )
    return voxel_result, sample_result, time_result, scale_result.reshape(rank)


def solution(mesh):
    return jax.shard_map(
        per_device,
        mesh=mesh,
        in_specs=(P("vox", "smp", None), P("vox", None), P("smp", None), P(), P()),
        out_specs=(P("vox", None), P("smp", None), P(), P()),
        check_vma=False,
    )
```

```python
import jax
import jax.numpy as jnp
from jax import lax
from jax.experimental import pallas as pl
from jax.experimental.pallas import tpu as pltpu
from jax.sharding import PartitionSpec as P

F32 = jnp.float32
BF16 = jnp.bfloat16
VMEM_LIMIT = 12 * 1024 * 1024
ALL = ("vox", "smp")


def halves(a, axis):
    high = a.astype(BF16)
    return jnp.concatenate([high, (a - high.astype(F32)).astype(BF16)], axis=axis)


def both(b):
    parts = halves(b, 1)
    return jnp.concatenate([parts, parts], axis=0)


def fold(product):
    width = product.shape[1] // 2
    return product[:, :width] + product[:, width:]


def dot(a, b):
    return fold(jnp.dot(halves(a, 1), both(b), preferred_element_type=F32))


def dot_rows(a, b):
    return fold(lax.dot_general(halves(a, 0), both(b), (((0,), (0,)), ((), ())), preferred_element_type=F32))


def step_of(coupled):
    sums = jnp.sum(jnp.abs(coupled), axis=0, keepdims=True)
    return 1.0 / jnp.max(sums, axis=1, keepdims=True)


def diagonal_row(gram):
    rows = lax.broadcasted_iota(jnp.int32, gram.shape, 0)
    columns = lax.broadcasted_iota(jnp.int32, gram.shape, 1)
    return jnp.sum(jnp.where(rows == columns, gram, 0.0), axis=0, keepdims=True)


def role_index():
    return (smp_index() ^ lax.axis_index("vox") // 2) & 1


def only_on(role, kernel):
    def run(*refs):
        pl.when(role_index() == role)(lambda: kernel(*refs))

    return run


def call(kernel, outs, operands, flops, scratch=(), in_hbm=0):
    spaces = [pltpu.HBM if i < in_hbm else pltpu.VMEM for i in range(len(operands))]
    placed = [pltpu.with_memory_space_constraint(x, space) for x, space in zip(operands, spaces)]
    specs = [pl.BlockSpec(memory_space=space) for space in spaces]
    return pl.pallas_call(
        kernel,
        out_shape=outs,
        in_specs=specs,
        out_specs=[pl.BlockSpec(memory_space=pltpu.VMEM)] * len(outs),
        scratch_shapes=list(scratch),
        compiler_params=pltpu.CompilerParams(vmem_limit_bytes=VMEM_LIMIT),
        cost_estimate=pl.CostEstimate(flops=flops, bytes_accessed=1 << 16, transcendentals=0),
    )(*placed)


def near(*shape):
    return pltpu.VMEM(shape, F32)


def far(*shape):
    return jax.ShapeDtypeStruct(shape, F32)


def bits_of(count):
    if count & (count - 1):
        raise ValueError("axis size")
    return [1 << b for b in range(count.bit_length() - 1)]


def groups_of(bits, size=2):
    return [bits[i : i + size] for i in range(0, len(bits), size)]


def masks_of(group):
    masks = [0]
    for bit in group:
        masks = [mask | bit for mask in masks] + masks
    return masks


def swap(values):
    return lax.ppermute(values, ALL, [(i, i ^ 1) for i in range(lax.axis_size(ALL))])


def send(values, holder, mask):
    smp_count, count = lax.axis_size("smp"), lax.axis_size(ALL)
    role = lambda i: (i ^ i // (2 * smp_count)) & 1
    pairs = []
    for i in range(count):
        target = i ^ mask if role(i) == holder else i
        pairs.append((i, target ^ 1 if role(target) == role(i) else target))
    return lax.ppermute(values, ALL, pairs)


def fan(values, holder, masks):
    sent = [send(values, holder, mask) if mask else swap(values) for mask in reversed(masks)]
    return sent[::-1]


def tree(parts):
    parts = parts[::-1]
    while len(parts) > 1:
        parts = [a + b for a, b in zip(parts[::2], parts[1::2])]
    return parts[0]


def smp_index():
    return lax.axis_index("smp")


def on_role(role, own, got):
    return jnp.where(role_index() == role, own, got)


def pack(gram):
    half = gram.shape[0] // 2
    rows = lax.broadcasted_iota(jnp.int32, (half, 2 * half), 0)
    columns = lax.broadcasted_iota(jnp.int32, (half, 2 * half), 1)
    top, bottom = gram[:half], gram[half:]
    packed = jnp.where(rows <= columns, top, pltpu.roll(bottom, half, 1))
    return packed, jnp.sum(jnp.where(columns == rows + half, bottom, 0.0), axis=0, keepdims=True)


def unpack(packed, diagonal):
    half = packed.shape[0]
    rows = lax.broadcasted_iota(jnp.int32, packed.shape, 0)
    columns = lax.broadcasted_iota(jnp.int32, packed.shape, 1)
    turned = jnp.concatenate([packed, packed], axis=0).T
    top = jnp.where(rows <= columns, packed, turned[:half])
    corner = jnp.where(columns < rows + half, pltpu.roll(packed, half, 1), turned[:half])
    corner = jnp.where(columns == rows + half, diagonal, corner)
    return jnp.concatenate([top, jnp.where(columns < half, turned[half:], corner)], axis=0)


def in_order(rows, scratch, chips, flip=0):
    size = scratch.shape[0] // chips // 2
    chip = smp_index() // 2
    for p in range(chips):
        for q in range(2):
            start = (2 * p + q) * size
            place = (chip ^ (chips - 1 - p)) * 2 + (q ^ flip)
            scratch[pl.ds(pl.multiple_of(place * size, size), size), :] = rows[start : start + size, :]
    return scratch[...]


def per_device(ensemble, voxel_factor, sample_factor, time_factor, weights):
    vox_rows, smp_rows, times = ensemble.shape
    rank = voxel_factor.shape[1]
    flat_rows = vox_rows * smp_rows
    vox_count, smp_count = lax.axis_size("vox"), lax.axis_size("smp")
    vox_total, smp_total = vox_rows * vox_count, smp_rows * smp_count
    chips, chip_rows = smp_count // 2, 2 * smp_rows
    chip_bits = bits_of(smp_count)[1:]
    vox_bits = [bit * smp_count for bit in bits_of(vox_count)]

    def open_kernel(x_hbm, c_hbm, b_hbm, a_hbm, w_hbm, x, c, a, w, out, con, sems):
        copies = [pltpu.make_async_copy(c_hbm, c, sems.at[0])]
        copies += [pltpu.make_async_copy(b_hbm, out.at[pl.ds(vox_rows, smp_rows), :], sems.at[1])]
        copies.append(pltpu.make_async_copy(x_hbm, x, sems.at[2]))
        copies.append(pltpu.make_async_copy(a_hbm, a, sems.at[3]))
        copies.append(pltpu.make_async_copy(w_hbm, w, sems.at[4]))
        for copy in copies:
            copy.start()
        copies[0].wait()
        copies[1].wait()
        factor = both(c[...])
        b = out[pl.ds(vox_rows, smp_rows), :]
        copies[2].wait()
        blocks = [x[pl.ds(j, vox_rows, stride=smp_rows), :] for j in range(smp_rows)]
        blocks = jnp.concatenate([halves(block, 1) for block in blocks], axis=0)
        made = fold(jnp.dot(blocks, factor, preferred_element_type=F32)).reshape(smp_rows, vox_rows, rank)
        con[...] = made
        total = made[0] * b[:1, :]
        for j in range(1, smp_rows):
            total = total + made[j] * b[j : j + 1, :]
        out[:vox_rows, :] = total
        copies[3].wait()
        copies[4].wait()

    x, c_near, a_near, w_row, opened, con = call(
        open_kernel,
        (
            near(flat_rows, times),
            near(times, rank),
            near(vox_rows, rank),
            near(1, rank),
            near(vox_rows + smp_rows, rank),
            near(smp_rows, vox_rows, rank),
        ),
        (ensemble.reshape(flat_rows, times), time_factor, sample_factor, voxel_factor, weights.reshape(1, rank)),
        2 * flat_rows * times * rank * 6,
        scratch=(pltpu.SemaphoreType.DMA((5,)),),
        in_hbm=5,
    )

    def weigh_kernel(c, w, outer, outer_c):
        squared = dot_rows(w[...], w[...])
        outer[...] = squared
        outer_c[...] = squared * dot_rows(c[...], c[...])

    outer, outer_c = call(
        weigh_kernel, (near(rank, rank), near(rank, rank)), (c_near, w_row), 2 * rank * rank * times * 4
    )

    got = swap(opened)
    terms = opened[:vox_rows] + got[:vox_rows]
    mate_con, mate_x = swap(con), swap(x)
    packet = jnp.concatenate([terms, got[vox_rows:], opened[vox_rows:]], axis=0)
    own = jnp.concatenate([terms, opened[vox_rows:], got[vox_rows:]], axis=0)
    rows_b = own[vox_rows:]
    holder = 1
    for group in groups_of(chip_bits):
        parts = [send(packet, holder, mask) for mask in masks_of(group)[:-1]] + [own]
        terms = tree([part[:vox_rows] for part in parts])
        rows_b = jnp.concatenate([part[vox_rows:] for part in parts], axis=0)
        packet = jnp.concatenate([terms, rows_b], axis=0)
        own = swap(packet)
        holder ^= 1
    voxel_role = holder

    half, sums_rows = rank // 2, rank // 2 + chip_rows

    def voxel_kernel(terms, rows, a, w, outer_c, con, mate_con, mate_x, moved_out, chip_b, out, all_b):
        b = in_order(rows, all_b, chips, lax.axis_index("vox") // 2 & 1)
        chip_b[...] = all_b[pl.ds(pl.multiple_of(smp_index() // 2 * chip_rows, chip_rows), chip_rows), :]
        coupled = outer_c[...] * dot_rows(b, b)
        moved = a[...] - step_of(coupled) * (dot(a[...], coupled) - terms[...] * w[...])
        moved_out[...] = moved
        packed, diagonal = pack(dot_rows(moved, moved))
        out[:half, :] = packed
        core = smp_index() & 1
        for place, source in ((core, con), (1 - core, mate_con)):
            made = [jnp.sum(source[j] * moved, axis=0, keepdims=True) for j in range(smp_rows)]
            start = pl.multiple_of(half + place * smp_rows, smp_rows)
            out[pl.ds(start, smp_rows), :] = jnp.concatenate(made, axis=0)
        out[sums_rows:, :] = jnp.broadcast_to(diagonal, (8, rank))

    moved_a, chip_b, sums = call(
        only_on(voxel_role, voxel_kernel),
        (near(vox_rows, rank), near(chip_rows, rank), near(sums_rows + 8, rank)),
        (terms, rows_b, a_near, w_row, outer_c, con, mate_con, mate_x),
        2 * rank * rank * vox_rows * 12,
        scratch=(near(smp_total, rank),),
    )

    mate_moved_a = swap(moved_a)

    for group in groups_of(vox_bits[:1] + vox_bits[:0:-1]):
        sums = tree(fan(sums, holder, masks_of(group)))
        holder ^= 1
    sample_role = holder
    if sample_role != voxel_role:
        chip_b = swap(chip_b)

    def time_kernel(x, mate_x, moved, mate_moved, each):
        moved = on_role(voxel_role, moved[...], mate_moved[...])
        core = smp_index() & 1
        for place, source in ((core, x), (1 - core, mate_x)):
            for j in range(smp_rows):
                block = source[pl.ds(j, vox_rows, stride=smp_rows), :]
                each[place * smp_rows + j] = dot_rows(block, moved)

    (each,) = call(
        only_on(sample_role, time_kernel),
        (near(chip_rows, times, rank),),
        (x, mate_x, moved_a, mate_moved_a),
        4 * flat_rows * times * rank * 6,
    )

    def sample_kernel(sums, b, w, outer_c, each, gram_out, out):
        gram = unpack(sums[:half, :], sums[sums_rows : sums_rows + 1, :])
        gram_out[...] = gram
        coupled = outer_c[...] * gram
        moved = b[...] - step_of(coupled) * (dot(b[...], coupled) - sums[half:sums_rows, :] * w[...])
        out[times:, :] = moved
        total = None
        for j in range(chip_rows):
            made = each[j] * moved[j : j + 1, :]
            total = made if total is None else total + made
        out[:times, :] = total

    gram_a, payload = call(
        only_on(sample_role, sample_kernel),
        (near(rank, rank), near(times + chip_rows, rank)),
        (sums, chip_b, w_row, outer_c, each),
        2 * rank * rank * chip_rows * 6,
    )
    mate_gram_a = swap(gram_a)

    def scale_kernel(gram, mate_gram, moved, mate_moved, outer, result, scales_out, weighed):
        gram = on_role(sample_role, gram[...], mate_gram[...])
        scales = jnp.sqrt(diagonal_row(gram) / vox_total + 1e-06)
        scales_out[...] = scales
        result[...] = on_role(voxel_role, moved[...], mate_moved[...]) / scales
        weighed[...] = outer[...] * gram

    voxel_result, scales_a, weighed = call(
        scale_kernel,
        (far(vox_rows, rank), near(1, rank), near(rank, rank)),
        (gram_a, mate_gram_a, moved_a, mate_moved_a, outer),
        vox_rows * rank * 8,
    )

    terms, rows_b, rows_role = payload[:times], payload[times:], holder
    smp_mask = sum(chip_bits)
    for group in groups_of(chip_bits + vox_bits[1:2] + vox_bits[:1] + vox_bits[2:]):
        masks = masks_of(group)
        if any(mask & smp_mask for mask in masks):
            packet = payload if rows_b.shape[0] == chip_rows else jnp.concatenate([terms, rows_b], axis=0)
            parts = fan(packet, holder, masks)
            gathered = [i for i, mask in enumerate(masks) if not mask & ~smp_mask]
            rows = rows_b.shape[0]

            def gather_kernel(*refs, gathered=gathered, rows=rows):
                parts, (terms, rows_out) = refs[-3::-1], refs[-2:]
                terms[...] = tree([part[:times, :] for part in parts])
                for p, i in enumerate(gathered):
                    rows_out[p * rows : (p + 1) * rows, :] = parts[i][times:, :]

            terms, rows_b = call(
                gather_kernel,
                (near(times, rank), near(len(gathered) * rows, rank)),
                parts[::-1],
                len(masks) * times * rank,
            )
            rows_role = holder ^ 1
        else:
            terms = tree(fan(terms, holder, masks))
        holder ^= 1
    last_role = holder
    mate_rows_b = swap(rows_b)

    def ready_kernel(rows, mate_rows, c, w, weighed, scales_a, b_out, base, gain, scale, all_b):
        b = in_order(on_role(rows_role, rows[...], mate_rows[...]), all_b, chips)
        coupled = weighed[...] * dot_rows(b, b)
        step = step_of(coupled)
        base[...] = c[...] - step * dot(c[...], coupled)
        gain[...] = step * w[...]
        scales_b = jnp.sqrt(jnp.sum(b * b, axis=0, keepdims=True) / smp_total + 1e-06)
        scale[...] = w[...] * scales_a[...] * scales_b
        b_out[...] = all_b[pl.ds(pl.multiple_of(smp_index() * smp_rows, smp_rows), smp_rows), :] / scales_b

    sample_result, base, gain, scale = call(
        ready_kernel,
        (far(smp_rows, rank), near(times, rank), near(1, rank), near(1, rank)),
        (rows_b, mate_rows_b, c_near, w_row, weighed, scales_a),
        2 * rank * rank * times * 4,
        scratch=(near(smp_total, rank),),
    )
    terms, base, gain, scale, voxel_result, sample_result = lax.optimization_barrier(
        (terms, base, gain, scale, voxel_result, sample_result)
    )
    mate_terms = swap(terms)

    def last_kernel(terms, mate_terms, base, gain, scale, c_out, w_out):
        moved = base[...] + on_role(last_role, terms[...], mate_terms[...]) * gain[...]
        scales_c = jnp.sqrt(jnp.sum(moved * moved, axis=0, keepdims=True) / times + 1e-06)
        c_out[...] = moved / scales_c
        w_out[...] = scale[...] * scales_c

    time_result, scale_result = call(
        last_kernel,
        (far(times, rank), far(1, rank)),
        (terms, mate_terms, base, gain, scale),
        rank * times * 8,
    )
    return voxel_result, sample_result, time_result, scale_result.reshape(rank)


def solution(mesh):
    return jax.shard_map(
        per_device,
        mesh=mesh,
        in_specs=(P("vox", "smp", None), P("vox", None), P("smp", None), P(), P()),
        out_specs=(P("vox", None), P("smp", None), P(), P()),
        check_vma=False,
    )
```

```python
import jax
import jax.numpy as jnp
from jax import lax
from jax.experimental import pallas as pl
from jax.experimental.pallas import tpu as pltpu
from jax.sharding import PartitionSpec as P

F32 = jnp.float32
BF16 = jnp.bfloat16
VMEM_LIMIT = 12 * 1024 * 1024
ALL = ("vox", "smp")


def halves(a, axis):
    high = a.astype(BF16)
    return jnp.concatenate([high, (a - high.astype(F32)).astype(BF16)], axis=axis)


def both(b):
    parts = halves(b, 1)
    return jnp.concatenate([parts, parts], axis=0)


def fold(product):
    width = product.shape[1] // 2
    return product[:, :width] + product[:, width:]


def dot(a, b):
    return fold(jnp.dot(halves(a, 1), both(b), preferred_element_type=F32))


def dot_rows(a, b):
    return fold(lax.dot_general(halves(a, 0), both(b), (((0,), (0,)), ((), ())), preferred_element_type=F32))


def step_of(coupled):
    sums = jnp.sum(jnp.abs(coupled), axis=0, keepdims=True)
    return 1.0 / jnp.max(sums, axis=1, keepdims=True)


def diagonal_row(gram):
    rows = lax.broadcasted_iota(jnp.int32, gram.shape, 0)
    columns = lax.broadcasted_iota(jnp.int32, gram.shape, 1)
    return jnp.sum(jnp.where(rows == columns, gram, 0.0), axis=0, keepdims=True)


def role_index():
    return (smp_index() ^ lax.axis_index("vox") // 2) & 1


def only_on(role, kernel):
    def run(*refs):
        pl.when(role_index() == role)(lambda: kernel(*refs))

    return run


def call(kernel, outs, operands, flops, scratch=(), in_hbm=0, aliases=None):
    spaces = [pltpu.HBM if i < in_hbm else pltpu.VMEM for i in range(len(operands))]
    placed = [pltpu.with_memory_space_constraint(x, space) for x, space in zip(operands, spaces)]
    specs = [pl.BlockSpec(memory_space=space) for space in spaces]
    return pl.pallas_call(
        kernel,
        out_shape=outs,
        in_specs=specs,
        out_specs=[pl.BlockSpec(memory_space=pltpu.VMEM)] * len(outs),
        scratch_shapes=list(scratch),
        input_output_aliases=aliases or {},
        compiler_params=pltpu.CompilerParams(vmem_limit_bytes=VMEM_LIMIT),
        cost_estimate=pl.CostEstimate(flops=flops, bytes_accessed=1 << 16, transcendentals=0),
    )(*placed)


def near(*shape):
    return pltpu.VMEM(shape, F32)


def far(*shape):
    return jax.ShapeDtypeStruct(shape, F32)


def bits_of(count):
    if count & (count - 1):
        raise ValueError("axis size")
    return [1 << b for b in range(count.bit_length() - 1)]


def groups_of(bits, size=2):
    return [bits[i : i + size] for i in range(0, len(bits), size)]


def masks_of(group):
    masks = [0]
    for bit in group:
        masks = [mask | bit for mask in masks] + masks
    return masks


def swap(values):
    return lax.ppermute(values, ALL, [(i, i ^ 1) for i in range(lax.axis_size(ALL))])


def send(values, holder, mask):
    smp_count, count = lax.axis_size("smp"), lax.axis_size(ALL)
    role = lambda i: (i ^ i // (2 * smp_count)) & 1
    pairs = []
    for i in range(count):
        target = i ^ mask if role(i) == holder else i
        pairs.append((i, target ^ 1 if role(target) == role(i) else target))
    return lax.ppermute(values, ALL, pairs)


def fan(values, holder, masks):
    sent = [send(values, holder, mask) if mask else swap(values) for mask in reversed(masks)]
    return sent[::-1]


def tree(parts):
    parts = parts[::-1]
    while len(parts) > 1:
        parts = [a + b for a, b in zip(parts[::2], parts[1::2])]
    return parts[0]


def smp_index():
    return lax.axis_index("smp")


def on_role(role, own, got):
    return jnp.where(role_index() == role, own, got)


def pack(gram):
    half = gram.shape[0] // 2
    rows = lax.broadcasted_iota(jnp.int32, (half, 2 * half), 0)
    columns = lax.broadcasted_iota(jnp.int32, (half, 2 * half), 1)
    top, bottom = gram[:half], gram[half:]
    packed = jnp.where(rows <= columns, top, pltpu.roll(bottom, half, 1))
    return packed, jnp.sum(jnp.where(columns == rows + half, bottom, 0.0), axis=0, keepdims=True)


def unpack(packed, diagonal):
    half = packed.shape[0]
    rows = lax.broadcasted_iota(jnp.int32, packed.shape, 0)
    columns = lax.broadcasted_iota(jnp.int32, packed.shape, 1)
    turned = jnp.concatenate([packed, packed], axis=0).T
    top = jnp.where(rows <= columns, packed, turned[:half])
    corner = jnp.where(columns < rows + half, pltpu.roll(packed, half, 1), turned[:half])
    corner = jnp.where(columns == rows + half, diagonal, corner)
    return jnp.concatenate([top, jnp.where(columns < half, turned[half:], corner)], axis=0)


def in_order(rows, scratch, chips, flip=0):
    size = scratch.shape[0] // chips // 2
    chip = smp_index() // 2
    for p in range(chips):
        for q in range(2):
            start = (2 * p + q) * size
            place = (chip ^ (chips - 1 - p)) * 2 + (q ^ flip)
            scratch[pl.ds(pl.multiple_of(place * size, size), size), :] = rows[start : start + size, :]
    return scratch[...]


def per_device(ensemble, voxel_factor, sample_factor, time_factor, weights):
    vox_rows, smp_rows, times = ensemble.shape
    rank = voxel_factor.shape[1]
    flat_rows = vox_rows * smp_rows
    vox_count, smp_count = lax.axis_size("vox"), lax.axis_size("smp")
    vox_total, smp_total = vox_rows * vox_count, smp_rows * smp_count
    chips, chip_rows = smp_count // 2, 2 * smp_rows
    chip_bits = bits_of(smp_count)[1:]
    vox_bits = [bit * smp_count for bit in bits_of(vox_count)]

    cut = vox_rows // 2

    def contract(x, c, b, con, out, first):
        blocks = [x[pl.ds(first * smp_rows + j, cut, stride=smp_rows), :] for j in range(smp_rows)]
        blocks = jnp.concatenate([halves(block, 1) for block in blocks], axis=0)
        made = fold(jnp.dot(blocks, both(c), preferred_element_type=F32)).reshape(smp_rows, cut, rank)
        con[:, first : first + cut, :] = made
        total = made[0] * b[:1, :]
        for j in range(1, smp_rows):
            total = total + made[j] * b[j : j + 1, :]
        out[:cut, :] = total

    def open_kernel(x_hbm, c_hbm, b_hbm, a_hbm, w_hbm, x, c, a, w, out, con, sems):
        near_half, far_half = pl.ds(0, cut * smp_rows), pl.ds(cut * smp_rows, cut * smp_rows)
        copies = [
            pltpu.make_async_copy(c_hbm, c, sems.at[0]),
            pltpu.make_async_copy(x_hbm.at[near_half, :], x.at[near_half, :], sems.at[1]),
            pltpu.make_async_copy(b_hbm, out.at[pl.ds(cut, smp_rows), :], sems.at[2]),
            pltpu.make_async_copy(x_hbm.at[far_half, :], x.at[far_half, :], sems.at[3]),
            pltpu.make_async_copy(a_hbm, a, sems.at[4]),
            pltpu.make_async_copy(w_hbm, w, sems.at[5]),
        ]
        for copy in copies:
            copy.start()
        for copy in copies[:3]:
            copy.wait()
        contract(x, c[...], out[pl.ds(cut, smp_rows), :], con, out, 0)
        for copy in copies[3:]:
            copy.wait()

    x, c_near, a_near, w_row, opened, con = call(
        open_kernel,
        (
            near(flat_rows, times),
            near(times, rank),
            near(vox_rows, rank),
            near(1, rank),
            near(cut + smp_rows, rank),
            near(smp_rows, vox_rows, rank),
        ),
        (ensemble.reshape(flat_rows, times), time_factor, sample_factor, voxel_factor, weights.reshape(1, rank)),
        flat_rows * times * rank * 4,
        scratch=(pltpu.SemaphoreType.DMA((6,)),),
        in_hbm=5,
    )

    def late_kernel(x, c, opened, con_in, out, con):
        contract(x, c[...], opened[cut:, :], con, out, cut)

    late_opened, con = call(
        late_kernel,
        (near(cut, rank), near(smp_rows, vox_rows, rank)),
        (x, c_near, opened, con),
        flat_rows * times * rank * 4,
        aliases={3: 1},
    )

    def weigh_kernel(c, w, outer, outer_c):
        squared = dot_rows(w[...], w[...])
        outer[...] = squared
        outer_c[...] = squared * dot_rows(c[...], c[...])

    outer, outer_c = call(
        weigh_kernel, (near(rank, rank), near(rank, rank)), (c_near, w_row), 2 * rank * rank * times * 4
    )

    late_x, late_opened = lax.optimization_barrier((x, late_opened))
    got, late_got = swap(opened), swap(late_opened)
    terms, late_terms = opened[:cut] + got[:cut], late_opened + late_got
    mate_con, mate_x = swap(con), swap(late_x)
    packet = jnp.concatenate([terms, got[cut:], opened[cut:]], axis=0)
    own = jnp.concatenate([terms, opened[cut:], got[cut:]], axis=0)
    late_own = late_terms
    holder = 1
    for group in groups_of(chip_bits):
        masks = masks_of(group)[:-1]
        parts = [send(packet, holder, mask) for mask in masks] + [own]
        late_terms = tree([send(late_terms, holder, mask) for mask in masks] + [late_own])
        terms = tree([part[:cut] for part in parts])
        rows_b = jnp.concatenate([part[cut:] for part in parts], axis=0)
        packet = jnp.concatenate([terms, rows_b], axis=0)
        own, late_own = swap(packet), swap(late_terms)
        holder ^= 1
    voxel_role = holder

    half, sums_rows = rank // 2, rank // 2 + chip_rows

    def voxel_kernel(terms, late_terms, rows, a, w, outer_c, con, mate_con, mate_x, moved_out, chip_b, out, all_b):
        b = in_order(rows, all_b, chips, lax.axis_index("vox") // 2 & 1)
        chip_b[...] = all_b[pl.ds(pl.multiple_of(smp_index() // 2 * chip_rows, chip_rows), chip_rows), :]
        coupled = outer_c[...] * dot_rows(b, b)
        terms = jnp.concatenate([terms[...], late_terms[...]], axis=0)
        moved = a[...] - step_of(coupled) * (dot(a[...], coupled) - terms * w[...])
        moved_out[...] = moved
        packed, diagonal = pack(dot_rows(moved, moved))
        out[:half, :] = packed
        core = smp_index() & 1
        for place, source in ((core, con), (1 - core, mate_con)):
            made = [jnp.sum(source[j] * moved, axis=0, keepdims=True) for j in range(smp_rows)]
            start = pl.multiple_of(half + place * smp_rows, smp_rows)
            out[pl.ds(start, smp_rows), :] = jnp.concatenate(made, axis=0)
        out[sums_rows:, :] = jnp.broadcast_to(diagonal, (8, rank))

    moved_a, chip_b, sums = call(
        only_on(voxel_role, voxel_kernel),
        (near(vox_rows, rank), near(chip_rows, rank), near(sums_rows + 8, rank)),
        (terms, late_terms, rows_b, a_near, w_row, outer_c, con, mate_con, mate_x),
        2 * rank * rank * vox_rows * 12,
        scratch=(near(smp_total, rank),),
    )

    mate_moved_a = swap(moved_a)

    for group in groups_of(vox_bits[:1] + vox_bits[:0:-1]):
        sums = tree(fan(sums, holder, masks_of(group)))
        holder ^= 1
    sample_role = holder
    if sample_role != voxel_role:
        chip_b = swap(chip_b)

    def time_kernel(x, mate_x, moved, mate_moved, each):
        moved = on_role(voxel_role, moved[...], mate_moved[...])
        core = smp_index() & 1
        for place, source in ((core, x), (1 - core, mate_x)):
            for j in range(smp_rows):
                block = source[pl.ds(j, vox_rows, stride=smp_rows), :]
                each[place * smp_rows + j] = dot_rows(block, moved)

    (each,) = call(
        only_on(sample_role, time_kernel),
        (near(chip_rows, times, rank),),
        (x, mate_x, moved_a, mate_moved_a),
        4 * flat_rows * times * rank * 6,
    )

    def sample_kernel(sums, b, w, outer_c, each, gram_out, out):
        gram = unpack(sums[:half, :], sums[sums_rows : sums_rows + 1, :])
        gram_out[...] = gram
        coupled = outer_c[...] * gram
        moved = b[...] - step_of(coupled) * (dot(b[...], coupled) - sums[half:sums_rows, :] * w[...])
        out[times:, :] = moved
        total = None
        for j in range(chip_rows):
            made = each[j] * moved[j : j + 1, :]
            total = made if total is None else total + made
        out[:times, :] = total

    gram_a, payload = call(
        only_on(sample_role, sample_kernel),
        (near(rank, rank), near(times + chip_rows, rank)),
        (sums, chip_b, w_row, outer_c, each),
        2 * rank * rank * chip_rows * 6,
    )
    mate_gram_a = swap(gram_a)

    def scale_kernel(gram, mate_gram, moved, mate_moved, outer, result, scales_out, weighed):
        gram = on_role(sample_role, gram[...], mate_gram[...])
        scales = jnp.sqrt(diagonal_row(gram) / vox_total + 1e-06)
        scales_out[...] = scales
        result[...] = on_role(voxel_role, moved[...], mate_moved[...]) / scales
        weighed[...] = outer[...] * gram

    voxel_result, scales_a, weighed = call(
        scale_kernel,
        (far(vox_rows, rank), near(1, rank), near(rank, rank)),
        (gram_a, mate_gram_a, moved_a, mate_moved_a, outer),
        vox_rows * rank * 8,
    )

    terms, rows_b, rows_role = payload[:times], payload[times:], holder
    smp_mask = sum(chip_bits)
    for group in groups_of(chip_bits + vox_bits[1:2] + vox_bits[:1] + vox_bits[2:]):
        masks = masks_of(group)
        if any(mask & smp_mask for mask in masks):
            packet = payload if rows_b.shape[0] == chip_rows else jnp.concatenate([terms, rows_b], axis=0)
            parts = fan(packet, holder, masks)
            gathered = [i for i, mask in enumerate(masks) if not mask & ~smp_mask]
            rows = rows_b.shape[0]

            def gather_kernel(*refs, gathered=gathered, rows=rows):
                parts, (terms, rows_out) = refs[-3::-1], refs[-2:]
                terms[...] = tree([part[:times, :] for part in parts])
                for p, i in enumerate(gathered):
                    rows_out[p * rows : (p + 1) * rows, :] = parts[i][times:, :]

            terms, rows_b = call(
                gather_kernel,
                (near(times, rank), near(len(gathered) * rows, rank)),
                parts[::-1],
                len(masks) * times * rank,
            )
            rows_role = holder ^ 1
        else:
            terms = tree(fan(terms, holder, masks))
        holder ^= 1
    last_role = holder
    mate_rows_b = swap(rows_b)

    def ready_kernel(rows, mate_rows, c, w, weighed, scales_a, b_out, base, gain, scale, all_b):
        b = in_order(on_role(rows_role, rows[...], mate_rows[...]), all_b, chips)
        coupled = weighed[...] * dot_rows(b, b)
        step = step_of(coupled)
        base[...] = c[...] - step * dot(c[...], coupled)
        gain[...] = step * w[...]
        scales_b = jnp.sqrt(jnp.sum(b * b, axis=0, keepdims=True) / smp_total + 1e-06)
        scale[...] = w[...] * scales_a[...] * scales_b
        b_out[...] = all_b[pl.ds(pl.multiple_of(smp_index() * smp_rows, smp_rows), smp_rows), :] / scales_b

    sample_result, base, gain, scale = call(
        ready_kernel,
        (far(smp_rows, rank), near(times, rank), near(1, rank), near(1, rank)),
        (rows_b, mate_rows_b, c_near, w_row, weighed, scales_a),
        2 * rank * rank * times * 4,
        scratch=(near(smp_total, rank),),
    )
    terms, base, gain, scale, voxel_result, sample_result = lax.optimization_barrier(
        (terms, base, gain, scale, voxel_result, sample_result)
    )
    mate_terms = swap(terms)

    def last_kernel(terms, mate_terms, base, gain, scale, c_out, w_out):
        moved = base[...] + on_role(last_role, terms[...], mate_terms[...]) * gain[...]
        scales_c = jnp.sqrt(jnp.sum(moved * moved, axis=0, keepdims=True) / times + 1e-06)
        c_out[...] = moved / scales_c
        w_out[...] = scale[...] * scales_c

    time_result, scale_result = call(
        last_kernel,
        (far(times, rank), far(1, rank)),
        (terms, mate_terms, base, gain, scale),
        rank * times * 8,
    )
    return voxel_result, sample_result, time_result, scale_result.reshape(rank)


def solution(mesh):
    return jax.shard_map(
        per_device,
        mesh=mesh,
        in_specs=(P("vox", "smp", None), P("vox", None), P("smp", None), P(), P()),
        out_specs=(P("vox", None), P("smp", None), P(), P()),
        check_vma=False,
    )
```

```python
import jax
import jax.numpy as jnp
from jax import lax
from jax.experimental import pallas as pl
from jax.experimental.pallas import tpu as pltpu
from jax.sharding import PartitionSpec as P

F32 = jnp.float32
BF16 = jnp.bfloat16
VMEM_LIMIT = 12 * 1024 * 1024
ALL = ("vox", "smp")


def halves(a, axis):
    high = a.astype(BF16)
    return jnp.concatenate([high, (a - high.astype(F32)).astype(BF16)], axis=axis)


def both(b):
    parts = halves(b, 1)
    return jnp.concatenate([parts, parts], axis=0)


def fold(product):
    width = product.shape[1] // 2
    return product[:, :width] + product[:, width:]


def dot(a, b):
    return fold(jnp.dot(halves(a, 1), both(b), preferred_element_type=F32))


def dot_rows(a, b):
    return fold(lax.dot_general(halves(a, 0), both(b), (((0,), (0,)), ((), ())), preferred_element_type=F32))


def step_of(coupled):
    sums = jnp.sum(jnp.abs(coupled), axis=0, keepdims=True)
    return 1.0 / jnp.max(sums, axis=1, keepdims=True)


def diagonal_row(gram):
    rows = lax.broadcasted_iota(jnp.int32, gram.shape, 0)
    columns = lax.broadcasted_iota(jnp.int32, gram.shape, 1)
    return jnp.sum(jnp.where(rows == columns, gram, 0.0), axis=0, keepdims=True)


def role_index():
    return (smp_index() ^ lax.axis_index("vox") // 2) & 1


def only_on(role, kernel):
    def run(*refs):
        pl.when(role_index() == role)(lambda: kernel(*refs))

    return run


def call(kernel, outs, operands, flops, scratch=(), in_hbm=0, aliases=None, out_space=pltpu.VMEM):
    spaces = [pltpu.HBM if i < in_hbm else pltpu.VMEM for i in range(len(operands))]
    placed = [pltpu.with_memory_space_constraint(x, space) for x, space in zip(operands, spaces)]
    specs = [pl.BlockSpec(memory_space=space) for space in spaces]
    return pl.pallas_call(
        kernel,
        out_shape=outs,
        in_specs=specs,
        out_specs=[pl.BlockSpec(memory_space=out_space)] * len(outs),
        scratch_shapes=list(scratch),
        input_output_aliases=aliases or {},
        compiler_params=pltpu.CompilerParams(vmem_limit_bytes=VMEM_LIMIT),
        cost_estimate=pl.CostEstimate(flops=flops, bytes_accessed=1 << 16, transcendentals=0),
    )(*placed)


def near(*shape):
    return pltpu.VMEM(shape, F32)


def far(*shape):
    return jax.ShapeDtypeStruct(shape, F32)


def bits_of(count):
    if count & (count - 1):
        raise ValueError("axis size")
    return [1 << b for b in range(count.bit_length() - 1)]


def groups_of(bits, size=2):
    return [bits[i : i + size] for i in range(0, len(bits), size)]


def masks_of(group):
    masks = [0]
    for bit in group:
        masks = [mask | bit for mask in masks] + masks
    return masks


def swap(values):
    return lax.ppermute(values, ALL, [(i, i ^ 1) for i in range(lax.axis_size(ALL))])


def send(values, holder, mask):
    smp_count, count = lax.axis_size("smp"), lax.axis_size(ALL)
    role = lambda i: (i ^ i // (2 * smp_count)) & 1
    pairs = []
    for i in range(count):
        target = i ^ mask if role(i) == holder else i
        pairs.append((i, target ^ 1 if role(target) == role(i) else target))
    return lax.ppermute(values, ALL, pairs)


def fan(values, holder, masks):
    sent = [send(values, holder, mask) if mask else swap(values) for mask in reversed(masks)]
    return sent[::-1]


def tree(parts):
    parts = parts[::-1]
    while len(parts) > 1:
        parts = [a + b for a, b in zip(parts[::2], parts[1::2])]
    return parts[0]


def smp_index():
    return lax.axis_index("smp")


def on_role(role, own, got):
    return jnp.where(role_index() == role, own, got)


def pack(gram):
    half = gram.shape[0] // 2
    rows = lax.broadcasted_iota(jnp.int32, (half, 2 * half), 0)
    columns = lax.broadcasted_iota(jnp.int32, (half, 2 * half), 1)
    top, bottom = gram[:half], gram[half:]
    packed = jnp.where(rows <= columns, top, pltpu.roll(bottom, half, 1))
    return packed, jnp.sum(jnp.where(columns == rows + half, bottom, 0.0), axis=0, keepdims=True)


def unpack(packed, diagonal):
    half = packed.shape[0]
    rows = lax.broadcasted_iota(jnp.int32, packed.shape, 0)
    columns = lax.broadcasted_iota(jnp.int32, packed.shape, 1)
    turned = jnp.concatenate([packed, packed], axis=0).T
    top = jnp.where(rows <= columns, packed, turned[:half])
    corner = jnp.where(columns < rows + half, pltpu.roll(packed, half, 1), turned[:half])
    corner = jnp.where(columns == rows + half, diagonal, corner)
    return jnp.concatenate([top, jnp.where(columns < half, turned[half:], corner)], axis=0)


def in_order(rows, scratch, chips, flip=0):
    size = scratch.shape[0] // chips // 2
    chip = smp_index() // 2
    for p in range(chips):
        for q in range(2):
            start = (2 * p + q) * size
            place = (chip ^ (chips - 1 - p)) * 2 + (q ^ flip)
            scratch[pl.ds(pl.multiple_of(place * size, size), size), :] = rows[start : start + size, :]
    return scratch[...]


def per_device(ensemble, voxel_factor, sample_factor, time_factor, weights):
    vox_rows, smp_rows, times = ensemble.shape
    rank = voxel_factor.shape[1]
    flat_rows = vox_rows * smp_rows
    vox_count, smp_count = lax.axis_size("vox"), lax.axis_size("smp")
    vox_total, smp_total = vox_rows * vox_count, smp_rows * smp_count
    chips, chip_rows = smp_count // 2, 2 * smp_rows
    chip_bits = bits_of(smp_count)[1:]
    vox_bits = [bit * smp_count for bit in bits_of(vox_count)]

    cut = vox_rows // 2

    def contract(x, c, b, con, out, first):
        blocks = [x[pl.ds(first * smp_rows + j, cut, stride=smp_rows), :] for j in range(smp_rows)]
        blocks = jnp.concatenate([halves(block, 1) for block in blocks], axis=0)
        made = fold(jnp.dot(blocks, both(c), preferred_element_type=F32)).reshape(smp_rows, cut, rank)
        con[:, first : first + cut, :] = made
        total = made[0] * b[:1, :]
        for j in range(1, smp_rows):
            total = total + made[j] * b[j : j + 1, :]
        out[:cut, :] = total

    def open_kernel(x_hbm, c_hbm, b_hbm, a_hbm, w_hbm, x, c, a, w, out, con, sems):
        near_half, far_half = pl.ds(0, cut * smp_rows), pl.ds(cut * smp_rows, cut * smp_rows)
        copies = [
            pltpu.make_async_copy(c_hbm, c, sems.at[0]),
            pltpu.make_async_copy(x_hbm.at[near_half, :], x.at[near_half, :], sems.at[1]),
            pltpu.make_async_copy(b_hbm, out.at[pl.ds(cut, smp_rows), :], sems.at[2]),
            pltpu.make_async_copy(x_hbm.at[far_half, :], x.at[far_half, :], sems.at[3]),
            pltpu.make_async_copy(a_hbm, a, sems.at[4]),
            pltpu.make_async_copy(w_hbm, w, sems.at[5]),
        ]
        for copy in copies:
            copy.start()
        for copy in copies[:3]:
            copy.wait()
        contract(x, c[...], out[pl.ds(cut, smp_rows), :], con, out, 0)
        for copy in copies[3:]:
            copy.wait()

    x, c_near, a_near, w_row, opened, con = call(
        open_kernel,
        (
            near(flat_rows, times),
            near(times, rank),
            near(vox_rows, rank),
            near(1, rank),
            near(cut + smp_rows, rank),
            near(smp_rows, vox_rows, rank),
        ),
        (ensemble.reshape(flat_rows, times), time_factor, sample_factor, voxel_factor, weights.reshape(1, rank)),
        flat_rows * times * rank * 4,
        scratch=(pltpu.SemaphoreType.DMA((6,)),),
        in_hbm=5,
    )

    def late_kernel(x, c, opened, con_in, out, con):
        contract(x, c[...], opened[cut:, :], con, out, cut)

    late_opened, con = call(
        late_kernel,
        (near(cut, rank), near(smp_rows, vox_rows, rank)),
        (x, c_near, opened, con),
        flat_rows * times * rank * 4,
        aliases={3: 1},
    )

    def weigh_kernel(c, w, outer, outer_c):
        squared = dot_rows(w[...], w[...])
        outer[...] = squared
        outer_c[...] = squared * dot_rows(c[...], c[...])

    outer, outer_c = call(
        weigh_kernel, (near(rank, rank), near(rank, rank)), (c_near, w_row), 2 * rank * rank * times * 4
    )

    late_x, late_opened = lax.optimization_barrier((x, late_opened))
    got, late_got = swap(opened), swap(late_opened)
    terms, late_terms = opened[:cut] + got[:cut], late_opened + late_got
    mate_con, mate_x = swap(con), swap(late_x)
    packet = jnp.concatenate([terms, got[cut:], opened[cut:]], axis=0)
    own = jnp.concatenate([terms, opened[cut:], got[cut:]], axis=0)
    late_own = late_terms
    holder = 1
    for group in groups_of(chip_bits):
        masks = masks_of(group)[:-1]
        parts = [send(packet, holder, mask) for mask in masks] + [own]
        late_terms = tree([send(late_terms, holder, mask) for mask in masks] + [late_own])
        terms = tree([part[:cut] for part in parts])
        rows_b = jnp.concatenate([part[cut:] for part in parts], axis=0)
        packet = jnp.concatenate([terms, rows_b], axis=0)
        own, late_own = swap(packet), swap(late_terms)
        holder ^= 1
    voxel_role = holder

    half, sums_rows = rank // 2, rank // 2 + chip_rows

    def voxel_kernel(terms, late_terms, rows, a, w, outer_c, con, mate_con, mate_x, moved_out, chip_b, out, all_b):
        b = in_order(rows, all_b, chips, lax.axis_index("vox") // 2 & 1)
        chip_b[...] = all_b[pl.ds(pl.multiple_of(smp_index() // 2 * chip_rows, chip_rows), chip_rows), :]
        coupled = outer_c[...] * dot_rows(b, b)
        terms = jnp.concatenate([terms[...], late_terms[...]], axis=0)
        moved = a[...] - step_of(coupled) * (dot(a[...], coupled) - terms * w[...])
        moved_out[...] = moved
        packed, diagonal = pack(dot_rows(moved, moved))
        out[:half, :] = packed
        core = smp_index() & 1
        for place, source in ((core, con), (1 - core, mate_con)):
            made = [jnp.sum(source[j] * moved, axis=0, keepdims=True) for j in range(smp_rows)]
            start = pl.multiple_of(half + place * smp_rows, smp_rows)
            out[pl.ds(start, smp_rows), :] = jnp.concatenate(made, axis=0)
        out[sums_rows:, :] = jnp.broadcast_to(diagonal, (8, rank))

    moved_a, chip_b, sums = call(
        only_on(voxel_role, voxel_kernel),
        (near(vox_rows, rank), near(chip_rows, rank), near(sums_rows + 8, rank)),
        (terms, late_terms, rows_b, a_near, w_row, outer_c, con, mate_con, mate_x),
        2 * rank * rank * vox_rows * 12,
        scratch=(near(smp_total, rank),),
    )

    mate_moved_a = swap(moved_a)

    for group in groups_of(vox_bits[:1] + vox_bits[:0:-1]):
        sums = tree(fan(sums, holder, masks_of(group)))
        holder ^= 1
    sample_role = holder
    if sample_role != voxel_role:
        chip_b = swap(chip_b)

    def time_kernel(x, mate_x, moved, mate_moved, each):
        moved = on_role(voxel_role, moved[...], mate_moved[...])
        core = smp_index() & 1
        for place, source in ((core, x), (1 - core, mate_x)):
            for j in range(smp_rows):
                block = source[pl.ds(j, vox_rows, stride=smp_rows), :]
                each[place * smp_rows + j] = dot_rows(block, moved)

    (each,) = call(
        only_on(sample_role, time_kernel),
        (near(chip_rows, times, rank),),
        (x, mate_x, moved_a, mate_moved_a),
        4 * flat_rows * times * rank * 6,
    )

    def sample_kernel(sums, b, w, outer_c, each, gram_out, out):
        gram = unpack(sums[:half, :], sums[sums_rows : sums_rows + 1, :])
        gram_out[...] = gram
        coupled = outer_c[...] * gram
        moved = b[...] - step_of(coupled) * (dot(b[...], coupled) - sums[half:sums_rows, :] * w[...])
        out[times:, :] = moved
        total = None
        for j in range(chip_rows):
            made = each[j] * moved[j : j + 1, :]
            total = made if total is None else total + made
        out[:times, :] = total

    gram_a, payload = call(
        only_on(sample_role, sample_kernel),
        (near(rank, rank), near(times + chip_rows, rank)),
        (sums, chip_b, w_row, outer_c, each),
        2 * rank * rank * chip_rows * 6,
    )
    mate_gram_a = swap(gram_a)

    def scale_kernel(gram, mate_gram, moved, mate_moved, outer, result, scales_out, weighed):
        gram = on_role(sample_role, gram[...], mate_gram[...])
        scales = jnp.sqrt(diagonal_row(gram) / vox_total + 1e-06)
        scales_out[...] = scales
        result[...] = on_role(voxel_role, moved[...], mate_moved[...]) / scales
        weighed[...] = outer[...] * gram

    voxel_result, scales_a, weighed = call(
        scale_kernel,
        (far(vox_rows, rank), near(1, rank), near(rank, rank)),
        (gram_a, mate_gram_a, moved_a, mate_moved_a, outer),
        vox_rows * rank * 8,
    )

    terms, rows_b, rows_role = payload[:times], payload[times:], holder
    smp_mask = sum(chip_bits)
    for group in groups_of(chip_bits + vox_bits[1:2] + vox_bits[:1] + vox_bits[2:]):
        masks = masks_of(group)
        if any(mask & smp_mask for mask in masks):
            packet = payload if rows_b.shape[0] == chip_rows else jnp.concatenate([terms, rows_b], axis=0)
            parts = fan(packet, holder, masks)
            gathered = [i for i, mask in enumerate(masks) if not mask & ~smp_mask]
            rows = rows_b.shape[0]

            def gather_kernel(*refs, gathered=gathered, rows=rows):
                parts, (terms, rows_out) = refs[-3::-1], refs[-2:]
                terms[...] = tree([part[:times, :] for part in parts])
                for p, i in enumerate(gathered):
                    rows_out[p * rows : (p + 1) * rows, :] = parts[i][times:, :]

            terms, rows_b = call(
                gather_kernel,
                (near(times, rank), near(len(gathered) * rows, rank)),
                parts[::-1],
                len(masks) * times * rank,
            )
            rows_role = holder ^ 1
        else:
            terms = tree(fan(terms, holder, masks))
        holder ^= 1
    last_role = holder
    mate_rows_b = swap(rows_b)

    def ready_kernel(rows, mate_rows, c, w, weighed, scales_a, b_out, base, gain, scale, all_b):
        b = in_order(on_role(rows_role, rows[...], mate_rows[...]), all_b, chips)
        coupled = weighed[...] * dot_rows(b, b)
        step = step_of(coupled)
        base[...] = c[...] - step * dot(c[...], coupled)
        gain[...] = step * w[...]
        scales_b = jnp.sqrt(jnp.sum(b * b, axis=0, keepdims=True) / smp_total + 1e-06)
        scale[...] = w[...] * scales_a[...] * scales_b
        b_out[...] = all_b[pl.ds(pl.multiple_of(smp_index() * smp_rows, smp_rows), smp_rows), :] / scales_b

    sample_result, base, gain, scale = call(
        ready_kernel,
        (far(smp_rows, rank), near(times, rank), near(1, rank), near(1, rank)),
        (rows_b, mate_rows_b, c_near, w_row, weighed, scales_a),
        2 * rank * rank * times * 4,
        scratch=(near(smp_total, rank),),
    )
    terms, base, gain, scale, voxel_result, sample_result = lax.optimization_barrier(
        (terms, base, gain, scale, voxel_result, sample_result)
    )
    mate_terms = swap(terms)

    def finish(terms, base, gain, scale, c_out, w_out, c, w, sems):
        moved = base[...] + terms[...] * gain[...]
        scales_c = jnp.sqrt(jnp.sum(moved * moved, axis=0, keepdims=True) / times + 1e-06)
        c[...] = moved / scales_c
        w[...] = scale[...] * scales_c
        copies = [pltpu.make_async_copy(c, c_out, sems.at[0]), pltpu.make_async_copy(w, w_out, sems.at[1])]
        for copy in copies:
            copy.start()
        for copy in copies:
            copy.wait()

    def mate_kernel(c_in, w_in, *refs):
        finish(*refs)

    results = (far(times, rank), far(1, rank))
    scratch = (near(times, rank), near(1, rank), pltpu.SemaphoreType.DMA((2,)))
    held = call(
        only_on(last_role, finish),
        results,
        (terms, base, gain, scale),
        rank * times * 8,
        scratch=scratch,
        out_space=pltpu.HBM,
    )
    time_result, scale_result = call(
        only_on(1 - last_role, mate_kernel),
        results,
        (*held, mate_terms, base, gain, scale),
        rank * times * 8,
        scratch=scratch,
        in_hbm=2,
        aliases={0: 0, 1: 1},
        out_space=pltpu.HBM,
    )
    return voxel_result, sample_result, time_result, scale_result.reshape(rank)


def solution(mesh):
    return jax.shard_map(
        per_device,
        mesh=mesh,
        in_specs=(P("vox", "smp", None), P("vox", None), P("smp", None), P(), P()),
        out_specs=(P("vox", None), P("smp", None), P(), P()),
        check_vma=False,
    )
```

```python
import jax
import jax.numpy as jnp
from jax import lax
from jax.experimental import pallas as pl
from jax.experimental.pallas import tpu as pltpu
from jax.sharding import PartitionSpec as P

F32 = jnp.float32
BF16 = jnp.bfloat16
VMEM_LIMIT = 12 * 1024 * 1024
ALL = ("vox", "smp")


def halves(a, axis):
    high = a.astype(BF16)
    return jnp.concatenate([high, (a - high.astype(F32)).astype(BF16)], axis=axis)


def both(b):
    parts = halves(b, 1)
    return jnp.concatenate([parts, parts], axis=0)


def fold(product):
    width = product.shape[1] // 2
    return product[:, :width] + product[:, width:]


def dot(a, b):
    return fold(jnp.dot(halves(a, 1), both(b), preferred_element_type=F32))


def dot_rows(a, b):
    return fold(lax.dot_general(halves(a, 0), both(b), (((0,), (0,)), ((), ())), preferred_element_type=F32))


def step_of(coupled):
    sums = jnp.sum(jnp.abs(coupled), axis=0, keepdims=True)
    return 1.0 / jnp.max(sums, axis=1, keepdims=True)


def diagonal_row(gram):
    rows = lax.broadcasted_iota(jnp.int32, gram.shape, 0)
    columns = lax.broadcasted_iota(jnp.int32, gram.shape, 1)
    return jnp.sum(jnp.where(rows == columns, gram, 0.0), axis=0, keepdims=True)


def role_index():
    return (smp_index() ^ lax.axis_index("vox") // 2) & 1


def only_on(role, kernel):
    def run(*refs):
        pl.when(role_index() == role)(lambda: kernel(*refs))

    return run


def call(kernel, outs, operands, flops, scratch=(), in_hbm=0, aliases=None, out_space=pltpu.VMEM):
    spaces = [pltpu.HBM if i < in_hbm else pltpu.VMEM for i in range(len(operands))]
    placed = [pltpu.with_memory_space_constraint(x, space) for x, space in zip(operands, spaces)]
    specs = [pl.BlockSpec(memory_space=space) for space in spaces]
    return pl.pallas_call(
        kernel,
        out_shape=outs,
        in_specs=specs,
        out_specs=[pl.BlockSpec(memory_space=out_space)] * len(outs),
        scratch_shapes=list(scratch),
        input_output_aliases=aliases or {},
        compiler_params=pltpu.CompilerParams(vmem_limit_bytes=VMEM_LIMIT),
        cost_estimate=pl.CostEstimate(flops=flops, bytes_accessed=1 << 16, transcendentals=0),
    )(*placed)


def near(*shape):
    return pltpu.VMEM(shape, F32)


def far(*shape):
    return jax.ShapeDtypeStruct(shape, F32)


def bits_of(count):
    if count & (count - 1):
        raise ValueError("axis size")
    return [1 << b for b in range(count.bit_length() - 1)]


def groups_of(bits, size=2):
    return [bits[i : i + size] for i in range(0, len(bits), size)]


def masks_of(group):
    masks = [0]
    for bit in group:
        masks = [mask | bit for mask in masks] + masks
    return masks


def swap(values):
    return lax.ppermute(values, ALL, [(i, i ^ 1) for i in range(lax.axis_size(ALL))])


def send(values, holder, mask):
    smp_count, count = lax.axis_size("smp"), lax.axis_size(ALL)
    role = lambda i: (i ^ i // (2 * smp_count)) & 1
    pairs = []
    for i in range(count):
        target = i ^ mask if role(i) == holder else i
        pairs.append((i, target ^ 1 if role(target) == role(i) else target))
    return lax.ppermute(values, ALL, pairs)


def fan(values, holder, masks):
    sent = [send(values, holder, mask) if mask else swap(values) for mask in reversed(masks)]
    return sent[::-1]


def tree(parts):
    parts = parts[::-1]
    while len(parts) > 1:
        parts = [a + b for a, b in zip(parts[::2], parts[1::2])]
    return parts[0]


def smp_index():
    return lax.axis_index("smp")


def on_role(role, own, got):
    return jnp.where(role_index() == role, own, got)


def pack(gram):
    half = gram.shape[0] // 2
    rows = lax.broadcasted_iota(jnp.int32, (half, 2 * half), 0)
    columns = lax.broadcasted_iota(jnp.int32, (half, 2 * half), 1)
    top, bottom = gram[:half], gram[half:]
    packed = jnp.where(rows <= columns, top, pltpu.roll(bottom, half, 1))
    return packed, jnp.sum(jnp.where(columns == rows + half, bottom, 0.0), axis=0, keepdims=True)


def unpack(packed, diagonal):
    half = packed.shape[0]
    rows = lax.broadcasted_iota(jnp.int32, packed.shape, 0)
    columns = lax.broadcasted_iota(jnp.int32, packed.shape, 1)
    turned = jnp.concatenate([packed, packed], axis=0).T
    top = jnp.where(rows <= columns, packed, turned[:half])
    corner = jnp.where(columns < rows + half, pltpu.roll(packed, half, 1), turned[:half])
    corner = jnp.where(columns == rows + half, diagonal, corner)
    return jnp.concatenate([top, jnp.where(columns < half, turned[half:], corner)], axis=0)


def in_order(rows, scratch, chips, flip=0):
    size = scratch.shape[0] // chips // 2
    chip = smp_index() // 2
    for p in range(chips):
        for q in range(2):
            start = (2 * p + q) * size
            place = (chip ^ (chips - 1 - p)) * 2 + (q ^ flip)
            scratch[pl.ds(pl.multiple_of(place * size, size), size), :] = rows[start : start + size, :]
    return scratch[...]


def per_device(ensemble, voxel_factor, sample_factor, time_factor, weights):
    vox_rows, smp_rows, times = ensemble.shape
    rank = voxel_factor.shape[1]
    flat_rows = vox_rows * smp_rows
    vox_count, smp_count = lax.axis_size("vox"), lax.axis_size("smp")
    vox_total, smp_total = vox_rows * vox_count, smp_rows * smp_count
    chips, chip_rows = smp_count // 2, 2 * smp_rows
    chip_bits = bits_of(smp_count)[1:]
    vox_bits = [bit * smp_count for bit in bits_of(vox_count)]

    cut = vox_rows // 2

    def contract(x, c, b, con, out, first):
        blocks = [x[pl.ds(first * smp_rows + j, cut, stride=smp_rows), :] for j in range(smp_rows)]
        blocks = jnp.concatenate([halves(block, 1) for block in blocks], axis=0)
        made = fold(jnp.dot(blocks, both(c), preferred_element_type=F32)).reshape(smp_rows, cut, rank)
        con[:, first : first + cut, :] = made
        total = made[0] * b[:1, :]
        for j in range(1, smp_rows):
            total = total + made[j] * b[j : j + 1, :]
        out[:cut, :] = total

    def open_kernel(x_hbm, c_hbm, b_hbm, a_hbm, w_hbm, x, c, a, w, out, con, sems):
        near_half, far_half = pl.ds(0, cut * smp_rows), pl.ds(cut * smp_rows, cut * smp_rows)
        copies = [
            pltpu.make_async_copy(c_hbm, c, sems.at[0]),
            pltpu.make_async_copy(x_hbm.at[near_half, :], x.at[near_half, :], sems.at[1]),
            pltpu.make_async_copy(b_hbm, out.at[pl.ds(cut, smp_rows), :], sems.at[2]),
            pltpu.make_async_copy(x_hbm.at[far_half, :], x.at[far_half, :], sems.at[3]),
            pltpu.make_async_copy(a_hbm, a, sems.at[4]),
            pltpu.make_async_copy(w_hbm, w, sems.at[5]),
        ]
        for copy in copies:
            copy.start()
        for copy in copies[:3]:
            copy.wait()
        contract(x, c[...], out[pl.ds(cut, smp_rows), :], con, out, 0)
        for copy in copies[3:]:
            copy.wait()

    x, c_near, a_near, w_row, opened, con = call(
        open_kernel,
        (
            near(flat_rows, times),
            near(times, rank),
            near(vox_rows, rank),
            near(1, rank),
            near(cut + smp_rows, rank),
            near(smp_rows, vox_rows, rank),
        ),
        (ensemble.reshape(flat_rows, times), time_factor, sample_factor, voxel_factor, weights.reshape(1, rank)),
        flat_rows * times * rank * 4,
        scratch=(pltpu.SemaphoreType.DMA((6,)),),
        in_hbm=5,
    )

    def late_kernel(x, c, opened, con_in, out, con):
        contract(x, c[...], opened[cut:, :], con, out, cut)

    late_opened, con = call(
        late_kernel,
        (near(cut, rank), near(smp_rows, vox_rows, rank)),
        (x, c_near, opened, con),
        flat_rows * times * rank * 4,
        aliases={3: 1},
    )

    def weigh_kernel(c, w, outer, outer_c):
        squared = dot_rows(w[...], w[...])
        outer[...] = squared
        outer_c[...] = squared * dot_rows(c[...], c[...])

    outer, outer_c = call(
        weigh_kernel, (near(rank, rank), near(rank, rank)), (c_near, w_row), 2 * rank * rank * times * 4
    )

    late_x, late_opened = lax.optimization_barrier((x, late_opened))
    got, late_got = swap(opened), swap(late_opened)
    terms, late_terms = opened[:cut] + got[:cut], late_opened + late_got
    mate_con, mate_x = swap(con), swap(late_x)
    packet = jnp.concatenate([terms, got[cut:], opened[cut:]], axis=0)
    own = jnp.concatenate([terms, opened[cut:], got[cut:]], axis=0)
    late_own = late_terms
    holder = 1
    for group in groups_of(chip_bits):
        masks = masks_of(group)[:-1]
        parts = [send(packet, holder, mask) for mask in masks] + [own]
        late_terms = tree([send(late_terms, holder, mask) for mask in masks] + [late_own])
        terms = tree([part[:cut] for part in parts])
        rows_b = jnp.concatenate([part[cut:] for part in parts], axis=0)
        packet = jnp.concatenate([terms, rows_b], axis=0)
        own, late_own = swap(packet), swap(late_terms)
        holder ^= 1
    voxel_role = holder

    half, sums_rows = rank // 2, rank // 2 + chip_rows

    def voxel_kernel(terms, late_terms, rows, a, w, outer_c, con, mate_con, mate_x, moved_out, chip_b, out, all_b):
        b = in_order(rows, all_b, chips, lax.axis_index("vox") // 2 & 1)
        chip_b[...] = all_b[pl.ds(pl.multiple_of(smp_index() // 2 * chip_rows, chip_rows), chip_rows), :]
        coupled = outer_c[...] * dot_rows(b, b)
        terms = jnp.concatenate([terms[...], late_terms[...]], axis=0)
        moved = a[...] - step_of(coupled) * (dot(a[...], coupled) - terms * w[...])
        moved_out[...] = moved
        packed, diagonal = pack(dot_rows(moved, moved))
        out[:half, :] = packed
        core = smp_index() & 1
        for place, source in ((core, con), (1 - core, mate_con)):
            made = [jnp.sum(source[j] * moved, axis=0, keepdims=True) for j in range(smp_rows)]
            start = pl.multiple_of(half + place * smp_rows, smp_rows)
            out[pl.ds(start, smp_rows), :] = jnp.concatenate(made, axis=0)
        out[sums_rows:, :] = jnp.broadcast_to(diagonal, (8, rank))

    moved_a, chip_b, sums = call(
        only_on(voxel_role, voxel_kernel),
        (near(vox_rows, rank), near(chip_rows, rank), near(sums_rows + 8, rank)),
        (terms, late_terms, rows_b, a_near, w_row, outer_c, con, mate_con, mate_x),
        2 * rank * rank * vox_rows * 12,
        scratch=(near(smp_total, rank),),
    )

    mate_moved_a = swap(moved_a)

    for group in groups_of(vox_bits[:1] + vox_bits[:0:-1]):
        sums = tree(fan(sums, holder, masks_of(group)))
        holder ^= 1
    sample_role = holder
    if sample_role != voxel_role:
        chip_b = swap(chip_b)

    def time_kernel(x, mate_x, moved, mate_moved, each):
        moved = on_role(voxel_role, moved[...], mate_moved[...])
        core = smp_index() & 1
        for place, source in ((core, x), (1 - core, mate_x)):
            for j in range(smp_rows):
                block = source[pl.ds(j, vox_rows, stride=smp_rows), :]
                each[place * smp_rows + j] = dot_rows(block, moved)

    (each,) = call(
        only_on(sample_role, time_kernel),
        (near(chip_rows, times, rank),),
        (x, mate_x, moved_a, mate_moved_a),
        4 * flat_rows * times * rank * 6,
    )

    def sample_kernel(sums, b, w, outer_c, each, gram_out, terms, out):
        gram = unpack(sums[:half, :], sums[sums_rows : sums_rows + 1, :])
        gram_out[...] = gram
        coupled = outer_c[...] * gram
        moved = b[...] - step_of(coupled) * (dot(b[...], coupled) - sums[half:sums_rows, :] * w[...])
        out[times:, :] = moved
        total = None
        for j in range(chip_rows):
            made = each[j] * moved[j : j + 1, :]
            total = made if total is None else total + made
        terms[...] = total
        out[:times, :] = total

    gram_a, terms, payload = call(
        only_on(sample_role, sample_kernel),
        (near(rank, rank), near(times, rank), near(times + chip_rows, rank)),
        (sums, chip_b, w_row, outer_c, each),
        2 * rank * rank * chip_rows * 6,
    )
    mate_gram_a = swap(gram_a)

    def scale_kernel(gram, mate_gram, moved, mate_moved, outer, result, scales_out, weighed):
        gram = on_role(sample_role, gram[...], mate_gram[...])
        scales = jnp.sqrt(diagonal_row(gram) / vox_total + 1e-06)
        scales_out[...] = scales
        result[...] = on_role(voxel_role, moved[...], mate_moved[...]) / scales
        weighed[...] = outer[...] * gram

    voxel_result, scales_a, weighed = call(
        scale_kernel,
        (far(vox_rows, rank), near(1, rank), near(rank, rank)),
        (gram_a, mate_gram_a, moved_a, mate_moved_a, outer),
        vox_rows * rank * 8,
    )

    rows_b, rows_role = payload[times:], holder
    smp_mask = sum(chip_bits)
    for group in groups_of(chip_bits + vox_bits[1:2] + vox_bits[:1] + vox_bits[2:]):
        masks = masks_of(group)
        if any(mask & smp_mask for mask in masks):
            packet = payload if rows_b.shape[0] == chip_rows else jnp.concatenate([terms, rows_b], axis=0)
            gathered = [i for i, mask in enumerate(masks) if mask | smp_mask == masks[0] | smp_mask]
            parts = [
                send(packet if i in gathered else terms, holder, mask) if mask else swap(packet if i in gathered else terms)
                for i, mask in enumerate(masks)
            ]
            rows = rows_b.shape[0]

            def gather_kernel(*refs, gathered=gathered, rows=rows):
                parts, (terms, rows_out) = refs[-3::-1], refs[-2:]
                terms[...] = tree([part[:times, :] for part in parts])
                for p, i in enumerate(gathered):
                    rows_out[p * rows : (p + 1) * rows, :] = parts[i][times:, :]

            terms, rows_b = call(
                gather_kernel,
                (near(times, rank), near(len(gathered) * rows, rank)),
                parts[::-1],
                len(masks) * times * rank,
            )
            rows_role = holder ^ 1
        else:
            terms = tree(fan(terms, holder, masks))
        holder ^= 1
    last_role = holder
    mate_rows_b = swap(rows_b)

    def ready_kernel(rows, mate_rows, c, w, weighed, scales_a, b_out, base, gain, scale, all_b):
        b = in_order(on_role(rows_role, rows[...], mate_rows[...]), all_b, chips)
        coupled = weighed[...] * dot_rows(b, b)
        step = step_of(coupled)
        base[...] = c[...] - step * dot(c[...], coupled)
        gain[...] = step * w[...]
        scales_b = jnp.sqrt(jnp.sum(b * b, axis=0, keepdims=True) / smp_total + 1e-06)
        scale[...] = w[...] * scales_a[...] * scales_b
        b_out[...] = all_b[pl.ds(pl.multiple_of(smp_index() * smp_rows, smp_rows), smp_rows), :] / scales_b

    sample_result, base, gain, scale = call(
        ready_kernel,
        (far(smp_rows, rank), near(times, rank), near(1, rank), near(1, rank)),
        (rows_b, mate_rows_b, c_near, w_row, weighed, scales_a),
        2 * rank * rank * times * 4,
        scratch=(near(smp_total, rank),),
    )
    terms, base, gain, scale, voxel_result, sample_result = lax.optimization_barrier(
        (terms, base, gain, scale, voxel_result, sample_result)
    )
    mate_terms = swap(terms)

    def finish(terms, base, gain, scale, c_out, w_out, c, w, sems):
        moved = base[...] + terms[...] * gain[...]
        scales_c = jnp.sqrt(jnp.sum(moved * moved, axis=0, keepdims=True) / times + 1e-06)
        c[...] = moved / scales_c
        w[...] = scale[...] * scales_c
        copies = [pltpu.make_async_copy(c, c_out, sems.at[0]), pltpu.make_async_copy(w, w_out, sems.at[1])]
        for copy in copies:
            copy.start()
        for copy in copies:
            copy.wait()

    def mate_kernel(c_in, w_in, *refs):
        finish(*refs)

    results = (far(times, rank), far(1, rank))
    scratch = (near(times, rank), near(1, rank), pltpu.SemaphoreType.DMA((2,)))
    held = call(
        only_on(last_role, finish),
        results,
        (terms, base, gain, scale),
        rank * times * 8,
        scratch=scratch,
        out_space=pltpu.HBM,
    )
    time_result, scale_result = call(
        only_on(1 - last_role, mate_kernel),
        results,
        (*held, mate_terms, base, gain, scale),
        rank * times * 8,
        scratch=scratch,
        in_hbm=2,
        aliases={0: 0, 1: 1},
        out_space=pltpu.HBM,
    )
    return voxel_result, sample_result, time_result, scale_result.reshape(rank)


def solution(mesh):
    return jax.shard_map(
        per_device,
        mesh=mesh,
        in_specs=(P("vox", "smp", None), P("vox", None), P("smp", None), P(), P()),
        out_specs=(P("vox", None), P("smp", None), P(), P()),
        check_vma=False,
    )
```

```python
import jax
import jax.numpy as jnp
from jax import lax
from jax.experimental import pallas as pl
from jax.experimental.pallas import tpu as pltpu
from jax.sharding import PartitionSpec as P

F32 = jnp.float32
BF16 = jnp.bfloat16
VMEM_LIMIT = 12 * 1024 * 1024
ALL = ("vox", "smp")


def halves(a, axis):
    high = a.astype(BF16)
    return jnp.concatenate([high, (a - high.astype(F32)).astype(BF16)], axis=axis)


def both(b):
    parts = halves(b, 1)
    return jnp.concatenate([parts, parts], axis=0)


def fold(product):
    width = product.shape[1] // 2
    return product[:, :width] + product[:, width:]


def dot(a, b):
    return fold(jnp.dot(halves(a, 1), both(b), preferred_element_type=F32))


def dot_rows(a, b):
    return fold(lax.dot_general(halves(a, 0), both(b), (((0,), (0,)), ((), ())), preferred_element_type=F32))


def step_of(coupled):
    sums = jnp.sum(jnp.abs(coupled), axis=0, keepdims=True)
    return 1.0 / jnp.max(sums, axis=1, keepdims=True)


def diagonal_row(gram):
    rows = lax.broadcasted_iota(jnp.int32, gram.shape, 0)
    columns = lax.broadcasted_iota(jnp.int32, gram.shape, 1)
    return jnp.sum(jnp.where(rows == columns, gram, 0.0), axis=0, keepdims=True)


def role_index():
    return (smp_index() ^ lax.axis_index("vox") // 2) & 1


def only_on(role, kernel):
    def run(*refs):
        pl.when(role_index() == role)(lambda: kernel(*refs))

    return run


def call(kernel, outs, operands, flops, scratch=(), in_hbm=0, aliases=None, out_space=pltpu.VMEM):
    spaces = [pltpu.HBM if i < in_hbm else pltpu.VMEM for i in range(len(operands))]
    placed = [pltpu.with_memory_space_constraint(x, space) for x, space in zip(operands, spaces)]
    specs = [pl.BlockSpec(memory_space=space) for space in spaces]
    return pl.pallas_call(
        kernel,
        out_shape=outs,
        in_specs=specs,
        out_specs=[pl.BlockSpec(memory_space=out_space)] * len(outs),
        scratch_shapes=list(scratch),
        input_output_aliases=aliases or {},
        compiler_params=pltpu.CompilerParams(vmem_limit_bytes=VMEM_LIMIT),
        cost_estimate=pl.CostEstimate(flops=flops, bytes_accessed=1 << 16, transcendentals=0),
    )(*placed)


def near(*shape):
    return pltpu.VMEM(shape, F32)


def far(*shape):
    return jax.ShapeDtypeStruct(shape, F32)


def bits_of(count):
    if count & (count - 1):
        raise ValueError("axis size")
    return [1 << b for b in range(count.bit_length() - 1)]


def groups_of(bits, size=2):
    return [bits[i : i + size] for i in range(0, len(bits), size)]


def masks_of(group):
    masks = [0]
    for bit in group:
        masks = [mask | bit for mask in masks] + masks
    return masks


def swap(values):
    return lax.ppermute(values, ALL, [(i, i ^ 1) for i in range(lax.axis_size(ALL))])


def send(values, holder, mask):
    smp_count, count = lax.axis_size("smp"), lax.axis_size(ALL)
    role = lambda i: (i ^ i // (2 * smp_count)) & 1
    pairs = []
    for i in range(count):
        target = i ^ mask if role(i) == holder else i
        pairs.append((i, target ^ 1 if role(target) == role(i) else target))
    return lax.ppermute(values, ALL, pairs)


def fan(values, holder, masks):
    sent = [send(values, holder, mask) if mask else swap(values) for mask in reversed(masks)]
    return sent[::-1]


def tree(parts):
    parts = parts[::-1]
    while len(parts) > 1:
        parts = [a + b for a, b in zip(parts[::2], parts[1::2])]
    return parts[0]


def smp_index():
    return lax.axis_index("smp")


def on_role(role, own, got):
    return jnp.where(role_index() == role, own, got)


def pack(gram):
    half = gram.shape[0] // 2
    rows = lax.broadcasted_iota(jnp.int32, (half, 2 * half), 0)
    columns = lax.broadcasted_iota(jnp.int32, (half, 2 * half), 1)
    top, bottom = gram[:half], gram[half:]
    packed = jnp.where(rows <= columns, top, pltpu.roll(bottom, half, 1))
    return packed, jnp.sum(jnp.where(columns == rows + half, bottom, 0.0), axis=0, keepdims=True)


def unpack(packed, diagonal):
    half = packed.shape[0]
    rows = lax.broadcasted_iota(jnp.int32, packed.shape, 0)
    columns = lax.broadcasted_iota(jnp.int32, packed.shape, 1)
    turned = jnp.concatenate([packed, packed], axis=0).T
    top = jnp.where(rows <= columns, packed, turned[:half])
    corner = jnp.where(columns < rows + half, pltpu.roll(packed, half, 1), turned[:half])
    corner = jnp.where(columns == rows + half, diagonal, corner)
    return jnp.concatenate([top, jnp.where(columns < half, turned[half:], corner)], axis=0)


def in_order(rows, scratch, chips, flip=0):
    size = scratch.shape[0] // chips // 2
    chip = smp_index() // 2
    for p in range(chips):
        for q in range(2):
            start = (2 * p + q) * size
            place = (chip ^ (chips - 1 - p)) * 2 + (q ^ flip)
            scratch[pl.ds(pl.multiple_of(place * size, size), size), :] = rows[start : start + size, :]
    return scratch[...]


def per_device(ensemble, voxel_factor, sample_factor, time_factor, weights):
    vox_rows, smp_rows, times = ensemble.shape
    rank = voxel_factor.shape[1]
    flat_rows = vox_rows * smp_rows
    vox_count, smp_count = lax.axis_size("vox"), lax.axis_size("smp")
    vox_total, smp_total = vox_rows * vox_count, smp_rows * smp_count
    chips, chip_rows = smp_count // 2, 2 * smp_rows
    chip_bits = bits_of(smp_count)[1:]
    vox_bits = [bit * smp_count for bit in bits_of(vox_count)]

    cut = vox_rows // 2

    def contract(x, c, b, con, out, first):
        blocks = [x[pl.ds(first * smp_rows + j, cut, stride=smp_rows), :] for j in range(smp_rows)]
        blocks = jnp.concatenate([halves(block, 1) for block in blocks], axis=0)
        made = fold(jnp.dot(blocks, both(c), preferred_element_type=F32)).reshape(smp_rows, cut, rank)
        con[:, first : first + cut, :] = made
        total = made[0] * b[:1, :]
        for j in range(1, smp_rows):
            total = total + made[j] * b[j : j + 1, :]
        out[:cut, :] = total

    def open_kernel(x_hbm, c_hbm, b_hbm, x, c, out, con, sems):
        near_half, far_half = pl.ds(0, cut * smp_rows), pl.ds(cut * smp_rows, cut * smp_rows)
        copies = [
            pltpu.make_async_copy(x_hbm.at[near_half, :], x.at[near_half, :], sems.at[0]),
            pltpu.make_async_copy(c_hbm, c, sems.at[1]),
            pltpu.make_async_copy(b_hbm, out.at[pl.ds(cut, smp_rows), :], sems.at[2]),
            pltpu.make_async_copy(x_hbm.at[far_half, :], x.at[far_half, :], sems.at[3]),
        ]
        for copy in copies:
            copy.start()
        for copy in copies[:3]:
            copy.wait()
        contract(x, c[...], out[pl.ds(cut, smp_rows), :], con, out, 0)
        for copy in copies[3:]:
            copy.wait()

    x, c_near, opened, con = call(
        open_kernel,
        (
            near(flat_rows, times),
            near(times, rank),
            near(cut + smp_rows, rank),
            near(smp_rows, vox_rows, rank),
        ),
        (ensemble.reshape(flat_rows, times), time_factor, sample_factor),
        flat_rows * times * rank * 4,
        scratch=(pltpu.SemaphoreType.DMA((4,)),),
        in_hbm=3,
    )

    def late_kernel(x, c, opened, con_in, out, con):
        contract(x, c[...], opened[cut:, :], con, out, cut)

    late_opened, con = call(
        late_kernel,
        (near(cut, rank), near(smp_rows, vox_rows, rank)),
        (x, c_near, opened, con),
        flat_rows * times * rank * 4,
        aliases={3: 1},
    )

    def weigh_kernel(a_hbm, w_hbm, c, a, w, outer, outer_c, sems):
        copies = [pltpu.make_async_copy(w_hbm, w, sems.at[0]), pltpu.make_async_copy(a_hbm, a, sems.at[1])]
        for copy in copies:
            copy.start()
        gram = dot_rows(c[...], c[...])
        copies[0].wait()
        squared = dot_rows(w[...], w[...])
        outer[...] = squared
        outer_c[...] = squared * gram
        copies[1].wait()

    a_near, w_row, outer, outer_c = call(
        weigh_kernel,
        (near(vox_rows, rank), near(1, rank), near(rank, rank), near(rank, rank)),
        (voxel_factor, weights.reshape(1, rank), c_near),
        2 * rank * rank * times * 4,
        scratch=(pltpu.SemaphoreType.DMA((2,)),),
        in_hbm=2,
    )

    late_x, late_opened = lax.optimization_barrier((x, late_opened))
    got, late_got = swap(opened), swap(late_opened)
    terms, late_terms = opened[:cut] + got[:cut], late_opened + late_got
    mate_con, mate_x = swap(con), swap(late_x)
    packet = jnp.concatenate([terms, got[cut:], opened[cut:]], axis=0)
    own = jnp.concatenate([terms, opened[cut:], got[cut:]], axis=0)
    late_own = late_terms
    holder = 1
    for group in groups_of(chip_bits):
        masks = masks_of(group)[:-1]
        parts = [send(packet, holder, mask) for mask in masks] + [own]
        late_terms = tree([send(late_terms, holder, mask) for mask in masks] + [late_own])
        terms = tree([part[:cut] for part in parts])
        rows_b = jnp.concatenate([part[cut:] for part in parts], axis=0)
        packet = jnp.concatenate([terms, rows_b], axis=0)
        own, late_own = swap(packet), swap(late_terms)
        holder ^= 1
    voxel_role = holder

    half, sums_rows = rank // 2, rank // 2 + chip_rows

    def voxel_kernel(terms, late_terms, rows, a, w, outer_c, con, mate_con, mate_x, moved_out, chip_b, out, all_b):
        b = in_order(rows, all_b, chips, lax.axis_index("vox") // 2 & 1)
        chip_b[...] = all_b[pl.ds(pl.multiple_of(smp_index() // 2 * chip_rows, chip_rows), chip_rows), :]
        coupled = outer_c[...] * dot_rows(b, b)
        terms = jnp.concatenate([terms[...], late_terms[...]], axis=0)
        moved = a[...] - step_of(coupled) * (dot(a[...], coupled) - terms * w[...])
        moved_out[...] = moved
        packed, diagonal = pack(dot_rows(moved, moved))
        out[:half, :] = packed
        core = smp_index() & 1
        for place, source in ((core, con), (1 - core, mate_con)):
            made = [jnp.sum(source[j] * moved, axis=0, keepdims=True) for j in range(smp_rows)]
            start = pl.multiple_of(half + place * smp_rows, smp_rows)
            out[pl.ds(start, smp_rows), :] = jnp.concatenate(made, axis=0)
        out[sums_rows:, :] = jnp.broadcast_to(diagonal, (8, rank))

    moved_a, chip_b, sums = call(
        only_on(voxel_role, voxel_kernel),
        (near(vox_rows, rank), near(chip_rows, rank), near(sums_rows + 8, rank)),
        (terms, late_terms, rows_b, a_near, w_row, outer_c, con, mate_con, mate_x),
        2 * rank * rank * vox_rows * 12,
        scratch=(near(smp_total, rank),),
    )

    mate_moved_a = swap(moved_a)

    for group in groups_of(vox_bits[:1] + vox_bits[:0:-1]):
        sums = tree(fan(sums, holder, masks_of(group)))
        holder ^= 1
    sample_role = holder
    if sample_role != voxel_role:
        chip_b = swap(chip_b)

    def time_kernel(x, mate_x, moved, mate_moved, each):
        moved = on_role(voxel_role, moved[...], mate_moved[...])
        core = smp_index() & 1
        for place, source in ((core, x), (1 - core, mate_x)):
            for j in range(smp_rows):
                block = source[pl.ds(j, vox_rows, stride=smp_rows), :]
                each[place * smp_rows + j] = dot_rows(block, moved)

    (each,) = call(
        only_on(sample_role, time_kernel),
        (near(chip_rows, times, rank),),
        (x, mate_x, moved_a, mate_moved_a),
        4 * flat_rows * times * rank * 6,
    )

    def sample_kernel(sums, b, w, outer_c, each, gram_out, out):
        gram = unpack(sums[:half, :], sums[sums_rows : sums_rows + 1, :])
        gram_out[...] = gram
        coupled = outer_c[...] * gram
        moved = b[...] - step_of(coupled) * (dot(b[...], coupled) - sums[half:sums_rows, :] * w[...])
        out[times:, :] = moved
        total = None
        for j in range(chip_rows):
            made = each[j] * moved[j : j + 1, :]
            total = made if total is None else total + made
        out[:times, :] = total

    gram_a, payload = call(
        only_on(sample_role, sample_kernel),
        (near(rank, rank), near(times + chip_rows, rank)),
        (sums, chip_b, w_row, outer_c, each),
        2 * rank * rank * chip_rows * 6,
    )
    mate_gram_a = swap(gram_a)

    def scale_kernel(gram, mate_gram, moved, mate_moved, outer, result, scales_out, weighed):
        gram = on_role(sample_role, gram[...], mate_gram[...])
        scales = jnp.sqrt(diagonal_row(gram) / vox_total + 1e-06)
        scales_out[...] = scales
        result[...] = on_role(voxel_role, moved[...], mate_moved[...]) / scales
        weighed[...] = outer[...] * gram

    voxel_result, scales_a, weighed = call(
        scale_kernel,
        (far(vox_rows, rank), near(1, rank), near(rank, rank)),
        (gram_a, mate_gram_a, moved_a, mate_moved_a, outer),
        vox_rows * rank * 8,
    )

    terms, rows_b, rows_role = payload[:times], payload[times:], holder
    smp_mask = sum(chip_bits)
    for group in groups_of(chip_bits + vox_bits[1:2] + vox_bits[:1] + vox_bits[2:]):
        masks = masks_of(group)
        if any(mask & smp_mask for mask in masks):
            packet = payload if rows_b.shape[0] == chip_rows else jnp.concatenate([terms, rows_b], axis=0)
            parts = fan(packet, holder, masks)
            gathered = [i for i, mask in enumerate(masks) if not mask & ~smp_mask]
            rows = rows_b.shape[0]

            def gather_kernel(*refs, gathered=gathered, rows=rows):
                parts, (terms, rows_out) = refs[-3::-1], refs[-2:]
                terms[...] = tree([part[:times, :] for part in parts])
                for p, i in enumerate(gathered):
                    rows_out[p * rows : (p + 1) * rows, :] = parts[i][times:, :]

            terms, rows_b = call(
                gather_kernel,
                (near(times, rank), near(len(gathered) * rows, rank)),
                parts[::-1],
                len(masks) * times * rank,
            )
            rows_role = holder ^ 1
        else:
            terms = tree(fan(terms, holder, masks))
        holder ^= 1
    last_role = holder
    mate_rows_b = swap(rows_b)

    def ready_kernel(rows, mate_rows, c, w, weighed, scales_a, b_out, base, gain, scale, all_b):
        b = in_order(on_role(rows_role, rows[...], mate_rows[...]), all_b, chips)
        coupled = weighed[...] * dot_rows(b, b)
        step = step_of(coupled)
        base[...] = c[...] - step * dot(c[...], coupled)
        gain[...] = step * w[...]
        scales_b = jnp.sqrt(jnp.sum(b * b, axis=0, keepdims=True) / smp_total + 1e-06)
        scale[...] = w[...] * scales_a[...] * scales_b
        b_out[...] = all_b[pl.ds(pl.multiple_of(smp_index() * smp_rows, smp_rows), smp_rows), :] / scales_b

    sample_result, base, gain, scale = call(
        ready_kernel,
        (far(smp_rows, rank), near(times, rank), near(1, rank), near(1, rank)),
        (rows_b, mate_rows_b, c_near, w_row, weighed, scales_a),
        2 * rank * rank * times * 4,
        scratch=(near(smp_total, rank),),
    )
    terms, base, gain, scale, voxel_result, sample_result = lax.optimization_barrier(
        (terms, base, gain, scale, voxel_result, sample_result)
    )
    mate_terms = swap(terms)

    def finish(terms, base, gain, scale, c_out, w_out, c, w, sems):
        moved = base[...] + terms[...] * gain[...]
        scales_c = jnp.sqrt(jnp.sum(moved * moved, axis=0, keepdims=True) / times + 1e-06)
        c[...] = moved / scales_c
        w[...] = scale[...] * scales_c
        copies = [pltpu.make_async_copy(c, c_out, sems.at[0]), pltpu.make_async_copy(w, w_out, sems.at[1])]
        for copy in copies:
            copy.start()
        for copy in copies:
            copy.wait()

    def mate_kernel(c_in, w_in, *refs):
        finish(*refs)

    results = (far(times, rank), far(1, rank))
    scratch = (near(times, rank), near(1, rank), pltpu.SemaphoreType.DMA((2,)))
    held = call(
        only_on(last_role, finish),
        results,
        (terms, base, gain, scale),
        rank * times * 8,
        scratch=scratch,
        out_space=pltpu.HBM,
    )
    time_result, scale_result = call(
        only_on(1 - last_role, mate_kernel),
        results,
        (*held, mate_terms, base, gain, scale),
        rank * times * 8,
        scratch=scratch,
        in_hbm=2,
        aliases={0: 0, 1: 1},
        out_space=pltpu.HBM,
    )
    return voxel_result, sample_result, time_result, scale_result.reshape(rank)


def solution(mesh):
    return jax.shard_map(
        per_device,
        mesh=mesh,
        in_specs=(P("vox", "smp", None), P("vox", None), P("smp", None), P(), P()),
        out_specs=(P("vox", None), P("smp", None), P(), P()),
        check_vma=False,
    )
```

```python
import jax
import jax.numpy as jnp
from jax import lax
from jax.experimental import pallas as pl
from jax.experimental.pallas import tpu as pltpu
from jax.sharding import PartitionSpec as P

F32 = jnp.float32
BF16 = jnp.bfloat16
VMEM_LIMIT = 12 * 1024 * 1024
ALL = ("vox", "smp")


def halves(a, axis):
    high = a.astype(BF16)
    return jnp.concatenate([high, (a - high.astype(F32)).astype(BF16)], axis=axis)


def both(b):
    parts = halves(b, 1)
    return jnp.concatenate([parts, parts], axis=0)


def fold(product):
    width = product.shape[1] // 2
    return product[:, :width] + product[:, width:]


def dot_halves(parts, b):
    return fold(jnp.dot(parts, both(b), preferred_element_type=F32))


def dot(a, b):
    return dot_halves(halves(a, 1), b)


def dot_rows(a, b):
    return fold(lax.dot_general(halves(a, 0), both(b), (((0,), (0,)), ((), ())), preferred_element_type=F32))


def step_of(coupled):
    sums = jnp.sum(jnp.abs(coupled), axis=0, keepdims=True)
    return 1.0 / jnp.max(sums, axis=1, keepdims=True)


def diagonal_row(gram):
    rows = lax.broadcasted_iota(jnp.int32, gram.shape, 0)
    columns = lax.broadcasted_iota(jnp.int32, gram.shape, 1)
    return jnp.sum(jnp.where(rows == columns, gram, 0.0), axis=0, keepdims=True)


def role_index():
    return (smp_index() ^ lax.axis_index("vox") // 2) & 1


def only_on(role, kernel):
    def run(*refs):
        pl.when(role_index() == role)(lambda: kernel(*refs))

    return run


def call(kernel, outs, operands, flops, scratch=(), in_hbm=0, aliases=None, out_space=pltpu.VMEM):
    spaces = [pltpu.HBM if i < in_hbm else pltpu.VMEM for i in range(len(operands))]
    placed = [pltpu.with_memory_space_constraint(x, space) for x, space in zip(operands, spaces)]
    specs = [pl.BlockSpec(memory_space=space) for space in spaces]
    return pl.pallas_call(
        kernel,
        out_shape=outs,
        in_specs=specs,
        out_specs=[pl.BlockSpec(memory_space=out_space)] * len(outs),
        scratch_shapes=list(scratch),
        input_output_aliases=aliases or {},
        compiler_params=pltpu.CompilerParams(vmem_limit_bytes=VMEM_LIMIT),
        cost_estimate=pl.CostEstimate(flops=flops, bytes_accessed=1 << 16, transcendentals=0),
    )(*placed)


def near(*shape):
    return pltpu.VMEM(shape, F32)


def far(*shape):
    return jax.ShapeDtypeStruct(shape, F32)


def bits_of(count):
    if count & (count - 1):
        raise ValueError("axis size")
    return [1 << b for b in range(count.bit_length() - 1)]


def groups_of(bits, size=2):
    return [bits[i : i + size] for i in range(0, len(bits), size)]


def masks_of(group):
    masks = [0]
    for bit in group:
        masks = [mask | bit for mask in masks] + masks
    return masks


def swap(values):
    return lax.ppermute(values, ALL, [(i, i ^ 1) for i in range(lax.axis_size(ALL))])


def send(values, holder, mask):
    smp_count, count = lax.axis_size("smp"), lax.axis_size(ALL)
    role = lambda i: (i ^ i // (2 * smp_count)) & 1
    pairs = []
    for i in range(count):
        target = i ^ mask if role(i) == holder else i
        pairs.append((i, target ^ 1 if role(target) == role(i) else target))
    return lax.ppermute(values, ALL, pairs)


def fan(values, holder, masks):
    sent = [send(values, holder, mask) if mask else swap(values) for mask in reversed(masks)]
    return sent[::-1]


def tree(parts):
    parts = parts[::-1]
    while len(parts) > 1:
        parts = [a + b for a, b in zip(parts[::2], parts[1::2])]
    return parts[0]


def smp_index():
    return lax.axis_index("smp")


def on_role(role, own, got):
    return jnp.where(role_index() == role, own, got)


def pack(gram):
    half = gram.shape[0] // 2
    rows = lax.broadcasted_iota(jnp.int32, (half, 2 * half), 0)
    columns = lax.broadcasted_iota(jnp.int32, (half, 2 * half), 1)
    top, bottom = gram[:half], gram[half:]
    packed = jnp.where(rows <= columns, top, pltpu.roll(bottom, half, 1))
    return packed, jnp.sum(jnp.where(columns == rows + half, bottom, 0.0), axis=0, keepdims=True)


def unpack(packed, diagonal):
    half = packed.shape[0]
    rows = lax.broadcasted_iota(jnp.int32, packed.shape, 0)
    columns = lax.broadcasted_iota(jnp.int32, packed.shape, 1)
    turned = jnp.concatenate([packed, packed], axis=0).T
    top = jnp.where(rows <= columns, packed, turned[:half])
    corner = jnp.where(columns < rows + half, pltpu.roll(packed, half, 1), turned[:half])
    corner = jnp.where(columns == rows + half, diagonal, corner)
    return jnp.concatenate([top, jnp.where(columns < half, turned[half:], corner)], axis=0)


def in_order(rows, scratch, chips, flip=0):
    size = scratch.shape[0] // chips // 2
    chip = smp_index() // 2
    for p in range(chips):
        for q in range(2):
            start = (2 * p + q) * size
            place = (chip ^ (chips - 1 - p)) * 2 + (q ^ flip)
            scratch[pl.ds(pl.multiple_of(place * size, size), size), :] = rows[start : start + size, :]
    return scratch[...]


def per_device(ensemble, voxel_factor, sample_factor, time_factor, weights):
    vox_rows, smp_rows, times = ensemble.shape
    rank = voxel_factor.shape[1]
    flat_rows = vox_rows * smp_rows
    vox_count, smp_count = lax.axis_size("vox"), lax.axis_size("smp")
    vox_total, smp_total = vox_rows * vox_count, smp_rows * smp_count
    chips, chip_rows = smp_count // 2, 2 * smp_rows
    chip_bits = bits_of(smp_count)[1:]
    vox_bits = [bit * smp_count for bit in bits_of(vox_count)]

    cut = vox_rows // 2

    def contract(x, c, b, con, out, first):
        blocks = [x[pl.ds(first * smp_rows + j, cut, stride=smp_rows), :] for j in range(smp_rows)]
        blocks = jnp.concatenate([halves(block, 1) for block in blocks], axis=0)
        made = fold(jnp.dot(blocks, both(c), preferred_element_type=F32)).reshape(smp_rows, cut, rank)
        con[:, first : first + cut, :] = made
        total = made[0] * b[:1, :]
        for j in range(1, smp_rows):
            total = total + made[j] * b[j : j + 1, :]
        out[:cut, :] = total

    def open_kernel(x_hbm, c_hbm, b_hbm, x, c, out, con, sems):
        near_half, far_half = pl.ds(0, cut * smp_rows), pl.ds(cut * smp_rows, cut * smp_rows)
        copies = [
            pltpu.make_async_copy(x_hbm.at[near_half, :], x.at[near_half, :], sems.at[0]),
            pltpu.make_async_copy(c_hbm, c, sems.at[1]),
            pltpu.make_async_copy(b_hbm, out.at[pl.ds(cut, smp_rows), :], sems.at[2]),
            pltpu.make_async_copy(x_hbm.at[far_half, :], x.at[far_half, :], sems.at[3]),
        ]
        for copy in copies:
            copy.start()
        for copy in copies[:3]:
            copy.wait()
        contract(x, c[...], out[pl.ds(cut, smp_rows), :], con, out, 0)
        for copy in copies[3:]:
            copy.wait()

    x, c_near, opened, con = call(
        open_kernel,
        (
            near(flat_rows, times),
            near(times, rank),
            near(cut + smp_rows, rank),
            near(smp_rows, vox_rows, rank),
        ),
        (ensemble.reshape(flat_rows, times), time_factor, sample_factor),
        flat_rows * times * rank * 4,
        scratch=(pltpu.SemaphoreType.DMA((4,)),),
        in_hbm=3,
    )

    def late_kernel(x, c, opened, con_in, out, con):
        contract(x, c[...], opened[cut:, :], con, out, cut)

    late_opened, con = call(
        late_kernel,
        (near(cut, rank), near(smp_rows, vox_rows, rank)),
        (x, c_near, opened, con),
        flat_rows * times * rank * 4,
        aliases={3: 1},
    )

    def weigh_kernel(a_hbm, w_hbm, c, a, w, outer, outer_c, a_parts, sems):
        copies = [pltpu.make_async_copy(w_hbm, w, sems.at[0]), pltpu.make_async_copy(a_hbm, a, sems.at[1])]
        for copy in copies:
            copy.start()
        gram = dot_rows(c[...], c[...])
        copies[0].wait()
        squared = dot_rows(w[...], w[...])
        outer[...] = squared
        outer_c[...] = squared * gram
        copies[1].wait()
        a_parts[...] = halves(a[...], 1)

    a_near, w_row, outer, outer_c, a_parts = call(
        weigh_kernel,
        (
            near(vox_rows, rank),
            near(1, rank),
            near(rank, rank),
            near(rank, rank),
            pltpu.VMEM((vox_rows, 2 * rank), BF16),
        ),
        (voxel_factor, weights.reshape(1, rank), c_near),
        2 * rank * rank * times * 4,
        scratch=(pltpu.SemaphoreType.DMA((2,)),),
        in_hbm=2,
    )

    late_x, late_opened = lax.optimization_barrier((x, late_opened))
    got, late_got = swap(opened), swap(late_opened)
    terms, late_terms = opened[:cut] + got[:cut], late_opened + late_got
    mate_con, mate_x = swap(con), swap(late_x)
    packet = jnp.concatenate([terms, got[cut:], opened[cut:]], axis=0)
    own = jnp.concatenate([terms, opened[cut:], got[cut:]], axis=0)
    late_own = late_terms
    holder = 1
    for group in groups_of(chip_bits):
        masks = masks_of(group)[:-1]
        parts = [send(packet, holder, mask) for mask in masks] + [own]
        late_terms = tree([send(late_terms, holder, mask) for mask in masks] + [late_own])
        terms = tree([part[:cut] for part in parts])
        rows_b = jnp.concatenate([part[cut:] for part in parts], axis=0)
        packet = jnp.concatenate([terms, rows_b], axis=0)
        own, late_own = swap(packet), swap(late_terms)
        holder ^= 1
    voxel_role = holder

    half, sums_rows = rank // 2, rank // 2 + chip_rows

    def voxel_kernel(terms, late_terms, rows, a, a_parts, w, outer_c, con, mate_con, mate_x, moved_out, chip_b, out, all_b):
        b = in_order(rows, all_b, chips, lax.axis_index("vox") // 2 & 1)
        chip_b[...] = all_b[pl.ds(pl.multiple_of(smp_index() // 2 * chip_rows, chip_rows), chip_rows), :]
        coupled = outer_c[...] * dot_rows(b, b)
        terms = jnp.concatenate([terms[...], late_terms[...]], axis=0)
        moved = a[...] - step_of(coupled) * (dot_halves(a_parts[...], coupled) - terms * w[...])
        moved_out[...] = moved
        packed, diagonal = pack(dot_rows(moved, moved))
        out[:half, :] = packed
        core = smp_index() & 1
        for place, source in ((core, con), (1 - core, mate_con)):
            made = [jnp.sum(source[j] * moved, axis=0, keepdims=True) for j in range(smp_rows)]
            start = pl.multiple_of(half + place * smp_rows, smp_rows)
            out[pl.ds(start, smp_rows), :] = jnp.concatenate(made, axis=0)
        out[sums_rows:, :] = jnp.broadcast_to(diagonal, (8, rank))

    moved_a, chip_b, sums = call(
        only_on(voxel_role, voxel_kernel),
        (near(vox_rows, rank), near(chip_rows, rank), near(sums_rows + 8, rank)),
        (terms, late_terms, rows_b, a_near, a_parts, w_row, outer_c, con, mate_con, mate_x),
        2 * rank * rank * vox_rows * 12,
        scratch=(near(smp_total, rank),),
    )

    mate_moved_a = swap(moved_a)

    for group in groups_of(vox_bits[:1] + vox_bits[:0:-1]):
        sums = tree(fan(sums, holder, masks_of(group)))
        holder ^= 1
    sample_role = holder
    if sample_role != voxel_role:
        chip_b = swap(chip_b)

    def time_kernel(x, mate_x, moved, mate_moved, each):
        moved = on_role(voxel_role, moved[...], mate_moved[...])
        core = smp_index() & 1
        for place, source in ((core, x), (1 - core, mate_x)):
            for j in range(smp_rows):
                block = source[pl.ds(j, vox_rows, stride=smp_rows), :]
                each[place * smp_rows + j] = dot_rows(block, moved)

    (each,) = call(
        only_on(sample_role, time_kernel),
        (near(chip_rows, times, rank),),
        (x, mate_x, moved_a, mate_moved_a),
        4 * flat_rows * times * rank * 6,
    )

    def sample_kernel(sums, b, w, outer_c, each, gram_out, out):
        gram = unpack(sums[:half, :], sums[sums_rows : sums_rows + 1, :])
        gram_out[...] = gram
        coupled = outer_c[...] * gram
        moved = b[...] - step_of(coupled) * (dot(b[...], coupled) - sums[half:sums_rows, :] * w[...])
        out[times:, :] = moved
        total = None
        for j in range(chip_rows):
            made = each[j] * moved[j : j + 1, :]
            total = made if total is None else total + made
        out[:times, :] = total

    gram_a, payload = call(
        only_on(sample_role, sample_kernel),
        (near(rank, rank), near(times + chip_rows, rank)),
        (sums, chip_b, w_row, outer_c, each),
        2 * rank * rank * chip_rows * 6,
    )
    mate_gram_a = swap(gram_a)

    def scale_kernel(gram, mate_gram, moved, mate_moved, outer, result, scales_out, weighed):
        gram = on_role(sample_role, gram[...], mate_gram[...])
        scales = jnp.sqrt(diagonal_row(gram) / vox_total + 1e-06)
        scales_out[...] = scales
        result[...] = on_role(voxel_role, moved[...], mate_moved[...]) / scales
        weighed[...] = outer[...] * gram

    voxel_result, scales_a, weighed = call(
        scale_kernel,
        (far(vox_rows, rank), near(1, rank), near(rank, rank)),
        (gram_a, mate_gram_a, moved_a, mate_moved_a, outer),
        vox_rows * rank * 8,
    )

    terms, rows_b, rows_role = payload[:times], payload[times:], holder
    smp_mask = sum(chip_bits)
    for group in groups_of(chip_bits + vox_bits[1:2] + vox_bits[:1] + vox_bits[2:]):
        masks = masks_of(group)
        if any(mask & smp_mask for mask in masks):
            packet = payload if rows_b.shape[0] == chip_rows else jnp.concatenate([terms, rows_b], axis=0)
            parts = fan(packet, holder, masks)
            gathered = [i for i, mask in enumerate(masks) if not mask & ~smp_mask]
            rows = rows_b.shape[0]

            def gather_kernel(*refs, gathered=gathered, rows=rows):
                parts, (terms, rows_out) = refs[-3::-1], refs[-2:]
                terms[...] = tree([part[:times, :] for part in parts])
                for p, i in enumerate(gathered):
                    rows_out[p * rows : (p + 1) * rows, :] = parts[i][times:, :]

            terms, rows_b = call(
                gather_kernel,
                (near(times, rank), near(len(gathered) * rows, rank)),
                parts[::-1],
                len(masks) * times * rank,
            )
            rows_role = holder ^ 1
        else:
            terms = tree(fan(terms, holder, masks))
        holder ^= 1
    last_role = holder
    mate_rows_b = swap(rows_b)

    def ready_kernel(rows, mate_rows, c, w, weighed, scales_a, b_out, base, gain, scale, all_b):
        b = in_order(on_role(rows_role, rows[...], mate_rows[...]), all_b, chips)
        coupled = weighed[...] * dot_rows(b, b)
        step = step_of(coupled)
        base[...] = c[...] - step * dot(c[...], coupled)
        gain[...] = step * w[...]
        scales_b = jnp.sqrt(jnp.sum(b * b, axis=0, keepdims=True) / smp_total + 1e-06)
        scale[...] = w[...] * scales_a[...] * scales_b
        b_out[...] = all_b[pl.ds(pl.multiple_of(smp_index() * smp_rows, smp_rows), smp_rows), :] / scales_b

    sample_result, base, gain, scale = call(
        ready_kernel,
        (far(smp_rows, rank), near(times, rank), near(1, rank), near(1, rank)),
        (rows_b, mate_rows_b, c_near, w_row, weighed, scales_a),
        2 * rank * rank * times * 4,
        scratch=(near(smp_total, rank),),
    )
    terms, base, gain, scale, voxel_result, sample_result = lax.optimization_barrier(
        (terms, base, gain, scale, voxel_result, sample_result)
    )
    mate_terms = swap(terms)

    def finish(terms, base, gain, scale, c_out, w_out, c, w, sems):
        moved = base[...] + terms[...] * gain[...]
        scales_c = jnp.sqrt(jnp.sum(moved * moved, axis=0, keepdims=True) / times + 1e-06)
        c[...] = moved / scales_c
        w[...] = scale[...] * scales_c
        copies = [pltpu.make_async_copy(c, c_out, sems.at[0]), pltpu.make_async_copy(w, w_out, sems.at[1])]
        for copy in copies:
            copy.start()
        for copy in copies:
            copy.wait()

    def mate_kernel(c_in, w_in, *refs):
        finish(*refs)

    results = (far(times, rank), far(1, rank))
    scratch = (near(times, rank), near(1, rank), pltpu.SemaphoreType.DMA((2,)))
    held = call(
        only_on(last_role, finish),
        results,
        (terms, base, gain, scale),
        rank * times * 8,
        scratch=scratch,
        out_space=pltpu.HBM,
    )
    time_result, scale_result = call(
        only_on(1 - last_role, mate_kernel),
        results,
        (*held, mate_terms, base, gain, scale),
        rank * times * 8,
        scratch=scratch,
        in_hbm=2,
        aliases={0: 0, 1: 1},
        out_space=pltpu.HBM,
    )
    return voxel_result, sample_result, time_result, scale_result.reshape(rank)


def solution(mesh):
    return jax.shard_map(
        per_device,
        mesh=mesh,
        in_specs=(P("vox", "smp", None), P("vox", None), P("smp", None), P(), P()),
        out_specs=(P("vox", None), P("smp", None), P(), P()),
        check_vma=False,
    )
```

```python
import jax
import jax.numpy as jnp
from jax import lax
from jax.experimental import pallas as pl
from jax.experimental.pallas import tpu as pltpu
from jax.sharding import PartitionSpec as P

F32 = jnp.float32
BF16 = jnp.bfloat16
VMEM_LIMIT = 12 * 1024 * 1024
ALL = ("vox", "smp")


def halves(a, axis):
    high = a.astype(BF16)
    return jnp.concatenate([high, (a - high.astype(F32)).astype(BF16)], axis=axis)


def both(b):
    parts = halves(b, 1)
    return jnp.concatenate([parts, parts], axis=0)


def fold(product):
    width = product.shape[1] // 2
    return product[:, :width] + product[:, width:]


def dot(a, b):
    return fold(jnp.dot(halves(a, 1), both(b), preferred_element_type=F32))


def dot_rows(a, b):
    return fold(lax.dot_general(halves(a, 0), both(b), (((0,), (0,)), ((), ())), preferred_element_type=F32))


def step_of(coupled):
    sums = jnp.sum(jnp.abs(coupled), axis=0, keepdims=True)
    return 1.0 / jnp.max(sums, axis=1, keepdims=True)


def diagonal_row(gram):
    rows = lax.broadcasted_iota(jnp.int32, gram.shape, 0)
    columns = lax.broadcasted_iota(jnp.int32, gram.shape, 1)
    return jnp.sum(jnp.where(rows == columns, gram, 0.0), axis=0, keepdims=True)


def role_index():
    return (smp_index() ^ lax.axis_index("vox") // 2) & 1


def only_on(role, kernel):
    def run(*refs):
        pl.when(role_index() == role)(lambda: kernel(*refs))

    return run


def call(kernel, outs, operands, flops, scratch=(), in_hbm=0, aliases=None, out_space=pltpu.VMEM):
    spaces = [pltpu.HBM if i < in_hbm else pltpu.VMEM for i in range(len(operands))]
    placed = [pltpu.with_memory_space_constraint(x, space) for x, space in zip(operands, spaces)]
    specs = [pl.BlockSpec(memory_space=space) for space in spaces]
    return pl.pallas_call(
        kernel,
        out_shape=outs,
        in_specs=specs,
        out_specs=[pl.BlockSpec(memory_space=out_space)] * len(outs),
        scratch_shapes=list(scratch),
        input_output_aliases=aliases or {},
        compiler_params=pltpu.CompilerParams(vmem_limit_bytes=VMEM_LIMIT),
        cost_estimate=pl.CostEstimate(flops=flops, bytes_accessed=1 << 16, transcendentals=0),
    )(*placed)


def near(*shape):
    return pltpu.VMEM(shape, F32)


def far(*shape):
    return jax.ShapeDtypeStruct(shape, F32)


def bits_of(count):
    if count & (count - 1):
        raise ValueError("axis size")
    return [1 << b for b in range(count.bit_length() - 1)]


def groups_of(bits, size=2):
    return [bits[i : i + size] for i in range(0, len(bits), size)]


def masks_of(group):
    masks = [0]
    for bit in group:
        masks = [mask | bit for mask in masks] + masks
    return masks


def swap(values):
    return lax.ppermute(values, ALL, [(i, i ^ 1) for i in range(lax.axis_size(ALL))])


def send(values, holder, mask):
    smp_count, count = lax.axis_size("smp"), lax.axis_size(ALL)
    role = lambda i: (i ^ i // (2 * smp_count)) & 1
    pairs = []
    for i in range(count):
        target = i ^ mask if role(i) == holder else i
        pairs.append((i, target ^ 1 if role(target) == role(i) else target))
    return lax.ppermute(values, ALL, pairs)


def fan(values, holder, masks):
    sent = [send(values, holder, mask) if mask else swap(values) for mask in reversed(masks)]
    return sent[::-1]


def tree(parts):
    parts = parts[::-1]
    while len(parts) > 1:
        parts = [a + b for a, b in zip(parts[::2], parts[1::2])]
    return parts[0]


def smp_index():
    return lax.axis_index("smp")


def on_role(role, own, got):
    return jnp.where(role_index() == role, own, got)


def pack(gram):
    half = gram.shape[0] // 2
    rows = lax.broadcasted_iota(jnp.int32, (half, 2 * half), 0)
    columns = lax.broadcasted_iota(jnp.int32, (half, 2 * half), 1)
    top, bottom = gram[:half], gram[half:]
    packed = jnp.where(rows <= columns, top, pltpu.roll(bottom, half, 1))
    return packed, jnp.sum(jnp.where(columns == rows + half, bottom, 0.0), axis=0, keepdims=True)


def unpack(packed, diagonal):
    half = packed.shape[0]
    rows = lax.broadcasted_iota(jnp.int32, packed.shape, 0)
    columns = lax.broadcasted_iota(jnp.int32, packed.shape, 1)
    turned = jnp.concatenate([packed, packed], axis=0).T
    top = jnp.where(rows <= columns, packed, turned[:half])
    corner = jnp.where(columns < rows + half, pltpu.roll(packed, half, 1), turned[:half])
    corner = jnp.where(columns == rows + half, diagonal, corner)
    return jnp.concatenate([top, jnp.where(columns < half, turned[half:], corner)], axis=0)


def in_order(rows, scratch, chips, flip=0):
    size = scratch.shape[0] // chips // 2
    chip = smp_index() // 2
    for p in range(chips):
        for q in range(2):
            start = (2 * p + q) * size
            place = (chip ^ (chips - 1 - p)) * 2 + (q ^ flip)
            scratch[pl.ds(pl.multiple_of(place * size, size), size), :] = rows[start : start + size, :]
    return scratch[...]


def per_device(ensemble, voxel_factor, sample_factor, time_factor, weights):
    vox_rows, smp_rows, times = ensemble.shape
    rank = voxel_factor.shape[1]
    flat_rows = vox_rows * smp_rows
    vox_count, smp_count = lax.axis_size("vox"), lax.axis_size("smp")
    vox_total, smp_total = vox_rows * vox_count, smp_rows * smp_count
    chips, chip_rows = smp_count // 2, 2 * smp_rows
    chip_bits = bits_of(smp_count)[1:]
    vox_bits = [bit * smp_count for bit in bits_of(vox_count)]

    cut = vox_rows // 2

    def contract(x, c, b, con, out, first):
        blocks = [x[pl.ds(first * smp_rows + j, cut, stride=smp_rows), :] for j in range(smp_rows)]
        blocks = jnp.concatenate([halves(block, 1) for block in blocks], axis=0)
        made = fold(jnp.dot(blocks, both(c), preferred_element_type=F32)).reshape(smp_rows, cut, rank)
        con[:, first : first + cut, :] = made
        total = made[0] * b[:1, :]
        for j in range(1, smp_rows):
            total = total + made[j] * b[j : j + 1, :]
        out[:cut, :] = total

    def open_kernel(x_hbm, c_hbm, b_hbm, x, c, out, con, sems):
        near_half, far_half = pl.ds(0, cut * smp_rows), pl.ds(cut * smp_rows, cut * smp_rows)
        copies = [
            pltpu.make_async_copy(x_hbm.at[near_half, :], x.at[near_half, :], sems.at[0]),
            pltpu.make_async_copy(c_hbm, c, sems.at[1]),
            pltpu.make_async_copy(b_hbm, out.at[pl.ds(cut, smp_rows), :], sems.at[2]),
            pltpu.make_async_copy(x_hbm.at[far_half, :], x.at[far_half, :], sems.at[3]),
        ]
        for copy in copies:
            copy.start()
        for copy in copies[:3]:
            copy.wait()
        contract(x, c[...], out[pl.ds(cut, smp_rows), :], con, out, 0)
        for copy in copies[3:]:
            copy.wait()

    x, c_near, opened, con = call(
        open_kernel,
        (
            near(flat_rows, times),
            near(times, rank),
            near(cut + smp_rows, rank),
            near(smp_rows, vox_rows, rank),
        ),
        (ensemble.reshape(flat_rows, times), time_factor, sample_factor),
        flat_rows * times * rank * 4,
        scratch=(pltpu.SemaphoreType.DMA((4,)),),
        in_hbm=3,
    )

    def late_kernel(x, c, opened, con_in, out, con):
        contract(x, c[...], opened[cut:, :], con, out, cut)

    late_opened, con = call(
        late_kernel,
        (near(cut, rank), near(smp_rows, vox_rows, rank)),
        (x, c_near, opened, con),
        flat_rows * times * rank * 4,
        aliases={3: 1},
    )

    def weigh_kernel(a_hbm, w_hbm, c, a, w, outer, outer_c, sems):
        copies = [pltpu.make_async_copy(w_hbm, w, sems.at[0]), pltpu.make_async_copy(a_hbm, a, sems.at[1])]
        for copy in copies:
            copy.start()
        gram = dot_rows(c[...], c[...])
        copies[0].wait()
        squared = dot_rows(w[...], w[...])
        outer[...] = squared
        outer_c[...] = squared * gram
        copies[1].wait()

    a_near, w_row, outer, outer_c = call(
        weigh_kernel,
        (near(vox_rows, rank), near(1, rank), near(rank, rank), near(rank, rank)),
        (voxel_factor, weights.reshape(1, rank), c_near),
        2 * rank * rank * times * 4,
        scratch=(pltpu.SemaphoreType.DMA((2,)),),
        in_hbm=2,
    )

    late_x, late_opened = lax.optimization_barrier((x, late_opened))
    got, late_got = swap(opened), swap(late_opened)
    terms, late_terms = opened[:cut] + got[:cut], late_opened + late_got
    mate_con, mate_x = swap(con), swap(late_x)
    packet = jnp.concatenate([terms, got[cut:], opened[cut:]], axis=0)
    own = jnp.concatenate([terms, opened[cut:], got[cut:]], axis=0)
    late_own = late_terms
    holder = 1
    for group in groups_of(chip_bits):
        masks = masks_of(group)[:-1]
        parts = [send(packet, holder, mask) for mask in masks] + [own]
        late_terms = tree([send(late_terms, holder, mask) for mask in masks] + [late_own])
        terms = tree([part[:cut] for part in parts])
        rows_b = jnp.concatenate([part[cut:] for part in parts], axis=0)
        packet = jnp.concatenate([terms, rows_b], axis=0)
        own, late_own = swap(packet), swap(late_terms)
        holder ^= 1
    voxel_role = holder

    half, sums_rows = rank // 2, rank // 2 + chip_rows

    def voxel_kernel(terms, late_terms, rows, a, w, outer_c, con, mate_con, mate_x, moved_out, chip_b, out, all_b):
        b = in_order(rows, all_b, chips, lax.axis_index("vox") // 2 & 1)
        chip_b[...] = all_b[pl.ds(pl.multiple_of(smp_index() // 2 * chip_rows, chip_rows), chip_rows), :]
        coupled = outer_c[...] * dot_rows(b, b)
        terms = jnp.concatenate([terms[...], late_terms[...]], axis=0)
        moved = a[...] - step_of(coupled) * (dot(a[...], coupled) - terms * w[...])
        moved_out[...] = moved
        packed, diagonal = pack(dot_rows(moved, moved))
        out[:half, :] = packed
        core = smp_index() & 1
        for place, source in ((core, con), (1 - core, mate_con)):
            made = [jnp.sum(source[j] * moved, axis=0, keepdims=True) for j in range(smp_rows)]
            start = pl.multiple_of(half + place * smp_rows, smp_rows)
            out[pl.ds(start, smp_rows), :] = jnp.concatenate(made, axis=0)
        out[sums_rows:, :] = jnp.broadcast_to(diagonal, (8, rank))

    moved_a, chip_b, sums = call(
        only_on(voxel_role, voxel_kernel),
        (near(vox_rows, rank), near(chip_rows, rank), near(sums_rows + 8, rank)),
        (terms, late_terms, rows_b, a_near, w_row, outer_c, con, mate_con, mate_x),
        2 * rank * rank * vox_rows * 12,
        scratch=(near(smp_total, rank),),
    )

    mate_moved_a = swap(moved_a)

    for group in groups_of(vox_bits[:1] + vox_bits[:0:-1]):
        sums = tree(fan(sums, holder, masks_of(group)))
        holder ^= 1
    sample_role = holder
    if sample_role != voxel_role:
        chip_b = swap(chip_b)

    def time_kernel(x, mate_x, moved, mate_moved, each):
        moved = on_role(voxel_role, moved[...], mate_moved[...])
        core = smp_index() & 1
        for place, source in ((core, x), (1 - core, mate_x)):
            for j in range(smp_rows):
                block = source[pl.ds(j, vox_rows, stride=smp_rows), :]
                each[place * smp_rows + j] = dot_rows(block, moved)

    (each,) = call(
        only_on(sample_role, time_kernel),
        (near(chip_rows, times, rank),),
        (x, mate_x, moved_a, mate_moved_a),
        4 * flat_rows * times * rank * 6,
    )

    def sample_kernel(sums, b, w, outer_c, each, gram_out, out):
        gram = unpack(sums[:half, :], sums[sums_rows : sums_rows + 1, :])
        gram_out[...] = gram
        coupled = outer_c[...] * gram
        moved = b[...] - step_of(coupled) * (dot(b[...], coupled) - sums[half:sums_rows, :] * w[...])
        out[times:, :] = moved
        total = None
        for j in range(chip_rows):
            made = each[j] * moved[j : j + 1, :]
            total = made if total is None else total + made
        out[:times, :] = total

    gram_a, payload = call(
        only_on(sample_role, sample_kernel),
        (near(rank, rank), near(times + chip_rows, rank)),
        (sums, chip_b, w_row, outer_c, each),
        2 * rank * rank * chip_rows * 6,
    )
    mate_gram_a = swap(gram_a)

    def scale_kernel(gram, mate_gram, moved, mate_moved, outer, result, scales_out, weighed):
        gram = on_role(sample_role, gram[...], mate_gram[...])
        scales = jnp.sqrt(diagonal_row(gram) / vox_total + 1e-06)
        scales_out[...] = scales
        result[...] = on_role(voxel_role, moved[...], mate_moved[...]) / scales
        weighed[...] = outer[...] * gram

    voxel_result, scales_a, weighed = call(
        scale_kernel,
        (far(vox_rows, rank), near(1, rank), near(rank, rank)),
        (gram_a, mate_gram_a, moved_a, mate_moved_a, outer),
        vox_rows * rank * 8,
    )

    terms, rows_b, rows_role = payload[:times], payload[times:], holder
    smp_mask = sum(chip_bits)
    for group in groups_of(chip_bits + vox_bits[1:2] + vox_bits[:1] + vox_bits[2:]):
        masks = masks_of(group)
        if any(mask & smp_mask for mask in masks):
            packet = payload if rows_b.shape[0] == chip_rows else jnp.concatenate([terms, rows_b], axis=0)
            parts = fan(packet, holder, masks)
            gathered = [i for i, mask in enumerate(masks) if not mask & ~smp_mask]
            rows = rows_b.shape[0]

            def gather_kernel(*refs, gathered=gathered, rows=rows):
                parts, (terms, rows_out) = refs[-3::-1], refs[-2:]
                terms[...] = tree([part[:times, :] for part in parts])
                for p, i in enumerate(gathered):
                    rows_out[p * rows : (p + 1) * rows, :] = parts[i][times:, :]

            terms, rows_b = call(
                gather_kernel,
                (near(times, rank), near(len(gathered) * rows, rank)),
                parts[::-1],
                len(masks) * times * rank,
            )
            rows_role = holder ^ 1
        else:
            terms = tree(fan(terms, holder, masks))
        holder ^= 1
    last_role = holder
    mate_rows_b = swap(rows_b)

    def ready_kernel(rows, mate_rows, c, w, weighed, scales_a, b_out, base, gain, scale, all_b):
        b = in_order(on_role(rows_role, rows[...], mate_rows[...]), all_b, chips)
        coupled = weighed[...] * dot_rows(b, b)
        step = step_of(coupled)
        base[...] = c[...] - step * dot(c[...], coupled)
        gain[...] = step * w[...]
        scales_b = jnp.sqrt(jnp.sum(b * b, axis=0, keepdims=True) / smp_total + 1e-06)
        scale[...] = w[...] * scales_a[...] * scales_b
        b_out[...] = all_b[pl.ds(pl.multiple_of(smp_index() * smp_rows, smp_rows), smp_rows), :] / scales_b

    sample_result, base, gain, scale = call(
        ready_kernel,
        (far(smp_rows, rank), near(times, rank), near(1, rank), near(1, rank)),
        (rows_b, mate_rows_b, c_near, w_row, weighed, scales_a),
        2 * rank * rank * times * 4,
        scratch=(near(smp_total, rank),),
    )
    terms, base, gain, scale, voxel_result, sample_result = lax.optimization_barrier(
        (terms, base, gain, scale, voxel_result, sample_result)
    )
    mate_terms = swap(terms)

    def finish(terms, base, gain, scale, c_out, w_out, c, w, sems):
        moved = base[...] + terms[...] * gain[...]
        scales_c = jnp.sqrt(jnp.sum(moved * moved, axis=0, keepdims=True) / times + 1e-06)
        w[...] = scale[...] * scales_c
        copies = [pltpu.make_async_copy(w, w_out, sems.at[0])]
        copies[0].start()
        for n in range(2):
            rows = pl.ds(n * (times // 2), times // 2)
            c[rows, :] = moved[n * (times // 2) : (n + 1) * (times // 2), :] / scales_c
            copies.append(pltpu.make_async_copy(c.at[rows, :], c_out.at[rows, :], sems.at[1 + n]))
            copies[-1].start()
        for copy in copies:
            copy.wait()

    def mate_kernel(c_in, w_in, *refs):
        finish(*refs)

    results = (far(times, rank), far(1, rank))
    scratch = (near(times, rank), near(1, rank), pltpu.SemaphoreType.DMA((3,)))
    held = call(
        only_on(last_role, finish),
        results,
        (terms, base, gain, scale),
        rank * times * 8,
        scratch=scratch,
        out_space=pltpu.HBM,
    )
    time_result, scale_result = call(
        only_on(1 - last_role, mate_kernel),
        results,
        (*held, mate_terms, base, gain, scale),
        rank * times * 8,
        scratch=scratch,
        in_hbm=2,
        aliases={0: 0, 1: 1},
        out_space=pltpu.HBM,
    )
    return voxel_result, sample_result, time_result, scale_result.reshape(rank)


def solution(mesh):
    return jax.shard_map(
        per_device,
        mesh=mesh,
        in_specs=(P("vox", "smp", None), P("vox", None), P("smp", None), P(), P()),
        out_specs=(P("vox", None), P("smp", None), P(), P()),
        check_vma=False,
    )
```
